128 devices in a mesh: dp: 8 (over y, x_lo), tensor: 16 (over z, x_hi, core).
Axes of the slice: x: 4 (x_hi: 2, x_lo: 2; x = x_hi * 2 + x_lo), y: 4, z: 4, core: 2. Of those that a mesh axis runs over, the one named last changes fastest.
Arguments:
- hidden: bfloat16 [8, 2048, 1024], P('dp', 'tensor'), may hold values from -6 to 6
- seg_ids: int32 [8, 2048], P('dp'), may hold values from 0 to 7, never falling along the last dimension, each value on 1 to 800 neighbouring positions
- key_mask: int32 [8, 2048], P('dp'), may hold values 0 or 1
- routes: int32 [8, 2048, 8], P('dp'), may hold values from 0 to 31, all different within a row; in each aligned block of 2048 rows (0 to 2047, 2048 to 4095, ..., all dimensions but the last counted through in order) at most 1024 rows name the same one
- gain_attn: bfloat16 [1024], P(('dp', 'tensor')), may hold values from 0.5 to 1.5
- w_query: bfloat16 [1024, 1024], P('dp', 'tensor'), may hold values from -0.1875 to 0.1875
- w_keyval: bfloat16 [1024, 1024], P(('dp', 'tensor')), may hold values from -0.1875 to 0.1875
- w_out: bfloat16 [1024, 1024], P(None, ('dp', 'tensor')), may hold values from -0.5 to 0.5
- gain_mlp: bfloat16 [1024], P(('dp', 'tensor')), may hold values from 0.5 to 1.5
- w_router: bfloat16 [1024, 32], P(('dp', 'tensor')), may hold values from -0.09375 to 0.09375
- w_gate_up: bfloat16 [32, 1024, 1024], P('tensor', 'dp'), may hold values from -0.1875 to 0.1875
- w_down: bfloat16 [32, 512, 1024], P('tensor', None, 'dp'), may hold values from -0.5 to 0.5
- cotangent: bfloat16 [8, 2048, 1024], P('dp', 'tensor'), may hold values from -6 to 6
Outputs:
- output: bfloat16 [8, 2048, 1024], P('dp', 'tensor')
- grad_hidden: bfloat16 [8, 2048, 1024], P('dp', 'tensor')
- grad_gain_attn: float32 [1024], P(('dp', 'tensor'))
- grad_query: float32 [1024, 1024], P('dp', 'tensor')
- grad_keyval: float32 [1024, 1024], P(('dp', 'tensor'))
- grad_out: float32 [1024, 1024], P(None, ('dp', 'tensor'))
- grad_gain_mlp: float32 [1024], P(('dp', 'tensor'))
- grad_router: float32 [1024, 32], P(('dp', 'tensor'))
- grad_gate_up: float32 [32, 1024, 1024], P('tensor', 'dp')
- grad_down: float32 [32, 512, 1024], P('tensor', None, 'dp')
The draws below stay inside these ranges and needn't reach their ends.
Inputs may be any that keep to these rules, and one draw needn't show every extreme that they name: `routes`: in each sequence no expert is named by more than 1024 tokens, a bound that some block reaches; a token names 8 different experts. `seg_ids`: document numbers never fall along a sequence; a document has at most 800 tokens and some document exactly 800.
All inputs are finite; a program needn't handle non-finite values. No bound on the sum of `key_mask` on one device may be relied on, other than what follows from the above.
Results may differ from the reference program's by a relative error of at most 0.025.
Values may be sent and summed in bfloat16 or wider, within the bound.
A program may use at most 192 MiB of HBM per device.

```python
import math
from functools import partial
import jax
import jax.numpy as jnp
import numpy as np
from jax import lax

D = 1024
HEADS = 16
HEAD = 64
KV_HEADS = 8
FF = 512
TOPK = 8
DOC_MOST = 800
EXPERTS = 32
SEQ = 2048
SEQS = 8
CAP = 1024
DOCS = 8


def place_ends(values, stream_key, least, top_value):
    shape = values.shape
    place = [jax.random.randint(jax.random.fold_in(stream_key, axis), (), 0, shape[axis]) for axis in range(len(shape))]
    values = values.at[tuple(place)].set(least)
    longest = shape.index(max(shape))
    place[longest] = (place[longest] + 1) % shape[longest]
    return values.at[tuple(place)].set(top_value)


def levels(rng, dims, split, low, largest):
    factor_of, own = 1.0, jax.random.fold_in(rng, 6)
    for dim, parts in split:
        steps = jnp.exp(jax.random.uniform(jax.random.fold_in(own, dim), (parts,), jnp.float32, low / len(split), largest / len(split)))
        factor_of = factor_of * jnp.repeat(steps, dims[dim] // parts).reshape([-1 if axis == dim else 1 for axis in range(len(dims))])
    return factor_of


def split_up(amount, total, reach, lean):
    weights = [(1 << 20) // math.isqrt(rank ** lean) + 1 for rank in range(2, amount + 1)]
    surplus, counts = total - reach - (amount - 1), [1] * (amount - 1)
    while surplus > 0:
        free = [i for i in range(amount - 1) if counts[i] < reach]
        whole, budget = sum([weights[i] for i in free]), surplus
        for i in free:
            addition = min(reach - counts[i], max(1, budget * weights[i] // whole), surplus)
            counts[i] = counts[i] + addition
            surplus = surplus - addition
    return np.array([reach] + counts)


def uneven_parts(stream_key, amount, total, reach, skew):
    if amount == 2:
        one = jax.random.randint(stream_key, (), max(1, total - reach), min(reach, total - 1) + 1)
        return jnp.stack([one, total - one])
    tallies = jnp.asarray(split_up(amount, total, reach, skew), jnp.int32)
    pairs = (amount - 1) // 2
    source_of, taker = tallies[1:1 + 2 * pairs:2], tallies[2:2 + 2 * pairs:2]
    margin = jnp.minimum(source_of - 1, reach - taker)
    moved = jax.random.randint(jax.random.fold_in(stream_key, 1), (pairs,), 0, 1 << 20) % (margin + 1)
    tallies = tallies.at[1:1 + 2 * pairs:2].set(source_of - moved).at[2:2 + 2 * pairs:2].set(taker + moved)
    return tallies[jax.random.permutation(jax.random.fold_in(stream_key, 2), amount)]


def routed_block(key, own, number, rows, number_of, top, most, slope):
    order = jax.random.permutation(key, number_of)
    heavy_load, ordinary = shares(number_of, rows * top, most, slope, True), shares(number_of, rows * top, most, slope, False)
    places = jnp.arange(number_of)

    def named(sizes, turn):
        used = int((sizes > 0).sum())
        fixed = max(1, used // 4)
        passed = fixed + (places - fixed + turn * (used - fixed)) % max(1, number_of - fixed)
        return jnp.zeros((number_of,), jnp.int32).at[order[jnp.where(places < fixed, places, passed)]].set(jnp.asarray(sizes, jnp.int32))

    sizes = jnp.where(number % 4 == 0, named(heavy_load, number // 4), named(ordinary, number - number // 4 - 1))
    mixed = jax.random.permutation(jax.random.fold_in(own, 3), number_of)
    source_of, taker = mixed[0:number_of // 2 * 2:2], mixed[1:number_of // 2 * 2:2]
    room = jnp.minimum(sizes[source_of] - 1, most - sizes[taker]) // 2
    room = jnp.where((source_of == order[0]) | (taker == order[0]) | (sizes[taker] == 0), 0, jnp.maximum(room, 0))
    passed = jax.random.randint(jax.random.fold_in(own, 4), (number_of // 2,), 0, 1 << 20) % (room + 1)
    sizes = sizes.at[source_of].add(-passed).at[taker].add(passed)
    members = jnp.searchsorted(jnp.cumsum(sizes), jnp.arange(rows * top), side="right").astype(jnp.int32)
    grid = members.reshape(top, rows).T
    grid = grid[jax.random.permutation(jax.random.fold_in(own, 1), rows)]
    turn = jax.random.randint(jax.random.fold_in(own, 2), (rows, 1), 0, top)
    return jnp.take_along_axis(grid, (jnp.arange(top)[None, :] + turn) % top, axis=1)


def shares(amount, total, most, skew, full):
    weights = [(1 << 20) // math.isqrt(standing ** skew) + 1 for standing in range(1, amount + 1)]
    largest = most if full else min(most, max(-(-total // amount), total * weights[0] // sum(weights)))
    least = 1 if total - largest >= amount - 1 else 0
    counts, rest = [largest] + [least] * (amount - 1), total - largest - least * (amount - 1)
    while rest > 0:
        candidates = [i for i in range(1, amount) if counts[i] < largest] or [i for i in range(1, amount) if counts[i] < most]
        mass, budget = sum([weights[i] for i in candidates]), rest
        for i in candidates:
            addition = min(most - counts[i], max(1, budget * weights[i] // mass), rest)
            counts[i] = counts[i] + addition
            rest = rest - addition
    return np.array(counts)


def centred(stream_key, shape, scale, limit, pieces=(), kind=jnp.bfloat16):
    drawn = jax.random.normal(stream_key, shape, jnp.float32) * scale
    if len(pieces) > 0:
        drawn = levels(stream_key, shape, pieces, -0.22, 0.18) * drawn
    return jnp.clip(drawn, min=-limit, max=limit).astype(kind)


def setup_inputs(seed: int = 0) -> dict:
    splits = jax.random.split(jax.random.key(seed), 14)
    hidden = centred(splits[0], (SEQS, SEQ, D), 1.0, 6.0, ((0, 8), (1, 16)))
    seg_ids = jax.vmap(lambda own: jnp.searchsorted(jnp.cumsum(uneven_parts(own, DOCS, SEQ, DOC_MOST, 0)), jnp.arange(SEQ), side="right"))(jax.random.split(splits[1], SEQS)).reshape((SEQS, SEQ)).astype(jnp.int32)
    key_mask = place_ends((jax.random.randint(splits[2], (SEQS, SEQ), 0, 8) < 7).astype(jnp.int32), jax.random.fold_in(splits[2], 1), 0, 1)
    routes_keys = jax.random.split(jax.random.fold_in(splits[3], 1), SEQS * SEQ // SEQ)
    routes_turns = jax.random.permutation(jax.random.fold_in(splits[3], 3), SEQS * SEQ // SEQ)
    routes = jax.vmap(lambda own, number: routed_block(jax.random.fold_in(splits[3], 2), own, number, SEQ, EXPERTS, TOPK, CAP, 2))(routes_keys, routes_turns).reshape((SEQS, SEQ, TOPK))
    gain_attn = jnp.clip(1.0 + 0.1 * jax.random.normal(splits[4], (D,), jnp.float32), 0.5, 1.5).astype(jnp.bfloat16)
    w_query = centred(splits[5], (D, HEADS * HEAD), D ** -0.5, 0.1875, ((0, 8), (1, 16)))
    w_keyval = centred(splits[6], (D, KV_HEADS * 2 * HEAD), D ** -0.5, 0.1875, ((0, 128),))
    w_out = centred(splits[7], (HEADS * HEAD, D), (HEADS * HEAD // 8) ** -0.5, 0.5, ((1, 128),))
    gain_mlp = jnp.clip(1.0 + 0.1 * jax.random.normal(splits[8], (D,), jnp.float32), 0.5, 1.5).astype(jnp.bfloat16)
    w_router = centred(splits[9], (D, EXPERTS), (4 * D) ** -0.5, 0.09375, ((0, 128),))
    w_gate_up = centred(splits[10], (EXPERTS, D, 2 * FF), D ** -0.5, 0.1875, ((0, 16), (1, 8)))
    w_down = centred(splits[11], (EXPERTS, FF, D), (FF // 4) ** -0.5, 0.5, ((0, 16), (2, 8)))
    cotangent = centred(splits[12], (SEQS, SEQ, D), 1.0, 6.0, ((0, 8), (1, 16)))
    return dict(hidden=hidden, seg_ids=seg_ids, key_mask=key_mask, routes=routes, gain_attn=gain_attn, w_query=w_query, w_keyval=w_keyval, w_out=w_out, gain_mlp=gain_mlp, w_router=w_router, w_gate_up=w_gate_up, w_down=w_down, cotangent=cotangent)


@jax.custom_vjp
def low(v):
    return lax.optimization_barrier(v.astype(jnp.bfloat16)).astype(jnp.float32)

@jax.custom_vjp
def low_back(v):
    return v

def low_keep(v):
    return (low(v), None)

def low_pass(kept, grad):
    return (grad,)

def back_keep(v):
    return (v, None)

def back_low(kept, grad):
    return (low(grad),)
low.defvjp(low_keep, low_pass)
low_back.defvjp(back_keep, back_low)

def matmul(left, right):
    return jnp.dot(left, right, precision=lax.Precision.HIGHEST, preferred_element_type=jnp.float32)

def rope_tables(length, width):
    half = width // 2
    freqs = jnp.exp(jnp.arange(half, dtype=jnp.float32) * (-2.0 * math.log(10000.0) / width))
    angles = jnp.arange(length, dtype=jnp.float32)[:, None] * freqs[None, :]
    return (jnp.cos(angles), jnp.sin(angles))

def rotate(values, cosine, sine):
    length = values.shape[0]
    half = cosine.shape[1]
    shaped = values.reshape(length, -1, 2 * half)
    first = shaped[:, :, :half]
    second = shaped[:, :, half:]
    cos_three = cosine[:, None, :]
    sin_three = sine[:, None, :]
    turned = jnp.concatenate([first * cos_three - second * sin_three, second * cos_three + first * sin_three], axis=-1)
    return turned.reshape(length, -1)

def rms_norm(values, gain):
    return values * lax.rsqrt(lax.optimization_barrier(jnp.mean(values * values, -1, keepdims=True)) + 1e-06) * gain

def layer(segment, live_keys, route_ids, hidden, gain_attn, w_query, w_keyval, w_out, gain_mlp, w_router, w_gate_up, w_down):
    length = hidden.shape[0]
    cosine, sine = rope_tables(length, HEAD)
    normed = low(rms_norm(hidden, gain_attn))
    query_pre = low_back(matmul(normed, w_query))
    keyval_pre = matmul(normed, w_keyval).reshape(length, KV_HEADS, 2, HEAD)
    queries = low(rotate(query_pre, cosine, sine))
    keys = low(rotate(keyval_pre[:, :, 0, :].reshape(length, KV_HEADS * HEAD), cosine, sine))
    values = low(keyval_pre[:, :, 1, :].reshape(length, KV_HEADS * HEAD))
    places = jnp.arange(length, dtype=jnp.int32)
    allowed = (segment[:, None] == segment[None, :]) & (places[None, :] <= places[:, None]) & ((live_keys[None, :] == 1) | (places[None, :] == places[:, None]))
    group = HEADS // KV_HEADS
    scale = 1.0 / math.sqrt(HEAD)

    def one_head(head):
        head_query = lax.dynamic_slice_in_dim(queries, head * HEAD, HEAD, 1)
        head_key = lax.dynamic_slice_in_dim(keys, head // group * HEAD, HEAD, 1)
        head_value = lax.dynamic_slice_in_dim(values, head // group * HEAD, HEAD, 1)
        raw = low_back(matmul(head_query, head_key.T))
        scores = jnp.where(allowed, raw * scale, -1000000000.0)
        probs = low(jax.nn.softmax(scores, axis=-1))
        return low_back(low(matmul(probs, head_value)))
    per_head = lax.map(jax.checkpoint(one_head), jnp.arange(HEADS, dtype=jnp.int32))
    attended = jnp.transpose(per_head, (1, 0, 2)).reshape(length, HEADS * HEAD)
    mid = hidden + low_back(matmul(attended, w_out))
    normed_mid = low(rms_norm(mid, gain_mlp))
    logits = matmul(normed_mid, w_router)
    chosen = jnp.take_along_axis(logits, route_ids, axis=1)
    gates = jax.nn.softmax(chosen, axis=-1)

    def expert_step(total, item):
        expert, gate_up_e, down_e = item
        hits = route_ids == expert
        used = jnp.any(hits, 1)
        weight = lax.optimization_barrier(jnp.sum(jnp.where(hits, gates, 0.0), 1))
        slot = jnp.cumsum(used.astype(jnp.int32), dtype=jnp.int32) - 1
        filled = jnp.sum(used.astype(jnp.int32), dtype=jnp.int32)
        target = jnp.where(used, slot, CAP)
        source_rows = jnp.zeros((CAP,), jnp.int32).at[target].set(jnp.arange(length, dtype=jnp.int32), mode='drop')
        live = jnp.arange(CAP, dtype=jnp.int32) < filled
        buffer = jnp.where(live[:, None], normed_mid[source_rows], 0.0)
        projected = low_back(matmul(buffer, gate_up_e))
        activated = low(jax.nn.silu(projected[:, :FF]) * projected[:, FF:])
        expert_out = low_back(matmul(activated, down_e))
        back = expert_out[jnp.clip(slot, 0, CAP - 1)]
        return (total + jnp.where(used[:, None], weight[:, None] * back, 0.0), None)
    moe, unused = lax.scan(jax.checkpoint(expert_step), jnp.zeros((length, D), jnp.float32), (jnp.arange(EXPERTS, dtype=jnp.int32), w_gate_up, w_down))
    return mid + moe

def reference(hidden, seg_ids, key_mask, routes, gain_attn, w_query, w_keyval, w_out, gain_mlp, w_router, w_gate_up, w_down, cotangent):
    weights = tuple((item.astype(jnp.float32) for item in (gain_attn, w_query, w_keyval, w_out, gain_mlp, w_router, w_gate_up, w_down)))

    def one_sequence(totals, item):
        hid, segment, live_keys, route_ids, cot = item
        func = partial(layer, segment, live_keys, route_ids)
        result, pull = jax.vjp(func, hid.astype(jnp.float32), *weights)
        grads = pull(cot.astype(jnp.float32))
        totals = tuple((acc + grad for acc, grad in zip(totals, grads[1:])))
        return (totals, (result.astype(jnp.bfloat16), grads[0].astype(jnp.bfloat16)))
    zeros = tuple((jnp.zeros_like(item) for item in weights))
    totals, outs = lax.scan(one_sequence, zeros, (hidden, seg_ids, key_mask, routes, cotangent))
    return (outs[0], outs[1], totals[0], totals[1], totals[2], totals[3], totals[4], totals[5], totals[6], totals[7])
```

```python
import math

import jax
import jax.numpy as jnp
import numpy as np
from jax import lax
from jax.experimental import pallas as pl
from jax.experimental.pallas import tpu as pltpu
from jax.sharding import PartitionSpec as P

HEAD = 64
LENGTH = 2048
WIDTH = 1024
UNITS = 512
ROWS = 128
PAIR = 256
REACH = 896
SPAN = REACH + PAIR
PADDED = REACH + LENGTH
CHIPS = 8
TENSOR = 16
DP = 8
TAIL = 304
SLOTS = 4
LOWEST = -1e30
BF = jnp.bfloat16
F32 = jnp.float32
MESH = pl.DeviceIdType.MESH
VMEM_BYTES = 60 * 1024 * 1024

NN = (((1,), (0,)), ((), ()))
NT = (((1,), (1,)), ((), ()))


def dot(left, right, dims=NN):
    return lax.dot_general(left, right, dims, preferred_element_type=F32)


def aligned(value, size):
    return pl.ds(pl.multiple_of(value * size, size), size)


def remote(src, dst, send, recv, axis, index):
    return pltpu.make_async_remote_copy(
        src_ref=src,
        dst_ref=dst,
        send_sem=send,
        recv_sem=recv,
        device_id={axis: index},
        device_id_type=MESH,
    )


class Place:
    def __init__(self):
        self.t = lax.axis_index("tensor")
        self.d = lax.axis_index("dp")
        self.core = lax.rem(self.t, 2)
        self.chip = self.t // 2
        self.twin = self.t + 1 - 2 * self.core
        self.x = lax.rem(self.d, 2)
        self.y = self.d // 2
        self.across = self.d + 1 - 2 * self.x

    def chip_at(self, k):
        return lax.rem(self.chip + k, CHIPS)

    def same_core(self, k):
        return 2 * self.chip_at(k) + self.core

    def tensor_at(self, k):
        return lax.rem(self.t + k, TENSOR)

    def dp_at(self, k):
        return lax.rem(self.d + k, DP)

    def y_at(self, k):
        return lax.rem(self.y + k, 4)

    def enter(self):
        barrier = pltpu.get_barrier_semaphore()
        for k in range(1, TENSOR):
            pl.semaphore_signal(
                barrier, inc=1, device_id={"tensor": self.tensor_at(k)}, device_id_type=MESH
            )
        for k in range(1, DP):
            pl.semaphore_signal(
                barrier, inc=1, device_id={"dp": self.dp_at(k)}, device_id_type=MESH
            )
        pl.semaphore_wait(barrier, TENSOR + DP - 2)


class Spread:
    def __init__(self, place, block, send, recv, source=None):
        self.place, self.block, self.send, self.recv = place, block, send, recv
        self.source = source

    def copy(self, number, index, dest, source=None):
        src = self.block(index) if source is None else source
        return remote(
            src, self.block(index), self.send.at[number], self.recv.at[index], "tensor", dest
        )

    def own(self, k):
        dest = self.place.twin if k == 0 else self.place.same_core(k)
        return self.copy(k, self.place.t, dest, self.source)

    def start(self):
        for k in range(1, CHIPS):
            self.own(k).start()
        self.own(0).start()

    def passed(self, k):
        return self.copy(CHIPS + k, self.place.same_core(k), self.place.twin)

    def arrived(self, index):
        self.copy(0, index, self.place.twin).wait_recv()

    def first(self, k):
        self.arrived(self.place.same_core(k))
        self.passed(k).start()

    def second(self, k):
        self.arrived(2 * self.place.chip_at(k) + 1 - self.place.core)

    def end(self):
        for k in range(CHIPS):
            self.own(k).wait_send()
        for k in range(1, CHIPS):
            self.passed(k).wait_send()


def lanes(shape):
    return lax.broadcasted_iota(jnp.int32, shape, len(shape) - 1)


def sublanes(shape):
    return lax.broadcasted_iota(jnp.int32, shape, 0)


def swapped(values):
    return jnp.where(
        lanes(values.shape) < HEAD // 2,
        pltpu.roll(values, 2 * HEAD - HEAD // 2, 1),
        pltpu.roll(values, HEAD // 2, 1),
    )


def document_starts(seg):
    starts = jnp.zeros(seg.shape, F32)
    for document in range(8):
        before = jnp.sum(jnp.where(seg < document, 1.0, 0.0), axis=1, keepdims=True)
        starts = starts + jnp.where(seg == document, before, 0.0)
    return starts


def key_codes(meta, code):
    code[0:REACH, :] = jnp.full((REACH, ROWS), -1.0, F32)

    @pl.loop(0, CHIPS)
    def _(i):
        live = meta[aligned(i, PAIR), 8:9] == 1
        places = (sublanes((PAIR, ROWS)) + i * PAIR).astype(F32)
        code[pl.ds(pl.multiple_of(REACH + i * PAIR, ROWS), PAIR), :] = jnp.where(
            live, places, -1.0
        )


def allowed(code, start_row, chunk):
    wide = jnp.concatenate([code, code], axis=1)
    ok = wide >= start_row
    if chunk >= REACH // ROWS:
        key = sublanes((ROWS, PAIR)) + (chunk * ROWS - REACH)
        query = lanes((ROWS, PAIR))
        ok = (ok & (key < query)) | (key == query)
    return ok


def attention_kernel(
    hid,
    cot,
    tiles,
    wq,
    rows,
    gu,
    down,
    cosine,
    sine,
    meta,
    seg,
    normed,
    queries,
    keyvals,
    keyvals_t,
    stats,
    heads_t,
    mid,
    normed_mid,
    wq_all,
    out_t,
    kv_full,
    small,
    gu_all,
    down_all,
    cot_all,
    hidden_all,
    tile_all,
    row_all,
    code,
    scores,
    probs,
    starts,
    wkv,
    att_src,
    att_t,
    h_send,
    h_recv,
    r_send,
    r_recv,
    c_send,
    c_recv,
    t1_send,
    t1_recv,
    t2_send,
    t2_recv,
    rd_send,
    rd_recv,
    wq_send,
    wq_recv,
    gu_send,
    gu_recv,
    dn_send,
    dn_recv,
    a_send,
    a_recv,
    local,
):
    at = Place()
    t, d = at.t, at.d
    hidden_all[aligned(t, ROWS), :] = hid[...]
    tile_all[d, t] = tiles[t]
    row_all[d, t] = rows[...]
    wq_all[HEAD : 2 * HEAD, :] = jnp.zeros((HEAD, WIDTH), BF)
    wq_all[0:HEAD, aligned(d, ROWS)] = wq[...]
    at.enter()

    spread_h = Spread(at, lambda b: hidden_all.at[aligned(b, ROWS)], h_send, h_recv)
    spread_r = Spread(at, lambda b: row_all.at[:, b], r_send, r_recv)
    spread_c = Spread(at, lambda b: cot_all.at[aligned(b, ROWS)], c_send, c_recv, cot)

    def tile_one(k, src):
        dest = at.tensor_at(k)
        return remote(
            tiles.at[dest], tile_all.at[d, src], t1_send.at[k], t1_recv.at[src], "tensor", dest
        )

    def tile_two(k, src):
        return remote(
            tile_all.at[src], tile_all.at[src], t2_send.at[k], t2_recv.at[src], "dp", at.dp_at(k)
        )

    def rows_dp(k, src):
        return remote(
            rows, row_all.at[src, t], rd_send.at[k], rd_recv.at[src], "dp", at.dp_at(k)
        )

    def wq_dp(k, src):
        return remote(
            wq,
            wq_all.at[pl.ds(0, HEAD), aligned(src, ROWS)],
            wq_send.at[k],
            wq_recv.at[src],
            "dp",
            at.dp_at(k),
        )

    def gu_block(s):
        return gu_all.at[:, aligned(s, ROWS), :]

    def down_block(s):
        return down_all.at[:, :, aligned(s, ROWS)]

    def expert(k, src, dest, first):
        return (
            remote(
                gu if first else gu_block(src),
                gu_block(src),
                gu_send.at[k],
                gu_recv.at[src],
                "dp",
                dest,
            ),
            remote(
                down if first else down_block(src),
                down_block(src),
                dn_send.at[k],
                dn_recv.at[src],
                "dp",
                dest,
            ),
        )

    def y_peer(k):
        return 2 * at.y_at(k) + at.x

    for k in range(1, TENSOR):
        tile_one(k, t).start()
    for k in range(1, DP):
        wq_dp(k, d).start()
        rows_dp(k, d).start()
    spread_h.start()
    for copy in expert(0, d, at.across, True):
        copy.start()
    for k in range(1, 4):
        for copy in expert(k, d, y_peer(k), True):
            copy.start()
    own_copies = (
        pltpu.make_async_copy(gu, gu_block(d), local.at[0]),
        pltpu.make_async_copy(down, down_block(d), local.at[1]),
        pltpu.make_async_copy(cot, cot_all.at[aligned(t, ROWS)], local.at[2]),
    )
    for copy in own_copies:
        copy.start()

    key_codes(meta, code)
    starts[...] = document_starts(seg[...])
    keyvals[0:REACH, :] = jnp.zeros((REACH, 2 * HEAD), BF)
    keyvals_t[:, 0:REACH] = jnp.zeros((2 * HEAD, REACH), BF)

    for k in range(1, TENSOR):
        tile_one(k, at.tensor_at(k)).wait_recv()
    for k in range(1, DP):
        tile_two(k, d).start()
    for k in range(1, DP):
        rows_dp(k, at.dp_at(k)).wait_recv()
        wq_dp(k, at.dp_at(k)).wait_recv()
    spread_r.start()
    for k in range(1, DP):
        tile_two(k, at.dp_at(k)).wait_recv()
    for j in range(DP):
        both = tile_all[j].astype(F32)
        wkv[j * ROWS : (j + 1) * ROWS, :] = both[:, 0:8].reshape(ROWS, ROWS).astype(BF)
        small[j * ROWS : (j + 1) * ROWS, :] = both[:, 8:16].reshape(ROWS, ROWS).astype(BF)
    columns = small[...].astype(F32).T
    gain_one = columns[32:33, :]
    gain_two = columns[33:34, :]

    @pl.loop(0, CHIPS)
    def _(i):
        @pl.when(i == 0)
        def _():
            spread_h.arrived(at.twin)

        @pl.when(i > 0)
        def _():
            spread_h.first(i)
            spread_h.second(i)

        block = at.chip_at(i)
        here = aligned(block, PAIR)
        hidden = hidden_all[here, :].astype(F32)
        inverse = lax.rsqrt(jnp.mean(hidden * hidden, axis=1, keepdims=True) + 1e-6)
        unit = (hidden * inverse * gain_one).astype(BF)
        normed[here, :] = unit
        cos, sin = cosine[here, :], sine[here, :]
        query = dot(unit, wq_all[...], NT)
        query = (query * cos + swapped(query) * sin).astype(BF)
        queries[here, :] = (query.astype(F32) * (1.0 / math.sqrt(HEAD))).astype(BF)
        keyval = dot(unit, wkv[...])
        keyval = keyval * cos + swapped(keyval) * sin
        later = pl.ds(pl.multiple_of(REACH + block * PAIR, ROWS), PAIR)
        keyvals[later, :] = keyval.astype(BF)
        keyvals_t[:, later] = keyval.T.astype(BF)

    for copy in expert(0, at.across, at.across, True):
        copy.wait_recv()
    for k in range(1, 4):
        for copy in expert(3 + k, at.across, y_peer(k), False):
            copy.start()
    for k in range(1, CHIPS):
        spread_r.first(k)
    for copy in own_copies:
        copy.wait()
    spread_c.start()

    def att_copy(dest, src):
        return remote(
            att_src.at[dest],
            att_t.at[aligned(src, HEAD), :],
            a_send.at[dest],
            a_recv.at[src],
            "tensor",
            dest,
        )

    @pl.loop(0, CHIPS)
    def _(i):
        block = at.chip_at(i + 1)
        here = aligned(block, PAIR)
        query = queries[here, :]
        start_row = starts[:, here]
        top = jnp.full((1, PAIR), LOWEST, F32)
        for chunk in range(SPAN // ROWS):
            keys = pl.ds(pl.multiple_of(block * PAIR + chunk * ROWS, ROWS), ROWS)
            score = dot(keyvals[keys, :], query, NT)
            score = jnp.where(allowed(code[keys, :], start_row, chunk), score, LOWEST)
            scores[chunk * ROWS : (chunk + 1) * ROWS, :] = score
            top = jnp.maximum(top, jnp.max(score, axis=0, keepdims=True))
        total = jnp.zeros((1, PAIR), F32)
        for chunk in range(SPAN // ROWS):
            place = slice(chunk * ROWS, (chunk + 1) * ROWS)
            weight = jnp.exp(scores[place, :] - top)
            total = total + jnp.sum(weight, axis=0, keepdims=True)
            probs[place, :] = weight.astype(BF)
        window = pl.ds(pl.multiple_of(block * PAIR, ROWS), SPAN)
        head = dot(keyvals_t[HEAD : 2 * HEAD, window], probs[...]) / total
        heads_t[:, here] = head
        stats[:, here] = top + jnp.log(total)
        att_src[2 * block] = head[:, 0:ROWS].astype(BF)
        att_src[2 * block + 1] = head[:, ROWS:PAIR].astype(BF)

        @pl.when(i < CHIPS - 1)
        def _():
            att_copy(2 * block, t).start()
            att_copy(2 * block + 1, t).start()

        @pl.when(i == CHIPS - 1)
        def _():
            att_copy(at.twin, t).start()

    att_t[aligned(t, HEAD), :] = att_src[t]
    spread_r.arrived(at.twin)
    for k in range(1, CHIPS):
        spread_r.second(k)

    @pl.loop(0, DP)
    def _(j):
        both = row_all[j].astype(F32)
        kv_full[aligned(j, ROWS), :] = both[:, 0:8].reshape(ROWS, WIDTH).astype(BF)
        out_t[aligned(j, ROWS), :] = both[:, 8:16].reshape(ROWS, WIDTH).astype(BF)

    for k in range(1, TENSOR):
        att_copy(at.tensor_at(k), at.tensor_at(k)).wait_recv()
    attended = att_t[...].astype(F32).T.astype(BF)
    middle = hid[...].astype(F32) + dot(attended, out_t[...], NT)
    mid[...] = middle
    inverse = lax.rsqrt(jnp.mean(middle * middle, axis=1, keepdims=True) + 1e-6)
    normed_mid[...] = (middle * inverse * gain_two).astype(BF)

    for k in range(1, CHIPS):
        spread_c.first(k)
    spread_c.arrived(at.twin)
    for k in range(1, CHIPS):
        spread_c.second(k)
    for k in range(1, 4):
        for other in (2 * at.y_at(k), 2 * at.y_at(k) + 1):
            for copy in expert(0, other, at.across, True):
                copy.wait_recv()
    for k in range(1, TENSOR):
        tile_one(k, t).wait_send()
        att_copy(at.tensor_at(k), t).wait_send()
    for k in range(1, DP):
        tile_two(k, d).wait_send()
        rows_dp(k, d).wait_send()
        wq_dp(k, d).wait_send()
    for k in range(7):
        for copy in expert(k, d, at.across, True):
            copy.wait_send()
    for spread in (spread_h, spread_r, spread_c):
        spread.end()


class Sum:
    def __init__(self, place, parts, twins, sums, landed, tw_send, tw_recv, send, recv):
        self.place, self.parts, self.twins = place, parts, twins
        self.sums, self.landed = sums, landed
        self.tw_send, self.tw_recv, self.send, self.recv = tw_send, tw_recv, send, recv

    def half(self, k):
        at = self.place
        return remote(
            self.parts.at[lax.rem(k, SLOTS), aligned(1 - at.core, ROWS), :],
            self.twins.at[k],
            self.tw_send.at[k],
            self.tw_recv.at[k],
            "tensor",
            at.twin,
        )

    def whole(self, k):
        return remote(
            self.sums.at[k],
            self.landed.at[k],
            self.send.at[k],
            self.recv.at[k],
            "tensor",
            self.place.same_core(k),
        )

    def put(self, k, value):
        @pl.when(k >= SLOTS)
        def _():
            self.half(k - SLOTS).wait_send()

        self.parts[lax.rem(k, SLOTS)] = value.astype(BF)
        self.half(k).start()

    def add(self, k):
        self.half(k).wait_recv()
        own = self.parts[lax.rem(k, SLOTS), aligned(self.place.core, ROWS), :].astype(F32)
        self.sums[k] = (own + self.twins[k].astype(F32)).astype(BF)

    def go(self, k):
        self.add(k)
        self.whole(k).start()

    def result(self):
        total = self.sums[0].astype(F32)
        for k in range(1, CHIPS):
            self.whole(k).wait_recv()
            total = total + self.landed[k].astype(F32)
        return total

    def end(self):
        for k in range(CHIPS - SLOTS, CHIPS):
            self.half(k).wait_send()
        for k in range(1, CHIPS):
            self.whole(k).wait_send()


def expert_kernel(
    normed_mid,
    cot_all,
    gu_all,
    down_all,
    small,
    meta,
    mid,
    cot,
    out_t,
    output,
    mid_grad,
    mid_low,
    att_grad_t,
    gu_grad,
    down_grad,
    router_t,
    gain_grad,
    nm_all,
    nm_t,
    cots,
    gus,
    downs,
    weighted_t,
    proj_grads,
    logit_t,
    n_parts,
    n_twins,
    n_sums,
    n_landed,
    m_parts,
    m_twins,
    m_sums,
    m_landed,
    g_send,
    g_recv,
    ntw_send,
    ntw_recv,
    ns_send,
    ns_recv,
    mtw_send,
    mtw_recv,
    ms_send,
    ms_recv,
    local,
):
    at = Place()
    t = at.t
    loads = (
        pltpu.make_async_copy(gu_all, gus, local.at[0]),
        pltpu.make_async_copy(down_all, downs, local.at[1]),
        pltpu.make_async_copy(cot_all, cots, local.at[2]),
    )
    for copy in loads:
        copy.start()
    nm_all[aligned(t, ROWS), :] = normed_mid[...]
    at.enter()
    spread = Spread(at, lambda b: nm_all.at[aligned(b, ROWS)], g_send, g_recv)
    spread.start()
    normed_sum = Sum(
        at, n_parts, n_twins, n_sums, n_landed, ntw_send, ntw_recv, ns_send, ns_recv
    )
    moe_sum = Sum(at, m_parts, m_twins, m_sums, m_landed, mtw_send, mtw_recv, ms_send, ms_recv)
    for copy in loads:
        copy.wait()

    @pl.loop(0, CHIPS)
    def _(i):
        @pl.when(i == 0)
        def _():
            spread.arrived(at.twin)

        @pl.when(i > 0)
        def _():
            spread.first(i)
            spread.second(i)

        here = aligned(at.chip_at(i), PAIR)
        nm = nm_all[here, :]
        nm_t[:, here] = nm.T
        cotangents = cots[here, :]
        place = lanes((PAIR, ROWS))
        routes = meta[here, :]
        named = place == routes[:, 0:1]
        for j in range(1, 8):
            named = named | (place == routes[:, j : j + 1])
        logits = jnp.where(named, dot(nm, small[...]), LOWEST)
        powers = jnp.exp(logits - jnp.max(logits, axis=1, keepdims=True))
        powers = jnp.where(named, powers, 0.0)
        gates = powers / jnp.sum(powers, axis=1, keepdims=True)
        gate_grads = jnp.zeros((PAIR, ROWS), F32)
        act_grads = dot(cotangents, downs[...], NT)
        weighted = []
        for e in range(2):
            mine = place == 2 * t + e
            gate = jnp.sum(jnp.where(mine, gates, 0.0), axis=1, keepdims=True)
            projected = dot(nm, gus[e])
            first, up = projected[:, :UNITS], projected[:, UNITS:]
            sigmoid = 1.0 / (1.0 + jnp.exp(-first))
            silu = first * sigmoid
            activated = silu * up
            act_grad = act_grads[:, e * UNITS : (e + 1) * UNITS]
            gate_grad = jnp.sum(activated * act_grad, axis=1, keepdims=True)
            gate_grads = gate_grads + jnp.where(mine, gate_grad, 0.0)
            weighted.append((activated * gate).astype(BF))
            act_grad = act_grad * gate
            proj_grads[here, e * WIDTH : e * WIDTH + UNITS] = (
                act_grad * up * (sigmoid * (1.0 + first * (1.0 - sigmoid)))
            ).astype(BF)
            proj_grads[here, e * WIDTH + UNITS : (e + 1) * WIDTH] = (act_grad * silu).astype(BF)
        mean = jnp.sum(gates * gate_grads, axis=1, keepdims=True)
        logit_grad = gates * (gate_grads - mean)
        logit_t[:, here] = logit_grad.T.astype(BF)
        normed_part = (
            dot(proj_grads[here, 0:WIDTH], gus[0], NT)
            + dot(proj_grads[here, WIDTH : 2 * WIDTH], gus[1], NT)
            + dot(logit_grad.astype(BF), small[...], NT)
        )
        normed_sum.put(i, normed_part)
        both = jnp.concatenate(weighted, axis=1)
        moe_sum.put(i, dot(both, downs[...]))
        weighted_t[:, here] = both.T

        @pl.when(i == 1)
        def _():
            normed_sum.add(0)
            moe_sum.add(0)

        @pl.when(i > 1)
        def _():
            normed_sum.go(i - 1)
            moe_sum.go(i - 1)

    normed_sum.go(CHIPS - 1)
    moe_sum.go(CHIPS - 1)

    @pl.loop(0, 4)
    def _(j):
        strip = aligned(j, PAIR)
        for e in range(2):
            gus[e, strip, :] = dot(
                nm_t[strip, :], proj_grads[:, e * WIDTH : (e + 1) * WIDTH]
            ).astype(BF)
        downs[strip, :] = dot(weighted_t[strip, :], cots[...]).astype(BF)

    stores = (
        pltpu.make_async_copy(gus, gu_grad, local.at[0]),
        pltpu.make_async_copy(downs, down_grad, local.at[1]),
    )
    for copy in stores:
        copy.start()
    router_t[...] = dot(logit_t[...], nm_all[...])

    columns = small[...].astype(F32).T
    gain_two = columns[33:34, :]
    normed_grad = normed_sum.result()
    middle = mid[...]
    inverse = lax.rsqrt(jnp.mean(middle * middle, axis=1, keepdims=True) + 1e-6)
    unit = middle * inverse
    gain_grad[...] = jnp.sum(normed_grad * unit, axis=0, keepdims=True)
    scaled = normed_grad * gain_two
    grad = cot[...].astype(F32) + inverse * (
        scaled - unit * jnp.mean(scaled * unit, axis=1, keepdims=True)
    )
    mid_grad[...] = grad
    low = grad.astype(BF)
    mid_low[...] = low
    att_grad_t[...] = dot(low, out_t[...]).T.astype(BF)
    output[...] = (middle + moe_sum.result()).astype(BF)
    for copy in stores:
        copy.wait()
    spread.end()
    normed_sum.end()
    moe_sum.end()


def back_kernel(
    att_grad_t,
    mid_low,
    mid_grad,
    gu_grad,
    down_grad,
    router_t,
    gain_grad,
    queries,
    keyvals,
    keyvals_t,
    stats,
    heads_t,
    meta,
    seg,
    cosine,
    sine,
    cosine_t,
    sine_t,
    wq_own,
    kv_full,
    normed,
    hid,
    small,
    hidden_grad,
    gu_out,
    down_out,
    query_out,
    kv_out,
    rest_out,
    grads_t,
    mid_all,
    wq_full,
    code,
    starts,
    kv_sum,
    tail_left,
    qg_src,
    kg_src,
    qg_all,
    kg_all,
    tail,
    tail_in,
    pieces,
    last,
    own_gu,
    own_down,
    gu_in,
    down_in,
    gu_half,
    down_half,
    gu_half_in,
    down_half_in,
    g_send,
    g_recv,
    m_send,
    m_recv,
    w_send,
    w_recv,
    q_send,
    q_recv,
    k_send,
    k_recv,
    gu_send,
    gu_recv,
    dn_send,
    dn_recv,
    t_send,
    t_recv,
    l_send,
    l_recv,
    local,
):
    at = Place()
    t, d = at.t, at.d
    grads_t[0:HEAD, :] = jnp.zeros((HEAD, LENGTH), BF)
    grads_t[HEAD : 2 * HEAD, aligned(t, ROWS)] = att_grad_t[aligned(t, HEAD), :]
    mid_all[aligned(t, ROWS), :] = mid_low[...]
    wq_full[aligned(t, HEAD), :] = wq_own[0:HEAD, :]
    at.enter()

    def back_copy(k, src):
        dest = at.tensor_at(k)
        return remote(
            att_grad_t.at[aligned(dest, HEAD), :],
            grads_t.at[pl.ds(HEAD, HEAD), aligned(src, ROWS)],
            g_send.at[k],
            g_recv.at[src],
            "tensor",
            dest,
        )

    def experts_y(k):
        y = at.y_at(k)
        dest = 2 * y + at.x
        return (
            remote(
                gu_grad.at[:, aligned(y, PAIR), :],
                gu_in.at[k],
                gu_send.at[k],
                gu_recv.at[k],
                "dp",
                dest,
            ),
            remote(
                down_grad.at[:, aligned(y, PAIR)],
                down_in.at[k],
                dn_send.at[k],
                dn_recv.at[k],
                "dp",
                dest,
            ),
        )

    def experts_x():
        return (
            remote(gu_half, gu_half_in, gu_send.at[0], gu_recv.at[0], "dp", at.across),
            remote(down_half, down_half_in, dn_send.at[0], dn_recv.at[0], "dp", at.across),
        )

    spread_m = Spread(at, lambda b: mid_all.at[aligned(b, ROWS)], m_send, m_recv)
    spread_w = Spread(at, lambda b: wq_full.at[aligned(b, HEAD)], w_send, w_recv)
    for k in range(1, TENSOR):
        back_copy(k, t).start()
    spread_w.start()
    for k in range(1, 4):
        for copy in experts_y(k):
            copy.start()
    own_copies = (
        pltpu.make_async_copy(gu_grad.at[:, aligned(at.y, PAIR), :], own_gu, local.at[0]),
        pltpu.make_async_copy(down_grad.at[:, aligned(at.y, PAIR)], own_down, local.at[1]),
    )
    for copy in own_copies:
        copy.start()
    spread_m.start()

    key_codes(meta, code)
    starts[...] = document_starts(seg[...])
    kv_sum[...] = jnp.zeros((PADDED, 2 * HEAD), F32)
    for k in range(1, TENSOR):
        back_copy(k, at.tensor_at(k)).wait_recv()

    def query_copy(dest, src):
        return remote(
            qg_src.at[dest],
            qg_all.at[aligned(src, HEAD), :],
            q_send.at[dest],
            q_recv.at[src],
            "tensor",
            dest,
        )

    def key_copy(dest, src):
        return remote(
            kg_src.at[dest], kg_all.at[src], k_send.at[dest], k_recv.at[src], "tensor", dest
        )

    @pl.loop(0, CHIPS)
    def _(i):
        here = aligned(i, PAIR)
        query = queries[here, :]
        start_row = starts[:, here]
        stat = stats[:, here]
        grad_t = grads_t[:, here]
        grad_rows = grad_t.astype(F32).T.astype(BF)
        head = heads_t[:, here]
        delta = jnp.sum(head * grad_t[HEAD : 2 * HEAD, :].astype(F32), axis=0, keepdims=True)
        query_grad = jnp.zeros((HEAD, PAIR), F32)
        for chunk in range(SPAN // ROWS):
            keys = pl.ds(pl.multiple_of(i * PAIR + chunk * ROWS, ROWS), ROWS)
            both = keyvals[keys, :]
            score = dot(both, query, NT)
            ok = allowed(code[keys, :], start_row, chunk)
            prob = jnp.exp(jnp.where(ok, score - stat, LOWEST))
            prob_grad = dot(both, grad_t)
            score_grad = (prob * (prob_grad - delta)).astype(BF)
            kv_sum[keys, :] += dot(score_grad, query) + dot(prob.astype(BF), grad_rows)
            query_grad = query_grad + dot(keyvals_t[0:HEAD, keys], score_grad)
        query_grad = query_grad * (1.0 / math.sqrt(HEAD))
        cos, sin = cosine_t[:, here], sine_t[:, here]
        upper, lower = query_grad[0 : HEAD // 2], query_grad[HEAD // 2 : HEAD]
        turned = jnp.concatenate(
            [upper * cos + lower * sin, lower * cos - upper * sin], axis=0
        ).astype(BF)
        tail_left[0:HEAD, here] = turned
        qg_src[2 * i] = turned[:, 0:ROWS]
        qg_src[2 * i + 1] = turned[:, ROWS:PAIR]

    @pl.loop(0, CHIPS)
    def _(i):
        here = aligned(i, PAIR)
        grad = kv_sum[pl.ds(pl.multiple_of(REACH + i * PAIR, ROWS), PAIR), :]
        grad = grad * cosine[here, :] - swapped(grad) * sine[here, :]
        tail_left[HEAD : 3 * HEAD, here] = grad.T.astype(BF)
        kg_src[2 * i] = grad[0:ROWS].astype(BF)
        kg_src[2 * i + 1] = grad[ROWS:PAIR].astype(BF)

    for k in range(1, TENSOR):
        key_copy(at.tensor_at(k), t).start()
        query_copy(at.tensor_at(k), t).start()
    qg_all[aligned(t, HEAD), :] = qg_src[t]
    kg_all[t] = kg_src[t]
    for k in range(1, CHIPS):
        spread_w.first(k)
    for k in range(1, CHIPS):
        spread_m.first(k)

    by_normed = dot(tail_left[...], normed[...])
    tail[0:HEAD, :] = by_normed[0:HEAD]
    tail[2 * HEAD : 4 * HEAD, :] = by_normed[HEAD : 3 * HEAD]

    spread_w.arrived(at.twin)
    for k in range(1, CHIPS):
        spread_w.second(k)
    for k in range(1, TENSOR):
        query_copy(at.tensor_at(k), at.tensor_at(k)).wait_recv()
        key_copy(at.tensor_at(k), at.tensor_at(k)).wait_recv()
    kv_rows = jnp.concatenate(
        [kg_all[2 * j].astype(F32) + kg_all[2 * j + 1].astype(F32) for j in range(CHIPS)], axis=1
    ).astype(BF)
    normed_grad = dot(qg_all[...].astype(F32).T.astype(BF), wq_full[...]) + dot(
        kv_rows, kv_full[...], NT
    )
    hidden = hid[...].astype(F32)
    inverse = lax.rsqrt(jnp.mean(hidden * hidden, axis=1, keepdims=True) + 1e-6)
    unit = hidden * inverse
    gain_one = small[...].astype(F32).T[32:33, :]
    gain_one_grad = jnp.sum(normed_grad * unit, axis=0, keepdims=True)
    scaled = normed_grad * gain_one
    hidden_grad[...] = (
        mid_grad[...]
        + inverse * (scaled - unit * jnp.mean(scaled * unit, axis=1, keepdims=True))
    ).astype(BF)

    spread_m.arrived(at.twin)
    for k in range(1, CHIPS):
        spread_m.second(k)
    tail[HEAD : 2 * HEAD, :] = dot(heads_t[...].astype(BF), mid_all[...])
    tail[4 * HEAD : 4 * HEAD + 32, :] = router_t[0:32, :]
    row = sublanes((16, WIDTH))
    tail[4 * HEAD + 32 : TAIL, :] = jnp.where(
        row == 0, gain_one_grad, jnp.where(row == 1, gain_grad[...], 0.0)
    )

    def tail_copy(k):
        dest = at.dp_at(k)
        return remote(
            tail.at[:, aligned(dest, ROWS)],
            tail_in.at[k],
            t_send.at[k],
            t_recv.at[k],
            "dp",
            dest,
        )

    for k in range(1, DP):
        tail_copy(k).start()

    for copy in own_copies:
        copy.wait()
    for k in range(1, 4):
        for copy in experts_y(k):
            copy.wait_recv()

    def gu_total(which):
        here = aligned(which, ROWS)
        total = own_gu[:, here, :].astype(F32)
        for k in range(1, 4):
            total = total + gu_in[k, :, here, :].astype(F32)
        return total

    def down_total(which):
        here = aligned(which, ROWS)
        total = own_down[:, here].astype(F32)
        for k in range(1, 4):
            total = total + down_in[k, :, here].astype(F32)
        return total

    gu_half[...] = gu_total(1 - at.x).astype(BF)
    down_half[...] = down_total(1 - at.x).astype(BF)
    for copy in experts_x():
        copy.start()

    total = tail[:, aligned(d, ROWS)]
    for k in range(1, DP):
        tail_copy(k).wait_recv()
        total = total + tail_in[k]
    query_out[...] = total[0:HEAD, :]
    turned = jnp.concatenate([total, jnp.zeros((384 - TAIL, ROWS), F32)], axis=0).T
    for j in range(TENSOR):
        pieces[j] = turned[j * 8 : (j + 1) * 8, :]

    def last_copy(k, src):
        dest = at.tensor_at(k)
        return remote(
            pieces.at[dest], last.at[src], l_send.at[k], l_recv.at[src], "tensor", dest
        )

    for k in range(1, TENSOR):
        last_copy(k, t).start()
    last[t] = pieces[t]

    gu_out[...] = gu_total(at.x)
    down_out[...] = down_total(at.x)
    for copy in experts_x():
        copy.wait_recv()
    gu_out[...] += gu_half_in[...].astype(F32)
    down_out[...] += down_half_in[...].astype(F32)

    for k in range(1, TENSOR):
        last_copy(k, at.tensor_at(k)).wait_recv()
    kv_out[...] = jnp.concatenate(
        [last[2 * j, :, 128:256] + last[2 * j + 1, :, 128:256] for j in range(CHIPS)], axis=1
    )
    shared = last[0, :, 256:384]
    for j in range(1, TENSOR):
        shared = shared + last[j, :, 256:384]
    rest_out[0] = shared
    for j in range(TENSOR):
        rest_out[j + 1] = last[j, :, 0:128]

    for k in range(1, TENSOR):
        back_copy(k, t).wait_send()
        query_copy(at.tensor_at(k), t).wait_send()
        key_copy(at.tensor_at(k), t).wait_send()
        last_copy(k, t).wait_send()
    for k in range(1, 4):
        for copy in experts_y(k):
            copy.wait_send()
    for copy in experts_x():
        copy.wait_send()
    for k in range(1, DP):
        tail_copy(k).wait_send()
    spread_m.end()
    spread_w.end()


def call(kernel, number, kinds, outs, scratch, args):
    spaces = {"v": pl.BlockSpec(memory_space=pltpu.VMEM), "h": pl.BlockSpec(memory_space=pl.ANY)}
    specs = [spaces[kind] for kind in kinds]
    return pl.pallas_call(
        kernel,
        out_shape=[jax.ShapeDtypeStruct(shape, dtype) for shape, dtype in outs],
        in_specs=specs[: len(args)],
        out_specs=specs[len(args) :],
        scratch_shapes=scratch,
        compiler_params=pltpu.CompilerParams(
            collective_id=number, has_side_effects=True, vmem_limit_bytes=VMEM_BYTES
        ),
    )(*args)


def sems(*counts):
    return [pltpu.SemaphoreType.DMA((count,)) for count in counts]


def rope_tables():
    half = HEAD // 2
    freqs = np.exp(
        np.arange(half, dtype=np.float32) * np.float32(-2.0 * math.log(10000.0) / HEAD)
    ).astype(np.float32)
    angles = np.arange(LENGTH, dtype=np.float32)[:, None] * freqs[None, :]
    cos, sin = np.cos(angles).astype(np.float32), np.sin(angles).astype(np.float32)
    ones, zeros = np.ones((LENGTH, HEAD), np.float32), np.zeros((LENGTH, HEAD), np.float32)
    return (
        np.concatenate([cos, cos, ones], axis=1),
        np.concatenate([-sin, sin, zeros], axis=1),
        np.ascontiguousarray(cos.T),
        np.ascontiguousarray(sin.T),
    )


def body(
    hidden,
    seg_ids,
    key_mask,
    routes,
    gain_attn,
    w_query,
    w_keyval,
    w_out,
    gain_mlp,
    w_router,
    w_gate_up,
    w_down,
    cotangent,
):
    V = pltpu.VMEM
    cosine, sine, cosine_t, sine_t = rope_tables()
    hid, cot = hidden[0], cotangent[0]
    meta = jnp.concatenate(
        [routes[0], key_mask[0][:, None], jnp.zeros((LENGTH, 7), jnp.int32)], axis=1
    )
    shares = jnp.concatenate(
        [w_router, gain_attn[:, None], gain_mlp[:, None], jnp.zeros((8, 94), BF)], axis=1
    )
    columns = jnp.repeat(w_keyval.reshape(8, CHIPS, ROWS).transpose(1, 0, 2), 2, axis=0)
    tiles = jnp.concatenate(
        [columns, jnp.broadcast_to(shares[None], (TENSOR, 8, ROWS))], axis=1
    )
    rows = jnp.concatenate([w_keyval, w_out.T], axis=0)
    (
        normed,
        queries,
        keyvals,
        keyvals_t,
        stats,
        heads_t,
        mid,
        normed_mid,
        wq_own,
        out_t,
        kv_full,
        small,
        gu_all,
        down_all,
        cot_all,
    ) = call(
        attention_kernel,
        1,
        "vhvvvhhvvvv" + "vvvvvvvvvvvvhhh",
        [
            ((LENGTH, WIDTH), BF),
            ((LENGTH, 2 * HEAD), BF),
            ((PADDED, 2 * HEAD), BF),
            ((2 * HEAD, PADDED), BF),
            ((1, LENGTH), F32),
            ((HEAD, LENGTH), F32),
            ((ROWS, WIDTH), F32),
            ((ROWS, WIDTH), BF),
            ((2 * HEAD, WIDTH), BF),
            ((WIDTH, WIDTH), BF),
            ((WIDTH, WIDTH), BF),
            ((WIDTH, ROWS), BF),
            ((2, WIDTH, WIDTH), BF),
            ((2, UNITS, WIDTH), BF),
            ((LENGTH, WIDTH), BF),
        ],
        [
            V((LENGTH, WIDTH), BF),
            V((DP, TENSOR, 16, ROWS), BF),
            V((DP, TENSOR, 16, WIDTH), BF),
            V((PADDED, ROWS), F32),
            V((SPAN, PAIR), F32),
            V((SPAN, PAIR), BF),
            V((1, LENGTH), F32),
            V((WIDTH, ROWS), BF),
            V((TENSOR, HEAD, ROWS), BF),
            V((WIDTH, ROWS), BF),
        ]
        + sems(16, 16, 16, 16, 16, 16, 16, 16, 8, 8, 8, 8, 8, 8, 8, 8, 8, 8, 16, 16, 3),
        (
            hid,
            cot,
            tiles,
            w_query.T,
            rows,
            w_gate_up,
            w_down,
            cosine,
            sine,
            meta,
            seg_ids,
        ),
    )
    parts = [
        V((SLOTS, PAIR, WIDTH), BF),
        V((CHIPS, ROWS, WIDTH), BF),
        V((CHIPS, ROWS, WIDTH), BF),
        V((CHIPS, ROWS, WIDTH), BF),
    ]
    output, mid_grad, mid_low, att_grad_t, gu_grad, down_grad, router_t, gain_grad = call(
        expert_kernel,
        2,
        "vhhhvvvvv" + "vvvvhhvv",
        [
            ((ROWS, WIDTH), BF),
            ((ROWS, WIDTH), F32),
            ((ROWS, WIDTH), BF),
            ((WIDTH, ROWS), BF),
            ((2, WIDTH, WIDTH), BF),
            ((WIDTH, WIDTH), BF),
            ((ROWS, WIDTH), F32),
            ((1, WIDTH), F32),
        ],
        [
            V((LENGTH, WIDTH), BF),
            V((WIDTH, LENGTH), BF),
            V((LENGTH, WIDTH), BF),
            V((2, WIDTH, WIDTH), BF),
            V((WIDTH, WIDTH), BF),
            V((WIDTH, LENGTH), BF),
            V((LENGTH, 2 * WIDTH), BF),
            V((ROWS, LENGTH), BF),
        ]
        + parts
        + parts
        + sems(16, 16, 8, 8, 8, 8, 8, 8, 8, 8, 3),
        (
            normed_mid,
            cot_all,
            gu_all,
            down_all.reshape(WIDTH, WIDTH),
            small,
            meta,
            mid,
            cot,
            out_t,
        ),
    )
    hidden_grad, gu_out, down_out, query_out, kv_out, rest = call(
        back_kernel,
        3,
        "vvvhhvvvvvvvvvvvvvvvvvv" + "vvvvvv",
        [
            ((ROWS, WIDTH), BF),
            ((2, ROWS, WIDTH), F32),
            ((WIDTH, ROWS), F32),
            ((HEAD, ROWS), F32),
            ((8, WIDTH), F32),
            ((TENSOR + 1, 8, ROWS), F32),
        ],
        [
            V((2 * HEAD, LENGTH), BF),
            V((LENGTH, WIDTH), BF),
            V((WIDTH, WIDTH), BF),
            V((PADDED, ROWS), F32),
            V((1, LENGTH), F32),
            V((PADDED, 2 * HEAD), F32),
            V((3 * HEAD, LENGTH), BF),
            V((TENSOR, HEAD, ROWS), BF),
            V((TENSOR, ROWS, ROWS), BF),
            V((WIDTH, ROWS), BF),
            V((TENSOR, ROWS, ROWS), BF),
            V((TAIL, WIDTH), F32),
            V((DP, TAIL, ROWS), F32),
            V((TENSOR, 8, 384), F32),
            V((TENSOR, 8, 384), F32),
            V((2, PAIR, WIDTH), BF),
            V((WIDTH, PAIR), BF),
            V((4, 2, PAIR, WIDTH), BF),
            V((4, WIDTH, PAIR), BF),
            V((2, ROWS, WIDTH), BF),
            V((WIDTH, ROWS), BF),
            V((2, ROWS, WIDTH), BF),
            V((WIDTH, ROWS), BF),
        ]
        + sems(16, 16, 16, 16, 16, 16, 16, 16, 16, 16, 8, 8, 8, 8, 8, 8, 16, 16, 2),
        (
            att_grad_t,
            mid_low,
            mid_grad,
            gu_grad,
            down_grad,
            router_t,
            gain_grad,
            queries,
            keyvals,
            keyvals_t,
            stats,
            heads_t,
            meta,
            seg_ids,
            cosine,
            sine,
            cosine_t,
            sine_t,
            wq_own,
            kv_full,
            normed,
            hid,
            small,
        ),
    )
    shared = rest[0]
    out_grad = rest[1:, :, HEAD : 2 * HEAD].transpose(0, 2, 1).reshape(WIDTH, 8)
    return (
        output[None],
        hidden_grad[None],
        shared[:, 32],
        query_out.T,
        kv_out,
        out_grad,
        shared[:, 33],
        shared[:, 0:32],
        gu_out,
        down_out.reshape(2, UNITS, ROWS),
    )


def solution(mesh):
    return jax.shard_map(
        body,
        mesh=mesh,
        in_specs=(
            P("dp", "tensor", None),
            P("dp", None),
            P("dp", None),
            P("dp", None, None),
            P(("dp", "tensor")),
            P("dp", "tensor"),
            P(("dp", "tensor"), None),
            P(None, ("dp", "tensor")),
            P(("dp", "tensor")),
            P(("dp", "tensor"), None),
            P("tensor", "dp", None),
            P("tensor", None, "dp"),
            P("dp", "tensor", None),
        ),
        out_specs=(
            P("dp", "tensor", None),
            P("dp", "tensor", None),
            P(("dp", "tensor")),
            P("dp", "tensor"),
            P(("dp", "tensor"), None),
            P(None, ("dp", "tensor")),
            P(("dp", "tensor")),
            P(("dp", "tensor"), None),
            P("tensor", "dp", None),
            P("tensor", None, "dp"),
        ),
        check_vma=False,
    )
```

```python
import math

import jax
import jax.numpy as jnp
import numpy as np
from jax import lax
from jax.experimental import pallas as pl
from jax.experimental.pallas import tpu as pltpu
from jax.sharding import PartitionSpec as P

HEAD = 64
LENGTH = 2048
WIDTH = 1024
UNITS = 512
ROWS = 128
PAIR = 256
REACH = 896
SPAN = REACH + PAIR
PADDED = REACH + LENGTH
CHIPS = 8
TENSOR = 16
DP = 8
TAIL = 240
SLOTS = 2
STEP_Z = (0, 0, 1, 3, 1, 3, 2, 2)
STEP_X = (0, 1, 0, 0, 1, 1, 0, 1)
SUM_Z = (1, 1, 2, 2, 3, 3, 0, 0)
SUM_X = (1, 0, 1, 0, 1, 0, 1, 0)
LOWEST = -1e30
BF = jnp.bfloat16
F32 = jnp.float32
MESH = pl.DeviceIdType.MESH
VMEM_BYTES = 62 * 1024 * 1024

NN = (((1,), (0,)), ((), ()))
NT = (((1,), (1,)), ((), ()))


def dot(left, right, dims=NN):
    return lax.dot_general(left, right, dims, preferred_element_type=F32)


def aligned(value, size):
    return pl.ds(pl.multiple_of(value * size, size), size)


def remote(src, dst, send, recv, axis, index):
    return pltpu.make_async_remote_copy(
        src_ref=src,
        dst_ref=dst,
        send_sem=send,
        recv_sem=recv,
        device_id={axis: index},
        device_id_type=MESH,
    )


class Place:
    def __init__(self):
        self.t = lax.axis_index("tensor")
        self.d = lax.axis_index("dp")
        self.core = lax.rem(self.t, 2)
        self.chip = self.t // 2
        self.twin = self.t + 1 - 2 * self.core
        self.x = lax.rem(self.d, 2)
        self.y = self.d // 2
        self.across = self.d + 1 - 2 * self.x
        self.z = self.chip // 2
        self.x_far = lax.rem(self.chip, 2)

    def chip_at(self, k):
        return lax.rem(self.chip + k, CHIPS)

    def same_core(self, k):
        return 2 * self.chip_at(k) + self.core

    def near(self, dz, dx):
        return 2 * lax.rem(self.z + dz, 4) + lax.rem(self.x_far + dx, 2)

    def near_core(self, dz, dx):
        return 2 * self.near(dz, dx) + self.core

    def listed(self, i, all_z, all_x):
        if isinstance(i, int):
            return self.near(all_z[i], all_x[i])
        dz, dx = jnp.int32(0), jnp.int32(0)
        for k in range(CHIPS):
            dz = jnp.where(i == k, all_z[k], dz)
            dx = jnp.where(i == k, all_x[k], dx)
        return self.near(dz, dx)

    def step(self, i):
        return self.listed(i, STEP_Z, STEP_X)

    def sum_step(self, i):
        return self.listed(i, SUM_Z, SUM_X)

    def step_core(self, i):
        return 2 * self.step(i) + self.core

    def tensor_at(self, k):
        return lax.rem(self.t + k, TENSOR)

    def dp_at(self, k):
        return lax.rem(self.d + k, DP)

    def y_at(self, k):
        return lax.rem(self.y + k, 4)

    def enter(self):
        barrier = pltpu.get_barrier_semaphore()
        for k in range(1, TENSOR):
            pl.semaphore_signal(
                barrier, inc=1, device_id={"tensor": self.tensor_at(k)}, device_id_type=MESH
            )
        for k in range(1, DP):
            pl.semaphore_signal(
                barrier, inc=1, device_id={"dp": self.dp_at(k)}, device_id_type=MESH
            )
        pl.semaphore_wait(barrier, TENSOR + DP - 2)


class Spread:
    def __init__(self, place, block, send, recv, source=None):
        self.place, self.block, self.send, self.recv = place, block, send, recv
        self.source = source

    def copy(self, number, index, dest, source=None):
        src = self.block(index) if source is None else source
        return remote(
            src, self.block(index), self.send.at[number], self.recv.at[index], "tensor", dest
        )

    def own(self, k):
        dest = self.place.twin if k == 0 else self.place.same_core(k)
        return self.copy(k, self.place.t, dest, self.source)

    def start(self):
        for k in range(1, CHIPS):
            self.own(k).start()
        self.own(0).start()

    def passed(self, k):
        return self.copy(CHIPS + k, self.place.same_core(k), self.place.twin)

    def arrived(self, index):
        self.copy(0, index, self.place.twin).wait_recv()

    def first(self, k):
        self.arrived(self.place.same_core(k))
        self.passed(k).start()

    def second(self, k):
        self.arrived(2 * self.place.chip_at(k) + 1 - self.place.core)

    def end(self):
        for k in range(CHIPS):
            self.own(k).wait_send()
        for k in range(1, CHIPS):
            self.passed(k).wait_send()


class Ring:
    SENDS = 17

    def __init__(self, place, block, half, send, recv, source=None):
        self.place, self.block, self.half = place, block, half
        self.send, self.recv, self.source = send, recv, source

    def copy(self, number, index, dest, source=None):
        src = self.block(index) if source is None else source
        return remote(
            src, self.block(index), self.send.at[number], self.recv.at[index], "tensor", dest
        )

    def piece(self, number, index, part, dest):
        ref = self.half(index, part)
        return remote(
            ref, ref, self.send.at[number], self.recv.at[TENSOR * part + index], "tensor", dest
        )

    def sent(self, number):
        at = self.place
        if number == 0:
            return self.copy(0, at.t, at.twin, self.source)
        if number < 4:
            return self.copy(number, at.t, at.step_core(number), self.source)
        if number < 6:
            return self.copy(number, at.step_core(1), at.step_core(number - 2))
        if number < 8:
            return self.piece(number, at.step_core(2 * number - 9), 0, at.step_core(2))
        if number < 10:
            return self.piece(number, at.step_core(2 * number - 14), 1, at.step_core(3))
        return self.copy(number, at.step_core(number - 9), at.twin)

    def start(self):
        for number in (1, 2, 3, 0):
            self.sent(number).start()

    def pass_on(self, i):
        index = self.place.step_core(i)
        if i < 6:
            self.copy(0, index, self.place.twin).wait_recv()
        else:
            self.piece(0, index, 0, self.place.twin).wait_recv()
            self.piece(0, index, 1, self.place.twin).wait_recv()
        for number in {1: (4, 5), 2: (8,), 3: (6,), 4: (9,), 5: (7,)}.get(i, ()):
            self.sent(number).start()
        self.sent(9 + i).start()

    def pass_on_at(self, i):
        for k in range(1, CHIPS):

            @pl.when(i == k - 1)
            def _(k=k):
                self.pass_on(k)

    def second(self, i):
        self.copy(0, 2 * self.place.step(i) + 1 - self.place.core, self.place.twin).wait_recv()

    def end(self):
        for number in range(self.SENDS):
            self.sent(number).wait_send()


def whole_ring(place, ref, send, recv, source=None):
    return Ring(
        place,
        lambda b: ref.at[aligned(b, ROWS)],
        lambda b, part: ref.at[pl.ds(pl.multiple_of(b * ROWS + part * HEAD, HEAD), HEAD)],
        send,
        recv,
        source,
    )


class Copies:
    def __init__(self, sems):
        self.sems, self.all, self.done = sems, [], 0

    def start(self, src, dst):
        copy = pltpu.make_async_copy(src, dst, self.sems.at[len(self.all)])
        copy.start()
        self.all.append(copy)

    def wait(self, count=None):
        end = len(self.all) if count is None else self.done + count
        for copy in self.all[self.done : end]:
            copy.wait()
        self.done = end


def lanes(shape):
    return lax.broadcasted_iota(jnp.int32, shape, len(shape) - 1)


def sublanes(shape):
    return lax.broadcasted_iota(jnp.int32, shape, 0)


def swapped(values):
    return jnp.where(
        lanes(values.shape) < HEAD // 2,
        pltpu.roll(values, 2 * HEAD - HEAD // 2, 1),
        pltpu.roll(values, HEAD // 2, 1),
    )


def document_starts(seg):
    starts = jnp.zeros(seg.shape, F32)
    for document in range(8):
        before = jnp.sum(jnp.where(seg < document, 1.0, 0.0), axis=1, keepdims=True)
        starts = starts + jnp.where(seg == document, before, 0.0)
    return starts


def key_codes(mask, code):
    code[0:REACH, :] = jnp.full((REACH, ROWS), -1.0, F32)

    @pl.loop(0, TENSOR)
    def _(i):
        row = mask[:, aligned(i, ROWS)].astype(F32)
        live = jnp.broadcast_to(row, (ROWS, ROWS)).T == 1.0
        places = (sublanes((ROWS, ROWS)) + i * ROWS).astype(F32)
        code[pl.ds(pl.multiple_of(REACH + i * ROWS, ROWS), ROWS), :] = jnp.where(
            live, places, -1.0
        )


def allowed(code, start_row, chunk):
    wide = jnp.concatenate([code, code], axis=1)
    ok = wide >= start_row
    if chunk >= REACH // ROWS:
        key = sublanes((ROWS, PAIR)) + (chunk * ROWS - REACH)
        query = lanes((ROWS, PAIR))
        ok = (ok & (key < query)) | (key == query)
    return ok


def turned_back(grad, r, here):
    cos, sin = r.cosine_t[:, here], r.sine_t[:, here]
    first, second = grad[0 : HEAD // 2], grad[HEAD // 2 : HEAD]
    return jnp.concatenate([first * cos + second * sin, second * cos - first * sin], axis=0)


class Halves:
    def __init__(self, place, parts, twins, sums, send, recv):
        self.place, self.parts, self.twins, self.sums = place, parts, twins, sums
        self.send, self.recv = send, recv

    def half(self, k):
        at = self.place
        return remote(
            self.parts.at[lax.rem(k, SLOTS), aligned(1 - at.core, ROWS), :],
            self.twins.at[k],
            self.send.at[k],
            self.recv.at[k],
            "tensor",
            at.twin,
        )

    def put(self, k, value):
        @pl.when(k >= SLOTS)
        def _():
            self.half(k - SLOTS).wait_send()

        self.parts[lax.rem(k, SLOTS)] = value.astype(BF)
        self.half(k).start()

    def add(self, k):
        self.half(k).wait_recv()
        own = self.parts[lax.rem(k, SLOTS), aligned(self.place.core, ROWS), :].astype(F32)
        self.sums[k] = (own + self.twins[k].astype(F32)).astype(BF)

    def end(self):
        for k in range(CHIPS - SLOTS, CHIPS):
            self.half(k).wait_send()


class Joined:
    def __init__(self, place, sums, crossed, joined, landed, sems):
        self.place, self.sums, self.crossed = place, sums, crossed
        self.joined, self.landed = joined, landed
        self.c_send, self.c_recv, self.send, self.recv = sems

    def cross(self, j):
        return remote(
            self.sums.at[2 * j],
            self.crossed.at[j],
            self.c_send.at[j],
            self.c_recv.at[j],
            "tensor",
            self.place.near_core(0, 1),
        )

    def whole(self, j):
        return remote(
            self.joined.at[j],
            self.landed.at[j],
            self.send.at[j],
            self.recv.at[j],
            "tensor",
            self.place.near_core(j + 1, 0),
        )

    def join(self, j):
        self.cross(j).wait_recv()
        total = self.sums[2 * j + 1].astype(F32) + self.crossed[j].astype(F32)
        self.joined[j] = total.astype(BF)
        self.whole(j).start()

    def result(self):
        self.cross(3).wait_recv()
        total = self.sums[7].astype(F32) + self.crossed[3].astype(F32)
        for j in range(3):
            self.whole(j).wait_recv()
            total = total + self.landed[j].astype(F32)
        return total

    def end(self):
        for j in range(4):
            self.cross(j).wait_send()
        for j in range(3):
            self.whole(j).wait_send()


def unpacked(ref, pair, first):
    both = ref[:, pl.ds(pl.multiple_of(first + pair * 16, 16), 16), :].astype(F32)
    return both[:, 0:8].reshape(ROWS, WIDTH), both[:, 8:16].reshape(ROWS, WIDTH)


def aligned_rows(ref, unit):
    def block(src, part=None):
        if part is None:
            return ref.at[pl.ds(pl.multiple_of(src * 2 * unit, unit), 2 * unit), :]
        return ref.at[pl.ds(pl.multiple_of((src * 2 + part) * unit, unit), unit), :]

    return block


def column_blocks(ref):
    def block(src, part=None):
        if part is None:
            return ref.at[:, aligned(src, ROWS)]
        return ref.at[pl.ds(part * PAIR, PAIR), aligned(src, ROWS)]

    return block


class Stream:
    def __init__(self, place, own, block, r, number):
        self.place, self.own, self.block = place, own, block
        self.send, self.recv = r.e_send, r.e_recv
        self.first_send, self.first_recv = 9 * number, 16 * number

    def at_y(self, k, other=False):
        at = self.place
        column = 1 - at.x if other else at.x
        return 2 * at.y_at(k) + column

    def copy(self, number, src, dest, part=None, own=False):
        ref = self.block(src, part)
        return remote(
            self.own if own else ref,
            ref,
            self.send.at[self.first_send + number],
            self.recv.at[self.first_recv + (8 if part == 1 else 0) + src],
            "dp",
            dest,
        )

    def sent(self, number):
        at, at_y = self.place, self.at_y
        if number == 0:
            return self.copy(0, at.d, at.across, own=True)
        if number < 3:
            return self.copy(number, at.d, at_y(2 * number - 1), own=True)
        if number < 5:
            return self.copy(number, at.across, at_y(2 * number - 5))
        other = number > 6
        if number % 2:
            return self.copy(number, at_y(3, other), at_y(1), 0)
        return self.copy(number, at_y(1, other), at_y(3), 1)

    def arrived(self, src, halves=False):
        for part in (0, 1) if halves else (None,):
            self.copy(0, src, self.place.across, part).wait_recv()

    def start(self):
        for number in (0, 1, 2):
            self.sent(number).start()

    def go_on(self):
        self.arrived(self.place.across)
        self.sent(3).start()
        self.sent(4).start()
        self.arrived(self.at_y(3))
        self.sent(5).start()
        self.arrived(self.at_y(1))
        self.sent(6).start()

    def go_further(self):
        self.arrived(self.at_y(3, True))
        self.sent(7).start()
        self.arrived(self.at_y(1, True))
        self.sent(8).start()

    def finish(self):
        self.arrived(self.at_y(2), True)
        self.arrived(self.at_y(2, True), True)

    def end(self):
        for number in range(9):
            self.sent(number).wait_send()


def expert_streams(at, r, e, gu_all, down_all):
    return (
        Stream(at, r.gu.at[e], aligned_rows(gu_all, HEAD), r, 0),
        Stream(at, r.down.at[e], column_blocks(down_all), r, 1),
    )


def attention_kernel(r):
    at = Place()
    t, d = at.t, at.d
    copies = Copies(r.local)
    copies.start(r.cosine, r.cosine_v)
    copies.start(r.sine, r.sine_v)
    r.hidden_all[aligned(t, ROWS), :] = r.hid[...]
    keyval, out_rows = r.w_keyval[...].astype(F32), r.w_out_t[...].astype(F32)
    r.rows[...] = jnp.concatenate([keyval, out_rows], axis=0).astype(BF)
    r.row_dp[d] = r.rows[...]
    r.shares[...] = jnp.zeros((8, ROWS), F32)
    r.shares[:, 0:32] = r.router[...].astype(F32)
    same = sublanes((8, 8)) == lanes((8, 8))
    for column, gain in ((32, r.gain_one), (33, r.gain_two)):
        wide = jnp.broadcast_to(gain[...].astype(F32), (8, 8))
        r.shares[:, column : column + 1] = jnp.sum(
            jnp.where(same, wide, 0.0), axis=1, keepdims=True
        )
    for j in range(CHIPS):
        tile = jnp.concatenate([keyval[:, j * ROWS : (j + 1) * ROWS], r.shares[...]], axis=0)
        r.tiles[2 * j] = tile.astype(BF)
        r.tiles[2 * j + 1] = tile.astype(BF)
    r.tile_all[d, t] = r.tiles[t]
    r.wq_all[HEAD : 2 * HEAD, :] = jnp.zeros((HEAD, WIDTH), BF)
    r.wq_all[0:HEAD, aligned(d, ROWS)] = r.w_query_t[...]
    at.enter()

    def tile_one(k, src):
        dest = at.tensor_at(k)
        return remote(
            r.tiles.at[dest],
            r.tile_all.at[d, src],
            r.t1_send.at[k],
            r.t1_recv.at[src],
            "tensor",
            dest,
        )

    def tile_two(k, src):
        ref = r.tile_all.at[src]
        return remote(ref, ref, r.t2_send.at[k], r.t2_recv.at[src], "dp", at.dp_at(k))

    def rows_dp(k, src):
        return remote(
            r.rows, r.row_dp.at[src], r.rd_send.at[k], r.rd_recv.at[src], "dp", at.dp_at(k)
        )

    def wq_dp(k, src):
        return remote(
            r.w_query_t,
            r.wq_all.at[pl.ds(0, HEAD), aligned(src, ROWS)],
            r.wq_send.at[k],
            r.wq_recv.at[src],
            "dp",
            at.dp_at(k),
        )

    streams = expert_streams(at, r, 0, r.gu_all, r.down_all)

    for k in range(1, TENSOR):
        tile_one(k, t).start()
    for k in range(1, DP):
        wq_dp(k, d).start()
    ring_h = whole_ring(at, r.hidden_all, r.h_send, r.h_recv)
    ring_h.start()
    copies.start(r.gu.at[0], r.gu_all.at[aligned(d, ROWS), :])
    copies.start(r.down.at[0], r.down_all.at[:, aligned(d, ROWS)])
    copies.start(r.cot, r.cot_all.at[aligned(t, ROWS)])

    key_codes(r.mask, r.code)
    r.starts[...] = document_starts(r.seg[...])
    r.keyvals_v[0:REACH, :] = jnp.zeros((REACH, 2 * HEAD), BF)
    r.keyvals_tv[:, 0:REACH] = jnp.zeros((2 * HEAD, REACH), BF)

    for k in range(1, TENSOR):
        tile_one(k, at.tensor_at(k)).wait_recv()
    for k in range(1, DP):
        tile_two(k, d).start()
    for k in range(1, DP):
        rows_dp(k, d).start()
    for stream in streams:
        stream.start()
    for i in range(1, 4):
        ring_h.pass_on(i)
    for k in range(1, DP):
        wq_dp(k, at.dp_at(k)).wait_recv()
        tile_two(k, at.dp_at(k)).wait_recv()
    for j in range(DP):
        both = r.tile_all[j].astype(F32)
        r.wqk[j * ROWS : (j + 1) * ROWS, ROWS:PAIR] = both[:, 0:8].reshape(ROWS, ROWS).astype(BF)
        r.small[j * ROWS : (j + 1) * ROWS, :] = both[:, 8:16].reshape(ROWS, ROWS).astype(BF)
    r.wqk[:, 0:ROWS] = r.wq_all[...].astype(F32).T.astype(BF)
    columns = r.small[...].astype(F32).T
    gain_one = columns[32:33, :]
    gain_two = columns[33:34, :]
    copies.wait(2)
    ring_o = Ring(
        at,
        lambda b: r.out_all.at[b],
        lambda b, part: r.out_all.at[b, pl.ds(part * 32, 32)],
        r.o_send,
        r.o_recv,
    )

    @pl.loop(0, CHIPS)
    def _(i):
        @pl.when(i == 1)
        def _():
            ring_h.pass_on(4)
            ring_h.pass_on(5)

        @pl.when(i == 2)
        def _():
            for k in range(1, DP):
                rows_dp(k, at.dp_at(k)).wait_recv()
            both = r.row_dp[...].astype(F32)
            r.wqkv_own[0:HEAD, :] = r.wq_all[0:HEAD, :]
            r.wqkv_own[HEAD : 2 * HEAD, :] = both[:, 0:8].reshape(HEAD, WIDTH).astype(BF)
            r.out_all[t] = both[:, 8:16].reshape(HEAD, WIDTH).astype(BF)
            ring_o.start()

        @pl.when(i == 5)
        def _():
            ring_h.pass_on(6)
            ring_h.pass_on(7)

        ring_h.second(i)
        block = at.step(i)
        here = aligned(block, PAIR)
        hidden = r.hidden_all[here, :].astype(F32)
        inverse = lax.rsqrt(jnp.mean(hidden * hidden, axis=1, keepdims=True) + 1e-6)
        unit = (hidden * inverse * gain_one).astype(BF)
        r.normed_v[here, :] = unit
        cos, sin = r.cosine_v[here, :], r.sine_v[here, :]
        projected = dot(unit, r.wqk[...])
        query, keyval = projected[:, 0:ROWS], projected[:, ROWS:PAIR]
        query = (query * cos + swapped(query) * sin).astype(BF)
        r.queries_v[here, :] = (query.astype(F32) * (1.0 / math.sqrt(HEAD))).astype(BF)
        keyval = keyval * cos + swapped(keyval) * sin
        later = pl.ds(pl.multiple_of(REACH + block * PAIR, ROWS), PAIR)
        r.keyvals_v[later, :] = keyval.astype(BF)
        r.keyvals_tv[:, later] = keyval.T.astype(BF)

    copies.start(r.normed_v, r.normed)
    copies.start(r.queries_v, r.queries)
    copies.start(r.keyvals_v, r.keyvals)
    copies.start(r.keyvals_tv, r.keyvals_t)
    ring_o.pass_on(1)
    ring_c = whole_ring(at, r.cot_all, r.c_send, r.c_recv, r.cot)
    ring_c.start()

    def att_copy(dest, src):
        return remote(
            r.att_src.at[dest],
            r.att_t.at[aligned(src, HEAD), :],
            r.a_send.at[dest],
            r.a_recv.at[src],
            "tensor",
            dest,
        )

    @pl.loop(0, CHIPS)
    def _(i):
        for step, chips in ((2, (2, 3)), (5, (4, 5))):

            @pl.when(i == step)
            def _(chips=chips):
                for k in chips:
                    ring_o.pass_on(k)

        block = at.chip_at(i + 1)
        here = aligned(block, PAIR)
        query = r.queries_v[here, :]
        start_row = r.starts[:, here]
        top = jnp.full((1, PAIR), LOWEST, F32)
        for chunk in range(SPAN // ROWS):
            keys = pl.ds(pl.multiple_of(block * PAIR + chunk * ROWS, ROWS), ROWS)
            score = dot(r.keyvals_v[keys, :], query, NT)
            score = jnp.where(allowed(r.code[keys, :], start_row, chunk), score, LOWEST)
            r.scores[chunk * ROWS : (chunk + 1) * ROWS, :] = score
            top = jnp.maximum(top, jnp.max(score, axis=0, keepdims=True))
        total = jnp.zeros((1, PAIR), F32)
        for chunk in range(SPAN // ROWS):
            place = slice(chunk * ROWS, (chunk + 1) * ROWS)
            weight = jnp.exp(r.scores[place, :] - top)
            total = total + jnp.sum(weight, axis=0, keepdims=True)
            r.probs[place, :] = weight.astype(BF)
        window = pl.ds(pl.multiple_of(block * PAIR, ROWS), SPAN)
        head = dot(r.keyvals_tv[HEAD : 2 * HEAD, window], r.probs[...]) / total
        r.heads_t[:, here] = head
        r.stats[:, here] = top + jnp.log(total)
        r.att_src[2 * block] = head[:, 0:ROWS].astype(BF)
        r.att_src[2 * block + 1] = head[:, ROWS:PAIR].astype(BF)

        @pl.when(i < CHIPS - 1)
        def _():
            att_copy(2 * block, t).start()
            att_copy(2 * block + 1, t).start()

        @pl.when(i == CHIPS - 1)
        def _():
            att_copy(at.twin, t).start()

    r.att_t[aligned(t, HEAD), :] = r.att_src[t]
    ring_o.pass_on(6)
    ring_o.pass_on(7)
    for stream in streams:
        stream.go_on()
    for i in range(1, 4):
        ring_c.pass_on(i)
    for i in range(CHIPS):
        ring_o.second(i)

    @pl.loop(0, 4)
    def _(j):
        first, second = unpacked(r.out_all, j, 0)
        r.out_tv[aligned(2 * j, ROWS), :] = first.astype(BF)
        r.out_tv[aligned(2 * j + 1, ROWS), :] = second.astype(BF)

    copies.start(r.out_tv, r.out_t)
    ring_c.pass_on(4)
    ring_c.pass_on(5)
    for k in range(1, TENSOR):
        att_copy(at.tensor_at(k), at.tensor_at(k)).wait_recv()
    attended = r.att_t[...].astype(F32).T.astype(BF)
    r.att_rows[...] = attended
    middle = r.hid[...].astype(F32) + dot(attended, r.out_tv[...], NT)
    r.mid[...] = middle
    inverse = lax.rsqrt(jnp.mean(middle * middle, axis=1, keepdims=True) + 1e-6)
    r.normed_mid[...] = (middle * inverse * gain_two).astype(BF)

    for stream in streams:
        stream.go_further()
    ring_c.pass_on(6)
    ring_c.pass_on(7)
    for i in range(CHIPS):
        ring_c.second(i)
    for stream in streams:
        stream.finish()
    for k in range(1, TENSOR):
        tile_one(k, t).wait_send()
        att_copy(at.tensor_at(k), t).wait_send()
    for k in range(1, DP):
        tile_two(k, d).wait_send()
        rows_dp(k, d).wait_send()
        wq_dp(k, d).wait_send()
    for stream in streams:
        stream.end()
    ring_h.end()
    ring_o.end()
    ring_c.end()
    copies.wait()


def expert_kernel(r):
    at = Place()
    t = at.t
    copies = Copies(r.local)
    copies.start(r.gu_all, r.gus.at[0])
    copies.start(r.down_all, r.downs.at[pl.ds(0, UNITS)])
    copies.start(r.cot_all, r.cots)
    copies.start(r.gu.at[1], r.gus.at[1, aligned(at.d, ROWS)])
    copies.start(r.down.at[1], r.downs.at[pl.ds(UNITS, UNITS), aligned(at.d, ROWS)])
    copies.start(r.out_t, r.out_tv)
    r.nm_all[aligned(t, ROWS), :] = r.normed_mid[...]
    at.enter()
    ring = whole_ring(at, r.nm_all, r.g_send, r.g_recv)
    ring.start()
    halves_n = Halves(at, r.n_parts, r.n_twins, r.n_sums, r.ntw_send, r.ntw_recv)
    halves_m = Halves(at, r.m_parts, r.m_twins, r.m_sums, r.mtw_send, r.mtw_recv)
    joined = Joined(
        at,
        r.n_sums,
        r.n_crossed,
        r.n_joined,
        r.n_landed,
        (r.nc_send, r.nc_recv, r.n_send, r.n_recv),
    )
    streams = expert_streams(at, r, 1, r.gus.at[1], r.downs.at[pl.ds(UNITS, UNITS)])
    for stream in streams:
        stream.start()

    def moe_along(j):
        return remote(
            r.m_sums.at[pl.ds(2 * j, 2)],
            r.m_landed.at[j],
            r.m_send.at[j],
            r.m_recv.at[j],
            "tensor",
            at.near_core(j + 1, 0),
        )

    copies.wait()

    def over_y(k):
        y = at.y_at(k)
        return (
            remote(
                r.gus.at[0, aligned(y, PAIR), :],
                r.y_gu.at[k],
                r.x_send.at[k],
                r.x_recv.at[k],
                "dp",
                2 * y + at.x,
            ),
            remote(
                r.down_first.at[:, aligned(y, PAIR)],
                r.y_down.at[k],
                r.y_send.at[k],
                r.y_recv.at[k],
                "dp",
                2 * y + at.x,
            ),
        )

    def one_pass(e):
        @pl.loop(0, CHIPS)
        def _(i):
            if e == 0:
                ring.pass_on_at(i)
                ring.second(i)

                @pl.when(i == 5)
                def _():
                    for stream in streams:
                        stream.go_on()

            here = aligned(at.step(i) if e == 0 else at.sum_step(i), PAIR)
            nm = r.nm_all[here, :]
            place = lanes((PAIR, ROWS))
            if e == 0:
                r.nm_t[:, here] = nm.T
                expert = sublanes((ROWS, PAIR))
                named = expert == r.routes_t[0:1, here]
                for j in range(1, 8):
                    named = named | (expert == r.routes_t[j : j + 1, here])
                named = jnp.where(named, 1.0, 0.0).T > 0.5
                logits = jnp.where(named, dot(nm, r.small[...]), LOWEST)
                powers = jnp.exp(logits - jnp.max(logits, axis=1, keepdims=True))
                powers = jnp.where(named, powers, 0.0)
                gates = powers / jnp.sum(powers, axis=1, keepdims=True)
            else:
                kept = r.gates[here, :]
                gates = jnp.where(place == 2 * HEAD - 1, 0.0, kept)
                earlier = kept[:, 2 * HEAD - 1 : 2 * HEAD]
            mine = place == 2 * t + e
            gate = jnp.sum(jnp.where(mine, gates, 0.0), axis=1, keepdims=True)
            act_grad = dot(r.cots[here, :], r.downs[e * UNITS : (e + 1) * UNITS, :], NT)
            projected = dot(nm, r.gus[e])
            first, up = projected[:, :UNITS], projected[:, UNITS:]
            sigmoid = 1.0 / (1.0 + jnp.exp(-first))
            silu = first * sigmoid
            activated = silu * up
            gate_grad = jnp.sum(activated * act_grad, axis=1, keepdims=True)
            gate_grads = jnp.where(mine, gate_grad, 0.0)
            weighted = (activated * gate).astype(BF)
            r.weighted_t[:, here] = weighted.T
            act_grad = act_grad * gate
            r.proj_grads[here, 0:UNITS] = (
                act_grad * up * (sigmoid * (1.0 + first * (1.0 - sigmoid)))
            ).astype(BF)
            r.proj_grads[here, UNITS:WIDTH] = (act_grad * silu).astype(BF)
            normed_part = dot(r.proj_grads[here, :], r.gus[e], NT)
            if e == 0:
                r.gates[here, :] = jnp.where(place == 2 * HEAD - 1, gate_grad, gates)
                r.weighted[here, :] = weighted
                r.n_first[here, :] = normed_part.astype(BF)
                return
            gate_grads = gate_grads + jnp.where(place == 2 * t, earlier, 0.0)
            mean = jnp.sum(gates * gate_grads, axis=1, keepdims=True)
            logit_grad = gates * (gate_grads - mean)
            r.logit_t[:, here] = logit_grad.T.astype(BF)
            normed_part = normed_part + dot(logit_grad.astype(BF), r.small[...], NT)
            halves_n.put(i, normed_part + r.n_first[here, :].astype(F32))
            both = jnp.concatenate([r.weighted[here, :], weighted], axis=1)
            halves_m.put(i, dot(both, r.downs[...]))

            @pl.when(i > 0)
            def _():
                halves_n.add(i - 1)
                halves_m.add(i - 1)

            for j in range(4):

                @pl.when(i == 2 * j + 1)
                def _(j=j):
                    joined.cross(j).start()

            for j in range(2):

                @pl.when(i == 2 * j + 4)
                def _(j=j):
                    joined.join(j)

            @pl.when(i == 3)
            def _():
                moe_along(0).start()

    def weight_gradients(e):
        @pl.loop(0, 4)
        def _(j):
            strip = aligned(j, PAIR)
            r.gus[e, strip, :] = dot(r.nm_t[strip, :], r.proj_grads[...]).astype(BF)

        @pl.loop(0, 2)
        def _(j):
            strip = aligned(j, PAIR)
            result = dot(r.weighted_t[strip, :], r.cots[...]).astype(BF)
            if e == 0:
                r.down_first[strip, :] = result
            else:
                r.downs[pl.ds(pl.multiple_of(UNITS + j * PAIR, PAIR), PAIR), :] = result

    one_pass(0)
    for stream in streams:
        stream.go_further()
    weight_gradients(0)
    for k in range(1, 4):
        for copy in over_y(k):
            copy.start()
    for stream in streams:
        stream.finish()
    one_pass(1)
    joined.join(2)
    halves_n.add(CHIPS - 1)
    halves_m.add(CHIPS - 1)
    moe_along(1).start()
    for stream in streams:
        stream.end()
    weight_gradients(1)
    copies.start(r.gus.at[1], r.gu_grad)
    copies.start(r.downs.at[pl.ds(UNITS, UNITS)], r.down_grad)
    r.router_t[...] = dot(r.logit_t[...], r.nm_all[...])[0:32, :]

    gain_two = r.small[...].astype(F32).T[33:34, :]
    normed_grad = joined.result()
    middle = r.mid[...]
    inverse = lax.rsqrt(jnp.mean(middle * middle, axis=1, keepdims=True) + 1e-6)
    unit = middle * inverse
    r.gain_grad[...] = jnp.sum(normed_grad * unit, axis=0, keepdims=True)
    scaled = normed_grad * gain_two
    grad = r.cot[...].astype(F32) + inverse * (
        scaled - unit * jnp.mean(scaled * unit, axis=1, keepdims=True)
    )
    r.mid_grad[...] = grad
    turned = grad.T.reshape(DP, TENSOR, 8, ROWS).transpose(1, 0, 2, 3)
    r.mid_t[...] = turned.reshape(WIDTH, ROWS).astype(BF)
    r.att_grad_t[...] = dot(grad.astype(BF), r.out_tv[...]).T.astype(BF)
    across, own = r.m_sums[6].astype(F32), r.mid[...] + r.m_sums[7].astype(F32)
    for j in range(2):
        moe_along(j).wait_recv()
        across = across + r.m_landed[j, 0].astype(F32)
        own = own + r.m_landed[j, 1].astype(F32)
    r.moe_across[...] = across
    r.moe_own[...] = own
    r.moe_last[...] = r.m_sums[4:6]
    gu = r.gus[0, aligned(at.y, PAIR), :].astype(F32)
    down = r.down_first[:, aligned(at.y, PAIR)].astype(F32)
    for k in range(1, 4):
        for copy in over_y(k):
            copy.wait_recv()
        gu = gu + r.y_gu[k].astype(F32)
        down = down + r.y_down[k].astype(F32)
    r.ys_gu[0] = gu[0:ROWS].astype(BF)
    r.ys_gu[1] = gu[ROWS:PAIR].astype(BF)
    r.ys_down[0] = down[:, 0:ROWS].astype(BF)
    r.ys_down[1] = down[:, ROWS:PAIR].astype(BF)
    for k in range(1, 4):
        for copy in over_y(k):
            copy.wait_send()
    ring.end()
    for j in range(2):
        moe_along(j).wait_send()
    halves_n.end()
    halves_m.end()
    joined.end()
    copies.wait()


def back_kernel(r):
    at = Place()
    t, d = at.t, at.d
    copies = Copies(r.local)
    copies.start(r.queries, r.queries_v)
    copies.start(r.keyvals, r.keyvals_v)
    copies.start(r.keyvals_t, r.keyvals_tv)
    copies.start(r.gu_grad.at[aligned(at.y, PAIR), :], r.gu_own)
    copies.start(r.down_grad.at[:, aligned(at.y, PAIR)], r.down_own)
    copies.start(r.normed, r.normed_v)
    r.grads_t[0:HEAD, :] = jnp.zeros((HEAD, LENGTH), BF)
    r.grads_t[HEAD : 2 * HEAD, aligned(t, ROWS)] = r.att_grad_t[aligned(t, HEAD), :]
    r.wqkv[t] = r.wqkv_own[...]
    at.enter()

    def back_copy(k, src):
        dest = at.tensor_at(k)
        return remote(
            r.att_grad_t.at[aligned(dest, HEAD), :],
            r.grads_t.at[pl.ds(HEAD, HEAD), aligned(src, ROWS)],
            r.g_send.at[k],
            r.g_recv.at[src],
            "tensor",
            dest,
        )

    def then_across():
        return (
            remote(
                r.ys_gu.at[1 - at.x], r.yx_gu0, r.x_send.at[0], r.x_recv.at[0], "dp", at.across
            ),
            remote(
                r.ys_down.at[1 - at.x], r.yx_down0, r.x_send.at[1], r.x_recv.at[1], "dp", at.across
            ),
        )

    def pair(gu_src, gu_dst, down_src, down_dst, number, dest):
        return (
            remote(gu_src, gu_dst, r.gu_send.at[number], r.gu_recv.at[number], "dp", dest),
            remote(down_src, down_dst, r.dn_send.at[number], r.dn_recv.at[number], "dp", dest),
        )

    def over_y(k):
        y = at.y_at(k)
        return pair(
            r.gu_grad.at[aligned(y, PAIR), :],
            r.y_gu.at[k],
            r.down_grad.at[:, aligned(y, PAIR)],
            r.y_down.at[k],
            k,
            2 * y + at.x,
        )

    def then_x():
        return pair(r.s_gu, r.yx_gu, r.s_down, r.yx_down, 0, at.across)

    for k in range(1, TENSOR):
        back_copy(k, t).start()
    ring_w = Ring(
        at,
        lambda b: r.wqkv.at[b],
        lambda b, part: r.wqkv.at[b, pl.ds(part * HEAD, HEAD)],
        r.w_send,
        r.w_recv,
    )
    ring_w.start()
    for k in range(1, 4):
        for copy in over_y(k):
            copy.start()
    for copy in then_across():
        copy.start()

    key_codes(r.mask, r.code)
    r.starts[...] = document_starts(r.seg[...])
    r.kv_sum[...] = jnp.zeros((PADDED, 2 * HEAD), F32)
    r.out_terms[...] = (
        dot(r.mid_t[...], r.att_rows[...]).reshape(CHIPS, ROWS, WIDTH).astype(BF)
    )

    def out_half():
        return remote(
            r.out_terms.at[:, aligned(1 - at.core, HEAD), :],
            r.out_twins,
            r.ot_send.at[0],
            r.ot_recv.at[0],
            "tensor",
            at.twin,
        )

    out_half().start()
    copies.wait(3)
    for k in range(1, TENSOR):
        back_copy(k, at.tensor_at(k)).wait_recv()

    def query_copy(dest, src):
        return remote(
            r.query_src.at[dest],
            r.query_all.at[src],
            r.b_send.at[dest],
            r.b_recv.at[src],
            "tensor",
            dest,
        )

    @pl.loop(0, CHIPS)
    def _(i):
        for step, chips in ((2, (1,)), (3, (2, 3)), (6, (4, 5))):

            @pl.when(i == step)
            def _(chips=chips):
                for k in chips:
                    ring_w.pass_on(k)

        block = at.chip_at(i + 1)
        here = aligned(block, PAIR)
        query = r.queries_v[here, :]
        start_row = r.starts[:, here]
        stat = r.stats[:, here]
        grad_t = r.grads_t[:, here]
        grad_rows = grad_t.astype(F32).T.astype(BF)
        head = r.heads_t[:, here]
        delta = jnp.sum(head * grad_t[HEAD : 2 * HEAD, :].astype(F32), axis=0, keepdims=True)
        query_grad = jnp.zeros((HEAD, PAIR), F32)
        for chunk in range(SPAN // ROWS):
            keys = pl.ds(pl.multiple_of(block * PAIR + chunk * ROWS, ROWS), ROWS)
            both = r.keyvals_v[keys, :]
            score = dot(both, query, NT)
            ok = allowed(r.code[keys, :], start_row, chunk)
            prob = jnp.exp(jnp.where(ok, score - stat, LOWEST))
            prob_grad = dot(both, grad_t)
            score_grad = (prob * (prob_grad - delta)).astype(BF)
            r.kv_sum[keys, :] += dot(score_grad, query) + dot(prob.astype(BF), grad_rows)
            query_grad = query_grad + dot(r.keyvals_tv[0:HEAD, keys], score_grad)
        turned = turned_back(query_grad * (1.0 / math.sqrt(HEAD)), r, here).astype(BF)
        r.tail_left[0:HEAD, here] = turned
        r.query_src[2 * block] = turned[:, 0:ROWS]
        r.query_src[2 * block + 1] = turned[:, ROWS:PAIR]

        @pl.when(i < CHIPS - 1)
        def _():
            query_copy(2 * block, t).start()
            query_copy(2 * block + 1, t).start()

        @pl.when(i == CHIPS - 1)
        def _():
            query_copy(at.twin, t).start()

    @pl.loop(0, CHIPS)
    def _(i):
        here = aligned(i, PAIR)
        grad = r.kv_sum[pl.ds(pl.multiple_of(REACH + i * PAIR, ROWS), PAIR), :].T
        grad = jnp.concatenate(
            [turned_back(grad[0:HEAD], r, here), grad[HEAD : 2 * HEAD]], axis=0
        ).astype(BF)
        r.tail_left[HEAD : 3 * HEAD, here] = grad
        r.back_src[2 * i] = grad[:, 0:ROWS]
        r.back_src[2 * i + 1] = grad[:, ROWS:PAIR]

    def grad_copy(k, src):
        dest = at.tensor_at(k)
        return remote(
            r.back_src.at[dest],
            r.back_all.at[src],
            r.q_send.at[k],
            r.q_recv.at[src],
            "tensor",
            dest,
        )

    for k in range(1, TENSOR):
        grad_copy(k, t).start()
    r.back_all[t] = r.back_src[t]
    r.query_all[t] = r.query_src[t]
    out_half().wait_recv()
    r.out_sums[...] = (
        r.out_terms[:, aligned(at.core, HEAD), :].astype(F32) + r.out_twins[...].astype(F32)
    ).astype(BF)

    def out_along(k):
        return remote(
            r.out_sums.at[pl.ds(2 * lax.rem(at.z + k, 4), 2)],
            r.out_landed.at[k],
            r.o_send.at[k],
            r.o_recv.at[k],
            "tensor",
            at.near_core(k, 0),
        )

    def out_across():
        return remote(
            r.out_joined,
            r.out_crossed,
            r.o_send.at[0],
            r.o_recv.at[0],
            "tensor",
            at.near_core(0, 1),
        )

    def out_total(x):
        total = r.out_sums[2 * at.z + x].astype(F32)
        for k in range(1, 4):
            total = total + r.out_landed[k, x].astype(F32)
        return total

    for k in range(1, 4):
        out_along(k).start()

    def moe_along():
        return remote(
            r.moe_last, r.m_landed, r.m_send.at[0], r.m_recv.at[0], "tensor", at.near_core(3, 0)
        )

    def moe_across():
        return remote(
            r.m_joined, r.m_crossed, r.m_send.at[1], r.m_recv.at[1], "tensor", at.near_core(0, 1)
        )

    moe_along().start()

    copies.wait()
    r.tail[0 : 3 * HEAD, :] = dot(r.tail_left[...], r.normed_v[...]).astype(BF)

    ring_w.pass_on(6)
    ring_w.pass_on(7)
    for i in range(CHIPS):
        ring_w.second(i)

    @pl.loop(0, 4)
    def _(j):
        first, second = unpacked(r.wqkv, j, HEAD)
        r.kv_full[aligned(2 * j, ROWS), :] = first.astype(BF)
        r.kv_full[aligned(2 * j + 1, ROWS), :] = second.astype(BF)

    for k in range(1, TENSOR):
        grad_copy(k, at.tensor_at(k)).wait_recv()
        query_copy(at.tensor_at(k), at.tensor_at(k)).wait_recv()
    query_rows = r.query_all[...].astype(F32).reshape(WIDTH, ROWS).T.astype(BF)
    pairs = r.back_all[...].astype(F32).reshape(CHIPS, 2, ROWS, ROWS)
    kv_rows = (pairs[:, 0] + pairs[:, 1]).reshape(WIDTH, ROWS).T.astype(BF)
    wq_full = r.wqkv[:, 0:HEAD, :].reshape(WIDTH, WIDTH)
    normed_grad = dot(query_rows, wq_full) + dot(kv_rows, r.kv_full[...], NT)
    hidden = r.hid[...].astype(F32)
    inverse = lax.rsqrt(jnp.mean(hidden * hidden, axis=1, keepdims=True) + 1e-6)
    unit = hidden * inverse
    gain_one = r.small[...].astype(F32).T[32:33, :]
    gain_one_grad = jnp.sum(normed_grad * unit, axis=0, keepdims=True)
    scaled = normed_grad * gain_one
    r.hidden_grad[...] = (
        r.mid_grad[...]
        + inverse * (scaled - unit * jnp.mean(scaled * unit, axis=1, keepdims=True))
    ).astype(BF)
    r.tail[3 * HEAD : 3 * HEAD + 32, :] = r.router_t[...].astype(BF)
    row = sublanes((16, WIDTH))
    r.tail[3 * HEAD + 32 : TAIL, :] = jnp.where(
        row == 0, gain_one_grad, jnp.where(row == 1, r.gain_grad[...], 0.0)
    ).astype(BF)

    def tail_copy(k):
        dest = at.dp_at(k)
        return remote(
            r.tail.at[:, aligned(dest, ROWS)],
            r.tail_in.at[k],
            r.t_send.at[k],
            r.t_recv.at[k],
            "dp",
            dest,
        )

    for k in range(1, DP):
        tail_copy(k).start()

    for k in range(1, 4):
        for copy in over_y(k):
            copy.wait_recv()

    def y_total(x):
        here = aligned(x, ROWS)
        gu = r.gu_own[here, :].astype(F32)
        down = r.down_own[:, here].astype(F32)
        for k in range(1, 4):
            gu = gu + r.y_gu[k, here, :].astype(F32)
            down = down + r.y_down[k, :, here].astype(F32)
        return gu, down

    gu, down = y_total(1 - at.x)
    r.s_gu[...] = gu.astype(BF)
    r.s_down[...] = down.astype(BF)
    for copy in then_x():
        copy.start()

    for k in range(1, 4):
        out_along(k).wait_recv()
    r.out_joined[...] = out_total(1 - at.x_far).astype(BF)
    out_across().start()
    moe_along().wait_recv()
    r.m_joined[...] = (r.moe_across[...] + r.m_landed[0].astype(F32)).astype(BF)
    moe_across().start()
    out_across().wait_recv()
    r.out_rows[...] = out_total(at.x_far) + r.out_crossed[...].astype(F32)

    def out_copy(k):
        dest = at.dp_at(k)
        return remote(
            r.out_rows.at[aligned(dest, 8), :],
            r.out_in.at[k],
            r.od_send.at[k],
            r.od_recv.at[k],
            "dp",
            dest,
        )

    for k in range(1, DP):
        out_copy(k).start()

    total = r.tail[:, aligned(d, ROWS)].astype(F32)
    for k in range(1, DP):
        tail_copy(k).wait_recv()
        total = total + r.tail_in[k].astype(F32)
    r.query_out[...] = total[0:HEAD, :]
    turned = jnp.concatenate(
        [total[HEAD:TAIL], jnp.zeros((256 + HEAD - TAIL, ROWS), F32)], axis=0
    ).T
    for j in range(TENSOR):
        r.pieces[j] = turned[j * 8 : (j + 1) * 8, :]

    def last_copy(k, src):
        dest = at.tensor_at(k)
        return remote(
            r.pieces.at[dest], r.last.at[src], r.l_send.at[k], r.l_recv.at[src], "tensor", dest
        )

    for k in range(1, TENSOR):
        last_copy(k, t).start()
    r.last[t] = r.pieces[t]

    moe_across().wait_recv()
    r.output[...] = (
        r.moe_own[...] + r.m_landed[1].astype(F32) + r.m_crossed[...].astype(F32)
    ).astype(BF)

    gu, down = y_total(at.x)
    for copy in then_x():
        copy.wait_recv()
    r.gu_out[1] = gu + r.yx_gu[...].astype(F32)
    r.down_out[1] = down + r.yx_down[...].astype(F32)
    for copy in then_across():
        copy.wait_recv()
    r.gu_out[0] = r.ys_gu[at.x].astype(F32) + r.yx_gu0[...].astype(F32)
    r.down_out[0] = r.ys_down[at.x].astype(F32) + r.yx_down0[...].astype(F32)

    total = r.out_rows[aligned(d, 8), :]
    for k in range(1, DP):
        out_copy(k).wait_recv()
        total = total + r.out_in[k]
    r.out_grad[...] = total
    for k in range(1, TENSOR):
        last_copy(k, at.tensor_at(k)).wait_recv()
    r.kv_out[...] = jnp.concatenate(
        [r.last[2 * j, :, 0:ROWS] + r.last[2 * j + 1, :, 0:ROWS] for j in range(CHIPS)], axis=1
    )
    shared = r.last[0, :, ROWS:PAIR]
    for j in range(1, TENSOR):
        shared = shared + r.last[j, :, ROWS:PAIR]
    r.router_out[...] = shared[:, 0:32]
    wide = jnp.concatenate([shared, jnp.zeros((ROWS - 8, ROWS), F32)], axis=0).T
    r.gain_one_out[...] = wide[32:33, 0:8]
    r.gain_two_out[...] = wide[33:34, 0:8]

    for k in range(1, TENSOR):
        back_copy(k, t).wait_send()
        grad_copy(k, t).wait_send()
        query_copy(at.tensor_at(k), t).wait_send()
        last_copy(k, t).wait_send()
    for k in range(1, 4):
        for copy in over_y(k):
            copy.wait_send()
    for copy in then_across():
        copy.wait_send()
    for copy in then_x():
        copy.wait_send()
    for k in range(1, DP):
        tail_copy(k).wait_send()
        out_copy(k).wait_send()
    out_half().wait_send()
    for k in range(1, 4):
        out_along(k).wait_send()
    out_across().wait_send()
    moe_along().wait_send()
    moe_across().wait_send()
    ring_w.end()


def store_kernel(r):
    copies = Copies(r.local)
    for name in STORED:
        copies.start(getattr(r, name), getattr(r, name + "_kept"))
    for name in STORED:
        copies.wait(1)
        copies.start(getattr(r, name + "_kept"), getattr(r, name + "_done"))
    copies.wait()


STORED = (
    "output",
    "hidden_grad",
    "gain_one_out",
    "query_out",
    "kv_out",
    "out_grad",
    "gain_two_out",
    "router_out",
    "gu_out",
    "down_out",
)


class Refs:
    def __init__(self, names, refs):
        for name, ref in zip(names, refs):
            setattr(self, name, ref)


def call(kernel, number, inputs, outputs, scratch, reaches=True):
    def space(name):
        return pl.BlockSpec(memory_space=pltpu.VMEM if name.endswith("_v") else pl.ANY)

    names = [name.removesuffix("_v") for name in (*inputs, *outputs)] + list(scratch)
    params = {"vmem_limit_bytes": VMEM_BYTES}
    if reaches:
        params |= {"collective_id": number, "has_side_effects": True}
    values = pl.pallas_call(
        lambda *refs: kernel(Refs(names, refs)),
        out_shape=[jax.ShapeDtypeStruct(shape, dtype) for shape, dtype in outputs.values()],
        in_specs=[space(name) for name in inputs],
        out_specs=[space(name) for name in outputs],
        scratch_shapes=list(scratch.values()),
        compiler_params=pltpu.CompilerParams(**params),
        name=kernel.__name__,
    )(*inputs.values())
    return Refs([name.removesuffix("_v") for name in outputs], values)


def sems(**counts):
    return {name: pltpu.SemaphoreType.DMA((count,)) for name, count in counts.items()}


def rope_tables():
    half = HEAD // 2
    freqs = np.exp(
        np.arange(half, dtype=np.float32) * np.float32(-2.0 * math.log(10000.0) / HEAD)
    ).astype(np.float32)
    angles = np.arange(LENGTH, dtype=np.float32)[:, None] * freqs[None, :]
    cos, sin = np.cos(angles).astype(np.float32), np.sin(angles).astype(np.float32)
    ones, zeros = np.ones((LENGTH, HEAD), np.float32), np.zeros((LENGTH, HEAD), np.float32)
    return (
        np.concatenate([cos, cos, ones], axis=1),
        np.concatenate([-sin, sin, zeros], axis=1),
        np.ascontiguousarray(cos.T),
        np.ascontiguousarray(sin.T),
    )


def body(
    hidden,
    seg_ids,
    key_mask,
    routes,
    gain_attn,
    w_query,
    w_keyval,
    w_out,
    gain_mlp,
    w_router,
    w_gate_up,
    w_down,
    cotangent,
):
    V = pltpu.VMEM
    cosine, sine, cosine_t, sine_t = rope_tables()
    hid, cot = hidden[0], cotangent[0]
    a = call(
        attention_kernel,
        1,
        dict(
            hid_v=hid,
            cot=cot,
            w_keyval_v=w_keyval,
            w_out_t_v=w_out.T,
            w_query_t_v=w_query.T,
            router_v=w_router,
            gain_one_v=gain_attn.reshape(1, 8),
            gain_two_v=gain_mlp.reshape(1, 8),
            gu=w_gate_up,
            down=w_down,
            cosine=cosine,
            sine=sine,
            mask_v=key_mask,
            seg_v=seg_ids,
        ),
        dict(
            normed=((LENGTH, WIDTH), BF),
            queries=((LENGTH, 2 * HEAD), BF),
            keyvals=((PADDED, 2 * HEAD), BF),
            keyvals_t=((2 * HEAD, PADDED), BF),
            stats_v=((1, LENGTH), F32),
            heads_t_v=((HEAD, LENGTH), F32),
            mid_v=((ROWS, WIDTH), F32),
            normed_mid_v=((ROWS, WIDTH), BF),
            att_rows_v=((ROWS, WIDTH), BF),
            wqkv_own_v=((ROWS, WIDTH), BF),
            out_t=((WIDTH, WIDTH), BF),
            small_v=((WIDTH, ROWS), BF),
            gu_all=((WIDTH, WIDTH), BF),
            down_all=((UNITS, WIDTH), BF),
            cot_all=((LENGTH, WIDTH), BF),
        ),
        dict(
            cosine_v=V((LENGTH, ROWS), F32),
            sine_v=V((LENGTH, ROWS), F32),
            hidden_all=V((LENGTH, WIDTH), BF),
            normed_v=V((LENGTH, WIDTH), BF),
            queries_v=V((LENGTH, 2 * HEAD), BF),
            keyvals_v=V((PADDED, 2 * HEAD), BF),
            keyvals_tv=V((2 * HEAD, PADDED), BF),
            out_tv=V((WIDTH, WIDTH), BF),
            rows=V((16, WIDTH), BF),
            row_dp=V((DP, 16, WIDTH), BF),
            shares=V((8, ROWS), F32),
            tiles=V((TENSOR, 16, ROWS), BF),
            tile_all=V((DP, TENSOR, 16, ROWS), BF),
            out_all=V((TENSOR, HEAD, WIDTH), BF),
            wq_all=V((2 * HEAD, WIDTH), BF),
            code=V((PADDED, ROWS), F32),
            scores=V((SPAN, PAIR), F32),
            probs=V((SPAN, PAIR), BF),
            starts=V((1, LENGTH), F32),
            wqk=V((WIDTH, PAIR), BF),
            att_src=V((TENSOR, HEAD, ROWS), BF),
            att_t=V((WIDTH, ROWS), BF),
        )
        | sems(
            h_send=17,
            h_recv=32,
            c_send=17,
            c_recv=32,
            o_send=17,
            o_recv=32,
            t1_send=16,
            t1_recv=16,
            t2_send=8,
            t2_recv=8,
            rd_send=8,
            rd_recv=8,
            wq_send=8,
            wq_recv=8,
            e_send=20,
            e_recv=32,
            a_send=16,
            a_recv=16,
            local=16,
        ),
    )
    b = call(
        expert_kernel,
        2,
        dict(
            normed_mid_v=a.normed_mid,
            cot_all=a.cot_all,
            gu_all=a.gu_all,
            down_all=a.down_all,
            gu=w_gate_up,
            down=w_down,
            small_v=a.small,
            routes_t_v=routes[0].T,
            mid_v=a.mid,
            cot_v=cot,
            out_t=a.out_t,
        ),
        dict(
            moe_across_v=((ROWS, WIDTH), F32),
            moe_own_v=((ROWS, WIDTH), F32),
            moe_last_v=((2, ROWS, WIDTH), BF),
            mid_grad_v=((ROWS, WIDTH), F32),
            mid_t_v=((WIDTH, ROWS), BF),
            att_grad_t_v=((WIDTH, ROWS), BF),
            gu_grad=((WIDTH, WIDTH), BF),
            down_grad=((UNITS, WIDTH), BF),
            ys_gu_v=((2, ROWS, WIDTH), BF),
            ys_down_v=((2, UNITS, ROWS), BF),
            router_t_v=((32, WIDTH), F32),
            gain_grad_v=((1, WIDTH), F32),
        ),
        dict(
            out_tv=V((WIDTH, WIDTH), BF),
            nm_all=V((LENGTH, WIDTH), BF),
            nm_t=V((WIDTH, LENGTH), BF),
            cots=V((LENGTH, WIDTH), BF),
            gus=V((2, WIDTH, WIDTH), BF),
            downs=V((WIDTH, WIDTH), BF),
            down_first=V((UNITS, WIDTH), BF),
            weighted=V((LENGTH, UNITS), BF),
            weighted_t=V((UNITS, LENGTH), BF),
            proj_grads=V((LENGTH, WIDTH), BF),
            gates=V((LENGTH, ROWS), F32),
            n_first=V((LENGTH, WIDTH), BF),
            y_gu=V((4, PAIR, WIDTH), BF),
            y_down=V((4, UNITS, PAIR), BF),
            logit_t=V((ROWS, LENGTH), BF),
            n_parts=V((SLOTS, PAIR, WIDTH), BF),
            n_twins=V((CHIPS, ROWS, WIDTH), BF),
            n_sums=V((CHIPS, ROWS, WIDTH), BF),
            n_crossed=V((4, ROWS, WIDTH), BF),
            n_joined=V((3, ROWS, WIDTH), BF),
            n_landed=V((3, ROWS, WIDTH), BF),
            m_parts=V((SLOTS, PAIR, WIDTH), BF),
            m_twins=V((CHIPS, ROWS, WIDTH), BF),
            m_sums=V((CHIPS, ROWS, WIDTH), BF),
            m_landed=V((2, 2, ROWS, WIDTH), BF),
        )
        | sems(
            g_send=17,
            g_recv=32,
            ntw_send=8,
            ntw_recv=8,
            nc_send=4,
            nc_recv=4,
            n_send=3,
            n_recv=3,
            e_send=20,
            e_recv=32,
            mtw_send=8,
            mtw_recv=8,
            x_send=4,
            x_recv=4,
            y_send=4,
            y_recv=4,
            m_send=8,
            m_recv=8,
            local=8,
        ),
    )
    c = call(
        back_kernel,
        3,
        dict(
            att_grad_t_v=b.att_grad_t,
            mid_t_v=b.mid_t,
            mid_grad_v=b.mid_grad,
            moe_across_v=b.moe_across,
            moe_own_v=b.moe_own,
            moe_last_v=b.moe_last,
            gu_grad=b.gu_grad,
            down_grad=b.down_grad,
            ys_gu_v=b.ys_gu,
            ys_down_v=b.ys_down,
            router_t_v=b.router_t,
            gain_grad_v=b.gain_grad,
            queries=a.queries,
            keyvals=a.keyvals,
            keyvals_t=a.keyvals_t,
            stats_v=a.stats,
            heads_t_v=a.heads_t,
            mask_v=key_mask,
            seg_v=seg_ids,
            cosine_t_v=cosine_t,
            sine_t_v=sine_t,
            wqkv_own_v=a.wqkv_own,
            att_rows_v=a.att_rows,
            normed=a.normed,
            hid_v=hid,
            small_v=a.small,
        ),
        dict(
            output_v=((ROWS, WIDTH), BF),
            hidden_grad_v=((ROWS, WIDTH), BF),
            gain_one_out_v=((1, 8), F32),
            query_out_v=((HEAD, ROWS), F32),
            kv_out_v=((8, WIDTH), F32),
            out_grad_v=((8, WIDTH), F32),
            gain_two_out_v=((1, 8), F32),
            router_out_v=((8, 32), F32),
            gu_out_v=((2, ROWS, WIDTH), F32),
            down_out_v=((2, UNITS, ROWS), F32),
        ),
        dict(
            queries_v=V((LENGTH, 2 * HEAD), BF),
            keyvals_v=V((PADDED, 2 * HEAD), BF),
            keyvals_tv=V((2 * HEAD, PADDED), BF),
            normed_v=V((LENGTH, WIDTH), BF),
            gu_own=V((PAIR, WIDTH), BF),
            down_own=V((UNITS, PAIR), BF),
            grads_t=V((2 * HEAD, LENGTH), BF),
            wqkv=V((TENSOR, ROWS, WIDTH), BF),
            kv_full=V((WIDTH, WIDTH), BF),
            code=V((PADDED, ROWS), F32),
            starts=V((1, LENGTH), F32),
            kv_sum=V((PADDED, 2 * HEAD), F32),
            tail_left=V((3 * HEAD, LENGTH), BF),
            query_src=V((TENSOR, HEAD, ROWS), BF),
            query_all=V((TENSOR, HEAD, ROWS), BF),
            back_src=V((TENSOR, ROWS, ROWS), BF),
            back_all=V((TENSOR, ROWS, ROWS), BF),
            out_terms=V((CHIPS, ROWS, WIDTH), BF),
            out_twins=V((CHIPS, HEAD, WIDTH), BF),
            out_sums=V((CHIPS, HEAD, WIDTH), BF),
            out_landed=V((4, 2, HEAD, WIDTH), BF),
            out_joined=V((HEAD, WIDTH), BF),
            out_crossed=V((HEAD, WIDTH), BF),
            out_rows=V((HEAD, WIDTH), F32),
            out_in=V((DP, 8, WIDTH), F32),
            m_landed=V((2, ROWS, WIDTH), BF),
            m_joined=V((ROWS, WIDTH), BF),
            m_crossed=V((ROWS, WIDTH), BF),
            tail=V((TAIL, WIDTH), BF),
            tail_in=V((DP, TAIL, ROWS), BF),
            pieces=V((TENSOR, 8, PAIR), F32),
            last=V((TENSOR, 8, PAIR), F32),
            yx_gu0=V((ROWS, WIDTH), BF),
            yx_down0=V((UNITS, ROWS), BF),
            y_gu=V((4, PAIR, WIDTH), BF),
            y_down=V((4, UNITS, PAIR), BF),
            s_gu=V((ROWS, WIDTH), BF),
            s_down=V((UNITS, ROWS), BF),
            yx_gu=V((ROWS, WIDTH), BF),
            yx_down=V((UNITS, ROWS), BF),
        )
        | sems(
            g_send=16,
            g_recv=16,
            w_send=17,
            w_recv=32,
            q_send=16,
            q_recv=16,
            b_send=16,
            b_recv=16,
            x_send=4,
            x_recv=4,
            gu_send=4,
            gu_recv=4,
            dn_send=4,
            dn_recv=4,
            ot_send=1,
            ot_recv=1,
            o_send=8,
            o_recv=8,
            m_send=8,
            m_recv=8,
            t_send=8,
            t_recv=8,
            od_send=8,
            od_recv=8,
            l_send=16,
            l_recv=16,
            local=8,
        ),
    )
    values = {name: getattr(c, name) for name in STORED}
    done = call(
        store_kernel,
        0,
        values,
        {name + "_done": (value.shape, value.dtype) for name, value in values.items()},
        {name + "_kept": V(value.shape, value.dtype) for name, value in values.items()}
        | sems(local=2 * len(STORED)),
        reaches=False,
    )
    return (
        done.output_done[None],
        done.hidden_grad_done[None],
        done.gain_one_out_done.reshape(8),
        done.query_out_done.T,
        done.kv_out_done,
        done.out_grad_done.T,
        done.gain_two_out_done.reshape(8),
        done.router_out_done,
        done.gu_out_done,
        done.down_out_done,
    )


def solution(mesh):
    return jax.shard_map(
        body,
        mesh=mesh,
        in_specs=(
            P("dp", "tensor", None),
            P("dp", None),
            P("dp", None),
            P("dp", None, None),
            P(("dp", "tensor")),
            P("dp", "tensor"),
            P(("dp", "tensor"), None),
            P(None, ("dp", "tensor")),
            P(("dp", "tensor")),
            P(("dp", "tensor"), None),
            P("tensor", "dp", None),
            P("tensor", None, "dp"),
            P("dp", "tensor", None),
        ),
        out_specs=(
            P("dp", "tensor", None),
            P("dp", "tensor", None),
            P(("dp", "tensor")),
            P("dp", "tensor"),
            P(("dp", "tensor"), None),
            P(None, ("dp", "tensor")),
            P(("dp", "tensor")),
            P(("dp", "tensor"), None),
            P("tensor", "dp", None),
            P("tensor", None, "dp"),
        ),
        check_vma=False,
    )
```

```python
import math

import jax
import jax.numpy as jnp
import numpy as np
from jax import lax
from jax.experimental import pallas as pl
from jax.experimental.pallas import tpu as pltpu
from jax.sharding import PartitionSpec as P

HEAD = 64
LENGTH = 2048
WIDTH = 1024
UNITS = 512
ROWS = 128
PAIR = 256
CHUNK = 384
REACH = 896
SPAN = REACH + PAIR
PADDED = REACH + LENGTH
CHIPS = 8
TENSOR = 16
DP = 8
TAIL = 240
SLOTS = 2
STEP_Z = (0, 0, 1, 3, 1, 3, 2, 2)
STEP_X = (0, 1, 0, 0, 1, 1, 0, 1)
SUM_Z = (2, 2, 1, 1, 3, 3, 0, 0)
SUM_X = (1, 0, 1, 0, 1, 0, 1, 0)
LOWEST = -1e30
TP = "tensor"
SP = "dp"
BF = jnp.bfloat16
F32 = jnp.float32
MESH = pl.DeviceIdType.MESH
VMEM_BYTES = 63 * 1024 * 1024

NN = (((1,), (0,)), ((), ()))
NT = (((1,), (1,)), ((), ()))
TN = (((0,), (0,)), ((), ()))


def dot(left, right, dims=NN):
    return lax.dot_general(left, right, dims, preferred_element_type=F32)


def aligned(value, size):
    return pl.ds(pl.multiple_of(value * size, size), size)


def remote(src, dst, send, recv, axis, index):
    return pltpu.make_async_remote_copy(
        src_ref=src,
        dst_ref=dst,
        send_sem=send,
        recv_sem=recv,
        device_id={axis: index},
        device_id_type=MESH,
    )


def all_sent(ref, sem, place):
    remote(ref, ref, sem, sem, TP, place.twin).wait_send()


def all_landed(ref, sem, place):
    remote(ref, ref, sem, sem, TP, place.twin).wait_recv()


class Place:
    def __init__(self):
        self.t = lax.axis_index(TP)
        self.d = lax.axis_index(SP)
        self.core = lax.rem(self.t, 2)
        self.chip = self.t // 2
        self.twin = self.t + 1 - 2 * self.core
        self.x = lax.rem(self.d, 2)
        self.y = self.d // 2
        self.across = self.d + 1 - 2 * self.x
        self.z = self.chip // 2
        self.x_far = lax.rem(self.chip, 2)

    def chip_at(self, k):
        return lax.rem(self.chip + k, CHIPS)

    def same_core(self, k):
        return 2 * self.chip_at(k) + self.core

    def near(self, dz, dx):
        return 2 * lax.rem(self.z + dz, 4) + lax.rem(self.x_far + dx, 2)

    def near_core(self, dz, dx):
        return 2 * self.near(dz, dx) + self.core

    def listed(self, i, all_z, all_x):
        if isinstance(i, int):
            return self.near(all_z[i], all_x[i])
        dz, dx = jnp.int32(0), jnp.int32(0)
        for k in range(CHIPS):
            dz = jnp.where(i == k, all_z[k], dz)
            dx = jnp.where(i == k, all_x[k], dx)
        return self.near(dz, dx)

    def step(self, i):
        return self.listed(i, STEP_Z, STEP_X)

    def sum_step(self, i):
        return self.listed(i, SUM_Z, SUM_X)

    def step_core(self, i):
        return 2 * self.step(i) + self.core

    def tensor_at(self, k):
        return lax.rem(self.t + k, TENSOR)

    def dp_at(self, k):
        return lax.rem(self.d + k, DP)

    def y_at(self, k):
        return lax.rem(self.y + k, 4)

    def enter(self):
        barrier = pltpu.get_barrier_semaphore()
        for k in range(1, TENSOR):
            pl.semaphore_signal(
                barrier, inc=1, device_id={TP: self.tensor_at(k)}, device_id_type=MESH
            )
        for k in range(1, DP):
            pl.semaphore_signal(
                barrier, inc=1, device_id={SP: self.dp_at(k)}, device_id_type=MESH
            )
        pl.semaphore_wait(barrier, TENSOR + DP - 2)


class Spread:
    def __init__(self, place, block, send, recv, source=None):
        self.place, self.block, self.send, self.recv = place, block, send, recv
        self.source = source

    def copy(self, number, index, dest, source=None):
        src = self.block(index) if source is None else source
        return remote(
            src, self.block(index), self.send.at[number], self.recv.at[index], TP, dest
        )

    def own(self, k):
        dest = self.place.twin if k == 0 else self.place.same_core(k)
        return self.copy(k, self.place.t, dest, self.source)

    def start(self):
        for k in range(1, CHIPS):
            self.own(k).start()
        self.own(0).start()

    def passed(self, k):
        return self.copy(CHIPS + k, self.place.same_core(k), self.place.twin)

    def arrived(self, index):
        self.copy(0, index, self.place.twin).wait_recv()

    def first(self, k):
        self.arrived(self.place.same_core(k))
        self.passed(k).start()

    def second(self, k):
        self.arrived(2 * self.place.chip_at(k) + 1 - self.place.core)

    def end(self):
        for k in range(CHIPS):
            self.own(k).wait_send()
        for k in range(1, CHIPS):
            self.passed(k).wait_send()


class Ring:
    SENDS = 17

    def __init__(self, place, block, half, send, recv, source=None, most=None):
        self.place, self.block, self.half = place, block, half
        self.send, self.recv, self.source, self.most = send, recv, source, most

    def send_sem(self, number):
        return self.send.at[number if self.most is None else 0]

    def copy(self, number, index, dest, source=None):
        src = self.block(index) if source is None else source
        return remote(
            src, self.block(index), self.send_sem(number), self.recv.at[index], TP, dest
        )

    def piece(self, number, index, part, dest):
        ref = self.half(index, part)
        place = TENSOR + lax.rem(index // 2, 2) if part else index
        return remote(ref, ref, self.send_sem(number), self.recv.at[place], TP, dest)

    def sent(self, number):
        at = self.place
        if number == 0:
            return self.copy(0, at.t, at.twin, self.source)
        if number < 4:
            return self.copy(number, at.t, at.step_core(number), self.source)
        if number < 6:
            return self.copy(number, at.step_core(1), at.step_core(number - 2))
        if number < 8:
            return self.piece(number, at.step_core(2 * number - 9), 0, at.step_core(2))
        if number < 10:
            return self.piece(number, at.step_core(2 * number - 14), 1, at.step_core(3))
        return self.copy(number, at.step_core(number - 9), at.twin)

    def start(self):
        for number in (1, 2, 3, 0):
            self.sent(number).start()

    def pass_on(self, i):
        index = self.place.step_core(i)
        if i < 6:
            self.copy(0, index, self.place.twin).wait_recv()
        else:
            self.piece(0, index, 0, self.place.twin).wait_recv()
            self.piece(0, index, 1, self.place.twin).wait_recv()
        for number in {1: (4, 5), 2: (8,), 3: (6,), 4: (9,), 5: (7,)}.get(i, ()):
            self.sent(number).start()
        self.sent(9 + i).start()

    def pass_on_at(self, i):
        for k in range(1, CHIPS):

            @pl.when(i == k - 1)
            def _(k=k):
                self.pass_on(k)

    def second(self, i):
        self.copy(0, 2 * self.place.step(i) + 1 - self.place.core, self.place.twin).wait_recv()

    def end(self):
        if self.most is not None:
            all_sent(self.most, self.send.at[0], self.place)
            return
        for number in range(self.SENDS):
            self.sent(number).wait_send()


def whole_ring(place, ref, send, recv, source=None):
    return Ring(
        place,
        lambda b: ref.at[aligned(b, ROWS)],
        lambda b, part: ref.at[pl.ds(pl.multiple_of(b * ROWS + part * HEAD, HEAD), HEAD)],
        send,
        recv,
        source,
        ref.at[pl.ds(0, 15 * ROWS)],
    )


class Copies:
    def __init__(self, sems):
        self.sems, self.all, self.done = sems, [], 0

    def start(self, src, dst):
        copy = pltpu.make_async_copy(src, dst, self.sems.at[len(self.all)])
        copy.start()
        self.all.append(copy)

    def wait(self, count=None):
        end = len(self.all) if count is None else self.done + count
        for copy in self.all[self.done : end]:
            copy.wait()
        self.done = end


def lanes(shape):
    return lax.broadcasted_iota(jnp.int32, shape, len(shape) - 1)


def sublanes(shape):
    return lax.broadcasted_iota(jnp.int32, shape, 0)


def swapped(values):
    return jnp.where(
        lanes(values.shape) < HEAD // 2,
        pltpu.roll(values, 2 * HEAD - HEAD // 2, 1),
        pltpu.roll(values, HEAD // 2, 1),
    )


def document_starts(seg):
    starts = jnp.zeros(seg.shape, F32)
    for document in range(8):
        before = jnp.sum(jnp.where(seg < document, 1.0, 0.0), axis=1, keepdims=True)
        starts = starts + jnp.where(seg == document, before, 0.0)
    return starts


def key_codes(mask, code):
    code[0:REACH, :] = jnp.full((REACH, ROWS), -1.0, F32)

    @pl.loop(0, TENSOR)
    def _(i):
        row = mask[:, aligned(i, ROWS)].astype(F32)
        live = jnp.broadcast_to(row, (ROWS, ROWS)).T == 1.0
        places = (sublanes((ROWS, ROWS)) + i * ROWS).astype(F32)
        code[pl.ds(pl.multiple_of(REACH + i * ROWS, ROWS), ROWS), :] = jnp.where(
            live, places, -1.0
        )


def allowed(code, start_row, chunk):
    ok = jnp.concatenate([code, code], axis=1) >= start_row
    if (chunk + 1) * CHUNK > REACH:
        key = sublanes((CHUNK, PAIR)) + (chunk * CHUNK - REACH)
        query = lanes((CHUNK, PAIR))
        ok = (ok & (key < query)) | (key == query)
    return ok


def turned_back(grad, r, here):
    cos, sin = r.cosine_t[:, here], r.sine_t[:, here]
    first, second = grad[0 : HEAD // 2], grad[HEAD // 2 : HEAD]
    return jnp.concatenate([first * cos + second * sin, second * cos - first * sin], axis=0)


class Halves:
    def __init__(self, place, parts, twins, sums, send, recv):
        self.place, self.parts, self.twins, self.sums = place, parts, twins, sums
        self.send, self.recv = send, recv

    def half(self, k):
        at = self.place
        return remote(
            self.parts.at[lax.rem(k, SLOTS), aligned(1 - at.core, ROWS), :],
            self.twins.at[k],
            self.send.at[lax.rem(k, SLOTS)],
            self.recv.at[k],
            TP,
            at.twin,
        )

    def put(self, k, value):
        @pl.when(k >= SLOTS)
        def _():
            self.half(k - SLOTS).wait_send()

        self.parts[lax.rem(k, SLOTS)] = value.astype(BF)
        self.half(k).start()

    def add(self, k):
        self.half(k).wait_recv()
        own = self.parts[lax.rem(k, SLOTS), aligned(self.place.core, ROWS), :].astype(F32)
        self.sums(k)[...] = (own + self.twins[k].astype(F32)).astype(BF)

    def end(self):
        for k in range(CHIPS - SLOTS, CHIPS):
            self.half(k).wait_send()


class Joined:
    def __init__(self, place, sums, crossed, landed, sems):
        self.place, self.sums, self.crossed, self.landed = place, sums, crossed, landed
        self.c_send, self.c_recv, self.send, self.recv = sems

    def cross(self, j):
        return remote(
            self.sums.at[2 * j],
            self.crossed.at[j],
            self.c_send.at[j],
            self.c_recv.at[j],
            TP,
            self.place.near_core(0, 1),
        )

    def whole(self, j):
        return remote(
            self.sums.at[2 * j + 1],
            self.landed.at[j],
            self.send.at[j],
            self.recv.at[j],
            TP,
            self.place.near_core(SUM_Z[2 * j], 0),
        )

    def join(self, j):
        self.cross(j).wait_recv()
        total = self.sums[2 * j + 1].astype(F32) + self.crossed[j].astype(F32)
        self.sums[2 * j + 1] = total.astype(BF)
        self.whole(j).start()

    def result(self):
        self.cross(3).wait_recv()
        total = self.sums[7].astype(F32) + self.crossed[3].astype(F32)
        for j in range(3):
            self.whole(j).wait_recv()
            total = total + self.landed[j].astype(F32)
        return total

    def end(self):
        for j in range(4):
            self.cross(j).wait_send()
        for j in range(3):
            self.whole(j).wait_send()


def unpacked(both):
    return both[:, 0:8].reshape(ROWS, WIDTH), both[:, 8:16].reshape(ROWS, WIDTH)


def aligned_rows(ref, unit):
    def block(src, part=None):
        if part is None:
            return ref.at[pl.ds(pl.multiple_of(src * 2 * unit, unit), 2 * unit), :]
        return ref.at[pl.ds(pl.multiple_of((src * 2 + part) * unit, unit), unit), :]

    return block


def column_blocks(ref):
    def block(src, part=None):
        if part is None:
            return ref.at[:, aligned(src, ROWS)]
        return ref.at[pl.ds(part * PAIR, PAIR), aligned(src, ROWS)]

    return block


class Stream:
    def __init__(self, place, own, block, most, r, number):
        self.place, self.own, self.block, self.most = place, own, block, most
        self.send, self.recv = r.e_send, r.e_recv
        self.number, self.first_recv = number, 10 * number

    def at_y(self, k, other=False):
        at = self.place
        column = 1 - at.x if other else at.x
        return 2 * at.y_at(k) + column

    def copy(self, number, src, dest, part=None, source=None):
        ref = self.block(src, part)
        return remote(
            ref if source is None else source,
            ref,
            self.send.at[self.number],
            self.recv.at[self.first_recv + (8 + lax.rem(src, 2) if part else src)],
            SP,
            dest,
        )

    def sent(self, number):
        at, at_y = self.place, self.at_y
        if number == 0:
            return self.copy(0, at.d, at.across, source=self.own)
        if number < 3:
            return self.copy(number, at.d, at_y(2 * number - 1), source=self.own)
        if number < 5:
            return self.copy(number, at.across, at_y(2 * number - 5))
        other = number > 6
        if number % 2:
            return self.copy(number, at_y(3, other), at_y(1), 0)
        return self.copy(number, at_y(1, other), at_y(3), 1)

    def arrived(self, src, halves=False):
        for part in (0, 1) if halves else (None,):
            self.copy(0, src, self.place.across, part).wait_recv()

    def start_x(self):
        self.sent(0).start()

    def start_y(self):
        self.sent(1).start()
        self.sent(2).start()

    def from_across(self):
        self.arrived(self.place.across)
        self.sent(3).start()
        self.sent(4).start()

    def from_y(self):
        self.arrived(self.at_y(3))
        self.sent(5).start()
        self.arrived(self.at_y(1))
        self.sent(6).start()

    def from_y_across(self):
        self.arrived(self.at_y(3, True))
        self.sent(7).start()
        self.arrived(self.at_y(1, True))
        self.sent(8).start()

    def finish(self):
        self.arrived(self.at_y(2), True)
        self.arrived(self.at_y(2, True), True)

    def end(self):
        all_sent(self.most, self.send.at[self.number], self.place)


def expert_streams(at, r, e):
    downs = r.downs.at[pl.ds(e * UNITS, UNITS)]
    return (
        Stream(
            at,
            r.gu.at[e],
            aligned_rows(r.gus.at[e], HEAD),
            r.gus.at[e, pl.ds(0, 7 * ROWS)],
            r,
            2 * e,
        ),
        Stream(
            at,
            r.down.at[e],
            column_blocks(downs),
            downs.at[:, pl.ds(0, 7 * ROWS)],
            r,
            2 * e + 1,
        ),
    )


def layer_kernel(r):
    at = Place()
    t, d = at.t, at.d
    copies = Copies(r.local)
    r.load()
    r.hidden_all[aligned(t, ROWS), :] = r.hid[...]
    keyval, out_rows = r.w_keyval[...].astype(F32), r.w_out_t[...].astype(F32)
    r.rows[...] = jnp.concatenate([keyval, out_rows], axis=0).astype(BF)
    r.row_dp[d] = r.rows[...]
    r.shares[...] = jnp.zeros((8, ROWS), F32)
    r.shares[:, 0:32] = r.router[...].astype(F32)
    same = sublanes((8, 8)) == lanes((8, 8))
    for column, gain in ((32, r.gain_one), (33, r.gain_two)):
        wide = jnp.broadcast_to(gain[...].astype(F32), (8, 8))
        r.shares[:, column : column + 1] = jnp.sum(
            jnp.where(same, wide, 0.0), axis=1, keepdims=True
        )
    for j in range(CHIPS):
        tile = jnp.concatenate([keyval[:, j * ROWS : (j + 1) * ROWS], r.shares[...]], axis=0)
        r.tiles[2 * j] = tile.astype(BF)
        r.tiles[2 * j + 1] = tile.astype(BF)
    r.tile_all[d, t] = r.tiles[t]
    r.wq_all[HEAD : 2 * HEAD, :] = jnp.zeros((HEAD, WIDTH), BF)
    r.wq_all[0:HEAD, aligned(d, ROWS)] = r.w_query_t[...]
    at.enter()

    def tile_one(k, src):
        dest = at.tensor_at(k)
        return remote(
            r.tiles.at[dest],
            r.tile_all.at[d, src],
            r.t1_send.at[0],
            r.t1_recv.at[0],
            TP,
            dest,
        )

    def tile_two(k, src):
        ref = r.tile_all.at[src]
        return remote(ref, ref, r.t2_send.at[0], r.t2_recv.at[0], SP, at.dp_at(k))

    def rows_dp(k, src):
        return remote(
            r.rows, r.row_dp.at[src], r.rd_send.at[0], r.rd_recv.at[0], SP, at.dp_at(k)
        )

    def wq_dp(k, src):
        return remote(
            r.w_query_t,
            r.wq_all.at[pl.ds(0, HEAD), aligned(src, ROWS)],
            r.wq_send.at[0],
            r.wq_recv.at[0],
            SP,
            at.dp_at(k),
        )

    first_expert, second_expert = expert_streams(at, r, 0), expert_streams(at, r, 1)

    for k in range(1, TENSOR):
        tile_one(k, t).start()
    for k in range(1, DP):
        wq_dp(k, d).start()
    ring_h = whole_ring(at, r.hidden_all, r.h_send, r.h_recv)
    ring_h.start()
    for e in range(2):
        copies.start(r.gu.at[e], r.gus.at[e, aligned(d, ROWS)])
        copies.start(r.down.at[e], r.downs.at[pl.ds(e * UNITS, UNITS), aligned(d, ROWS)])
    copies.start(r.cot, r.cots.at[aligned(t, ROWS)])

    key_codes(r.mask, r.code)
    r.starts[...] = document_starts(r.seg[...])
    r.keyvals[0:REACH, :] = jnp.zeros((REACH, 2 * HEAD), BF)
    r.keyvals_t[:, 0:REACH] = jnp.zeros((2 * HEAD, REACH), BF)

    all_landed(r.tile_all.at[0, pl.ds(0, 15)], r.t1_recv.at[0], at)
    for k in range(1, DP):
        tile_two(k, d).start()
    for k in range(1, DP):
        rows_dp(k, d).start()
    for stream in first_expert:
        stream.start_x()
        stream.start_y()
    for i in range(1, 4):
        ring_h.pass_on(i)
    seven_wq = r.wq_all.at[pl.ds(0, HEAD), pl.ds(0, 7 * ROWS)]
    all_landed(seven_wq, r.wq_recv.at[0], at)
    all_landed(r.tile_all.at[pl.ds(0, 7)], r.t2_recv.at[0], at)
    for j in range(DP):
        both = r.tile_all[j].astype(F32)
        r.wqk[j * ROWS : (j + 1) * ROWS, ROWS:PAIR] = both[:, 0:8].reshape(ROWS, ROWS).astype(BF)
        r.small[j * ROWS : (j + 1) * ROWS, :] = both[:, 8:16].reshape(ROWS, ROWS).astype(BF)
    r.wqk[:, 0:ROWS] = r.wq_all[...].astype(F32).T.astype(BF)
    columns = r.small[...].astype(F32).T
    gain_one = columns[32:33, :]
    gain_two = columns[33:34, :]
    r.need("cosine", "sine")
    ring_o = Ring(
        at,
        lambda b: r.out_all.at[b // 2, aligned(lax.rem(b, 2), HEAD)],
        lambda b, part: r.out_all.at[b // 2, aligned(2 * lax.rem(b, 2) + part, 32)],
        r.o_send,
        r.o_recv,
    )

    ring_c = whole_ring(at, r.cots, r.c_send, r.c_recv, r.cot)
    @pl.loop(0, CHIPS)
    def _(i):
        @pl.when(i == 1)
        def _():
            ring_h.pass_on(4)
            ring_h.pass_on(5)

        @pl.when(i == 2)
        def _():
            all_landed(r.row_dp.at[pl.ds(0, 7)], r.rd_recv.at[0], at)
            both = r.row_dp[...].astype(F32)
            r.wqkv_own[0:HEAD, :] = r.wq_all[0:HEAD, :]
            r.wqkv_own[HEAD : 2 * HEAD, :] = both[:, 0:8].reshape(HEAD, WIDTH).astype(BF)
            r.out_all[at.chip, aligned(at.core, HEAD), :] = (
                both[:, 8:16].reshape(HEAD, WIDTH).astype(BF)
            )
            ring_o.start()

        @pl.when(i == 4)
        def _():
            ring_c.start()

        @pl.when(i == 5)
        def _():
            ring_h.pass_on(6)
            ring_h.pass_on(7)

        ring_h.second(i)
        block = at.step(i)
        here = aligned(block, PAIR)
        hidden = r.hidden_all[here, :].astype(F32)
        inverse = lax.rsqrt(jnp.mean(hidden * hidden, axis=1, keepdims=True) + 1e-6)
        unit = (hidden * inverse * gain_one).astype(BF)
        r.normed[here, :] = unit
        cos, sin = r.cosine[here, :], r.sine[here, :]
        projected = dot(unit, r.wqk[...])
        query, keyval = projected[:, 0:ROWS], projected[:, ROWS:PAIR]
        query = (query * cos + swapped(query) * sin).astype(BF)
        r.queries[here, :] = (query.astype(F32) * (1.0 / math.sqrt(HEAD))).astype(BF)
        keyval = keyval * cos + swapped(keyval) * sin
        later = pl.ds(pl.multiple_of(REACH + block * PAIR, ROWS), PAIR)
        r.keyvals[later, :] = keyval.astype(BF)
        r.keyvals_t[:, later] = keyval.T.astype(BF)

    r.save("normed", "queries", "keyvals", "keyvals_t", "small")
    ring_o.pass_on(1)
    for stream in first_expert:
        stream.from_across()
    for stream in first_expert:
        stream.from_y()
    for stream in second_expert:
        stream.start_x()

    def att_copy(dest, src):
        return remote(
            r.att_src.at[dest],
            r.att_t.at[aligned(src, HEAD), :],
            r.a_send.at[0],
            r.a_recv.at[0],
            TP,
            dest,
        )

    @pl.loop(0, CHIPS)
    def _(i):
        for step, ring, chips in (
            (0, ring_o, (2, 3)),
            (4, ring_o, (4, 5)),
        ):

            @pl.when(i == step)
            def _(ring=ring, chips=chips):
                for k in chips:
                    ring.pass_on(k)

        block = at.chip_at(i + 1)
        here = aligned(block, PAIR)
        query = r.queries[here, :]
        start_row = r.starts[:, here]
        top = jnp.full((1, PAIR), LOWEST, F32)
        for chunk in range(SPAN // CHUNK):
            keys = pl.ds(pl.multiple_of(block * PAIR + chunk * CHUNK, ROWS), CHUNK)
            score = dot(r.keyvals[keys, :], query, NT)
            score = jnp.where(allowed(r.code[keys, :], start_row, chunk), score, LOWEST)
            r.scores[chunk * CHUNK : (chunk + 1) * CHUNK, :] = score
            top = jnp.maximum(top, jnp.max(score, axis=0, keepdims=True))
        total = jnp.zeros((1, PAIR), F32)
        for chunk in range(SPAN // CHUNK):
            place = slice(chunk * CHUNK, (chunk + 1) * CHUNK)
            weight = jnp.exp(r.scores[place, :] - top)
            total = total + jnp.sum(weight, axis=0, keepdims=True)
            r.probs[place, :] = weight.astype(BF)
        window = pl.ds(pl.multiple_of(block * PAIR, ROWS), SPAN)
        head = dot(r.keyvals_t[HEAD : 2 * HEAD, window], r.probs[...]) / total
        r.heads_t[:, here] = head
        r.stats[:, here] = top + jnp.log(total)
        r.att_src[2 * block] = head[:, 0:ROWS].astype(BF)
        r.att_src[2 * block + 1] = head[:, ROWS:PAIR].astype(BF)

        @pl.when(i < CHIPS - 1)
        def _():
            att_copy(2 * block, t).start()
            att_copy(2 * block + 1, t).start()

        @pl.when(i == CHIPS - 1)
        def _():
            att_copy(at.twin, t).start()

    r.save("stats", "heads_t")
    ring_c.pass_on(1)
    r.att_t[aligned(t, HEAD), :] = r.att_src[t]
    ring_o.pass_on(6)
    ring_o.pass_on(7)
    for i in range(CHIPS):
        ring_o.second(i)

    @pl.loop(0, 4)
    def _(j):
        sides = [
            r.out_all[:, pl.ds(pl.multiple_of(core * HEAD + j * 16, 16), 16), :].astype(F32)
            for core in range(2)
        ]
        first, second = unpacked(jnp.stack(sides, axis=1).reshape(TENSOR, 16, WIDTH))
        r.out_t[aligned(2 * j, ROWS), :] = first.astype(BF)
        r.out_t[aligned(2 * j + 1, ROWS), :] = second.astype(BF)

    r.save("out_t")
    for stream in first_expert:
        stream.from_y_across()
    all_landed(r.att_t.at[pl.ds(0, 15 * HEAD)], r.a_recv.at[0], at)
    attended = r.att_t[...].astype(F32).T.astype(BF)
    r.att_rows[...] = attended
    middle = r.hid[...].astype(F32) + dot(attended, r.out_t[...], NT)
    r.mid[...] = middle
    inverse = lax.rsqrt(jnp.mean(middle * middle, axis=1, keepdims=True) + 1e-6)
    r.nm_all[aligned(t, ROWS), :] = (middle * inverse * gain_two).astype(BF)
    ring = whole_ring(at, r.nm_all, r.g_send, r.g_recv)
    ring.start()
    r.save("att_rows")
    for stream in second_expert:
        stream.start_y()
    ring_c.pass_on(2)
    ring_c.pass_on(3)
    for stream in second_expert:
        stream.from_across()
    for stream in first_expert:
        stream.finish()
    copies.wait()
    ring_h.end()
    ring_o.end()
    r.finish("normed")
    r.finish("out_t")
    r.proj_grads, r.n_first, r.gates, r.n_sums = r.hidden_all, r.normed, r.cosine, r.out_all
    r.m_sums = r.out_t


    def moe_sums(k, count=1):
        return r.m_sums.at[pl.ds(pl.multiple_of(k * ROWS, ROWS), count * ROWS)]

    halves_n = Halves(at, r.n_parts, r.n_twins, lambda k: r.n_sums.at[k], r.ntw_send, r.ntw_recv)
    halves_m = Halves(at, r.m_parts, r.m_twins, moe_sums, r.mtw_send, r.mtw_recv)
    joined = Joined(
        at,
        r.n_sums,
        r.n_crossed,
        r.n_landed,
        (r.nc_send, r.nc_recv, r.n_send, r.n_recv),
    )
    ring_w = Ring(
        at,
        lambda b: r.wqkv.at[b],
        lambda b, part: r.wqkv.at[b, pl.ds(part * HEAD, HEAD)],
        r.h_send,
        r.h_recv,
        r.wqkv_own,
        r.wqkv.at[pl.ds(0, 15)],
    )
    copies.start(r.wqkv_own, r.wqkv.at[t])

    def moe_along():
        return remote(
            moe_sums(0, 2),
            r.m_landed,
            r.m_send.at[0],
            r.m_recv.at[0],
            TP,
            at.near_core(SUM_Z[0], 0),
        )

    def gu_over_y(k):
        y = at.y_at(k)
        return remote(
            r.gus.at[0, aligned(y, PAIR), :],
            r.y_gu.at[k - 1],
            r.x_send.at[k],
            r.x_recv.at[k],
            SP,
            2 * y + at.x,
        )

    def down_over_y(e, k):
        y = at.y_at(k)
        return remote(
            r.down_grads.at[e, :, aligned(y, PAIR)],
            r.y_down.at[e, k - 1],
            r.y_send.at[4 * e + k],
            r.y_recv.at[4 * e + k],
            SP,
            2 * y + at.x,
        )

    def gate_copy(dest, src):
        return remote(
            r.gate_src.at[dest],
            r.gate_all.at[src],
            r.gg_send.at[0],
            r.gg_recv.at[0],
            TP,
            dest,
        )

    def one_pass(e):
        @pl.loop(0, CHIPS)
        def _(i):
            if e == 0:
                for k in range(2, CHIPS):

                    @pl.when(i == k - 1)
                    def _(k=k):
                        ring.pass_on(k)

                ring.second(i)

                @pl.when(i == 1)
                def _():
                    ring_c.pass_on(4)
                    ring_c.pass_on(5)

                @pl.when(i == 4)
                def _():
                    for stream in second_expert:
                        stream.from_y()

                @pl.when(i == 5)
                def _():
                    ring_c.pass_on(6)
                    ring_c.pass_on(7)

                ring_c.second(i)

                @pl.when(i == 6)
                def _():
                    ring_w.start()

            here = aligned(at.step(i) if e == 0 else at.sum_step(i), PAIR)
            nm = r.nm_all[here, :]
            place = lanes((PAIR, ROWS))
            if e == 0:
                expert = sublanes((ROWS, PAIR))
                named = expert == r.routes_t[0:1, here]
                for j in range(1, 8):
                    named = named | (expert == r.routes_t[j : j + 1, here])
                named = jnp.where(named, 1.0, 0.0).T > 0.5
                logits = jnp.where(named, dot(nm, r.small[...]), LOWEST)
                powers = jnp.exp(logits - jnp.max(logits, axis=1, keepdims=True))
                powers = jnp.where(named, powers, 0.0)
                gates = powers / jnp.sum(powers, axis=1, keepdims=True)
            else:
                kept = r.gates[here, :]
                gates = jnp.where(place == 2 * HEAD - 1, 0.0, kept)
                earlier = kept[:, 2 * HEAD - 1 : 2 * HEAD]
            mine = place == 2 * t + e
            gate = jnp.sum(jnp.where(mine, gates, 0.0), axis=1, keepdims=True)
            act_grad = dot(r.cots[here, :], r.downs[e * UNITS : (e + 1) * UNITS, :], NT)
            projected = dot(nm, r.gus[e])
            first, up = projected[:, :UNITS], projected[:, UNITS:]
            sigmoid = 1.0 / (1.0 + jnp.exp(-first))
            silu = first * sigmoid
            activated = silu * up
            gate_grad = jnp.sum(activated * act_grad, axis=1, keepdims=True)
            weighted = (activated * gate).astype(BF)
            r.weighted_t[:, here] = weighted.T
            act_grad = act_grad * gate
            r.proj_grads[here, 0:UNITS] = (
                act_grad * up * (sigmoid * (1.0 + first * (1.0 - sigmoid)))
            ).astype(BF)
            r.proj_grads[here, UNITS:WIDTH] = (act_grad * silu).astype(BF)
            normed_part = dot(r.proj_grads[here, :], r.gus[e], NT)
            if e == 0:
                r.gates[here, :] = jnp.where(place == 2 * HEAD - 1, gate_grad, gates)
                r.weighted[here, :] = weighted
                r.n_first[here, :] = normed_part.astype(BF)

                @pl.when(i == 0)
                def _():
                    ring.pass_on(1)

                return
            row = 2 * lax.rem(t, 4)
            gate_grads = jnp.where(
                place == row, earlier, jnp.where(place == row + 1, gate_grad, 0.0)
            ).T
            chip = at.sum_step(i)
            r.gate_src[2 * chip] = gate_grads[0:8, 0:ROWS]
            r.gate_src[2 * chip + 1] = gate_grads[0:8, ROWS:PAIR]

            @pl.when(i < CHIPS - 1)
            def _():
                gate_copy(2 * chip, t).start()
                gate_copy(2 * chip + 1, t).start()

            @pl.when(i == CHIPS - 1)
            def _():
                gate_copy(at.twin, t).start()

            halves_n.put(i, normed_part + r.n_first[here, :].astype(F32))
            both = jnp.concatenate([r.weighted[here, :], weighted], axis=1)
            halves_m.put(i, dot(both, r.downs[...]))

            @pl.when(i > 0)
            def _():
                halves_n.add(i - 1)
                halves_m.add(i - 1)

            for j in range(4):

                @pl.when(i == 2 * j + 1)
                def _(j=j):
                    joined.cross(j).start()

            for j in range(2):

                @pl.when(i == 2 * j + 4)
                def _(j=j):
                    joined.join(j)

            @pl.when(i == 3)
            def _():
                moe_along().start()

            for step, chips in ((0, (2, 3)), (2, (4, 5))):

                @pl.when(i == step)
                def _(chips=chips):
                    for k in chips:
                        ring_w.pass_on(k)

    def down_gradients(e):
        @pl.loop(0, 2)
        def _(j):
            strip = aligned(j, PAIR)
            r.down_grads[e, strip, :] = dot(r.weighted_t[strip, :], r.cots[...]).astype(BF)

    def gate_up_gradients(e):
        @pl.loop(0, 4)
        def _(j):
            strip = aligned(j, PAIR)
            r.gus[e, strip, :] = dot(r.nm_all[:, strip], r.proj_grads[...], TN).astype(BF)

    one_pass(0)
    for stream in second_expert:
        stream.from_y_across()
    for stream in first_expert:
        stream.end()
    down_gradients(0)
    for k in range(1, 4):
        down_over_y(0, k).start()
    gate_up_gradients(0)
    ring_w.pass_on(1)
    for k in range(1, 4):
        gu_over_y(k).start()
    for stream in second_expert:
        stream.finish()
    one_pass(1)
    joined.join(2)
    halves_n.add(CHIPS - 1)
    halves_m.add(CHIPS - 1)
    out_rows = r.n_first.at[pl.ds(0, WIDTH)]
    copies.start(r.out_t_d, out_rows)
    for stream in second_expert:
        stream.end()
    down_gradients(1)
    for k in range(1, 4):
        down_over_y(1, k).start()
    gate_up_gradients(1)
    copies.start(r.gus.at[1], r.gu_grad)
    r.gate_all[t] = r.gate_src[t]
    all_landed(r.gate_all.at[pl.ds(0, 15)], r.gg_recv.at[0], at)
    groups = r.gate_all[...].reshape(4, 4, 8, ROWS)
    gate_grads = (groups[:, 0] + groups[:, 1] + groups[:, 2] + groups[:, 3]).reshape(32, ROWS)
    gate_grads = jnp.concatenate([gate_grads, jnp.zeros((ROWS - 32, ROWS), F32)], axis=0).T
    own_rows = aligned(t, ROWS)
    gates = jnp.where(lanes((ROWS, ROWS)) < 32, r.gates[own_rows, :], 0.0)
    mean = jnp.sum(gates * gate_grads, axis=1, keepdims=True)
    logit_grad = gates * (gate_grads - mean)
    r.router_t[...] = dot(logit_grad.T.astype(BF), r.nm_all[own_rows, :])[0:32, :]
    by_router = dot(logit_grad.astype(BF), r.small[...], NT)

    gain_two = r.small[...].astype(F32).T[33:34, :]
    normed_grad = joined.result() + by_router
    middle = r.mid[...]
    inverse = lax.rsqrt(jnp.mean(middle * middle, axis=1, keepdims=True) + 1e-6)
    unit = middle * inverse
    r.gain_grad[...] = jnp.sum(normed_grad * unit, axis=0, keepdims=True)
    scaled = normed_grad * gain_two
    grad = r.cots[aligned(t, ROWS), :].astype(F32) + inverse * (
        scaled - unit * jnp.mean(scaled * unit, axis=1, keepdims=True)
    )
    r.mid_grad[...] = grad
    turned = grad.T.reshape(DP, TENSOR, 8, ROWS).transpose(1, 0, 2, 3)
    r.mid_t[...] = turned.reshape(WIDTH, ROWS).astype(BF)
    copies.wait()
    r.att_grad_t[...] = dot(grad.astype(BF), out_rows[...]).T.astype(BF)
    r.save("att_grad_t", "mid_grad", "mid_t", "gain_grad", "router_t")
    across, own = moe_sums(6)[...].astype(F32), middle + moe_sums(7)[...].astype(F32)
    moe_along().wait_recv()
    r.moe_across[...] = across + r.m_landed[0:ROWS, :].astype(F32)
    r.mid[...] = own + r.m_landed[ROWS:PAIR, :].astype(F32)
    copies.start(moe_sums(2, 4), r.moe_last)
    r.save("moe_across", "mid")
    gu = r.gus[0, aligned(at.y, PAIR), :].astype(F32)
    for k in range(1, 4):
        gu_over_y(k).wait_recv()
        gu = gu + r.y_gu[k - 1].astype(F32)
    r.ys_gu[0] = gu[0:ROWS].astype(BF)
    r.ys_gu[1] = gu[ROWS:PAIR].astype(BF)
    for e in range(2):
        down = r.down_grads[e, :, aligned(at.y, PAIR)].astype(F32)
        for k in range(1, 4):
            down_over_y(e, k).wait_recv()
            down = down + r.y_down[e, k - 1].astype(F32)
        r.ys_down[0, e] = down[:, 0:ROWS].astype(BF)
        r.ys_down[1, e] = down[:, ROWS:PAIR].astype(BF)
    r.save("ys_gu", "ys_down")
    for k in range(1, 4):
        gu_over_y(k).wait_send()
        for e in range(2):
            down_over_y(e, k).wait_send()
    ring_w.pass_on(6)
    ring_w.pass_on(7)
    all_sent(r.tiles.at[pl.ds(0, 15)], r.t1_send.at[0], at)
    all_sent(r.tile_all.at[pl.ds(0, 7)], r.t2_send.at[0], at)
    all_sent(r.row_dp.at[pl.ds(0, 7)], r.rd_send.at[0], at)
    all_sent(seven_wq, r.wq_send.at[0], at)
    all_sent(r.att_src.at[pl.ds(0, 15)], r.a_send.at[0], at)
    all_sent(r.gate_src.at[pl.ds(0, 15)], r.gg_send.at[0], at)
    ring.end()
    ring_c.end()
    moe_along().wait_send()
    for i in range(CHIPS):
        ring_w.second(i)
    ring_w.end()
    halves_n.end()
    halves_m.end()
    joined.end()
    copies.wait()
    r.end()


def back_kernel(r):
    at = Place()
    t, d = at.t, at.d
    copies = Copies(r.local)
    r.load()
    copies.start(r.gu_grad.at[aligned(at.y, PAIR), :], r.gu_own)
    r.need("att_grad_t")
    r.grads_t[0:HEAD, :] = jnp.zeros((HEAD, LENGTH), BF)
    r.grads_t[HEAD : 2 * HEAD, aligned(t, ROWS)] = r.att_grad_t[aligned(t, HEAD), :]
    at.enter()

    def back_copy(k, src):
        dest = at.tensor_at(k)
        return remote(
            r.att_grad_t.at[aligned(dest, HEAD), :],
            r.grads_t.at[pl.ds(HEAD, HEAD), aligned(src, ROWS)],
            r.g_send.at[0],
            r.g_recv.at[0],
            TP,
            dest,
        )

    def then_across():
        return (
            remote(
                r.ys_gu.at[1 - at.x], r.yx_gu0, r.x_send.at[0], r.x_recv.at[0], SP, at.across
            ),
            remote(
                r.ys_down.at[1 - at.x], r.yx_down, r.x_send.at[1], r.x_recv.at[1], SP, at.across
            ),
        )

    def over_y(k):
        y = at.y_at(k)
        return remote(
            r.gu_grad.at[aligned(y, PAIR), :],
            r.y_gu.at[k],
            r.gu_send.at[k],
            r.gu_recv.at[k],
            SP,
            2 * y + at.x,
        )

    def then_x():
        return remote(r.s_gu, r.yx_gu, r.gu_send.at[0], r.gu_recv.at[0], SP, at.across)

    def moe_along(j):
        return remote(
            r.moe_last.at[aligned(j, PAIR)],
            r.m_landed.at[j],
            r.m_send.at[j],
            r.m_recv.at[j],
            TP,
            at.near_core(SUM_Z[2 * j + 2], 0),
        )

    for k in range(1, TENSOR):
        back_copy(k, t).start()
    for j in range(2):
        moe_along(j).start()
    for k in range(1, 4):
        over_y(k).start()
    r.need("ys_gu", "ys_down")
    for copy in then_across():
        copy.start()

    r.need("mid_t", "att_rows")
    r.out_terms[...] = (
        dot(r.mid_t[...], r.att_rows[...]).reshape(CHIPS, ROWS, WIDTH).astype(BF)
    )

    def out_half():
        return remote(
            r.out_terms.at[:, aligned(1 - at.core, HEAD), :],
            r.out_twins,
            r.ot_send.at[0],
            r.ot_recv.at[0],
            TP,
            at.twin,
        )

    out_half().start()
    key_codes(r.mask, r.code)
    r.starts[...] = document_starts(r.seg[...])
    r.kv_sum[...] = jnp.zeros((PADDED, 2 * HEAD), F32)

    def out_along(k):
        return remote(
            r.out_sums.at[pl.ds(2 * lax.rem(at.z + k, 4), 2)],
            r.out_landed.at[k],
            r.o_send.at[k],
            r.o_recv.at[k],
            TP,
            at.near_core(k, 0),
        )

    def out_across():
        return remote(
            r.out_joined, r.out_crossed, r.o_send.at[0], r.o_recv.at[0], TP, at.near_core(0, 1)
        )

    def out_total(x):
        total = r.out_sums[2 * at.z + x].astype(F32)
        for k in range(1, 4):
            total = total + r.out_landed[k, x].astype(F32)
        return total


    def moe_across():
        return remote(
            r.m_joined, r.m_crossed, r.m_send.at[2], r.m_recv.at[2], TP, at.near_core(0, 1)
        )

    out_half().wait_recv()
    r.out_sums[...] = (
        r.out_terms[:, aligned(at.core, HEAD), :].astype(F32) + r.out_twins[...].astype(F32)
    ).astype(BF)
    r.need("queries", "keyvals", "keyvals_t", "stats", "heads_t", "cosine_t", "sine_t")
    all_landed(r.grads_t.at[pl.ds(HEAD, HEAD), pl.ds(0, 15 * ROWS)], r.g_recv.at[0], at)

    def query_copy(dest, src):
        return remote(
            r.query_src.at[dest],
            r.query_all.at[src],
            r.b_send.at[0],
            r.b_recv.at[0],
            TP,
            dest,
        )

    @pl.loop(0, CHIPS)
    def _(i):
        block = at.chip_at(i + 1)
        here = aligned(block, PAIR)
        query = r.queries[here, :]
        start_row = r.starts[:, here]
        stat = r.stats[:, here]
        grad_t = r.grads_t[:, here]
        grad_rows = grad_t.astype(F32).T.astype(BF)
        head = r.heads_t[:, here]
        delta = jnp.sum(head * grad_t[HEAD : 2 * HEAD, :].astype(F32), axis=0, keepdims=True)
        query_grad = jnp.zeros((HEAD, PAIR), F32)
        for chunk in range(SPAN // CHUNK):
            keys = pl.ds(pl.multiple_of(block * PAIR + chunk * CHUNK, ROWS), CHUNK)
            both = r.keyvals[keys, :]
            score = dot(both, query, NT)
            ok = allowed(r.code[keys, :], start_row, chunk)
            prob = jnp.exp(jnp.where(ok, score - stat, LOWEST))
            prob_grad = dot(both, grad_t)
            score_grad = (prob * (prob_grad - delta)).astype(BF)
            r.kv_sum[keys, :] += dot(score_grad, query) + dot(prob.astype(BF), grad_rows)
            query_grad = query_grad + dot(r.keyvals_t[0:HEAD, keys], score_grad)
        turned = turned_back(query_grad * (1.0 / math.sqrt(HEAD)), r, here).astype(BF)
        r.tail_left[0:HEAD, here] = turned
        r.query_src[2 * block] = turned[:, 0:ROWS]
        r.query_src[2 * block + 1] = turned[:, ROWS:PAIR]

        @pl.when(i < CHIPS - 1)
        def _():
            query_copy(2 * block, t).start()
            query_copy(2 * block + 1, t).start()

        @pl.when(i == CHIPS - 1)
        def _():
            query_copy(at.twin, t).start()

    @pl.loop(0, CHIPS)
    def _(i):
        here = aligned(i, PAIR)
        grad = r.kv_sum[pl.ds(pl.multiple_of(REACH + i * PAIR, ROWS), PAIR), :].T
        grad = jnp.concatenate(
            [turned_back(grad[0:HEAD], r, here), grad[HEAD : 2 * HEAD]], axis=0
        ).astype(BF)
        r.tail_left[HEAD : 3 * HEAD, here] = grad
        r.back_src[2 * i] = grad[:, 0:ROWS]
        r.back_src[2 * i + 1] = grad[:, ROWS:PAIR]

    def grad_copy(k, src):
        dest = at.tensor_at(k)
        return remote(
            r.back_src.at[dest],
            r.back_all.at[src],
            r.q_send.at[0],
            r.q_recv.at[0],
            TP,
            dest,
        )

    for k in range(1, TENSOR):
        grad_copy(k, t).start()
    r.back_all[t] = r.back_src[t]
    r.query_all[t] = r.query_src[t]
    for k in range(1, 4):
        out_along(k).start()
    r.need("moe_across", "moe_own")
    across = r.moe_across[...]
    for j in range(2):
        moe_along(j).wait_recv()
        across = across + r.m_landed[j, 0:ROWS].astype(F32)
    r.m_joined[...] = across.astype(BF)
    moe_across().start()

    copies.wait()
    r.need("normed")
    r.tail[0 : 3 * HEAD, :] = dot(r.tail_left[...], r.normed[...]).astype(BF)

    r.need("wqkv")

    @pl.loop(0, 4)
    def _(j):
        rows = pl.ds(pl.multiple_of(HEAD + j * 16, 16), 16)
        first, second = unpacked(r.wqkv[:, rows, :].astype(F32))
        r.kv_full[aligned(2 * j, ROWS), :] = first.astype(BF)
        r.kv_full[aligned(2 * j + 1, ROWS), :] = second.astype(BF)

    all_landed(r.query_all.at[pl.ds(0, 15)], r.b_recv.at[0], at)
    all_landed(r.back_all.at[pl.ds(0, 15)], r.q_recv.at[0], at)
    r.need("hid", "small", "mid_grad", "router_t", "gain_grad")
    query_rows = r.query_all[...].astype(F32).reshape(WIDTH, ROWS).T.astype(BF)
    pairs = r.back_all[...].astype(F32).reshape(CHIPS, 2, ROWS, ROWS)
    kv_rows = (pairs[:, 0] + pairs[:, 1]).reshape(WIDTH, ROWS).T.astype(BF)
    wq_full = r.wqkv[:, 0:HEAD, :].reshape(WIDTH, WIDTH)
    normed_grad = dot(query_rows, wq_full) + dot(kv_rows, r.kv_full[...], NT)
    hidden = r.hid[...].astype(F32)
    inverse = lax.rsqrt(jnp.mean(hidden * hidden, axis=1, keepdims=True) + 1e-6)
    unit = hidden * inverse
    gain_one = r.small[...].astype(F32).T[32:33, :]
    gain_one_grad = jnp.sum(normed_grad * unit, axis=0, keepdims=True)
    scaled = normed_grad * gain_one
    r.hidden_grad[...] = (
        r.mid_grad[...]
        + inverse * (scaled - unit * jnp.mean(scaled * unit, axis=1, keepdims=True))
    ).astype(BF)
    r.tail[3 * HEAD : 3 * HEAD + 32, :] = r.router_t[...].astype(BF)
    row = sublanes((16, WIDTH))
    r.tail[3 * HEAD + 32 : TAIL, :] = jnp.where(
        row == 0, gain_one_grad, jnp.where(row == 1, r.gain_grad[...], 0.0)
    ).astype(BF)

    def tail_copy(k):
        dest = at.dp_at(k)
        return remote(
            r.tail.at[:, aligned(dest, ROWS)],
            r.tail_in.at[k],
            r.t_send.at[0],
            r.t_recv.at[0],
            SP,
            dest,
        )

    for k in range(1, DP):
        tail_copy(k).start()

    for k in range(1, 4):
        over_y(k).wait_recv()

    def y_total(x):
        here = aligned(x, ROWS)
        gu = r.gu_own[here, :].astype(F32)
        for k in range(1, 4):
            gu = gu + r.y_gu[k, here, :].astype(F32)
        return gu

    r.s_gu[...] = y_total(1 - at.x).astype(BF)
    then_x().start()

    for k in range(1, 4):
        out_along(k).wait_recv()
    r.out_joined[...] = out_total(1 - at.x_far).astype(BF)
    out_across().start()
    moe_across().wait_recv()
    own = r.moe_own[...] + r.m_crossed[...].astype(F32)
    for j in range(2):
        own = own + r.m_landed[j, ROWS:PAIR].astype(F32)
    r.output[...] = own.astype(BF)
    r.save("output")
    out_across().wait_recv()
    r.out_rows[...] = out_total(at.x_far) + r.out_crossed[...].astype(F32)

    def out_copy(k):
        dest = at.dp_at(k)
        return remote(
            r.out_rows.at[aligned(dest, 8), :],
            r.out_in.at[k],
            r.od_send.at[0],
            r.od_recv.at[0],
            SP,
            dest,
        )

    for k in range(1, DP):
        out_copy(k).start()

    total = r.tail[:, aligned(d, ROWS)].astype(F32)
    all_landed(r.tail_in.at[pl.ds(0, 7)], r.t_recv.at[0], at)
    for k in range(1, DP):
        total = total + r.tail_in[k].astype(F32)
    r.query_out[...] = total[0:HEAD, :]
    r.save("hidden_grad", "query_out")
    turned = jnp.concatenate(
        [total[HEAD:TAIL], jnp.zeros((256 + HEAD - TAIL, ROWS), F32)], axis=0
    ).T
    for j in range(TENSOR):
        r.pieces[j] = turned[j * 8 : (j + 1) * 8, :]

    def last_copy(k, src):
        dest = at.tensor_at(k)
        return remote(
            r.pieces.at[dest], r.last.at[src], r.l_send.at[0], r.l_recv.at[0], TP, dest
        )

    for k in range(1, TENSOR):
        last_copy(k, t).start()
    r.last[t] = r.pieces[t]

    for copy in then_across():
        copy.wait_recv()
    r.gu_out[0] = r.ys_gu[at.x].astype(F32) + r.yx_gu0[...].astype(F32)
    r.down_out[...] = r.ys_down[at.x].astype(F32) + r.yx_down[...].astype(F32)
    then_x().wait_recv()
    r.gu_out[1] = y_total(at.x) + r.yx_gu[...].astype(F32)
    r.save("gu_out", "down_out")
    total = r.out_rows[aligned(d, 8), :]
    all_landed(r.out_in.at[pl.ds(0, 7)], r.od_recv.at[0], at)
    for k in range(1, DP):
        total = total + r.out_in[k]
    r.out_grad[...] = total
    all_landed(r.last.at[pl.ds(0, 15)], r.l_recv.at[0], at)
    r.kv_out[...] = jnp.concatenate(
        [r.last[2 * j, :, 0:ROWS] + r.last[2 * j + 1, :, 0:ROWS] for j in range(CHIPS)], axis=1
    )
    shared = r.last[0, :, ROWS:PAIR]
    for j in range(1, TENSOR):
        shared = shared + r.last[j, :, ROWS:PAIR]
    r.router_out[...] = shared[:, 0:32]
    wide = jnp.concatenate([shared, jnp.zeros((ROWS - 8, ROWS), F32)], axis=0).T
    r.gain_one_out[...] = wide[32:33, 0:8]
    r.gain_two_out[...] = wide[33:34, 0:8]
    r.save("out_grad", "kv_out", "router_out", "gain_one_out", "gain_two_out")

    all_sent(r.att_grad_t.at[pl.ds(0, 15 * HEAD)], r.g_send.at[0], at)
    all_sent(r.query_src.at[pl.ds(0, 15)], r.b_send.at[0], at)
    all_sent(r.back_src.at[pl.ds(0, 15)], r.q_send.at[0], at)
    all_sent(r.pieces.at[pl.ds(0, 15)], r.l_send.at[0], at)
    all_sent(r.tail_in.at[pl.ds(0, 7)], r.t_send.at[0], at)
    all_sent(r.out_in.at[pl.ds(0, 7)], r.od_send.at[0], at)
    for k in range(1, 4):
        over_y(k).wait_send()
    for copy in then_across():
        copy.wait_send()
    then_x().wait_send()
    out_half().wait_send()
    for k in range(1, 4):
        out_along(k).wait_send()
    out_across().wait_send()
    for j in range(2):
        moe_along(j).wait_send()
    moe_across().wait_send()
    r.end()


def store_kernel(r):
    copies = Copies(r.local)
    for name in STORED:
        copies.start(getattr(r, name), getattr(r, name + "_kept"))
    for name in STORED:
        copies.wait(1)
        copies.start(getattr(r, name + "_kept"), getattr(r, name + "_done"))
    copies.wait()


STORED = (
    "output",
    "hidden_grad",
    "gain_one_out",
    "query_out",
    "kv_out",
    "out_grad",
    "gain_two_out",
    "router_out",
    "gu_out",
    "down_out",
)


class Refs:
    def __init__(self, names, refs, loads=(), saves=()):
        for name, ref in zip(names, refs):
            setattr(self, name, ref)
        self.loads, self.saves, self.saved = list(loads), list(saves), []

    def copy_in(self, name):
        sem = self.load_sems.at[self.loads.index(name)]
        return pltpu.make_async_copy(getattr(self, name + "_d"), getattr(self, name), sem)

    def copy_out(self, name):
        sem = self.save_sems.at[self.saves.index(name)]
        return pltpu.make_async_copy(getattr(self, name), getattr(self, name + "_d"), sem)

    def load(self):
        for name in self.loads:
            self.copy_in(name).start()

    def need(self, *names):
        for name in names:
            self.copy_in(name).wait()

    def save(self, *names):
        for name in names:
            self.copy_out(name).start()
            self.saved.append(name)

    def finish(self, name):
        self.copy_out(name).wait()
        self.saved.remove(name)

    def end(self):
        for name in self.saved:
            self.copy_out(name).wait()


def call(kernel, number, inputs, outputs, scratch, reaches=True):
    def space(name):
        return pl.BlockSpec(memory_space=pltpu.VMEM if name.endswith("_v") else pl.ANY)

    outputs = {name: jax.ShapeDtypeStruct(shape, dtype) for name, (shape, dtype) in outputs.items()}
    loads = [name[:-2] for name in inputs if name.endswith("_d")]
    saves = [name[:-2] for name in outputs if name.endswith("_d")]
    scratch = dict(scratch)
    for name in loads:
        scratch[name] = pltpu.VMEM(inputs[name + "_d"].shape, inputs[name + "_d"].dtype)
    for name in saves:
        scratch[name] = pltpu.VMEM(outputs[name + "_d"].shape, outputs[name + "_d"].dtype)
    scratch |= sems(load_sems=max(1, len(loads)), save_sems=max(1, len(saves)))
    names = [name.removesuffix("_v") for name in (*inputs, *outputs)] + list(scratch)
    params = {"vmem_limit_bytes": VMEM_BYTES}
    if reaches:
        params |= {"collective_id": number, "has_side_effects": True}
    values = pl.pallas_call(
        lambda *refs: kernel(Refs(names, refs, loads, saves)),
        out_shape=list(outputs.values()),
        in_specs=[space(name) for name in inputs],
        out_specs=[space(name) for name in outputs],
        scratch_shapes=list(scratch.values()),
        compiler_params=pltpu.CompilerParams(**params),
        name=kernel.__name__,
    )(*inputs.values())
    return Refs([name.removesuffix("_v").removesuffix("_d") for name in outputs], values)


def sems(**counts):
    return {name: pltpu.SemaphoreType.DMA((count,)) for name, count in counts.items()}


def rope_tables():
    half = HEAD // 2
    freqs = np.exp(
        np.arange(half, dtype=np.float32) * np.float32(-2.0 * math.log(10000.0) / HEAD)
    ).astype(np.float32)
    angles = np.arange(LENGTH, dtype=np.float32)[:, None] * freqs[None, :]
    cos, sin = np.cos(angles).astype(np.float32), np.sin(angles).astype(np.float32)
    ones, zeros = np.ones((LENGTH, HEAD), np.float32), np.zeros((LENGTH, HEAD), np.float32)
    return (
        np.concatenate([cos, cos, ones], axis=1),
        np.concatenate([-sin, sin, zeros], axis=1),
        np.ascontiguousarray(cos.T),
        np.ascontiguousarray(sin.T),
    )


def body(
    hidden,
    seg_ids,
    key_mask,
    routes,
    gain_attn,
    w_query,
    w_keyval,
    w_out,
    gain_mlp,
    w_router,
    w_gate_up,
    w_down,
    cotangent,
):
    V = pltpu.VMEM
    cosine, sine, cosine_t, sine_t = rope_tables()
    hid, cot = hidden[0], cotangent[0]
    a = call(
        layer_kernel,
        1,
        dict(
            hid_v=hid,
            cot=cot,
            w_keyval_v=w_keyval,
            w_out_t_v=w_out.T,
            w_query_t_v=w_query.T,
            router_v=w_router,
            gain_one_v=gain_attn.reshape(1, 8),
            gain_two_v=gain_mlp.reshape(1, 8),
            gu=w_gate_up,
            down=w_down,
            cosine_d=cosine,
            sine_d=sine,
            mask_v=key_mask,
            seg_v=seg_ids,
            routes_t_v=routes[0].T,
        ),
        dict(
            normed_d=((LENGTH, WIDTH), BF),
            queries_d=((LENGTH, 2 * HEAD), BF),
            keyvals_d=((PADDED, 2 * HEAD), BF),
            keyvals_t_d=((2 * HEAD, PADDED), BF),
            stats_d=((1, LENGTH), F32),
            heads_t_d=((HEAD, LENGTH), F32),
            att_rows_d=((ROWS, WIDTH), BF),
            small_d=((WIDTH, ROWS), BF),
            out_t_d=((WIDTH, WIDTH), BF),
            wqkv=((TENSOR, ROWS, WIDTH), BF),
            moe_across_d=((ROWS, WIDTH), F32),
            mid_d=((ROWS, WIDTH), F32),
            moe_last=((2 * PAIR, WIDTH), BF),
            mid_grad_d=((ROWS, WIDTH), F32),
            mid_t_d=((WIDTH, ROWS), BF),
            att_grad_t_d=((WIDTH, ROWS), BF),
            gu_grad=((WIDTH, WIDTH), BF),
            ys_gu_d=((2, ROWS, WIDTH), BF),
            ys_down_d=((2, 2, UNITS, ROWS), BF),
            router_t_d=((32, WIDTH), F32),
            gain_grad_d=((1, WIDTH), F32),
        ),
        dict(
            hidden_all=V((LENGTH, WIDTH), BF),
            nm_all=V((LENGTH, WIDTH), BF),
            cots=V((LENGTH, WIDTH), BF),
            gus=V((2, WIDTH, WIDTH), BF),
            downs=V((WIDTH, WIDTH), BF),
            down_grads=V((2, UNITS, WIDTH), BF),
            weighted=V((LENGTH, UNITS), BF),
            weighted_t=V((UNITS, LENGTH), BF),
            wqkv_own=V((ROWS, WIDTH), BF),
            rows=V((16, WIDTH), BF),
            row_dp=V((DP, 16, WIDTH), BF),
            shares=V((8, ROWS), F32),
            tiles=V((TENSOR, 16, ROWS), BF),
            tile_all=V((DP, TENSOR, 16, ROWS), BF),
            out_all=V((CHIPS, ROWS, WIDTH), BF),
            wq_all=V((2 * HEAD, WIDTH), BF),
            code=V((PADDED, ROWS), F32),
            scores=V((SPAN, PAIR), F32),
            probs=V((SPAN, PAIR), BF),
            starts=V((1, LENGTH), F32),
            wqk=V((WIDTH, PAIR), BF),
            att_src=V((TENSOR, HEAD, ROWS), BF),
            att_t=V((WIDTH, ROWS), BF),
            y_gu=V((3, PAIR, WIDTH), BF),
            y_down=V((2, 3, UNITS, PAIR), BF),
            n_parts=V((SLOTS, PAIR, WIDTH), BF),
            n_twins=V((CHIPS, ROWS, WIDTH), BF),
            n_crossed=V((4, ROWS, WIDTH), BF),
            n_landed=V((3, ROWS, WIDTH), BF),
            m_parts=V((SLOTS, PAIR, WIDTH), BF),
            m_twins=V((CHIPS, ROWS, WIDTH), BF),
            m_landed=V((PAIR, WIDTH), BF),
            gate_src=V((TENSOR, 8, ROWS), F32),
            gate_all=V((TENSOR, 8, ROWS), F32),
        )
        | sems(
            h_send=1,
            h_recv=18,
            c_send=1,
            c_recv=18,
            o_send=17,
            o_recv=18,
            g_send=1,
            g_recv=18,
            t1_send=1,
            t1_recv=1,
            t2_send=1,
            t2_recv=1,
            rd_send=1,
            rd_recv=1,
            wq_send=1,
            wq_recv=1,
            e_send=4,
            e_recv=40,
            a_send=1,
            a_recv=1,
            ntw_send=SLOTS,
            ntw_recv=8,
            nc_send=4,
            nc_recv=4,
            n_send=3,
            n_recv=3,
            mtw_send=SLOTS,
            mtw_recv=8,
            m_send=1,
            m_recv=1,
            gg_send=1,
            gg_recv=1,
            x_send=4,
            x_recv=4,
            y_send=8,
            y_recv=8,
            local=12,
        ),
    )
    c = call(
        back_kernel,
        3,
        dict(
            att_grad_t_d=a.att_grad_t,
            mid_t_d=a.mid_t,
            mid_grad_d=a.mid_grad,
            moe_across_d=a.moe_across,
            moe_own_d=a.mid,
            moe_last=a.moe_last,
            wqkv_d=a.wqkv,
            gu_grad=a.gu_grad,
            ys_gu_d=a.ys_gu,
            ys_down_d=a.ys_down,
            router_t_d=a.router_t,
            gain_grad_d=a.gain_grad,
            queries_d=a.queries,
            keyvals_d=a.keyvals,
            keyvals_t_d=a.keyvals_t,
            stats_d=a.stats,
            heads_t_d=a.heads_t,
            mask_v=key_mask,
            seg_v=seg_ids,
            cosine_t_d=cosine_t,
            sine_t_d=sine_t,
            att_rows_d=a.att_rows,
            normed_d=a.normed,
            hid_d=hid,
            small_d=a.small,
        ),
        dict(
            output_d=((ROWS, WIDTH), BF),
            hidden_grad_d=((ROWS, WIDTH), BF),
            gain_one_out_d=((1, 8), F32),
            query_out_d=((HEAD, ROWS), F32),
            kv_out_d=((8, WIDTH), F32),
            out_grad_d=((8, WIDTH), F32),
            gain_two_out_d=((1, 8), F32),
            router_out_d=((8, 32), F32),
            gu_out_d=((2, ROWS, WIDTH), F32),
            down_out_d=((2, UNITS, ROWS), F32),
        ),
        dict(
            gu_own=V((PAIR, WIDTH), BF),
            grads_t=V((2 * HEAD, LENGTH), BF),
            kv_full=V((WIDTH, WIDTH), BF),
            code=V((PADDED, ROWS), F32),
            starts=V((1, LENGTH), F32),
            kv_sum=V((PADDED, 2 * HEAD), F32),
            tail_left=V((3 * HEAD, LENGTH), BF),
            query_src=V((TENSOR, HEAD, ROWS), BF),
            query_all=V((TENSOR, HEAD, ROWS), BF),
            back_src=V((TENSOR, ROWS, ROWS), BF),
            back_all=V((TENSOR, ROWS, ROWS), BF),
            out_terms=V((CHIPS, ROWS, WIDTH), BF),
            out_twins=V((CHIPS, HEAD, WIDTH), BF),
            out_sums=V((CHIPS, HEAD, WIDTH), BF),
            out_landed=V((4, 2, HEAD, WIDTH), BF),
            out_joined=V((HEAD, WIDTH), BF),
            out_crossed=V((HEAD, WIDTH), BF),
            out_rows=V((HEAD, WIDTH), F32),
            out_in=V((DP, 8, WIDTH), F32),
            m_landed=V((2, PAIR, WIDTH), BF),
            m_joined=V((ROWS, WIDTH), BF),
            m_crossed=V((ROWS, WIDTH), BF),
            tail=V((TAIL, WIDTH), BF),
            tail_in=V((DP, TAIL, ROWS), BF),
            pieces=V((TENSOR, 8, PAIR), F32),
            last=V((TENSOR, 8, PAIR), F32),
            yx_gu0=V((ROWS, WIDTH), BF),
            y_gu=V((4, PAIR, WIDTH), BF),
            s_gu=V((ROWS, WIDTH), BF),
            yx_gu=V((ROWS, WIDTH), BF),
            yx_down=V((2, UNITS, ROWS), BF),
        )
        | sems(
            g_send=1,
            g_recv=1,
            q_send=1,
            q_recv=1,
            b_send=1,
            b_recv=1,
            x_send=4,
            x_recv=4,
            gu_send=4,
            gu_recv=4,
            ot_send=1,
            ot_recv=1,
            o_send=8,
            o_recv=8,
            m_send=3,
            m_recv=3,
            t_send=1,
            t_recv=1,
            od_send=1,
            od_recv=1,
            l_send=1,
            l_recv=1,
            local=8,
        ),
    )
    values = {name: getattr(c, name) for name in STORED}
    done = call(
        store_kernel,
        0,
        values,
        {name + "_done": (value.shape, value.dtype) for name, value in values.items()},
        {name + "_kept": V(value.shape, value.dtype) for name, value in values.items()}
        | sems(local=2 * len(STORED)),
        reaches=False,
    )
    return (
        done.output_done[None],
        done.hidden_grad_done[None],
        done.gain_one_out_done.reshape(8),
        done.query_out_done.T,
        done.kv_out_done,
        done.out_grad_done.T,
        done.gain_two_out_done.reshape(8),
        done.router_out_done,
        done.gu_out_done,
        done.down_out_done,
    )


def solution(mesh):
    return jax.shard_map(
        body,
        mesh=mesh,
        in_specs=(
            P("dp", "tensor", None),
            P("dp", None),
            P("dp", None),
            P("dp", None, None),
            P(("dp", "tensor")),
            P("dp", "tensor"),
            P(("dp", "tensor"), None),
            P(None, ("dp", "tensor")),
            P(("dp", "tensor")),
            P(("dp", "tensor"), None),
            P("tensor", "dp", None),
            P("tensor", None, "dp"),
            P("dp", "tensor", None),
        ),
        out_specs=(
            P("dp", "tensor", None),
            P("dp", "tensor", None),
            P(("dp", "tensor")),
            P("dp", "tensor"),
            P(("dp", "tensor"), None),
            P(None, ("dp", "tensor")),
            P(("dp", "tensor")),
            P(("dp", "tensor"), None),
            P("tensor", "dp", None),
            P("tensor", None, "dp"),
        ),
        check_vma=False,
    )
```

```python
import math

import jax
import jax.numpy as jnp
import numpy as np
from jax import lax
from jax.experimental import pallas as pl
from jax.experimental.pallas import tpu as pltpu
from jax.sharding import PartitionSpec as P

HEAD = 64
LENGTH = 2048
WIDTH = 1024
UNITS = 512
ROWS = 128
PAIR = 256
CHUNK = 384
REACH = 896
SPAN = REACH + PAIR
PADDED = REACH + LENGTH
CHIPS = 8
TENSOR = 16
DP = 8
TAIL = 240
SLOTS = 2
STEP_Z = (0, 0, 1, 3, 1, 3, 2, 2)
STEP_X = (0, 1, 0, 0, 1, 1, 0, 1)
SUM_Z = (2, 2, 1, 1, 3, 3, 0, 0)
SUM_X = (1, 0, 1, 0, 1, 0, 1, 0)
LOWEST = -1e30
TP = "tensor"
SP = "dp"
BF = jnp.bfloat16
F32 = jnp.float32
MESH = pl.DeviceIdType.MESH
VMEM_BYTES = 63 * 1024 * 1024

NN = (((1,), (0,)), ((), ()))
NT = (((1,), (1,)), ((), ()))
TN = (((0,), (0,)), ((), ()))


def dot(left, right, dims=NN):
    return lax.dot_general(left, right, dims, preferred_element_type=F32)


def aligned(value, size):
    return pl.ds(pl.multiple_of(value * size, size), size)


def remote(src, dst, send, recv, axis, index):
    return pltpu.make_async_remote_copy(
        src_ref=src,
        dst_ref=dst,
        send_sem=send,
        recv_sem=recv,
        device_id={axis: index},
        device_id_type=MESH,
    )


def all_sent(ref, sem, place):
    remote(ref, ref, sem, sem, TP, place.twin).wait_send()


def all_landed(ref, sem, place):
    remote(ref, ref, sem, sem, TP, place.twin).wait_recv()


class Place:
    def __init__(self):
        self.t = lax.axis_index(TP)
        self.d = lax.axis_index(SP)
        self.core = lax.rem(self.t, 2)
        self.chip = self.t // 2
        self.twin = self.t + 1 - 2 * self.core
        self.x = lax.rem(self.d, 2)
        self.y = self.d // 2
        self.across = self.d + 1 - 2 * self.x
        self.z = self.chip // 2
        self.x_far = lax.rem(self.chip, 2)

    def chip_at(self, k):
        return lax.rem(self.chip + k, CHIPS)

    def same_core(self, k):
        return 2 * self.chip_at(k) + self.core

    def near(self, dz, dx):
        return 2 * lax.rem(self.z + dz, 4) + lax.rem(self.x_far + dx, 2)

    def near_core(self, dz, dx):
        return 2 * self.near(dz, dx) + self.core

    def listed(self, i, all_z, all_x):
        if isinstance(i, int):
            return self.near(all_z[i], all_x[i])
        dz, dx = jnp.int32(0), jnp.int32(0)
        for k in range(CHIPS):
            dz = jnp.where(i == k, all_z[k], dz)
            dx = jnp.where(i == k, all_x[k], dx)
        return self.near(dz, dx)

    def step(self, i):
        return self.listed(i, STEP_Z, STEP_X)

    def sum_step(self, i):
        return self.listed(i, SUM_Z, SUM_X)

    def step_core(self, i):
        return 2 * self.step(i) + self.core

    def tensor_at(self, k):
        return lax.rem(self.t + k, TENSOR)

    def dp_at(self, k):
        return lax.rem(self.d + k, DP)

    def y_at(self, k):
        return lax.rem(self.y + k, 4)

    def enter(self):
        barrier = pltpu.get_barrier_semaphore()
        for k in range(1, TENSOR):
            pl.semaphore_signal(
                barrier, inc=1, device_id={TP: self.tensor_at(k)}, device_id_type=MESH
            )
        for k in range(1, DP):
            pl.semaphore_signal(
                barrier, inc=1, device_id={SP: self.dp_at(k)}, device_id_type=MESH
            )
        pl.semaphore_wait(barrier, TENSOR + DP - 2)


class Spread:
    def __init__(self, place, block, send, recv, source=None):
        self.place, self.block, self.send, self.recv = place, block, send, recv
        self.source = source

    def copy(self, number, index, dest, source=None):
        src = self.block(index) if source is None else source
        return remote(
            src, self.block(index), self.send.at[number], self.recv.at[index], TP, dest
        )

    def own(self, k):
        dest = self.place.twin if k == 0 else self.place.same_core(k)
        return self.copy(k, self.place.t, dest, self.source)

    def start(self):
        for k in range(1, CHIPS):
            self.own(k).start()
        self.own(0).start()

    def passed(self, k):
        return self.copy(CHIPS + k, self.place.same_core(k), self.place.twin)

    def arrived(self, index):
        self.copy(0, index, self.place.twin).wait_recv()

    def first(self, k):
        self.arrived(self.place.same_core(k))
        self.passed(k).start()

    def second(self, k):
        self.arrived(2 * self.place.chip_at(k) + 1 - self.place.core)

    def end(self):
        for k in range(CHIPS):
            self.own(k).wait_send()
        for k in range(1, CHIPS):
            self.passed(k).wait_send()


class Ring:
    def __init__(self, place, block, half, send, recv, most, source=None, source_half=None):
        self.place, self.block, self.half = place, block, half
        self.send, self.recv, self.most = send, recv, most
        self.source, self.source_half = source, source_half

    def send_sem(self, number):
        return self.send.at[0]

    def copy(self, number, index, dest, source=None):
        src = self.block(index) if source is None else source
        return remote(
            src, self.block(index), self.send_sem(number), self.recv.at[index], TP, dest
        )

    def piece(self, number, index, part, dest, source=None):
        ref = self.half(index, part)
        place = TENSOR + index // 2 if part else index
        return remote(
            ref if source is None else source,
            ref,
            self.send_sem(number),
            self.recv.at[place],
            TP,
            dest,
        )

    def sent(self, number):
        at = self.place
        if number == 0:
            return self.copy(0, at.t, at.twin, self.source)
        if number < 4:
            return self.copy(number, at.t, at.step_core(number), self.source)
        if number < 6:
            return self.copy(number, at.step_core(1), at.step_core(number - 2))
        if number < 8:
            return self.piece(number, at.step_core(2 * number - 9), 0, at.step_core(2))
        if number < 10:
            return self.piece(number, at.step_core(2 * number - 14), 1, at.step_core(3))
        return self.copy(number, at.step_core(number - 9), at.twin)

    def start(self):
        at = self.place
        for part in range(2):
            src = None if self.source_half is None else self.source_half(part)
            self.piece(1, at.t, part, at.step_core(1), src).start()
        for number in (2, 3, 0):
            self.sent(number).start()

    def piece_arrived(self, index, part):
        self.piece(0, index, part, self.place.twin).wait_recv()

    def pass_on(self, i):
        at = self.place
        index = at.step_core(i)
        if i in (2, 3):
            self.copy(0, index, at.twin).wait_recv()
            self.sent(8 if i == 2 else 6).start()
        elif i == 1:
            for part in range(2):
                self.piece_arrived(index, part)
                self.piece(4, index, part, at.step_core(2)).start()
                self.piece(5, index, part, at.step_core(3)).start()
        elif i == 4:
            self.piece_arrived(index, 1)
            self.sent(9).start()
            self.piece_arrived(index, 0)
        elif i == 5:
            self.piece_arrived(index, 0)
            self.sent(7).start()
            self.piece_arrived(index, 1)
        else:
            self.piece_arrived(index, 0)
            self.piece_arrived(index, 1)
        self.sent(9 + i).start()

    def pass_on_at(self, i):
        for k in range(1, CHIPS):

            @pl.when(i == k - 1)
            def _(k=k):
                self.pass_on(k)

    def second(self, i):
        self.copy(0, 2 * self.place.step(i) + 1 - self.place.core, self.place.twin).wait_recv()

    def end(self):
        all_sent(self.most, self.send.at[0], self.place)


def whole_ring(place, ref, send, recv, source=None):
    return Ring(
        place,
        lambda b: ref.at[aligned(b, ROWS)],
        lambda b, part: ref.at[pl.ds(pl.multiple_of(b * ROWS + part * HEAD, HEAD), HEAD)],
        send,
        recv,
        ref.at[pl.ds(0, 15 * ROWS)],
        source,
        None if source is None else lambda part: source.at[pl.ds(part * HEAD, HEAD)],
    )


class Copies:
    def __init__(self, sems):
        self.sems, self.pending, self.used = sems, [], 0

    def start(self, src, dst):
        copy = pltpu.make_async_copy(src, dst, self.sems.at[self.used])
        copy.start()
        self.used += 1
        self.pending.append(copy)
        return copy

    def wait(self, count=None):
        count = len(self.pending) if count is None else count
        for copy in self.pending[:count]:
            copy.wait()
        self.pending = self.pending[count:]

    def need(self, *copies):
        for copy in copies:
            copy.wait()
            self.pending = [other for other in self.pending if other is not copy]


def lanes(shape):
    return lax.broadcasted_iota(jnp.int32, shape, len(shape) - 1)


def sublanes(shape):
    return lax.broadcasted_iota(jnp.int32, shape, 0)


def swapped(values):
    return jnp.where(
        lanes(values.shape) < HEAD // 2,
        pltpu.roll(values, 2 * HEAD - HEAD // 2, 1),
        pltpu.roll(values, HEAD // 2, 1),
    )


def document_starts(seg):
    starts = jnp.zeros(seg.shape, F32)
    for document in range(8):
        before = jnp.sum(jnp.where(seg < document, 1.0, 0.0), axis=1, keepdims=True)
        starts = starts + jnp.where(seg == document, before, 0.0)
    return starts


def key_codes(mask, code):
    code[0:REACH, :] = jnp.full((REACH, ROWS), -1.0, F32)

    @pl.loop(0, TENSOR)
    def _(i):
        row = mask[:, aligned(i, ROWS)].astype(F32)
        live = jnp.broadcast_to(row, (ROWS, ROWS)).T == 1.0
        places = (sublanes((ROWS, ROWS)) + i * ROWS).astype(F32)
        code[pl.ds(pl.multiple_of(REACH + i * ROWS, ROWS), ROWS), :] = jnp.where(
            live, places, -1.0
        )


def allowed(code, start_row, chunk):
    ok = jnp.concatenate([code, code], axis=1) >= start_row
    if (chunk + 1) * CHUNK > REACH:
        key = sublanes((CHUNK, PAIR)) + (chunk * CHUNK - REACH)
        query = lanes((CHUNK, PAIR))
        ok = (ok & (key < query)) | (key == query)
    return ok


def turned_back(grad, r, here):
    cos, sin = r.cosine_t[:, here], r.sine_t[:, here]
    first, second = grad[0 : HEAD // 2], grad[HEAD // 2 : HEAD]
    return jnp.concatenate([first * cos + second * sin, second * cos - first * sin], axis=0)


class Halves:
    def __init__(self, place, parts, twins, sums, send, recv, credit):
        self.place, self.parts, self.twins, self.sums = place, parts, twins, sums
        self.send, self.recv, self.credit = send, recv, credit

    def half(self, k):
        at, slot = self.place, lax.rem(k, SLOTS)
        return remote(
            self.parts.at[slot, aligned(1 - at.core, ROWS), :],
            self.twins.at[slot],
            self.send.at[slot],
            self.recv.at[slot],
            TP,
            at.twin,
        )

    def put(self, k, value):
        @pl.when(k >= SLOTS)
        def _():
            self.half(k - SLOTS).wait_send()
            pl.semaphore_wait(self.credit, 1)

        self.parts[lax.rem(k, SLOTS)] = value.astype(BF)
        self.half(k).start()

    def add(self, k):
        slot = lax.rem(k, SLOTS)
        self.half(k).wait_recv()
        own = self.parts[slot, aligned(self.place.core, ROWS), :].astype(F32)
        self.sums(k)[...] = (own + self.twins[slot].astype(F32)).astype(BF)

        @pl.when(k < CHIPS - SLOTS)
        def _():
            pl.semaphore_signal(
                self.credit, inc=1, device_id={TP: self.place.twin}, device_id_type=MESH
            )

    def end(self):
        for k in range(CHIPS - SLOTS, CHIPS):
            self.half(k).wait_send()


class Joined:
    def __init__(self, place, sums, crossed, landed, sems):
        self.place, self.sums, self.crossed, self.landed = place, sums, crossed, landed
        self.c_send, self.c_recv, self.send, self.recv = sems

    def cross(self, j):
        return remote(
            self.sums.at[2 * j],
            self.crossed.at[j],
            self.c_send.at[j],
            self.c_recv.at[j],
            TP,
            self.place.near_core(0, 1),
        )

    def whole(self, j):
        return remote(
            self.sums.at[2 * j + 1],
            self.landed.at[j],
            self.send.at[j],
            self.recv.at[j],
            TP,
            self.place.near_core(SUM_Z[2 * j], 0),
        )

    def join(self, j):
        self.cross(j).wait_recv()
        total = self.sums[2 * j + 1].astype(F32) + self.crossed[j].astype(F32)
        self.sums[2 * j + 1] = total.astype(BF)
        self.whole(j).start()

    def result(self):
        self.cross(3).wait_recv()
        total = self.sums[7].astype(F32) + self.crossed[3].astype(F32)
        for j in range(3):
            self.whole(j).wait_recv()
            total = total + self.landed[j].astype(F32)
        return total

    def end(self):
        for j in range(4):
            self.cross(j).wait_send()
        for j in range(3):
            self.whole(j).wait_send()


def unpacked(both):
    return both[:, 0:8].reshape(ROWS, WIDTH), both[:, 8:16].reshape(ROWS, WIDTH)


def aligned_rows(ref, unit):
    def block(src, part=None):
        if part is None:
            return ref.at[pl.ds(pl.multiple_of(src * 2 * unit, unit), 2 * unit), :]
        return ref.at[pl.ds(pl.multiple_of((src * 2 + part) * unit, unit), unit), :]

    return block


def column_blocks(ref):
    def block(src, part=None):
        if part is None:
            return ref.at[:, aligned(src, ROWS)]
        return ref.at[pl.ds(part * PAIR, PAIR), aligned(src, ROWS)]

    return block


class Stream:
    def __init__(self, place, own, block, most, r, number):
        self.place, self.own, self.block, self.most = place, own, block, most
        self.send, self.recv = r.e_send, r.e_recv
        self.number, self.first_recv = number, 10 * number

    def at_y(self, k, other=False):
        at = self.place
        column = 1 - at.x if other else at.x
        return 2 * at.y_at(k) + column

    def copy(self, number, src, dest, part=None, source=None):
        ref = self.block(src, part)
        return remote(
            ref if source is None else source,
            ref,
            self.send.at[self.number],
            self.recv.at[self.first_recv + (8 + lax.rem(src, 2) if part else src)],
            SP,
            dest,
        )

    def sent(self, number):
        at, at_y = self.place, self.at_y
        if number == 0:
            return self.copy(0, at.d, at.across, source=self.own)
        if number < 3:
            return self.copy(number, at.d, at_y(2 * number - 1), source=self.own)
        if number < 5:
            return self.copy(number, at.across, at_y(2 * number - 5))
        other = number > 6
        if number % 2:
            return self.copy(number, at_y(3, other), at_y(1), 0)
        return self.copy(number, at_y(1, other), at_y(3), 1)

    def arrived(self, src, halves=False):
        for part in (0, 1) if halves else (None,):
            self.copy(0, src, self.place.across, part).wait_recv()

    def start_x(self):
        self.sent(0).start()

    def start_y(self):
        self.sent(1).start()
        self.sent(2).start()

    def from_across(self):
        self.arrived(self.place.across)
        self.sent(3).start()
        self.sent(4).start()

    def from_y(self):
        self.arrived(self.at_y(3))
        self.sent(5).start()
        self.arrived(self.at_y(1))
        self.sent(6).start()

    def from_y_across(self):
        self.arrived(self.at_y(3, True))
        self.sent(7).start()
        self.arrived(self.at_y(1, True))
        self.sent(8).start()

    def finish(self):
        self.arrived(self.at_y(2), True)
        self.arrived(self.at_y(2, True), True)

    def end(self):
        all_sent(self.most, self.send.at[self.number], self.place)


def expert_streams(at, r, e):
    downs = r.downs.at[pl.ds(e * UNITS, UNITS)]
    return (
        Stream(
            at,
            r.gu.at[e],
            aligned_rows(r.gus.at[e], HEAD),
            r.gus.at[e, pl.ds(0, 7 * ROWS)],
            r,
            2 * e,
        ),
        Stream(
            at,
            r.down.at[e],
            column_blocks(downs),
            downs.at[:, pl.ds(0, 7 * ROWS)],
            r,
            2 * e + 1,
        ),
    )


def layer_kernel(r):
    at = Place()
    t, d = at.t, at.d
    copies = Copies(r.local)
    r.load()
    r.hidden_all[aligned(t, ROWS), :] = r.hid[...]
    keyval, out_rows = r.w_keyval[...].astype(F32), r.w_out_t[...].astype(F32)
    r.rows[...] = jnp.concatenate([keyval, out_rows], axis=0).astype(BF)
    r.row_dp[d] = r.rows[...]
    r.shares[...] = jnp.zeros((8, ROWS), F32)
    r.shares[:, 0:32] = r.router[...].astype(F32)
    same = sublanes((8, 8)) == lanes((8, 8))
    for column, gain in ((32, r.gain_one), (33, r.gain_two)):
        wide = jnp.broadcast_to(gain[...].astype(F32), (8, 8))
        r.shares[:, column : column + 1] = jnp.sum(
            jnp.where(same, wide, 0.0), axis=1, keepdims=True
        )
    for j in range(CHIPS):
        tile = jnp.concatenate([keyval[:, j * ROWS : (j + 1) * ROWS], r.shares[...]], axis=0)
        r.tiles[2 * j] = tile.astype(BF)
        r.tiles[2 * j + 1] = tile.astype(BF)
    r.tile_all[d, t] = r.tiles[t]
    r.wq_all[HEAD : 2 * HEAD, :] = jnp.zeros((HEAD, WIDTH), BF)
    r.wq_all[0:HEAD, aligned(d, ROWS)] = r.w_query_t[...]
    at.enter()

    def tile_one(k, src):
        dest = at.tensor_at(k)
        return remote(
            r.tiles.at[dest],
            r.tile_all.at[d, src],
            r.t1_send.at[0],
            r.t1_recv.at[0],
            TP,
            dest,
        )

    def tile_two(k, src):
        ref = r.tile_all.at[src]
        return remote(ref, ref, r.t2_send.at[0], r.t2_recv.at[0], SP, at.dp_at(k))

    def rows_dp(k, src):
        return remote(
            r.rows, r.row_dp.at[src], r.rd_send.at[0], r.rd_recv.at[0], SP, at.dp_at(k)
        )

    def wq_dp(k, src):
        return remote(
            r.w_query_t,
            r.wq_all.at[pl.ds(0, HEAD), aligned(src, ROWS)],
            r.wq_send.at[0],
            r.wq_recv.at[0],
            SP,
            at.dp_at(k),
        )

    first_expert, second_expert = expert_streams(at, r, 0), expert_streams(at, r, 1)

    for k in range(1, TENSOR):
        tile_one(k, t).start()
    for k in range(1, DP):
        wq_dp(k, d).start()
    ring_h = whole_ring(at, r.hidden_all, r.h_send, r.h_recv)
    ring_h.start()
    for e in range(2):
        copies.start(r.gu.at[e], r.gus.at[e, aligned(d, ROWS)])
        copies.start(r.down.at[e], r.downs.at[pl.ds(e * UNITS, UNITS), aligned(d, ROWS)])
    copies.start(r.cot, r.cots.at[aligned(t, ROWS)])

    key_codes(r.mask, r.code)
    r.starts[...] = document_starts(r.seg[...])
    r.keyvals[0:REACH, :] = jnp.zeros((REACH, 2 * HEAD), BF)
    r.keyvals_t[:, 0:REACH] = jnp.zeros((2 * HEAD, REACH), BF)

    all_landed(r.tile_all.at[0, pl.ds(0, 15)], r.t1_recv.at[0], at)
    for k in range(1, DP):
        tile_two(k, d).start()
    for k in range(1, DP):
        rows_dp(k, d).start()
    for stream in first_expert:
        stream.start_x()
        stream.start_y()
    for i in range(1, 4):
        ring_h.pass_on(i)
    seven_wq = r.wq_all.at[pl.ds(0, HEAD), pl.ds(0, 7 * ROWS)]
    all_landed(seven_wq, r.wq_recv.at[0], at)
    all_landed(r.tile_all.at[pl.ds(0, 7)], r.t2_recv.at[0], at)
    for j in range(DP):
        both = r.tile_all[j].astype(F32)
        r.wqk[j * ROWS : (j + 1) * ROWS, ROWS:PAIR] = both[:, 0:8].reshape(ROWS, ROWS).astype(BF)
        r.small[j * ROWS : (j + 1) * ROWS, :] = both[:, 8:16].reshape(ROWS, ROWS).astype(BF)
    r.wqk[:, 0:ROWS] = r.wq_all[...].astype(F32).T.astype(BF)
    columns = r.small[...].astype(F32).T
    gain_one = columns[32:33, :]
    gain_two = columns[33:34, :]
    r.need("turns")
    ring_o = Ring(
        at,
        lambda b: r.out_all.at[b // 2, aligned(lax.rem(b, 2), HEAD)],
        lambda b, part: r.out_all.at[b // 2, aligned(2 * lax.rem(b, 2) + part, 32)],
        r.o_send,
        r.o_recv,
        r.nm_all.at[pl.ds(0, 15 * HEAD)],
    )

    ring_c = whole_ring(at, r.cots, r.c_send, r.c_recv, r.cot)
    @pl.loop(0, CHIPS)
    def _(i):
        @pl.when(i == 1)
        def _():
            ring_h.pass_on(4)
            ring_h.pass_on(5)

        @pl.when(i == 2)
        def _():
            all_landed(r.row_dp.at[pl.ds(0, 7)], r.rd_recv.at[0], at)
            both = r.row_dp[...].astype(F32)
            r.wqkv_own[0:HEAD, :] = r.wq_all[0:HEAD, :]
            r.wqkv_own[HEAD : 2 * HEAD, :] = both[:, 0:8].reshape(HEAD, WIDTH).astype(BF)
            r.out_all[at.chip, aligned(at.core, HEAD), :] = (
                both[:, 8:16].reshape(HEAD, WIDTH).astype(BF)
            )
            ring_o.start()

        @pl.when(i == 4)
        def _():
            ring_c.start()

        @pl.when(i == 5)
        def _():
            ring_h.pass_on(6)
            ring_h.pass_on(7)

        ring_h.second(i)
        block = at.step(i)
        here = aligned(block, PAIR)
        hidden = r.hidden_all[here, :].astype(F32)
        inverse = lax.rsqrt(jnp.mean(hidden * hidden, axis=1, keepdims=True) + 1e-6)
        unit = (hidden * inverse * gain_one).astype(BF)
        r.normed[here, :] = unit
        table = r.turns[here, :]
        turned = lanes(table.shape) < HEAD
        cos = jnp.where(turned, table, 1.0)
        sin = jnp.where(turned, pltpu.roll(table, HEAD, 1), 0.0)
        projected = dot(unit, r.wqk[...])
        query, keyval = projected[:, 0:ROWS], projected[:, ROWS:PAIR]
        query = (query * cos + swapped(query) * sin).astype(BF)
        r.queries[here, :] = (query.astype(F32) * (1.0 / math.sqrt(HEAD))).astype(BF)
        keyval = keyval * cos + swapped(keyval) * sin
        later = pl.ds(pl.multiple_of(REACH + block * PAIR, ROWS), PAIR)
        r.keyvals[later, :] = keyval.astype(BF)
        r.keyvals_t[:, later] = keyval.T.astype(BF)

    r.save("normed")
    ring_o.pass_on(1)

    def att_copy(dest, src):
        return remote(
            r.att_src.at[dest],
            r.att_t.at[aligned(src, HEAD), :],
            r.a_send.at[0],
            r.a_recv.at[0],
            TP,
            dest,
        )

    @pl.loop(0, CHIPS)
    def _(i):
        for step, ring, chips in (
            (0, ring_o, (2, 3)),
            (4, ring_o, (4, 5)),
        ):

            @pl.when(i == step)
            def _(ring=ring, chips=chips):
                for k in chips:
                    ring.pass_on(k)

        @pl.when(i == 2)
        def _():
            for stream in first_expert:
                stream.from_across()
            for stream in first_expert:
                stream.from_y()

        block = at.chip_at(i + 1)
        here = aligned(block, PAIR)
        query = r.queries[here, :]
        start_row = r.starts[:, here]
        top = jnp.full((1, PAIR), LOWEST, F32)
        for chunk in range(SPAN // CHUNK):
            keys = pl.ds(pl.multiple_of(block * PAIR + chunk * CHUNK, ROWS), CHUNK)
            score = dot(r.keyvals[keys, :], query, NT)
            score = jnp.where(allowed(r.code[keys, :], start_row, chunk), score, LOWEST)
            r.scores[chunk * CHUNK : (chunk + 1) * CHUNK, :] = score
            top = jnp.maximum(top, jnp.max(score, axis=0, keepdims=True))
        total = jnp.zeros((1, PAIR), F32)
        for chunk in range(SPAN // CHUNK):
            place = slice(chunk * CHUNK, (chunk + 1) * CHUNK)
            weight = jnp.exp(r.scores[place, :] - top)
            total = total + jnp.sum(weight, axis=0, keepdims=True)
            r.weighted[place, 0:PAIR] = weight.astype(BF)
        window = pl.ds(pl.multiple_of(block * PAIR, ROWS), SPAN)
        head = dot(r.keyvals_t[HEAD : 2 * HEAD, window], r.weighted[0:SPAN, 0:PAIR]) / total
        r.heads_t[:, here] = head
        r.stats[:, here] = top + jnp.log(total)
        r.att_src[2 * block] = head[:, 0:ROWS].astype(BF)
        r.att_src[2 * block + 1] = head[:, ROWS:PAIR].astype(BF)

        @pl.when(i < CHIPS - 1)
        def _():
            att_copy(2 * block, t).start()
            att_copy(2 * block + 1, t).start()

        @pl.when(i == CHIPS - 1)
        def _():
            att_copy(at.twin, t).start()

    ring_c.pass_on(1)
    for stream in second_expert:
        stream.start_x()
    r.att_t[aligned(t, HEAD), :] = r.att_src[t]
    ring_o.pass_on(6)
    ring_o.pass_on(7)
    for i in range(CHIPS):
        ring_o.second(i)

    @pl.loop(0, 4)
    def _(j):
        sides = [
            r.out_all[:, pl.ds(pl.multiple_of(core * HEAD + j * 16, 16), 16), :].astype(F32)
            for core in range(2)
        ]
        first, second = unpacked(jnp.stack(sides, axis=1).reshape(TENSOR, 16, WIDTH))
        r.out_t[aligned(2 * j, ROWS), :] = first.astype(BF)
        r.out_t[aligned(2 * j + 1, ROWS), :] = second.astype(BF)

    r.save("out_t")
    for stream in first_expert:
        stream.from_y_across()
    all_landed(r.att_t.at[pl.ds(0, 15 * HEAD)], r.a_recv.at[0], at)
    attended = r.att_t[...].astype(F32).T.astype(BF)
    r.att_rows[...] = attended
    middle = r.hid[...].astype(F32) + dot(attended, r.out_t[...], NT)
    r.mid[...] = middle
    inverse = lax.rsqrt(jnp.mean(middle * middle, axis=1, keepdims=True) + 1e-6)
    r.nm_all[aligned(t, ROWS), :] = (middle * inverse * gain_two).astype(BF)
    ring = whole_ring(at, r.nm_all, r.g_send, r.g_recv)
    ring.start()
    for stream in second_expert:
        stream.start_y()
    ring_c.pass_on(2)
    ring_c.pass_on(3)
    for stream in first_expert:
        stream.finish()
    copies.wait()
    ring_h.end()
    ring_o.end()
    r.finish("normed")
    r.finish("out_t")
    r.proj_grads, r.n_first, r.gates, r.n_sums = r.hidden_all, r.normed, r.turns, r.out_all
    r.m_sums = r.out_t


    def moe_sums(k, count=1):
        return r.m_sums.at[pl.ds(pl.multiple_of(k * ROWS, ROWS), count * ROWS)]

    halves_n = Halves(at, r.n_parts, r.n_twins, lambda k: r.n_sums.at[k], r.ntw_send, r.ntw_recv, r.n_credit)
    halves_m = Halves(at, r.m_parts, r.m_twins, moe_sums, r.mtw_send, r.mtw_recv, r.m_credit)
    joined = Joined(
        at,
        r.n_sums,
        r.n_crossed,
        r.n_landed,
        (r.nc_send, r.nc_recv, r.n_send, r.n_recv),
    )
    ring_w = whole_ring(at, r.wqkv, r.h_send, r.h_recv, r.wqkv_own)
    copies.start(r.wqkv_own, r.wqkv.at[aligned(t, ROWS)])

    def moe_along(j):
        return remote(
            moe_sums(2 * j, 2),
            r.m_landed.at[j],
            r.m_send.at[j],
            r.m_recv.at[j],
            TP,
            at.near_core(SUM_Z[2 * j], 0),
        )

    def gu_over_y(e, k):
        y = at.y_at(k)
        return remote(
            r.gus.at[e, aligned(y, PAIR), :],
            r.y_gu.at[e, k - 1],
            r.x_send.at[4 * e + k],
            r.x_recv.at[4 * e + k],
            SP,
            2 * y + at.x,
        )

    def down_over_y(e, k):
        y = at.y_at(k)
        return remote(
            r.down_grads.at[e, :, aligned(y, PAIR)],
            r.y_down.at[e, k - 1],
            r.y_send.at[4 * e + k],
            r.y_recv.at[4 * e + k],
            SP,
            2 * y + at.x,
        )

    def across_x(number, src, dst):
        return remote(src, dst, r.tx_send.at[number], r.tx_recv.at[number], SP, at.across)

    def gu_across(e):
        return across_x(e, r.ys_gu.at[e, 1 - at.x], r.yx_gu.at[e])

    def down_across(e):
        return across_x(2 + e, r.ys_down.at[e, 1 - at.x], r.yx_down.at[e])

    def gate_copy(dest, src):
        return remote(
            r.gate_src.at[dest],
            r.gate_all.at[src],
            r.gg_send.at[0],
            r.gg_recv.at[0],
            TP,
            dest,
        )

    def one_pass(e):
        @pl.loop(0, CHIPS)
        def _(i):
            if e == 0:
                for k in range(2, CHIPS):

                    @pl.when(i == k - 1)
                    def _(k=k):
                        ring.pass_on(k)

                ring.second(i)

                @pl.when(i == 1)
                def _():
                    ring_c.pass_on(4)
                    ring_c.pass_on(5)

                @pl.when(i == 2)
                def _():
                    for stream in second_expert:
                        stream.from_across()

                @pl.when(i == 4)
                def _():
                    for stream in second_expert:
                        stream.from_y()

                @pl.when(i == 5)
                def _():
                    ring_c.pass_on(6)
                    ring_c.pass_on(7)

                ring_c.second(i)

                @pl.when(i == 6)
                def _():
                    ring_w.start()

            here = aligned(at.step(i) if e == 0 else at.sum_step(i), PAIR)
            nm = r.nm_all[here, :]
            place = lanes((PAIR, ROWS))
            if e == 0:
                expert = sublanes((ROWS, PAIR))
                named = expert == r.routes_t[0:1, here]
                for j in range(1, 8):
                    named = named | (expert == r.routes_t[j : j + 1, here])
                named = jnp.where(named, 1.0, 0.0).T > 0.5
                logits = jnp.where(named, dot(nm, r.small[...]), LOWEST)
                powers = jnp.exp(logits - jnp.max(logits, axis=1, keepdims=True))
                powers = jnp.where(named, powers, 0.0)
                gates = powers / jnp.sum(powers, axis=1, keepdims=True)
            else:
                kept = r.gates[here, :]
                gates = jnp.where(place == 2 * HEAD - 1, 0.0, kept)
                earlier = kept[:, 2 * HEAD - 1 : 2 * HEAD]
            mine = place == 2 * t + e
            gate = jnp.sum(jnp.where(mine, gates, 0.0), axis=1, keepdims=True)
            act_grad = dot(r.cots[here, :], r.downs[e * UNITS : (e + 1) * UNITS, :], NT)
            projected = dot(nm, r.gus[e])
            first, up = projected[:, :UNITS], projected[:, UNITS:]
            sigmoid = 1.0 / (1.0 + jnp.exp(-first))
            silu = first * sigmoid
            activated = silu * up
            gate_grad = jnp.sum(activated * act_grad, axis=1, keepdims=True)
            weighted = (activated * gate).astype(BF)
            r.weighted_t[:, here] = weighted.T
            act_grad = act_grad * gate
            r.proj_grads[here, 0:UNITS] = (
                act_grad * up * (sigmoid * (1.0 + first * (1.0 - sigmoid)))
            ).astype(BF)
            r.proj_grads[here, UNITS:WIDTH] = (act_grad * silu).astype(BF)
            normed_part = dot(r.proj_grads[here, :], r.gus[e], NT)
            if e == 0:
                r.gates[here, :] = jnp.where(place == 2 * HEAD - 1, gate_grad, gates)
                r.weighted[here, :] = weighted
                r.n_first[here, :] = normed_part.astype(BF)

                @pl.when(i == 0)
                def _():
                    ring.pass_on(1)

                return
            row = 2 * lax.rem(t, 4)
            gate_grads = jnp.where(
                place == row, earlier, jnp.where(place == row + 1, gate_grad, 0.0)
            ).T
            chip = at.sum_step(i)
            r.gate_src[2 * chip] = gate_grads[0:8, 0:ROWS]
            r.gate_src[2 * chip + 1] = gate_grads[0:8, ROWS:PAIR]

            @pl.when(i < CHIPS - 1)
            def _():
                gate_copy(2 * chip, t).start()
                gate_copy(2 * chip + 1, t).start()

            @pl.when(i == CHIPS - 1)
            def _():
                gate_copy(at.twin, t).start()

            halves_n.put(i, normed_part + r.n_first[here, :].astype(F32))
            both = jnp.concatenate([r.weighted[here, :], weighted], axis=1)
            halves_m.put(i, dot(both, r.downs[...]))

            @pl.when(i > 0)
            def _():
                halves_n.add(i - 1)
                halves_m.add(i - 1)

            for j in range(4):

                @pl.when(i == 2 * j + 1)
                def _(j=j):
                    joined.cross(j).start()

            for j in range(2):

                @pl.when(i == 2 * j + 4)
                def _(j=j):
                    joined.join(j)

            @pl.when(i == 2)
            def _():
                moe_along(0).start()

            for step, chips in ((0, (2, 3)), (2, (4, 5))):

                @pl.when(i == step)
                def _(chips=chips):
                    for k in chips:
                        ring_w.pass_on(k)

    def down_gradients(e):
        @pl.loop(0, 2)
        def _(j):
            strip = aligned(j, PAIR)
            r.down_grads[e, strip, :] = dot(r.weighted_t[strip, :], r.cots[...]).astype(BF)

    def gate_up_gradients(e):
        @pl.loop(0, 4)
        def _(j):
            strip = aligned(j, PAIR)
            r.gus[e, strip, :] = dot(r.nm_all[:, strip], r.proj_grads[...], TN).astype(BF)

    one_pass(0)
    for stream in second_expert:
        stream.from_y_across()
    for stream in first_expert:
        stream.end()
    down_gradients(0)
    for k in range(1, 4):
        down_over_y(0, k).start()
    gate_up_gradients(0)
    ring_w.pass_on(1)
    for k in range(1, 4):
        gu_over_y(0, k).start()
    for stream in second_expert:
        stream.finish()
    one_pass(1)
    joined.join(2)
    halves_n.add(CHIPS - 1)
    halves_m.add(CHIPS - 1)
    out_rows = r.n_first.at[pl.ds(0, WIDTH)]
    copies.start(r.out_t_d, out_rows)
    for stream in second_expert:
        stream.end()
    down_gradients(1)
    for k in range(1, 4):
        down_over_y(1, k).start()
    gate_up_gradients(1)
    for k in range(1, 4):
        gu_over_y(1, k).start()
    r.gate_all[t] = r.gate_src[t]
    all_landed(r.gate_all.at[pl.ds(0, 15)], r.gg_recv.at[0], at)
    groups = r.gate_all[...].reshape(4, 4, 8, ROWS)
    gate_grads = (groups[:, 0] + groups[:, 1] + groups[:, 2] + groups[:, 3]).reshape(32, ROWS)
    gate_grads = jnp.concatenate([gate_grads, jnp.zeros((ROWS - 32, ROWS), F32)], axis=0).T
    own_rows = aligned(t, ROWS)
    gates = jnp.where(lanes((ROWS, ROWS)) < 32, r.gates[own_rows, :], 0.0)
    mean = jnp.sum(gates * gate_grads, axis=1, keepdims=True)
    logit_grad = gates * (gate_grads - mean)
    r.router_t[...] = dot(logit_grad.T.astype(BF), r.nm_all[own_rows, :])[0:32, :]
    by_router = dot(logit_grad.astype(BF), r.small[...], NT)

    gain_two = r.small[...].astype(F32).T[33:34, :]
    normed_grad = joined.result() + by_router
    middle = r.mid[...]
    inverse = lax.rsqrt(jnp.mean(middle * middle, axis=1, keepdims=True) + 1e-6)
    unit = middle * inverse
    r.gain_grad[...] = jnp.sum(normed_grad * unit, axis=0, keepdims=True)
    scaled = normed_grad * gain_two
    grad = r.cots[aligned(t, ROWS), :].astype(F32) + inverse * (
        scaled - unit * jnp.mean(scaled * unit, axis=1, keepdims=True)
    )
    r.mid_grad[...] = grad
    turned = grad.T.reshape(DP, TENSOR, 8, ROWS).transpose(1, 0, 2, 3)
    r.att_grad_t, r.mid_t = r.att_t, r.wqk.at[:, pl.ds(0, ROWS)]
    r.mid_t[...] = turned.reshape(WIDTH, ROWS).astype(BF)
    copies.wait()
    r.att_grad_t[...] = dot(grad.astype(BF), out_rows[...]).T.astype(BF)

    def back_copy(k, src):
        dest = at.tensor_at(k)
        return remote(
            r.att_grad_t.at[aligned(dest, HEAD), :],
            r.grads.at[:, aligned(src, ROWS)],
            r.b_send.at[0],
            r.b_recv.at[0],
            TP,
            dest,
        )

    for k in range(1, TENSOR):
        back_copy(k, t).start()
    own_grads = copies.start(
        r.att_grad_t.at[aligned(t, HEAD), :], r.grads.at[:, aligned(t, ROWS)]
    )
    moe_along(1).start()
    moe_along(2).start()
    normed_load = copies.start(r.normed_d, r.normed)
    for number in (6, 7):
        ring_w.pass_on(number)
    for i in range(CHIPS):
        ring_w.second(i)
    ring_c.end()
    weights_load = copies.start(r.wqkv, r.cots)
    joined.end()
    r.n_sums[...] = (
        dot(r.mid_t[...], r.att_rows[...]).reshape(CHIPS, ROWS, WIDTH).astype(BF)
    )

    def out_half():
        return remote(
            r.n_sums.at[:, aligned(1 - at.core, HEAD), :],
            r.out_twins,
            r.ot_send.at[0],
            r.ot_recv.at[0],
            TP,
            at.twin,
        )

    out_half().start()
    r.kv_sum, r.query_src = r.gates, r.att_src
    r.tail_left, r.grads_t = r.weighted_t.at[pl.ds(PAIR, 3 * HEAD)], r.weighted_t
    r.kv_sum[...] = jnp.zeros((LENGTH, 2 * HEAD), F32)
    r.grads_t[0:HEAD, :] = jnp.zeros((HEAD, LENGTH), BF)
    all_sent(r.att_src.at[pl.ds(0, 15)], r.a_send.at[0], at)
    halves_n.end()
    halves_m.end()
    r.tail = r.n_parts.at[0]
    r.s_gu, r.m_joined = r.m_parts.at[0, pl.ds(0, ROWS)], r.m_parts.at[0, pl.ds(ROWS, ROWS)]

    def gu_sums(e):
        places = [r.proj_grads.at[pl.ds((3 * e + k) * PAIR, PAIR)] for k in range(3)]
        loads = []
        for k in range(3):
            gu_over_y(e, k + 1).wait_recv()
            loads.append(copies.start(r.y_gu.at[e, k], places[k]))
        copies.need(*loads)
        total = r.gus[e, aligned(at.y, PAIR), :].astype(F32)
        for place in places:
            total = total + place[...].astype(F32)
        r.ys_gu[e, 0] = total[0:ROWS].astype(BF)
        r.ys_gu[e, 1] = total[ROWS:PAIR].astype(BF)
        gu_across(e).start()

    def down_sums(e):
        places = [
            r.weighted.at[pl.ds(k * UNITS, UNITS), pl.ds(e * PAIR, PAIR)] for k in range(3)
        ]
        loads = []
        for k in range(3):
            down_over_y(e, k + 1).wait_recv()
            loads.append(copies.start(r.y_down.at[e, k], places[k]))
        copies.need(*loads)
        total = r.down_grads[e, :, aligned(at.y, PAIR)].astype(F32)
        for place in places:
            total = total + place[...].astype(F32)
        r.ys_down[e, 0] = total[:, 0:ROWS].astype(BF)
        r.ys_down[e, 1] = total[:, ROWS:PAIR].astype(BF)
        down_across(e).start()

    down_sums(0)
    gu_sums(0)

    def out_along(k):
        return remote(
            r.out_twins.at[pl.ds(2 * lax.rem(at.z + k, 4), 2)],
            r.out_landed.at[k - 1],
            r.oz_send.at[k],
            r.oz_recv.at[k],
            TP,
            at.near_core(k, 0),
        )

    def out_across():
        return remote(
            r.out_joined, r.out_crossed, r.oz_send.at[0], r.oz_recv.at[0], TP, at.near_core(0, 1)
        )

    out_half().wait_recv()
    r.out_twins[...] = (
        r.n_sums[:, aligned(at.core, HEAD), :].astype(F32) + r.out_twins[...].astype(F32)
    ).astype(BF)
    out_along(1).start()
    all_landed(r.grads.at[:, pl.ds(0, 15 * ROWS)], r.b_recv.at[0], at)
    copies.need(own_grads)
    copies.need(copies.start(r.grads, r.grads_t.at[pl.ds(HEAD, HEAD)]))
    r.need("cosine_t", "sine_t")

    def query_copy(dest, src):
        return remote(
            r.query_src.at[dest],
            r.query_all.at[src],
            r.qb_send.at[0],
            r.qb_recv.at[0],
            TP,
            dest,
        )

    @pl.loop(0, CHIPS)
    def _(i):
        block = at.chip_at(i + 1)
        here = aligned(block, PAIR)
        query = r.queries[here, :]
        start_row = r.starts[:, here]
        stat = r.stats[:, here]
        grad_t = r.grads_t[0 : 2 * HEAD, here]
        grad_rows = grad_t.astype(F32).T.astype(BF)
        head = r.heads_t[:, here]
        delta = jnp.sum(head * grad_t[HEAD : 2 * HEAD, :].astype(F32), axis=0, keepdims=True)
        query_grad = jnp.zeros((HEAD, PAIR), F32)
        for chunk in range(SPAN // CHUNK):
            keys = pl.ds(pl.multiple_of(block * PAIR + chunk * CHUNK, ROWS), CHUNK)
            both = r.keyvals[keys, :]
            score = dot(both, query, NT)
            ok = allowed(r.code[keys, :], start_row, chunk)
            prob = jnp.exp(jnp.where(ok, score - stat, LOWEST))
            prob_grad = dot(both, grad_t)
            score_grad = (prob * (prob_grad - delta)).astype(BF)
            update = dot(score_grad, query) + dot(prob.astype(BF), grad_rows)
            for part in range(CHUNK // ROWS):
                row = jnp.maximum(block * PAIR + (chunk * CHUNK + part * ROWS - REACH), 0)
                place = pl.ds(pl.multiple_of(row, ROWS), ROWS)
                r.kv_sum[place, :] += update[part * ROWS : (part + 1) * ROWS]

            query_grad = query_grad + dot(r.keyvals_t[0:HEAD, keys], score_grad)
        turned = turned_back(query_grad * (1.0 / math.sqrt(HEAD)), r, here).astype(BF)
        r.tail_left[0:HEAD, here] = turned
        r.query_src[2 * block] = turned[:, 0:ROWS]
        r.query_src[2 * block + 1] = turned[:, ROWS:PAIR]

        @pl.when(i < CHIPS - 1)
        def _():
            query_copy(2 * block, t).start()
            query_copy(2 * block + 1, t).start()

        @pl.when(i == CHIPS - 1)
        def _():
            query_copy(at.twin, t).start()

    @pl.loop(0, CHIPS)
    def _(i):
        here = aligned(i, PAIR)
        grad = r.kv_sum[here, :].T
        grad = jnp.concatenate(
            [turned_back(grad[0:HEAD], r, here), grad[HEAD : 2 * HEAD]], axis=0
        ).astype(BF)
        r.tail_left[HEAD : 3 * HEAD, here] = grad
        r.back_src[2 * i] = grad[:, 0:ROWS]
        r.back_src[2 * i + 1] = grad[:, ROWS:PAIR]

    def grad_copy(k, src):
        dest = at.tensor_at(k)
        return remote(
            r.back_src.at[dest],
            r.back_all.at[src],
            r.kb_send.at[0],
            r.kb_recv.at[0],
            TP,
            dest,
        )

    for k in range(1, TENSOR):
        grad_copy(k, t).start()
    r.back_all[t] = r.back_src[t]
    r.query_all[t] = r.query_src[t]
    for k in (2, 3):
        out_along(k).start()
    down_sums(1)
    across, own = moe_sums(6)[...].astype(F32), middle + moe_sums(7)[...].astype(F32)
    for j in range(3):
        moe_along(j).wait_recv()
        across = across + r.m_landed[j, 0:ROWS].astype(F32)
        own = own + r.m_landed[j, ROWS:PAIR].astype(F32)
    r.m_joined[...] = across.astype(BF)
    r.mid[...] = own

    def moe_across():
        return remote(
            r.m_joined, r.m_crossed, r.mx_send.at[0], r.mx_recv.at[0], TP, at.near_core(0, 1)
        )

    moe_across().start()
    copies.need(normed_load)
    r.tail[0 : 3 * HEAD, :] = dot(r.tail_left[...], r.normed[...]).astype(BF)

    copies.need(weights_load)
    whole = r.cots
    for j in range(4):
        rows = [
            whole[i * ROWS + HEAD + j * 16 : i * ROWS + HEAD + (j + 1) * 16, :].astype(F32)
            for i in range(TENSOR)
        ]
        first, second = unpacked(jnp.stack(rows, axis=0))
        r.downs[2 * j * ROWS : (2 * j + 1) * ROWS, :] = first.astype(BF)
        r.downs[(2 * j + 1) * ROWS : (2 * j + 2) * ROWS, :] = second.astype(BF)
    all_landed(r.query_all.at[pl.ds(0, 15)], r.qb_recv.at[0], at)
    all_landed(r.back_all.at[pl.ds(0, 15)], r.kb_recv.at[0], at)
    query_rows = r.query_all[...].astype(F32).reshape(WIDTH, ROWS).T.astype(BF)
    pairs = r.back_all[...].astype(F32).reshape(CHIPS, 2, ROWS, ROWS)
    kv_rows = (pairs[:, 0] + pairs[:, 1]).reshape(WIDTH, ROWS).T.astype(BF)
    wq_full = jnp.concatenate(
        [whole[i * ROWS : i * ROWS + HEAD, :] for i in range(TENSOR)], axis=0
    )
    normed_grad = dot(query_rows, wq_full) + dot(kv_rows, r.downs[...], NT)
    hidden = r.hid[...].astype(F32)
    inverse = lax.rsqrt(jnp.mean(hidden * hidden, axis=1, keepdims=True) + 1e-6)
    unit = hidden * inverse
    gain_one = r.small[...].astype(F32).T[32:33, :]
    gain_one_grad = jnp.sum(normed_grad * unit, axis=0, keepdims=True)
    scaled = normed_grad * gain_one
    r.hidden_grad[...] = (
        r.mid_grad[...]
        + inverse * (scaled - unit * jnp.mean(scaled * unit, axis=1, keepdims=True))
    ).astype(BF)
    r.save("hidden_grad")
    r.tail[3 * HEAD : 3 * HEAD + 32, :] = r.router_t[...].astype(BF)
    row = sublanes((16, WIDTH))
    r.tail[3 * HEAD + 32 : TAIL, :] = jnp.where(
        row == 0, gain_one_grad, jnp.where(row == 1, r.gain_grad[...], 0.0)
    ).astype(BF)

    def tail_copy(k):
        dest = at.dp_at(k)
        return remote(
            r.tail.at[pl.ds(0, TAIL), aligned(dest, ROWS)],
            r.tail_in.at[k],
            r.t_send.at[0],
            r.t_recv.at[0],
            SP,
            dest,
        )

    for k in range(1, DP):
        tail_copy(k).start()

    landed = [
        [r.nm_all.at[pl.ds((2 * k + x) * HEAD, HEAD)] for x in range(2)] for k in range(3)
    ]
    ring.end()
    loads = []
    for k in range(3):
        out_along(k + 1).wait_recv()
        for x in range(2):
            loads.append(copies.start(r.out_landed.at[k, x], landed[k][x]))
    copies.need(*loads)

    def out_total(x):
        total = r.out_twins[2 * at.z + x].astype(F32)
        for k in range(3):
            rows = aligned(2 * k + x, HEAD)
            total = total + r.nm_all[rows, :].astype(F32)
        return total

    r.out_joined[...] = out_total(1 - at.x_far).astype(BF)
    out_across().start()
    gu_sums(1)
    out_across().wait_recv()
    crossed = r.proj_grads.at[pl.ds(6 * PAIR, HEAD)]
    copies.need(copies.start(r.out_crossed, crossed))
    r.out_rows[...] = out_total(at.x_far) + crossed[...].astype(F32)

    def out_copy(k):
        dest = at.dp_at(k)
        return remote(
            r.out_rows.at[aligned(dest, 8), :],
            r.out_in.at[k],
            r.od_send.at[0],
            r.od_recv.at[0],
            SP,
            dest,
        )

    for k in range(1, DP):
        out_copy(k).start()
    total = r.tail[0:TAIL, aligned(d, ROWS)].astype(F32)
    all_landed(r.tail_in.at[pl.ds(0, 7)], r.t_recv.at[0], at)
    for k in range(1, DP):
        total = total + r.tail_in[k].astype(F32)
    r.query_out[...] = total[0:HEAD, :]
    r.save("query_out")
    turned = jnp.concatenate(
        [total[HEAD:TAIL], jnp.zeros((256 + HEAD - TAIL, ROWS), F32)], axis=0
    ).T
    for j in range(TENSOR):
        r.pieces[j] = turned[j * 8 : (j + 1) * 8, :]

    def last_copy(k, src):
        dest = at.tensor_at(k)
        return remote(
            r.pieces.at[dest], r.last.at[src], r.l_send.at[0], r.l_recv.at[0], TP, dest
        )

    for k in range(1, TENSOR):
        last_copy(k, t).start()
    r.last[t] = r.pieces[t]

    moe_across().wait_recv()
    crossed = r.proj_grads.at[pl.ds(7 * PAIR, ROWS)]
    copies.need(copies.start(r.m_crossed, crossed))
    r.output[...] = (r.mid[...] + crossed[...].astype(F32)).astype(BF)
    r.save("output")
    loads, crossed = [], []
    for e in range(2):
        down_across(e).wait_recv()
        crossed.append(r.weighted.at[pl.ds(3 * UNITS, UNITS), pl.ds(e * ROWS, ROWS)])
        loads.append(copies.start(r.yx_down.at[e], crossed[-1]))
    for e in range(2):
        gu_across(e).wait_recv()
        crossed.append(r.nm_all.at[pl.ds(WIDTH + e * ROWS, ROWS)])
        loads.append(copies.start(r.yx_gu.at[e], crossed[-1]))
    copies.need(*loads)
    for e, total in ((0, r.mid_grad), (1, r.mid)):
        total[...] = r.ys_gu[e, at.x].astype(F32) + crossed[2 + e][...].astype(F32)
        copies.start(total, r.gu_out.at[e])
        r.down_out[e] = r.ys_down[e, at.x].astype(F32) + crossed[e][...].astype(F32)
    r.save("down_out")
    total = r.out_rows[aligned(d, 8), :]
    all_landed(r.out_in.at[pl.ds(0, 7)], r.od_recv.at[0], at)
    for k in range(1, DP):
        total = total + r.out_in[k]
    r.out_grad[...] = total
    all_landed(r.last.at[pl.ds(0, 15)], r.l_recv.at[0], at)
    r.kv_out[...] = jnp.concatenate(
        [r.last[2 * j, :, 0:ROWS] + r.last[2 * j + 1, :, 0:ROWS] for j in range(CHIPS)], axis=1
    )
    shared = r.last[0, :, ROWS:PAIR]
    for j in range(1, TENSOR):
        shared = shared + r.last[j, :, ROWS:PAIR]
    r.router_out[...] = shared[:, 0:32]
    wide = jnp.concatenate([shared, jnp.zeros((ROWS - 8, ROWS), F32)], axis=0).T
    r.gain_one_out[...] = wide[32:33, 0:8]
    r.gain_two_out[...] = wide[33:34, 0:8]
    r.save("out_grad", "kv_out", "router_out", "gain_one_out", "gain_two_out")

    all_sent(r.tiles.at[pl.ds(0, 15)], r.t1_send.at[0], at)
    all_sent(r.tile_all.at[pl.ds(0, 7)], r.t2_send.at[0], at)
    all_sent(r.row_dp.at[pl.ds(0, 7)], r.rd_send.at[0], at)
    all_sent(seven_wq, r.wq_send.at[0], at)
    all_sent(r.gate_src.at[pl.ds(0, 15)], r.gg_send.at[0], at)
    all_sent(r.att_grad_t.at[pl.ds(0, 15 * HEAD)], r.b_send.at[0], at)
    all_sent(r.query_src.at[pl.ds(0, 15)], r.qb_send.at[0], at)
    all_sent(r.back_src.at[pl.ds(0, 15)], r.kb_send.at[0], at)
    all_sent(r.pieces.at[pl.ds(0, 15)], r.l_send.at[0], at)
    all_sent(r.tail_in.at[pl.ds(0, 7)], r.t_send.at[0], at)
    all_sent(r.out_in.at[pl.ds(0, 7)], r.od_send.at[0], at)
    for j in range(3):
        moe_along(j).wait_send()
    moe_across().wait_send()
    for k in range(1, 4):
        out_along(k).wait_send()
    out_across().wait_send()
    out_half().wait_send()
    for e in range(2):
        for k in range(1, 4):
            gu_over_y(e, k).wait_send()
            down_over_y(e, k).wait_send()
        gu_across(e).wait_send()
        down_across(e).wait_send()
    ring_w.end()
    copies.wait()
    r.end()


def store_kernel(r):
    copies = Copies(r.local)
    for name in STORED:
        copies.start(getattr(r, name), getattr(r, name + "_kept"))
    for name in STORED:
        copies.wait(1)
        copies.start(getattr(r, name + "_kept"), getattr(r, name + "_done"))
    copies.wait()


STORED = (
    "output",
    "hidden_grad",
    "gain_one_out",
    "query_out",
    "kv_out",
    "out_grad",
    "gain_two_out",
    "router_out",
    "gu_out",
    "down_out",
)


class Refs:
    def __init__(self, names, refs, loads=(), saves=()):
        for name, ref in zip(names, refs):
            setattr(self, name, ref)
        self.loads, self.saves, self.saved = list(loads), list(saves), []

    def copy_in(self, name):
        sem = self.load_sems.at[self.loads.index(name)]
        return pltpu.make_async_copy(getattr(self, name + "_d"), getattr(self, name), sem)

    def copy_out(self, name):
        sem = self.save_sems.at[self.saves.index(name)]
        return pltpu.make_async_copy(getattr(self, name), getattr(self, name + "_d"), sem)

    def load(self):
        for name in self.loads:
            self.copy_in(name).start()

    def need(self, *names):
        for name in names:
            self.copy_in(name).wait()

    def save(self, *names):
        for name in names:
            self.copy_out(name).start()
            self.saved.append(name)

    def finish(self, name):
        self.copy_out(name).wait()
        self.saved.remove(name)

    def end(self):
        for name in self.saved:
            self.copy_out(name).wait()


def call(kernel, number, inputs, outputs, scratch, reaches=True):
    def space(name):
        return pl.BlockSpec(memory_space=pltpu.VMEM if name.endswith("_v") else pl.ANY)

    outputs = {name: jax.ShapeDtypeStruct(shape, dtype) for name, (shape, dtype) in outputs.items()}
    loads = [name[:-2] for name in inputs if name.endswith("_d")]
    saves = [name[:-2] for name in outputs if name.endswith("_d")]
    scratch = dict(scratch)
    for name in loads:
        scratch[name] = pltpu.VMEM(inputs[name + "_d"].shape, inputs[name + "_d"].dtype)
    for name in saves:
        scratch[name] = pltpu.VMEM(outputs[name + "_d"].shape, outputs[name + "_d"].dtype)
    scratch |= sems(load_sems=max(1, len(loads)), save_sems=max(1, len(saves)))
    names = [name.removesuffix("_v") for name in (*inputs, *outputs)] + list(scratch)
    params = {"vmem_limit_bytes": VMEM_BYTES}
    if reaches:
        params |= {"collective_id": number, "has_side_effects": True}
    values = pl.pallas_call(
        lambda *refs: kernel(Refs(names, refs, loads, saves)),
        out_shape=list(outputs.values()),
        in_specs=[space(name) for name in inputs],
        out_specs=[space(name) for name in outputs],
        scratch_shapes=list(scratch.values()),
        compiler_params=pltpu.CompilerParams(**params),
        name=kernel.__name__,
    )(*inputs.values())
    return Refs([name.removesuffix("_v").removesuffix("_d") for name in outputs], values)


def sems(**counts):
    return {name: pltpu.SemaphoreType.DMA((count,)) for name, count in counts.items()}


def rope_tables():
    half = HEAD // 2
    freqs = np.exp(
        np.arange(half, dtype=np.float32) * np.float32(-2.0 * math.log(10000.0) / HEAD)
    ).astype(np.float32)
    angles = np.arange(LENGTH, dtype=np.float32)[:, None] * freqs[None, :]
    cos, sin = np.cos(angles).astype(np.float32), np.sin(angles).astype(np.float32)
    return (
        np.concatenate([cos, cos, -sin, sin], axis=1),
        np.ascontiguousarray(cos.T),
        np.ascontiguousarray(sin.T),
    )


def body(
    hidden,
    seg_ids,
    key_mask,
    routes,
    gain_attn,
    w_query,
    w_keyval,
    w_out,
    gain_mlp,
    w_router,
    w_gate_up,
    w_down,
    cotangent,
):
    V = pltpu.VMEM
    turns, cosine_t, sine_t = rope_tables()
    hid, cot = hidden[0], cotangent[0]
    c = call(
        layer_kernel,
        1,
        dict(
            hid_v=hid,
            cot=cot,
            w_keyval_v=w_keyval,
            w_out_t_v=w_out.T,
            w_query_t_v=w_query.T,
            router_v=w_router,
            gain_one_v=gain_attn.reshape(1, 8),
            gain_two_v=gain_mlp.reshape(1, 8),
            gu=w_gate_up,
            down=w_down,
            turns_d=turns,
            cosine_t_d=cosine_t,
            sine_t_d=sine_t,
            mask_v=key_mask,
            seg_v=seg_ids,
            routes_t_v=routes[0].T,
        ),
        dict(
            output_d=((ROWS, WIDTH), BF),
            hidden_grad_d=((ROWS, WIDTH), BF),
            gain_one_out_d=((1, 8), F32),
            query_out_d=((HEAD, ROWS), F32),
            kv_out_d=((8, WIDTH), F32),
            out_grad_d=((8, WIDTH), F32),
            gain_two_out_d=((1, 8), F32),
            router_out_d=((8, 32), F32),
            gu_out=((2, ROWS, WIDTH), F32),
            down_out_d=((2, UNITS, ROWS), F32),
            normed_d=((LENGTH, WIDTH), BF),
            out_t_d=((WIDTH, WIDTH), BF),
            wqkv=((LENGTH, WIDTH), BF),
            grads=((HEAD, LENGTH), BF),
            y_gu=((2, 3, PAIR, WIDTH), BF),
            y_down=((2, 3, UNITS, PAIR), BF),
            yx_gu=((2, ROWS, WIDTH), BF),
            yx_down=((2, UNITS, ROWS), BF),
            out_landed=((3, 2, HEAD, WIDTH), BF),
            out_crossed=((HEAD, WIDTH), BF),
            m_crossed=((ROWS, WIDTH), BF),
        ),
        dict(
            hidden_all=V((LENGTH, WIDTH), BF),
            nm_all=V((LENGTH, WIDTH), BF),
            cots=V((LENGTH, WIDTH), BF),
            gus=V((2, WIDTH, WIDTH), BF),
            downs=V((WIDTH, WIDTH), BF),
            down_grads=V((2, UNITS, WIDTH), BF),
            weighted=V((LENGTH, UNITS), BF),
            weighted_t=V((UNITS, LENGTH), BF),
            queries=V((LENGTH, 2 * HEAD), BF),
            keyvals=V((PADDED, 2 * HEAD), BF),
            keyvals_t=V((2 * HEAD, PADDED), BF),
            stats=V((1, LENGTH), F32),
            heads_t=V((HEAD, LENGTH), F32),
            small=V((WIDTH, ROWS), BF),
            mid=V((ROWS, WIDTH), F32),
            mid_grad=V((ROWS, WIDTH), F32),
            router_t=V((32, WIDTH), F32),
            gain_grad=V((1, WIDTH), F32),
            wqkv_own=V((ROWS, WIDTH), BF),
            rows=V((16, WIDTH), BF),
            row_dp=V((DP, 16, WIDTH), BF),
            shares=V((8, ROWS), F32),
            tiles=V((TENSOR, 16, ROWS), BF),
            tile_all=V((DP, TENSOR, 16, ROWS), BF),
            out_all=V((CHIPS, ROWS, WIDTH), BF),
            wq_all=V((2 * HEAD, WIDTH), BF),
            code=V((PADDED, ROWS), F32),
            scores=V((SPAN, PAIR), F32),
            starts=V((1, LENGTH), F32),
            wqk=V((WIDTH, PAIR), BF),
            att_src=V((TENSOR, HEAD, ROWS), BF),
            att_t=V((WIDTH, ROWS), BF),
            att_rows=V((ROWS, WIDTH), BF),
            ys_gu=V((2, 2, ROWS, WIDTH), BF),
            ys_down=V((2, 2, UNITS, ROWS), BF),
            n_parts=V((SLOTS, PAIR, WIDTH), BF),
            n_twins=V((SLOTS, ROWS, WIDTH), BF),
            n_credit=pltpu.SemaphoreType.REGULAR,
            n_crossed=V((4, ROWS, WIDTH), BF),
            n_landed=V((3, ROWS, WIDTH), BF),
            m_parts=V((SLOTS, PAIR, WIDTH), BF),
            m_twins=V((SLOTS, ROWS, WIDTH), BF),
            m_credit=pltpu.SemaphoreType.REGULAR,
            m_landed=V((3, PAIR, WIDTH), BF),
            gate_src=V((TENSOR, 8, ROWS), F32),
            gate_all=V((TENSOR, 8, ROWS), F32),
            query_all=V((TENSOR, HEAD, ROWS), BF),
            back_src=V((TENSOR, ROWS, ROWS), BF),
            back_all=V((TENSOR, ROWS, ROWS), BF),
            out_twins=V((CHIPS, HEAD, WIDTH), BF),
            out_joined=V((HEAD, WIDTH), BF),
            out_rows=V((HEAD, WIDTH), F32),
            out_in=V((DP, 8, WIDTH), F32),
            tail_in=V((DP, TAIL, ROWS), BF),
            pieces=V((TENSOR, 8, PAIR), F32),
            last=V((TENSOR, 8, PAIR), F32),
        )
        | sems(
            h_send=1,
            h_recv=24,
            c_send=1,
            c_recv=24,
            o_send=1,
            o_recv=24,
            g_send=1,
            g_recv=24,
            t1_send=1,
            t1_recv=1,
            t2_send=1,
            t2_recv=1,
            rd_send=1,
            rd_recv=1,
            wq_send=1,
            wq_recv=1,
            e_send=4,
            e_recv=40,
            a_send=1,
            a_recv=1,
            ntw_send=SLOTS,
            ntw_recv=SLOTS,
            nc_send=4,
            nc_recv=4,
            n_send=3,
            n_recv=3,
            mtw_send=SLOTS,
            mtw_recv=SLOTS,
            m_send=3,
            m_recv=3,
            mx_send=1,
            mx_recv=1,
            gg_send=1,
            gg_recv=1,
            b_send=1,
            b_recv=1,
            ot_send=1,
            ot_recv=1,
            oz_send=4,
            oz_recv=4,
            qb_send=1,
            qb_recv=1,
            kb_send=1,
            kb_recv=1,
            x_send=8,
            x_recv=8,
            y_send=8,
            y_recv=8,
            tx_send=4,
            tx_recv=4,
            t_send=1,
            t_recv=1,
            od_send=1,
            od_recv=1,
            l_send=1,
            l_recv=1,
            local=48,
        ),
    )
    values = {name: getattr(c, name) for name in STORED}
    done = call(
        store_kernel,
        0,
        values,
        {name + "_done": (value.shape, value.dtype) for name, value in values.items()},
        {name + "_kept": V(value.shape, value.dtype) for name, value in values.items()}
        | sems(local=2 * len(STORED)),
        reaches=False,
    )
    return (
        done.output_done[None],
        done.hidden_grad_done[None],
        done.gain_one_out_done.reshape(8),
        done.query_out_done.T,
        done.kv_out_done,
        done.out_grad_done.T,
        done.gain_two_out_done.reshape(8),
        done.router_out_done,
        done.gu_out_done,
        done.down_out_done,
    )


def solution(mesh):
    return jax.shard_map(
        body,
        mesh=mesh,
        in_specs=(
            P("dp", "tensor", None),
            P("dp", None),
            P("dp", None),
            P("dp", None, None),
            P(("dp", "tensor")),
            P("dp", "tensor"),
            P(("dp", "tensor"), None),
            P(None, ("dp", "tensor")),
            P(("dp", "tensor")),
            P(("dp", "tensor"), None),
            P("tensor", "dp", None),
            P("tensor", None, "dp"),
            P("dp", "tensor", None),
        ),
        out_specs=(
            P("dp", "tensor", None),
            P("dp", "tensor", None),
            P(("dp", "tensor")),
            P("dp", "tensor"),
            P(("dp", "tensor"), None),
            P(None, ("dp", "tensor")),
            P(("dp", "tensor")),
            P(("dp", "tensor"), None),
            P("tensor", "dp", None),
            P("tensor", None, "dp"),
        ),
        check_vma=False,
    )
```

```python
import math

import jax
import jax.numpy as jnp
import numpy as np
from jax import lax
from jax.experimental import pallas as pl
from jax.experimental.pallas import tpu as pltpu
from jax.sharding import PartitionSpec as P

HEAD = 64
LENGTH = 2048
WIDTH = 1024
UNITS = 512
ROWS = 128
PAIR = 256
CHUNK = 384
REACH = 896
SPAN = REACH + PAIR
PADDED = REACH + LENGTH
CHIPS = 8
TENSOR = 16
DP = 8
TAIL = 240
SLOTS = 2
STEP_Z = (0, 0, 1, 3, 1, 3, 2, 2)
STEP_X = (0, 1, 0, 0, 1, 1, 0, 1)
SUM_Z = (2, 2, 1, 1, 3, 3, 0, 0)
SUM_X = (1, 0, 1, 0, 1, 0, 1, 0)
LOWEST = -1e30
TP = "tensor"
SP = "dp"
BF = jnp.bfloat16
F32 = jnp.float32
MESH = pl.DeviceIdType.MESH
VMEM_BYTES = 63 * 1024 * 1024

NN = (((1,), (0,)), ((), ()))
NT = (((1,), (1,)), ((), ()))
TN = (((0,), (0,)), ((), ()))


def dot(left, right, dims=NN):
    return lax.dot_general(left, right, dims, preferred_element_type=F32)


def aligned(value, size):
    return pl.ds(pl.multiple_of(value * size, size), size)


def remote(src, dst, send, recv, axis, index):
    return pltpu.make_async_remote_copy(
        src_ref=src,
        dst_ref=dst,
        send_sem=send,
        recv_sem=recv,
        device_id={axis: index},
        device_id_type=MESH,
    )


def all_sent(ref, sem, place):
    remote(ref, ref, sem, sem, TP, place.twin).wait_send()


def all_landed(ref, sem, place):
    remote(ref, ref, sem, sem, TP, place.twin).wait_recv()


class Place:
    def __init__(self):
        self.t = lax.axis_index(TP)
        self.d = lax.axis_index(SP)
        self.core = lax.rem(self.t, 2)
        self.chip = self.t // 2
        self.twin = self.t + 1 - 2 * self.core
        self.x = lax.rem(self.d, 2)
        self.y = self.d // 2
        self.across = self.d + 1 - 2 * self.x
        self.z = self.chip // 2
        self.x_far = lax.rem(self.chip, 2)

    def chip_at(self, k):
        return lax.rem(self.chip + k, CHIPS)

    def same_core(self, k):
        return 2 * self.chip_at(k) + self.core

    def near(self, dz, dx):
        return 2 * lax.rem(self.z + dz, 4) + lax.rem(self.x_far + dx, 2)

    def near_core(self, dz, dx):
        return 2 * self.near(dz, dx) + self.core

    def listed(self, i, all_z, all_x):
        if isinstance(i, int):
            return self.near(all_z[i], all_x[i])
        dz, dx = jnp.int32(0), jnp.int32(0)
        for k in range(CHIPS):
            dz = jnp.where(i == k, all_z[k], dz)
            dx = jnp.where(i == k, all_x[k], dx)
        return self.near(dz, dx)

    def step(self, i):
        return self.listed(i, STEP_Z, STEP_X)

    def sum_step(self, i):
        return self.listed(i, SUM_Z, SUM_X)

    def step_core(self, i):
        return 2 * self.step(i) + self.core

    def tensor_at(self, k):
        return lax.rem(self.t + k, TENSOR)

    def dp_at(self, k):
        return lax.rem(self.d + k, DP)

    def y_at(self, k):
        return lax.rem(self.y + k, 4)

    def enter(self):
        barrier = pltpu.get_barrier_semaphore()
        for k in range(1, TENSOR):
            pl.semaphore_signal(
                barrier, inc=1, device_id={TP: self.tensor_at(k)}, device_id_type=MESH
            )
        for k in range(1, DP):
            pl.semaphore_signal(
                barrier, inc=1, device_id={SP: self.dp_at(k)}, device_id_type=MESH
            )
        pl.semaphore_wait(barrier, TENSOR + DP - 2)


class Ring:
    def __init__(self, place, block, half, send, recv, most, source=None, source_half=None):
        self.place, self.block, self.half = place, block, half
        self.send, self.recv, self.most = send, recv, most
        self.source, self.source_half = source, source_half

    def send_sem(self, number):
        return self.send.at[0]

    def copy(self, number, index, dest, source=None):
        src = self.block(index) if source is None else source
        return remote(
            src, self.block(index), self.send_sem(number), self.recv.at[index], TP, dest
        )

    def piece(self, number, index, part, dest, source=None):
        ref = self.half(index, part)
        place = TENSOR + index // 2 if part else index
        return remote(
            ref if source is None else source,
            ref,
            self.send_sem(number),
            self.recv.at[place],
            TP,
            dest,
        )

    def sent(self, number):
        at = self.place
        if number == 0:
            return self.copy(0, at.t, at.twin, self.source)
        if number < 4:
            return self.copy(number, at.t, at.step_core(number), self.source)
        if number < 6:
            return self.copy(number, at.step_core(1), at.step_core(number - 2))
        if number < 8:
            return self.piece(number, at.step_core(2 * number - 9), 0, at.step_core(2))
        if number < 10:
            return self.piece(number, at.step_core(2 * number - 14), 1, at.step_core(3))
        return self.copy(number, at.step_core(number - 9), at.twin)

    def start(self):
        at = self.place
        for part in range(2):
            src = None if self.source_half is None else self.source_half(part)
            self.piece(1, at.t, part, at.step_core(1), src).start()
        for number in (2, 3, 0):
            self.sent(number).start()

    def piece_arrived(self, index, part):
        self.piece(0, index, part, self.place.twin).wait_recv()

    def pass_on(self, i):
        at = self.place
        index = at.step_core(i)
        if i in (2, 3):
            self.copy(0, index, at.twin).wait_recv()
            self.sent(8 if i == 2 else 6).start()
        elif i == 1:
            for part in range(2):
                self.piece_arrived(index, part)
                self.piece(4, index, part, at.step_core(2)).start()
                self.piece(5, index, part, at.step_core(3)).start()
        elif i == 4:
            self.piece_arrived(index, 1)
            self.sent(9).start()
            self.piece_arrived(index, 0)
        elif i == 5:
            self.piece_arrived(index, 0)
            self.sent(7).start()
            self.piece_arrived(index, 1)
        else:
            self.piece_arrived(index, 0)
            self.piece_arrived(index, 1)
        self.sent(9 + i).start()

    def pass_on_at(self, i):
        for k in range(1, CHIPS):

            @pl.when(i == k - 1)
            def _(k=k):
                self.pass_on(k)

    def second(self, i):
        self.copy(0, 2 * self.place.step(i) + 1 - self.place.core, self.place.twin).wait_recv()

    def end(self):
        all_sent(self.most, self.send.at[0], self.place)


def whole_ring(place, ref, send, recv, source=None):
    return Ring(
        place,
        lambda b: ref.at[aligned(b, ROWS)],
        lambda b, part: ref.at[pl.ds(pl.multiple_of(b * ROWS + part * HEAD, HEAD), HEAD)],
        send,
        recv,
        ref.at[pl.ds(0, 15 * ROWS)],
        source,
        None if source is None else lambda part: source.at[pl.ds(part * HEAD, HEAD)],
    )


class Copies:
    def __init__(self, sems):
        self.sems, self.pending, self.free, self.used = sems, [], [], 0

    def start(self, src, dst):
        if self.free:
            number = self.free.pop()
        else:
            number, self.used = self.used, self.used + 1
        copy = pltpu.make_async_copy(src, dst, self.sems.at[number])
        copy.start()
        self.pending.append((copy, number))
        return copy

    def wait(self, count=None):
        count = len(self.pending) if count is None else count
        for copy, number in self.pending[:count]:
            copy.wait()
            self.free.append(number)
        self.pending = self.pending[count:]

    def need(self, *copies):
        for copy in copies:
            copy.wait()
            self.free += [number for other, number in self.pending if other is copy]
            self.pending = [pair for pair in self.pending if pair[0] is not copy]


def lanes(shape):
    return lax.broadcasted_iota(jnp.int32, shape, len(shape) - 1)


def sublanes(shape):
    return lax.broadcasted_iota(jnp.int32, shape, 0)


def swapped(values):
    return jnp.where(
        lanes(values.shape) < HEAD // 2,
        pltpu.roll(values, 2 * HEAD - HEAD // 2, 1),
        pltpu.roll(values, HEAD // 2, 1),
    )


def document_starts(seg):
    starts = jnp.zeros(seg.shape, F32)
    for document in range(8):
        before = jnp.sum(jnp.where(seg < document, 1.0, 0.0), axis=1, keepdims=True)
        starts = starts + jnp.where(seg == document, before, 0.0)
    return starts


def key_codes(mask, code):
    code[0:REACH, :] = jnp.full((REACH, ROWS), -1.0, F32)

    @pl.loop(0, TENSOR)
    def _(i):
        row = mask[:, aligned(i, ROWS)].astype(F32)
        live = jnp.broadcast_to(row, (ROWS, ROWS)).T == 1.0
        places = (sublanes((ROWS, ROWS)) + i * ROWS).astype(F32)
        code[pl.ds(pl.multiple_of(REACH + i * ROWS, ROWS), ROWS), :] = jnp.where(
            live, places, -1.0
        )


def allowed(code, start_row, chunk):
    ok = jnp.concatenate([code, code], axis=1) >= start_row
    if (chunk + 1) * CHUNK > REACH:
        key = sublanes((CHUNK, PAIR)) + (chunk * CHUNK - REACH)
        query = lanes((CHUNK, PAIR))
        ok = (ok & (key < query)) | (key == query)
    return ok


def turned_back(grad, r, here):
    cos, sin = r.cosine_t[:, here], r.sine_t[:, here]
    first, second = grad[0 : HEAD // 2], grad[HEAD // 2 : HEAD]
    return jnp.concatenate([first * cos + second * sin, second * cos - first * sin], axis=0)


class Halves:
    def __init__(self, place, parts, twins, sums, send, recv, credit):
        self.place, self.parts, self.twins, self.sums = place, parts, twins, sums
        self.send, self.recv, self.credit = send, recv, credit

    def half(self, k):
        at, slot = self.place, lax.rem(k, SLOTS)
        return remote(
            self.parts.at[slot, aligned(1 - at.core, ROWS), :],
            self.twins.at[slot],
            self.send.at[slot],
            self.recv.at[slot],
            TP,
            at.twin,
        )

    def put(self, k, value):
        @pl.when(k >= SLOTS)
        def _():
            self.half(k - SLOTS).wait_send()
            pl.semaphore_wait(self.credit, 1)

        self.parts[lax.rem(k, SLOTS)] = value.astype(BF)
        self.half(k).start()

    def add(self, k):
        slot = lax.rem(k, SLOTS)
        self.half(k).wait_recv()
        own = self.parts[slot, aligned(self.place.core, ROWS), :].astype(F32)
        self.sums(k)[...] = (own + self.twins[slot].astype(F32)).astype(BF)

        @pl.when(k < CHIPS - SLOTS)
        def _():
            pl.semaphore_signal(
                self.credit, inc=1, device_id={TP: self.place.twin}, device_id_type=MESH
            )

    def end(self):
        for k in range(CHIPS - SLOTS, CHIPS):
            self.half(k).wait_send()


class Joined:
    def __init__(self, place, sums, crossed, landed, sems):
        self.place, self.sums, self.crossed, self.landed = place, sums, crossed, landed
        self.c_send, self.c_recv, self.send, self.recv = sems

    def cross(self, j):
        return remote(
            self.sums.at[2 * j],
            self.crossed.at[j],
            self.c_send.at[j],
            self.c_recv.at[j],
            TP,
            self.place.near_core(0, 1),
        )

    def whole(self, j):
        return remote(
            self.sums.at[2 * j + 1],
            self.landed.at[j],
            self.send.at[j],
            self.recv.at[j],
            TP,
            self.place.near_core(SUM_Z[2 * j], 0),
        )

    def join(self, j):
        self.cross(j).wait_recv()
        total = self.sums[2 * j + 1].astype(F32) + self.crossed[j].astype(F32)
        self.sums[2 * j + 1] = total.astype(BF)
        self.whole(j).start()

    def result(self):
        self.cross(3).wait_recv()
        total = self.sums[7].astype(F32) + self.crossed[3].astype(F32)
        for j in range(3):
            self.whole(j).wait_recv()
            total = total + self.landed[j].astype(F32)
        return total

    def end(self):
        for j in range(4):
            self.cross(j).wait_send()
        for j in range(3):
            self.whole(j).wait_send()


def unpacked(both):
    return both[:, 0:8].reshape(ROWS, WIDTH), both[:, 8:16].reshape(ROWS, WIDTH)


def aligned_rows(ref, unit):
    def block(src, part=None):
        if part is None:
            return ref.at[pl.ds(pl.multiple_of(src * 2 * unit, unit), 2 * unit), :]
        return ref.at[pl.ds(pl.multiple_of((src * 2 + part) * unit, unit), unit), :]

    return block


def column_blocks(ref):
    def block(src, part=None):
        if part is None:
            return ref.at[:, aligned(src, ROWS)]
        return ref.at[pl.ds(part * PAIR, PAIR), aligned(src, ROWS)]

    return block


class Stream:
    def __init__(self, place, own, block, most, r, number):
        self.place, self.own, self.block, self.most = place, own, block, most
        self.send, self.recv = r.e_send, r.e_recv
        self.number, self.first_recv = number, 10 * number

    def at_y(self, k, other=False):
        at = self.place
        column = 1 - at.x if other else at.x
        return 2 * at.y_at(k) + column

    def copy(self, number, src, dest, part=None, source=None):
        ref = self.block(src, part)
        return remote(
            ref if source is None else source,
            ref,
            self.send.at[self.number],
            self.recv.at[self.first_recv + (8 + lax.rem(src, 2) if part else src)],
            SP,
            dest,
        )

    def sent(self, number):
        at, at_y = self.place, self.at_y
        if number == 0:
            return self.copy(0, at.d, at.across, source=self.own)
        if number < 3:
            return self.copy(number, at.d, at_y(2 * number - 1), source=self.own)
        if number < 5:
            return self.copy(number, at.across, at_y(2 * number - 5))
        other = number > 6
        if number % 2:
            return self.copy(number, at_y(3, other), at_y(1), 0)
        return self.copy(number, at_y(1, other), at_y(3), 1)

    def arrived(self, src, halves=False):
        for part in (0, 1) if halves else (None,):
            self.copy(0, src, self.place.across, part).wait_recv()

    def start_x(self):
        self.sent(0).start()

    def start_y(self):
        self.sent(1).start()
        self.sent(2).start()

    def from_across(self):
        self.arrived(self.place.across)
        self.sent(3).start()
        self.sent(4).start()

    def from_y(self):
        self.arrived(self.at_y(3))
        self.sent(5).start()
        self.arrived(self.at_y(1))
        self.sent(6).start()

    def from_y_across(self):
        self.arrived(self.at_y(3, True))
        self.sent(7).start()
        self.arrived(self.at_y(1, True))
        self.sent(8).start()

    def finish(self):
        self.arrived(self.at_y(2), True)
        self.arrived(self.at_y(2, True), True)

    def end(self):
        all_sent(self.most, self.send.at[self.number], self.place)


def expert_streams(at, r, e):
    downs = r.downs.at[pl.ds(e * UNITS, UNITS)]
    return (
        Stream(
            at,
            r.gu.at[e],
            aligned_rows(r.gus.at[e], HEAD),
            r.gus.at[e, pl.ds(0, 7 * ROWS)],
            r,
            2 * e,
        ),
        Stream(
            at,
            r.down.at[e],
            column_blocks(downs),
            downs.at[:, pl.ds(0, 7 * ROWS)],
            r,
            2 * e + 1,
        ),
    )


def layer_kernel(r):
    at = Place()
    t, d = at.t, at.d
    copies = Copies(r.local)
    r.load()
    r.hidden_all[aligned(t, ROWS), :] = r.hid[...]
    keyval, out_rows = r.w_keyval[...].astype(F32), r.w_out_t[...].astype(F32)
    r.rows[...] = jnp.concatenate([keyval, out_rows], axis=0).astype(BF)
    r.row_dp[d] = r.rows[...]
    r.shares[...] = jnp.zeros((8, ROWS), F32)
    r.shares[:, 0:32] = r.router[...].astype(F32)
    same = sublanes((8, 8)) == lanes((8, 8))
    for column, gain in ((32, r.gain_one), (33, r.gain_two)):
        wide = jnp.broadcast_to(gain[...].astype(F32), (8, 8))
        r.shares[:, column : column + 1] = jnp.sum(
            jnp.where(same, wide, 0.0), axis=1, keepdims=True
        )
    for j in range(CHIPS):
        tile = jnp.concatenate([keyval[:, j * ROWS : (j + 1) * ROWS], r.shares[...]], axis=0)
        r.tiles[2 * j] = tile.astype(BF)
        r.tiles[2 * j + 1] = tile.astype(BF)
    r.tile_all[d, t] = r.tiles[t]
    r.wq_all[HEAD : 2 * HEAD, :] = jnp.zeros((HEAD, WIDTH), BF)
    r.wq_all[0:HEAD, aligned(d, ROWS)] = r.w_query_t[...]
    at.enter()

    def tile_one(k, src):
        dest = at.tensor_at(k)
        return remote(
            r.tiles.at[dest],
            r.tile_all.at[d, src],
            r.t1_send.at[0],
            r.t1_recv.at[0],
            TP,
            dest,
        )

    def y_peer(k):
        return 2 * at.y_at(k) + at.x

    def tile_two(src, dest, recv):
        ref = r.tile_all.at[src]
        return remote(ref, ref, r.t2_send.at[0], recv.at[0], SP, dest)

    def rows_dp(src, dest, recv, source=None):
        ref = r.row_dp.at[src]
        return remote(
            ref if source is None else source, ref, r.rd_send.at[0], recv.at[0], SP, dest
        )

    def wq_dp(k, src):
        return remote(
            r.w_query_t,
            r.wq_all.at[pl.ds(0, HEAD), aligned(src, ROWS)],
            r.wq_send.at[0],
            r.wq_recv.at[0],
            SP,
            at.dp_at(k),
        )

    first_expert, second_expert = expert_streams(at, r, 0), expert_streams(at, r, 1)

    for k in range(1, TENSOR):
        tile_one(k, t).start()
    for k in range(1, DP):
        wq_dp(k, d).start()
    ring_h = whole_ring(at, r.hidden_all, r.h_send, r.h_recv)
    ring_h.start()
    for e in range(2):
        copies.start(r.gu.at[e], r.gus.at[e, aligned(d, ROWS)])
        copies.start(r.down.at[e], r.downs.at[pl.ds(e * UNITS, UNITS), aligned(d, ROWS)])
    copies.start(r.cot, r.cots.at[aligned(t, ROWS)])

    key_codes(r.mask, r.code)
    r.starts[...] = document_starts(r.seg[...])
    r.keyvals[0:REACH, :] = jnp.zeros((REACH, 2 * HEAD), BF)
    r.keyvals_t[:, 0:REACH] = jnp.zeros((2 * HEAD, REACH), BF)

    all_landed(r.tile_all.at[0, pl.ds(0, 15)], r.t1_recv.at[0], at)
    tile_two(d, at.across, r.t2x_recv).start()
    rows_dp(d, at.across, r.rdx_recv, r.rows).start()
    for k in range(1, 4):
        tile_two(d, y_peer(k), r.t2_recv).start()
        rows_dp(d, y_peer(k), r.rd_recv, r.rows).start()
    for stream in first_expert:
        stream.start_x()
    for i in range(1, 4):
        ring_h.pass_on(i)
    tile_two(at.across, at.across, r.t2x_recv).wait_recv()
    for k in range(1, 4):
        tile_two(at.across, y_peer(k), r.t2_recv).start()
    rows_dp(at.across, at.across, r.rdx_recv).wait_recv()
    for k in range(1, 4):
        rows_dp(at.across, y_peer(k), r.rd_recv).start()
    for stream in first_expert:
        stream.start_y()
    seven_wq = r.wq_all.at[pl.ds(0, HEAD), pl.ds(0, 7 * ROWS)]
    all_landed(seven_wq, r.wq_recv.at[0], at)
    all_landed(r.tile_all.at[pl.ds(0, 6)], r.t2_recv.at[0], at)
    for j in range(DP):
        both = r.tile_all[j].astype(F32)
        r.wqk[j * ROWS : (j + 1) * ROWS, ROWS:PAIR] = both[:, 0:8].reshape(ROWS, ROWS).astype(BF)
        r.small[j * ROWS : (j + 1) * ROWS, :] = both[:, 8:16].reshape(ROWS, ROWS).astype(BF)
    r.wqk[:, 0:ROWS] = r.wq_all[...].astype(F32).T.astype(BF)
    columns = r.small[...].astype(F32).T
    gain_one = columns[32:33, :]
    gain_two = columns[33:34, :]
    r.need("turns")
    ring_o = Ring(
        at,
        lambda b: r.out_all.at[b // 2, aligned(lax.rem(b, 2), HEAD)],
        lambda b, part: r.out_all.at[b // 2, aligned(2 * lax.rem(b, 2) + part, 32)],
        r.o_send,
        r.o_recv,
        r.nm_all.at[pl.ds(0, 15 * HEAD)],
    )

    ring_c = whole_ring(at, r.cots, r.c_send, r.c_recv, r.cot)
    @pl.loop(0, CHIPS)
    def _(i):
        @pl.when(i == 1)
        def _():
            ring_h.pass_on(4)
            ring_h.pass_on(5)

        @pl.when(i == 2)
        def _():
            all_landed(r.row_dp.at[pl.ds(0, 6)], r.rd_recv.at[0], at)
            both = r.row_dp[...].astype(F32)
            r.wqkv_own[0:HEAD, :] = r.wq_all[0:HEAD, :]
            r.wqkv_own[HEAD : 2 * HEAD, :] = both[:, 0:8].reshape(HEAD, WIDTH).astype(BF)
            r.out_all[at.chip, aligned(at.core, HEAD), :] = (
                both[:, 8:16].reshape(HEAD, WIDTH).astype(BF)
            )
            ring_o.start()

        @pl.when(i == 4)
        def _():
            ring_c.start()

        @pl.when(i == 5)
        def _():
            ring_h.pass_on(6)
            ring_h.pass_on(7)

        ring_h.second(i)
        block = at.step(i)
        here = aligned(block, PAIR)
        hidden = r.hidden_all[here, :].astype(F32)
        inverse = lax.rsqrt(jnp.mean(hidden * hidden, axis=1, keepdims=True) + 1e-6)
        unit = (hidden * inverse * gain_one).astype(BF)
        r.normed[here, :] = unit
        table = r.turns[here, :]
        turned = lanes(table.shape) < HEAD
        cos = jnp.where(turned, table, 1.0)
        sin = jnp.where(turned, pltpu.roll(table, HEAD, 1), 0.0)
        projected = dot(unit, r.wqk[...])
        query, keyval = projected[:, 0:ROWS], projected[:, ROWS:PAIR]
        query = (query * cos + swapped(query) * sin).astype(BF)
        r.queries[here, :] = (query.astype(F32) * (1.0 / math.sqrt(HEAD))).astype(BF)
        keyval = keyval * cos + swapped(keyval) * sin
        later = pl.ds(pl.multiple_of(REACH + block * PAIR, ROWS), PAIR)
        r.keyvals[later, :] = keyval.astype(BF)
        r.keyvals_t[:, later] = keyval.T.astype(BF)

    r.save("normed")

    def att_copy(dest, src):
        return remote(
            r.att_src.at[dest],
            r.att_t.at[aligned(src, HEAD), :],
            r.a_send.at[0],
            r.a_recv.at[0],
            TP,
            dest,
        )

    @pl.loop(0, CHIPS)
    def _(i):
        @pl.when(i == 0)
        def _():
            for stream in first_expert:
                stream.from_across()

        @pl.when(i == 1)
        def _():
            for k in range(1, 4):
                ring_o.pass_on(k)

        @pl.when(i == 3)
        def _():
            for stream in first_expert:
                stream.from_y()

        @pl.when(i == 5)
        def _():
            ring_o.pass_on(4)
            ring_o.pass_on(5)

        block = at.chip_at(i + 1)
        here = aligned(block, PAIR)
        query = r.queries[here, :]
        start_row = r.starts[:, here]
        top = jnp.full((1, PAIR), LOWEST, F32)
        for chunk in range(SPAN // CHUNK):
            keys = pl.ds(pl.multiple_of(block * PAIR + chunk * CHUNK, ROWS), CHUNK)
            score = dot(r.keyvals[keys, :], query, NT)
            score = jnp.where(allowed(r.code[keys, :], start_row, chunk), score, LOWEST)
            r.scores[chunk * CHUNK : (chunk + 1) * CHUNK, :] = score
            top = jnp.maximum(top, jnp.max(score, axis=0, keepdims=True))
        total = jnp.zeros((1, PAIR), F32)
        for chunk in range(SPAN // CHUNK):
            place = slice(chunk * CHUNK, (chunk + 1) * CHUNK)
            weight = jnp.exp(r.scores[place, :] - top)
            total = total + jnp.sum(weight, axis=0, keepdims=True)
            r.weighted[place, 0:PAIR] = weight.astype(BF)
        window = pl.ds(pl.multiple_of(block * PAIR, ROWS), SPAN)
        head = dot(r.keyvals_t[HEAD : 2 * HEAD, window], r.weighted[0:SPAN, 0:PAIR]) / total
        r.heads_t[:, here] = head
        r.stats[:, here] = top + jnp.log(total)
        r.att_src[2 * block] = head[:, 0:ROWS].astype(BF)
        r.att_src[2 * block + 1] = head[:, ROWS:PAIR].astype(BF)

        @pl.when(i < CHIPS - 1)
        def _():
            att_copy(2 * block, t).start()
            att_copy(2 * block + 1, t).start()

        @pl.when(i == CHIPS - 1)
        def _():
            att_copy(at.twin, t).start()

    ring_c.pass_on(1)
    r.att_t[aligned(t, HEAD), :] = r.att_src[t]
    ring_o.pass_on(6)
    ring_o.pass_on(7)
    for stream in first_expert:
        stream.from_y_across()
    for i in range(CHIPS):
        ring_o.second(i)

    @pl.loop(0, 4)
    def _(j):
        sides = [
            r.out_all[:, pl.ds(pl.multiple_of(core * HEAD + j * 16, 16), 16), :].astype(F32)
            for core in range(2)
        ]
        first, second = unpacked(jnp.stack(sides, axis=1).reshape(TENSOR, 16, WIDTH))
        r.out_t[aligned(2 * j, ROWS), :] = first.astype(BF)
        r.out_t[aligned(2 * j + 1, ROWS), :] = second.astype(BF)

    r.save("out_t")
    all_landed(r.att_t.at[pl.ds(0, 15 * HEAD)], r.a_recv.at[0], at)
    attended = r.att_t[...].astype(F32).T.astype(BF)
    r.att_rows[...] = attended
    middle = r.hid[...].astype(F32) + dot(attended, r.out_t[...], NT)
    r.mid[...] = middle
    inverse = lax.rsqrt(jnp.mean(middle * middle, axis=1, keepdims=True) + 1e-6)
    r.nm_all[aligned(t, ROWS), :] = (middle * inverse * gain_two).astype(BF)
    ring = whole_ring(at, r.nm_all, r.g_send, r.g_recv)
    ring.start()
    for stream in second_expert:
        stream.start_x()
        stream.start_y()
    ring_c.pass_on(2)
    ring_c.pass_on(3)
    for stream in first_expert:
        stream.finish()
    copies.wait()
    ring_h.end()
    ring_o.end()
    r.finish("normed")
    r.finish("out_t")
    r.proj_grads, r.n_first, r.gates, r.n_sums = r.hidden_all, r.normed, r.turns, r.out_all
    r.m_sums = r.out_t


    def moe_sums(k, count=1):
        return r.m_sums.at[pl.ds(pl.multiple_of(k * ROWS, ROWS), count * ROWS)]

    halves_n = Halves(at, r.n_parts, r.n_twins, lambda k: r.n_sums.at[k], r.ntw_send, r.ntw_recv, r.n_credit)
    halves_m = Halves(at, r.m_parts, r.m_twins, moe_sums, r.mtw_send, r.mtw_recv, r.m_credit)
    joined = Joined(
        at,
        r.n_sums,
        r.n_crossed,
        r.n_landed,
        (r.nc_send, r.nc_recv, r.n_send, r.n_recv),
    )
    ring_w = whole_ring(at, r.wqkv, r.h_send, r.h_recv, r.wqkv_own)
    own_weights = copies.start(r.wqkv_own, r.wqkv.at[aligned(t, ROWS)])

    def moe_first():
        return remote(
            moe_sums(0, 2),
            r.m_landed.at[0],
            r.m_send.at[0],
            r.m_recv.at[0],
            TP,
            at.near_core(SUM_Z[0], 0),
        )

    def moe_along(j, part):
        number = 2 * j - 1 + part
        return remote(
            moe_sums(2 * j + part),
            r.m_landed.at[j, pl.ds(part * ROWS, ROWS)],
            r.m_send.at[number],
            r.m_recv.at[number],
            TP,
            at.near_core(SUM_Z[2 * j], 0),
        )

    def gu_over_y(e, k):
        y = at.y_at(k)
        return remote(
            r.gus.at[e, aligned(y, PAIR), :],
            r.y_gu.at[e, k - 1],
            r.x_send.at[4 * e + k],
            r.x_recv.at[4 * e + k],
            SP,
            2 * y + at.x,
        )

    def down_over_y(e, k):
        y = at.y_at(k)
        return remote(
            r.down_grads.at[e, :, aligned(y, PAIR)],
            r.y_down.at[e, k - 1],
            r.y_send.at[4 * e + k],
            r.y_recv.at[4 * e + k],
            SP,
            2 * y + at.x,
        )

    def across_x(number, src, dst):
        return remote(src, dst, r.tx_send.at[number], r.tx_recv.at[number], SP, at.across)

    def gu_across(e):
        return across_x(e, r.ys_gu.at[e, 1 - at.x], r.yx_gu.at[e])

    def down_across(e):
        return across_x(2 + e, r.ys_down.at[e, 1 - at.x], r.yx_down.at[e])

    def gate_copy(dest, src):
        return remote(
            r.gate_src.at[dest],
            r.gate_all.at[src],
            r.gg_send.at[0],
            r.gg_recv.at[0],
            TP,
            dest,
        )

    def one_pass(e):
        @pl.loop(0, CHIPS)
        def _(i):
            if e == 0:
                for k in range(2, CHIPS):

                    @pl.when(i == k - 1)
                    def _(k=k):
                        ring.pass_on(k)

                ring.second(i)

                @pl.when(i == 1)
                def _():
                    ring_c.pass_on(4)
                    ring_c.pass_on(5)

                @pl.when(i == 2)
                def _():
                    for stream in second_expert:
                        stream.from_across()

                @pl.when(i == 4)
                def _():
                    for stream in second_expert:
                        stream.from_y()

                @pl.when(i == 5)
                def _():
                    ring_c.pass_on(6)
                    ring_c.pass_on(7)

                ring_c.second(i)

                @pl.when(i == 6)
                def _():
                    ring_w.start()

            here = aligned(at.step(i) if e == 0 else at.sum_step(i), PAIR)
            nm = r.nm_all[here, :]
            place = lanes((PAIR, ROWS))
            if e == 0:
                expert = sublanes((ROWS, PAIR))
                named = expert == r.routes_t[0:1, here]
                for j in range(1, 8):
                    named = named | (expert == r.routes_t[j : j + 1, here])
                named = jnp.where(named, 1.0, 0.0).T > 0.5
                logits = jnp.where(named, dot(nm, r.small[...]), LOWEST)
                powers = jnp.exp(logits - jnp.max(logits, axis=1, keepdims=True))
                powers = jnp.where(named, powers, 0.0)
                gates = powers / jnp.sum(powers, axis=1, keepdims=True)
            else:
                kept = r.gates[here, :]
                gates = jnp.where(place == 2 * HEAD - 1, 0.0, kept)
                earlier = kept[:, 2 * HEAD - 1 : 2 * HEAD]
            mine = place == 2 * t + e
            gate = jnp.sum(jnp.where(mine, gates, 0.0), axis=1, keepdims=True)
            act_grad = dot(r.cots[here, :], r.downs[e * UNITS : (e + 1) * UNITS, :], NT)
            projected = dot(nm, r.gus[e])
            first, up = projected[:, :UNITS], projected[:, UNITS:]
            sigmoid = 1.0 / (1.0 + jnp.exp(-first))
            silu = first * sigmoid
            activated = silu * up
            gate_grad = jnp.sum(activated * act_grad, axis=1, keepdims=True)
            weighted = (activated * gate).astype(BF)
            r.weighted_t[:, here] = weighted.T
            act_grad = act_grad * gate
            r.proj_grads[here, 0:UNITS] = (
                act_grad * up * (sigmoid * (1.0 + first * (1.0 - sigmoid)))
            ).astype(BF)
            r.proj_grads[here, UNITS:WIDTH] = (act_grad * silu).astype(BF)
            normed_part = dot(r.proj_grads[here, :], r.gus[e], NT)
            if e == 0:
                r.gates[here, :] = jnp.where(place == 2 * HEAD - 1, gate_grad, gates)
                r.weighted[here, :] = weighted
                r.n_first[here, :] = normed_part.astype(BF)

                @pl.when(i == 0)
                def _():
                    ring.pass_on(1)

                return
            row = 2 * lax.rem(t, 4)
            gate_grads = jnp.where(
                place == row, earlier, jnp.where(place == row + 1, gate_grad, 0.0)
            ).T
            chip = at.sum_step(i)
            r.gate_src[2 * chip] = gate_grads[0:8, 0:ROWS]
            r.gate_src[2 * chip + 1] = gate_grads[0:8, ROWS:PAIR]

            @pl.when(i < CHIPS - 1)
            def _():
                gate_copy(2 * chip, t).start()
                gate_copy(2 * chip + 1, t).start()

            @pl.when(i == CHIPS - 1)
            def _():
                gate_copy(at.twin, t).start()

            halves_n.put(i, normed_part + r.n_first[here, :].astype(F32))
            both = jnp.concatenate([r.weighted[here, :], weighted], axis=1)
            halves_m.put(i, dot(both, r.downs[...]))

            @pl.when(i > 0)
            def _():
                halves_n.add(i - 1)
                halves_m.add(i - 1)

            for j in range(4):

                @pl.when(i == 2 * j + 1)
                def _(j=j):
                    joined.cross(j).start()

            for j in range(2):

                @pl.when(i == 2 * j + 4)
                def _(j=j):
                    joined.join(j)

            @pl.when(i == 2)
            def _():
                moe_first().start()

            for step, chips in ((0, (2, 3)), (2, (4, 5))):

                @pl.when(i == step)
                def _(chips=chips):
                    for k in chips:
                        ring_w.pass_on(k)

    def down_gradients(e):
        @pl.loop(0, 2)
        def _(j):
            strip = aligned(j, PAIR)
            r.down_grads[e, strip, :] = dot(r.weighted_t[strip, :], r.cots[...]).astype(BF)

    def gate_up_gradients(e):
        @pl.loop(0, 4)
        def _(j):
            strip = aligned(j, PAIR)
            r.gus[e, strip, :] = dot(r.nm_all[:, strip], r.proj_grads[...], TN).astype(BF)

    one_pass(0)
    for stream in second_expert:
        stream.from_y_across()
    for stream in first_expert:
        stream.end()
    down_gradients(0)
    for k in range(1, 4):
        down_over_y(0, k).start()
    gate_up_gradients(0)
    ring_w.pass_on(1)
    for k in range(1, 4):
        gu_over_y(0, k).start()
    for stream in second_expert:
        stream.finish()
    one_pass(1)
    joined.join(2)
    halves_n.add(CHIPS - 1)
    halves_m.add(CHIPS - 1)
    for j in (1, 2):
        moe_along(j, 0).start()
    def gu_loads(e):
        ref, first = (r.n_first, WIDTH) if e == 0 else (r.proj_grads, 0)
        places = [ref.at[pl.ds(first + k * PAIR, PAIR)] for k in range(3)]
        loads = []
        for k in range(3):
            gu_over_y(e, k + 1).wait_recv()
            loads.append(copies.start(r.y_gu.at[e, k], places[k]))
        return places, loads

    def gu_sums(e, places, loads):
        copies.need(*loads)
        total = r.gus[e, aligned(at.y, PAIR), :].astype(F32)
        for place in places:
            total = total + place[...].astype(F32)
        r.ys_gu[e, 0] = total[0:ROWS].astype(BF)
        r.ys_gu[e, 1] = total[ROWS:PAIR].astype(BF)
        gu_across(e).start()

    def down_loads(e):
        places = [
            r.weighted.at[pl.ds(k * UNITS, UNITS), pl.ds(e * PAIR, PAIR)] for k in range(3)
        ]
        loads = []
        for k in range(3):
            down_over_y(e, k + 1).wait_recv()
            loads.append(copies.start(r.y_down.at[e, k], places[k]))
        return places, loads

    def down_sums(e, places, loads):
        copies.need(*loads)
        total = r.down_grads[e, :, aligned(at.y, PAIR)].astype(F32)
        for place in places:
            total = total + place[...].astype(F32)
        r.ys_down[e, 0] = total[:, 0:ROWS].astype(BF)
        r.ys_down[e, 1] = total[:, ROWS:PAIR].astype(BF)
        down_across(e).start()

    out_rows = r.n_first.at[pl.ds(0, WIDTH)]
    out_load = copies.start(r.out_t_d, out_rows)
    for stream in second_expert:
        stream.end()
    down_gradients(1)
    for k in range(1, 4):
        down_over_y(1, k).start()
    gate_up_gradients(1)
    first_down, first_gu = down_loads(0), gu_loads(0)
    for k in range(1, 4):
        gu_over_y(1, k).start()
    r.gate_all[t] = r.gate_src[t]
    all_landed(r.gate_all.at[pl.ds(0, 15)], r.gg_recv.at[0], at)
    groups = r.gate_all[...].reshape(4, 4, 8, ROWS)
    gate_grads = (groups[:, 0] + groups[:, 1] + groups[:, 2] + groups[:, 3]).reshape(32, ROWS)
    gate_grads = jnp.concatenate([gate_grads, jnp.zeros((ROWS - 32, ROWS), F32)], axis=0).T
    own_rows = aligned(t, ROWS)
    gates = jnp.where(lanes((ROWS, ROWS)) < 32, r.gates[own_rows, :], 0.0)
    mean = jnp.sum(gates * gate_grads, axis=1, keepdims=True)
    logit_grad = gates * (gate_grads - mean)
    r.router_t[...] = dot(logit_grad.T.astype(BF), r.nm_all[own_rows, :])[0:32, :]
    by_router = dot(logit_grad.astype(BF), r.small[...], NT)

    gain_two = r.small[...].astype(F32).T[33:34, :]
    normed_grad = joined.result() + by_router
    middle = r.mid[...]
    inverse = lax.rsqrt(jnp.mean(middle * middle, axis=1, keepdims=True) + 1e-6)
    unit = middle * inverse
    r.gain_grad[...] = jnp.sum(normed_grad * unit, axis=0, keepdims=True)
    scaled = normed_grad * gain_two
    grad = r.cots[aligned(t, ROWS), :].astype(F32) + inverse * (
        scaled - unit * jnp.mean(scaled * unit, axis=1, keepdims=True)
    )
    r.mid_grad[...] = grad
    turned = grad.T.reshape(DP, TENSOR, 8, ROWS).transpose(1, 0, 2, 3)
    r.att_grad_t, r.mid_t = r.att_t, r.wqk.at[:, pl.ds(0, ROWS)]
    r.mid_t[...] = turned.reshape(WIDTH, ROWS).astype(BF)
    copies.need(out_load)
    r.att_grad_t[...] = dot(grad.astype(BF), out_rows[...]).T.astype(BF)

    def back_copy(k, src):
        dest = at.tensor_at(k)
        return remote(
            r.att_grad_t.at[aligned(dest, HEAD), :],
            r.grads.at[:, aligned(src, ROWS)],
            r.b_send.at[0],
            r.b_recv.at[0],
            TP,
            dest,
        )

    for k in range(1, TENSOR):
        back_copy(k, t).start()
    own_grads = copies.start(
        r.att_grad_t.at[aligned(t, HEAD), :], r.grads.at[:, aligned(t, ROWS)]
    )
    joined.end()
    r.n_sums[...] = (
        dot(r.mid_t[...], r.att_rows[...]).reshape(CHIPS, ROWS, WIDTH).astype(BF)
    )

    def out_half():
        return remote(
            r.n_sums.at[:, aligned(1 - at.core, HEAD), :],
            r.out_twins,
            r.ot_send.at[0],
            r.ot_recv.at[0],
            TP,
            at.twin,
        )

    out_half().start()
    r.kv_sum, r.query_src = r.gates, r.att_src
    r.tail_left, r.grads_t = r.weighted_t.at[pl.ds(PAIR, 3 * HEAD)], r.weighted_t
    r.kv_sum[...] = jnp.zeros((LENGTH, 2 * HEAD), F32)
    r.grads_t[0:HEAD, :] = jnp.zeros((HEAD, LENGTH), BF)
    all_sent(r.att_src.at[pl.ds(0, 15)], r.a_send.at[0], at)
    halves_n.end()
    halves_m.end()
    r.tail = r.n_parts.at[0]
    r.s_gu, r.m_joined = r.m_parts.at[0, pl.ds(0, ROWS)], r.m_parts.at[0, pl.ds(ROWS, ROWS)]

    down_sums(0, *first_down)
    gu_sums(0, *first_gu)
    normed_load = copies.start(r.normed_d, r.normed)

    def out_along(k):
        return remote(
            r.out_twins.at[pl.ds(2 * lax.rem(at.z + k, 4), 2)],
            r.out_landed.at[k - 1],
            r.oz_send.at[k],
            r.oz_recv.at[k],
            TP,
            at.near_core(k, 0),
        )

    def out_across():
        return remote(
            r.out_joined, r.out_crossed, r.oz_send.at[0], r.oz_recv.at[0], TP, at.near_core(0, 1)
        )

    out_half().wait_recv()
    r.out_twins[...] = (
        r.n_sums[:, aligned(at.core, HEAD), :].astype(F32) + r.out_twins[...].astype(F32)
    ).astype(BF)
    for k in range(1, 4):
        out_along(k).start()
    def moe_across():
        return remote(
            r.m_joined, r.m_crossed, r.mx_send.at[0], r.mx_recv.at[0], TP, at.near_core(0, 1)
        )

    moe_first().wait_recv()
    across = moe_sums(6)[...].astype(F32) + r.m_landed[0, 0:ROWS].astype(F32)
    for j in (1, 2):
        moe_along(j, 0).wait_recv()
        across = across + r.m_landed[j, 0:ROWS].astype(F32)
    r.m_joined[...] = across.astype(BF)
    moe_across().start()
    all_landed(r.grads.at[:, pl.ds(0, 15 * ROWS)], r.b_recv.at[0], at)
    copies.need(own_grads)
    copies.need(copies.start(r.grads, r.grads_t.at[pl.ds(HEAD, HEAD)]))
    r.need("cosine_t", "sine_t")

    def query_copy(dest, src):
        return remote(
            r.query_src.at[dest],
            r.query_all.at[src],
            r.qb_send.at[0],
            r.qb_recv.at[0],
            TP,
            dest,
        )

    @pl.loop(0, CHIPS)
    def _(i):
        block = at.chip_at(i + 1)
        here = aligned(block, PAIR)
        query = r.queries[here, :]
        start_row = r.starts[:, here]
        stat = r.stats[:, here]
        grad_t = r.grads_t[0 : 2 * HEAD, here]
        grad_rows = grad_t.astype(F32).T.astype(BF)
        head = r.heads_t[:, here]
        delta = jnp.sum(head * grad_t[HEAD : 2 * HEAD, :].astype(F32), axis=0, keepdims=True)
        query_grad = jnp.zeros((HEAD, PAIR), F32)
        for chunk in range(SPAN // CHUNK):
            keys = pl.ds(pl.multiple_of(block * PAIR + chunk * CHUNK, ROWS), CHUNK)
            both = r.keyvals[keys, :]
            score = dot(both, query, NT)
            ok = allowed(r.code[keys, :], start_row, chunk)
            prob = jnp.exp(jnp.where(ok, score - stat, LOWEST))
            prob_grad = dot(both, grad_t)
            score_grad = (prob * (prob_grad - delta)).astype(BF)
            update = dot(score_grad, query) + dot(prob.astype(BF), grad_rows)
            for part in range(CHUNK // ROWS):
                row = jnp.maximum(block * PAIR + (chunk * CHUNK + part * ROWS - REACH), 0)
                place = pl.ds(pl.multiple_of(row, ROWS), ROWS)
                r.kv_sum[place, :] += update[part * ROWS : (part + 1) * ROWS]

            query_grad = query_grad + dot(r.keyvals_t[0:HEAD, keys], score_grad)
        turned = turned_back(query_grad * (1.0 / math.sqrt(HEAD)), r, here).astype(BF)
        r.tail_left[0:HEAD, here] = turned
        r.query_src[2 * block] = turned[:, 0:ROWS]
        r.query_src[2 * block + 1] = turned[:, ROWS:PAIR]

        @pl.when(i < CHIPS - 1)
        def _():
            query_copy(2 * block, t).start()
            query_copy(2 * block + 1, t).start()

        @pl.when(i == CHIPS - 1)
        def _():
            query_copy(at.twin, t).start()

    @pl.loop(0, CHIPS)
    def _(i):
        here = aligned(i, PAIR)
        grad = r.kv_sum[here, :].T
        grad = jnp.concatenate(
            [turned_back(grad[0:HEAD], r, here), grad[HEAD : 2 * HEAD]], axis=0
        ).astype(BF)
        r.tail_left[HEAD : 3 * HEAD, here] = grad
        r.back_src[2 * i] = grad[:, 0:ROWS]
        r.back_src[2 * i + 1] = grad[:, ROWS:PAIR]

    def grad_copy(k, src):
        dest = at.tensor_at(k)
        return remote(
            r.back_src.at[dest],
            r.back_all.at[src],
            r.kb_send.at[0],
            r.kb_recv.at[0],
            TP,
            dest,
        )

    for k in range(1, TENSOR):
        grad_copy(k, t).start()
    r.back_all[t] = r.back_src[t]
    r.query_all[t] = r.query_src[t]
    for j in (1, 2):
        moe_along(j, 1).start()
    down_sums(1, *down_loads(1))
    landed = [
        [r.nm_all.at[pl.ds((2 * k + x) * HEAD, HEAD)] for x in range(2)] for k in range(3)
    ]
    ring.end()
    loads = []
    for k in range(3):
        out_along(k + 1).wait_recv()
        for x in range(2):
            loads.append(copies.start(r.out_landed.at[k, x], landed[k][x]))
    copies.need(*loads)

    def out_total(x):
        total = r.out_twins[2 * at.z + x].astype(F32)
        for k in range(3):
            rows = aligned(2 * k + x, HEAD)
            total = total + r.nm_all[rows, :].astype(F32)
        return total

    r.out_joined[...] = out_total(1 - at.x_far).astype(BF)
    out_across().start()
    for number in (6, 7):
        ring_w.pass_on(number)
    for i in range(CHIPS):
        ring_w.second(i)
    ring_c.end()
    copies.need(own_weights)
    weights_load = copies.start(r.wqkv, r.cots)
    copies.need(normed_load)
    r.tail[0 : 3 * HEAD, :] = dot(r.tail_left[...], r.normed[...]).astype(BF)

    copies.need(weights_load)
    whole = r.cots
    for j in range(4):
        rows = [
            whole[i * ROWS + HEAD + j * 16 : i * ROWS + HEAD + (j + 1) * 16, :].astype(F32)
            for i in range(TENSOR)
        ]
        first, second = unpacked(jnp.stack(rows, axis=0))
        r.downs[2 * j * ROWS : (2 * j + 1) * ROWS, :] = first.astype(BF)
        r.downs[(2 * j + 1) * ROWS : (2 * j + 2) * ROWS, :] = second.astype(BF)
    all_landed(r.query_all.at[pl.ds(0, 15)], r.qb_recv.at[0], at)
    all_landed(r.back_all.at[pl.ds(0, 15)], r.kb_recv.at[0], at)
    query_rows = r.query_all[...].astype(F32).reshape(WIDTH, ROWS).T.astype(BF)
    pairs = r.back_all[...].astype(F32).reshape(CHIPS, 2, ROWS, ROWS)
    kv_rows = (pairs[:, 0] + pairs[:, 1]).reshape(WIDTH, ROWS).T.astype(BF)
    wq_full = jnp.concatenate(
        [whole[i * ROWS : i * ROWS + HEAD, :] for i in range(TENSOR)], axis=0
    )
    normed_grad = dot(query_rows, wq_full) + dot(kv_rows, r.downs[...], NT)
    hidden = r.hid[...].astype(F32)
    inverse = lax.rsqrt(jnp.mean(hidden * hidden, axis=1, keepdims=True) + 1e-6)
    unit = hidden * inverse
    gain_one = r.small[...].astype(F32).T[32:33, :]
    gain_one_grad = jnp.sum(normed_grad * unit, axis=0, keepdims=True)
    scaled = normed_grad * gain_one
    r.hidden_grad[...] = (
        r.mid_grad[...]
        + inverse * (scaled - unit * jnp.mean(scaled * unit, axis=1, keepdims=True))
    ).astype(BF)
    r.save("hidden_grad")
    r.tail[3 * HEAD : 3 * HEAD + 32, :] = r.router_t[...].astype(BF)
    row = sublanes((16, WIDTH))
    r.tail[3 * HEAD + 32 : TAIL, :] = jnp.where(
        row == 0, gain_one_grad, jnp.where(row == 1, r.gain_grad[...], 0.0)
    ).astype(BF)

    def tail_copy(k):
        dest = at.dp_at(k)
        return remote(
            r.tail.at[pl.ds(0, TAIL), aligned(dest, ROWS)],
            r.tail_in.at[k],
            r.t_send.at[0],
            r.t_recv.at[0],
            SP,
            dest,
        )

    for k in range(1, DP):
        tail_copy(k).start()

    gu_sums(1, *gu_loads(1))
    out_across().wait_recv()
    crossed = r.proj_grads.at[pl.ds(6 * PAIR, HEAD)]
    copies.need(copies.start(r.out_crossed, crossed))
    r.out_rows[...] = out_total(at.x_far) + crossed[...].astype(F32)

    def out_copy(k):
        dest = at.dp_at(k)
        return remote(
            r.out_rows.at[aligned(dest, 8), :],
            r.out_in.at[k],
            r.od_send.at[0],
            r.od_recv.at[0],
            SP,
            dest,
        )

    for k in range(1, DP):
        out_copy(k).start()
    total = r.tail[0:TAIL, aligned(d, ROWS)].astype(F32)
    all_landed(r.tail_in.at[pl.ds(0, 7)], r.t_recv.at[0], at)
    for k in range(1, DP):
        total = total + r.tail_in[k].astype(F32)
    r.query_out[...] = total[0:HEAD, :]
    r.save("query_out")
    turned = jnp.concatenate(
        [total[HEAD:TAIL], jnp.zeros((256 + HEAD - TAIL, ROWS), F32)], axis=0
    ).T
    for j in range(TENSOR):
        r.pieces[j] = turned[j * 8 : (j + 1) * 8, :]

    def last_copy(k, src):
        dest = at.tensor_at(k)
        return remote(
            r.pieces.at[dest], r.last.at[src], r.l_send.at[0], r.l_recv.at[0], TP, dest
        )

    for k in range(1, TENSOR):
        last_copy(k, t).start()
    r.last[t] = r.pieces[t]

    moe_across().wait_recv()
    crossed = r.nm_all.at[pl.ds(WIDTH + PAIR, ROWS)]
    load = copies.start(r.m_crossed, crossed)
    own = r.mid[...] + moe_sums(7)[...].astype(F32) + r.m_landed[0, ROWS:PAIR].astype(F32)
    for j in (1, 2):
        moe_along(j, 1).wait_recv()
        own = own + r.m_landed[j, ROWS:PAIR].astype(F32)
    copies.need(load)
    r.output[...] = (own + crossed[...].astype(F32)).astype(BF)
    r.save("output")
    loads, crossed = [], []
    for e in range(2):
        down_across(e).wait_recv()
        crossed.append(r.weighted.at[pl.ds(3 * UNITS, UNITS), pl.ds(e * ROWS, ROWS)])
        loads.append(copies.start(r.yx_down.at[e], crossed[-1]))
    for e in range(2):
        gu_across(e).wait_recv()
        crossed.append(r.nm_all.at[pl.ds(WIDTH + e * ROWS, ROWS)])
        loads.append(copies.start(r.yx_gu.at[e], crossed[-1]))
    copies.need(*loads)
    for e, total in ((0, r.mid_grad), (1, r.mid)):
        total[...] = r.ys_gu[e, at.x].astype(F32) + crossed[2 + e][...].astype(F32)
        copies.start(total, r.gu_out.at[e])
        r.down_out[e] = r.ys_down[e, at.x].astype(F32) + crossed[e][...].astype(F32)
    r.save("down_out")
    total = r.out_rows[aligned(d, 8), :]
    all_landed(r.out_in.at[pl.ds(0, 7)], r.od_recv.at[0], at)
    for k in range(1, DP):
        total = total + r.out_in[k]
    r.out_grad[...] = total
    all_landed(r.last.at[pl.ds(0, 15)], r.l_recv.at[0], at)
    r.kv_out[...] = jnp.concatenate(
        [r.last[2 * j, :, 0:ROWS] + r.last[2 * j + 1, :, 0:ROWS] for j in range(CHIPS)], axis=1
    )
    shared = r.last[0, :, ROWS:PAIR]
    for j in range(1, TENSOR):
        shared = shared + r.last[j, :, ROWS:PAIR]
    r.router_out[...] = shared[:, 0:32]
    wide = jnp.concatenate([shared, jnp.zeros((ROWS - 8, ROWS), F32)], axis=0).T
    r.gain_one_out[...] = wide[32:33, 0:8]
    r.gain_two_out[...] = wide[33:34, 0:8]
    r.save("out_grad", "kv_out", "router_out", "gain_one_out", "gain_two_out")

    all_sent(r.tiles.at[pl.ds(0, 15)], r.t1_send.at[0], at)
    all_sent(r.tile_all.at[pl.ds(0, 7)], r.t2_send.at[0], at)
    all_sent(r.row_dp.at[pl.ds(0, 7)], r.rd_send.at[0], at)
    all_sent(seven_wq, r.wq_send.at[0], at)
    all_sent(r.gate_src.at[pl.ds(0, 15)], r.gg_send.at[0], at)
    all_sent(r.att_grad_t.at[pl.ds(0, 15 * HEAD)], r.b_send.at[0], at)
    all_sent(r.query_src.at[pl.ds(0, 15)], r.qb_send.at[0], at)
    all_sent(r.back_src.at[pl.ds(0, 15)], r.kb_send.at[0], at)
    all_sent(r.pieces.at[pl.ds(0, 15)], r.l_send.at[0], at)
    all_sent(r.tail_in.at[pl.ds(0, 7)], r.t_send.at[0], at)
    all_sent(r.out_in.at[pl.ds(0, 7)], r.od_send.at[0], at)
    moe_first().wait_send()
    for j in (1, 2):
        for part in range(2):
            moe_along(j, part).wait_send()
    moe_across().wait_send()
    for k in range(1, 4):
        out_along(k).wait_send()
    out_across().wait_send()
    out_half().wait_send()
    for e in range(2):
        for k in range(1, 4):
            gu_over_y(e, k).wait_send()
            down_over_y(e, k).wait_send()
        gu_across(e).wait_send()
        down_across(e).wait_send()
    ring_w.end()
    copies.wait()
    r.end()


def store_kernel(r):
    copies = Copies(r.local)
    for name in STORED:
        copies.start(getattr(r, name), getattr(r, name + "_kept"))
    for name in STORED:
        copies.wait(1)
        copies.start(getattr(r, name + "_kept"), getattr(r, name + "_done"))
    copies.wait()


STORED = (
    "output",
    "hidden_grad",
    "gain_one_out",
    "query_out",
    "kv_out",
    "out_grad",
    "gain_two_out",
    "router_out",
    "gu_out",
    "down_out",
)


class Refs:
    def __init__(self, names, refs, loads=(), saves=()):
        for name, ref in zip(names, refs):
            setattr(self, name, ref)
        self.loads, self.saves, self.saved = list(loads), list(saves), []

    def copy_in(self, name):
        sem = self.load_sems.at[self.loads.index(name)]
        return pltpu.make_async_copy(getattr(self, name + "_d"), getattr(self, name), sem)

    def copy_out(self, name):
        sem = self.save_sems.at[self.saves.index(name)]
        return pltpu.make_async_copy(getattr(self, name), getattr(self, name + "_d"), sem)

    def load(self):
        for name in self.loads:
            self.copy_in(name).start()

    def need(self, *names):
        for name in names:
            self.copy_in(name).wait()

    def save(self, *names):
        for name in names:
            self.copy_out(name).start()
            self.saved.append(name)

    def finish(self, name):
        self.copy_out(name).wait()
        self.saved.remove(name)

    def end(self):
        for name in self.saved:
            self.copy_out(name).wait()


def call(kernel, number, inputs, outputs, scratch, reaches=True):
    def space(name):
        return pl.BlockSpec(memory_space=pltpu.VMEM if name.endswith("_v") else pl.ANY)

    outputs = {name: jax.ShapeDtypeStruct(shape, dtype) for name, (shape, dtype) in outputs.items()}
    loads = [name[:-2] for name in inputs if name.endswith("_d")]
    saves = [name[:-2] for name in outputs if name.endswith("_d")]
    scratch = dict(scratch)
    for name in loads:
        scratch[name] = pltpu.VMEM(inputs[name + "_d"].shape, inputs[name + "_d"].dtype)
    for name in saves:
        scratch[name] = pltpu.VMEM(outputs[name + "_d"].shape, outputs[name + "_d"].dtype)
    scratch |= sems(load_sems=max(1, len(loads)), save_sems=max(1, len(saves)))
    names = [name.removesuffix("_v") for name in (*inputs, *outputs)] + list(scratch)
    params = {"vmem_limit_bytes": VMEM_BYTES}
    if reaches:
        params |= {"collective_id": number, "has_side_effects": True}
    values = pl.pallas_call(
        lambda *refs: kernel(Refs(names, refs, loads, saves)),
        out_shape=list(outputs.values()),
        in_specs=[space(name) for name in inputs],
        out_specs=[space(name) for name in outputs],
        scratch_shapes=list(scratch.values()),
        compiler_params=pltpu.CompilerParams(**params),
        name=kernel.__name__,
    )(*inputs.values())
    return Refs([name.removesuffix("_v").removesuffix("_d") for name in outputs], values)


def sems(**counts):
    return {name: pltpu.SemaphoreType.DMA((count,)) for name, count in counts.items()}


def rope_tables():
    half = HEAD // 2
    freqs = np.exp(
        np.arange(half, dtype=np.float32) * np.float32(-2.0 * math.log(10000.0) / HEAD)
    ).astype(np.float32)
    angles = np.arange(LENGTH, dtype=np.float32)[:, None] * freqs[None, :]
    cos, sin = np.cos(angles).astype(np.float32), np.sin(angles).astype(np.float32)
    return (
        np.concatenate([cos, cos, -sin, sin], axis=1),
        np.ascontiguousarray(cos.T),
        np.ascontiguousarray(sin.T),
    )


def body(
    hidden,
    seg_ids,
    key_mask,
    routes,
    gain_attn,
    w_query,
    w_keyval,
    w_out,
    gain_mlp,
    w_router,
    w_gate_up,
    w_down,
    cotangent,
):
    V = pltpu.VMEM
    turns, cosine_t, sine_t = rope_tables()
    hid, cot = hidden[0], cotangent[0]
    c = call(
        layer_kernel,
        1,
        dict(
            hid_v=hid,
            cot=cot,
            w_keyval_v=w_keyval,
            w_out_t_v=w_out.T,
            w_query_t_v=w_query.T,
            router_v=w_router,
            gain_one_v=gain_attn.reshape(1, 8),
            gain_two_v=gain_mlp.reshape(1, 8),
            gu=w_gate_up,
            down=w_down,
            turns_d=turns,
            cosine_t_d=cosine_t,
            sine_t_d=sine_t,
            mask_v=key_mask,
            seg_v=seg_ids,
            routes_t_v=routes[0].T,
        ),
        dict(
            output_d=((ROWS, WIDTH), BF),
            hidden_grad_d=((ROWS, WIDTH), BF),
            gain_one_out_d=((1, 8), F32),
            query_out_d=((HEAD, ROWS), F32),
            kv_out_d=((8, WIDTH), F32),
            out_grad_d=((8, WIDTH), F32),
            gain_two_out_d=((1, 8), F32),
            router_out_d=((8, 32), F32),
            gu_out=((2, ROWS, WIDTH), F32),
            down_out_d=((2, UNITS, ROWS), F32),
            normed_d=((LENGTH, WIDTH), BF),
            out_t_d=((WIDTH, WIDTH), BF),
            wqkv=((LENGTH, WIDTH), BF),
            grads=((HEAD, LENGTH), BF),
            y_gu=((2, 3, PAIR, WIDTH), BF),
            y_down=((2, 3, UNITS, PAIR), BF),
            yx_gu=((2, ROWS, WIDTH), BF),
            yx_down=((2, UNITS, ROWS), BF),
            out_landed=((3, 2, HEAD, WIDTH), BF),
            out_crossed=((HEAD, WIDTH), BF),
            m_crossed=((ROWS, WIDTH), BF),
        ),
        dict(
            hidden_all=V((LENGTH, WIDTH), BF),
            nm_all=V((LENGTH, WIDTH), BF),
            cots=V((LENGTH, WIDTH), BF),
            gus=V((2, WIDTH, WIDTH), BF),
            downs=V((WIDTH, WIDTH), BF),
            down_grads=V((2, UNITS, WIDTH), BF),
            weighted=V((LENGTH, UNITS), BF),
            weighted_t=V((UNITS, LENGTH), BF),
            queries=V((LENGTH, 2 * HEAD), BF),
            keyvals=V((PADDED, 2 * HEAD), BF),
            keyvals_t=V((2 * HEAD, PADDED), BF),
            stats=V((1, LENGTH), F32),
            heads_t=V((HEAD, LENGTH), F32),
            small=V((WIDTH, ROWS), BF),
            mid=V((ROWS, WIDTH), F32),
            mid_grad=V((ROWS, WIDTH), F32),
            router_t=V((32, WIDTH), F32),
            gain_grad=V((1, WIDTH), F32),
            wqkv_own=V((ROWS, WIDTH), BF),
            rows=V((16, WIDTH), BF),
            row_dp=V((DP, 16, WIDTH), BF),
            shares=V((8, ROWS), F32),
            tiles=V((TENSOR, 16, ROWS), BF),
            tile_all=V((DP, TENSOR, 16, ROWS), BF),
            out_all=V((CHIPS, ROWS, WIDTH), BF),
            wq_all=V((2 * HEAD, WIDTH), BF),
            code=V((PADDED, ROWS), F32),
            scores=V((SPAN, PAIR), F32),
            starts=V((1, LENGTH), F32),
            wqk=V((WIDTH, PAIR), BF),
            att_src=V((TENSOR, HEAD, ROWS), BF),
            att_t=V((WIDTH, ROWS), BF),
            att_rows=V((ROWS, WIDTH), BF),
            ys_gu=V((2, 2, ROWS, WIDTH), BF),
            ys_down=V((2, 2, UNITS, ROWS), BF),
            n_parts=V((SLOTS, PAIR, WIDTH), BF),
            n_twins=V((SLOTS, ROWS, WIDTH), BF),
            n_credit=pltpu.SemaphoreType.REGULAR,
            n_crossed=V((4, ROWS, WIDTH), BF),
            n_landed=V((3, ROWS, WIDTH), BF),
            m_parts=V((SLOTS, PAIR, WIDTH), BF),
            m_twins=V((SLOTS, ROWS, WIDTH), BF),
            m_credit=pltpu.SemaphoreType.REGULAR,
            m_landed=V((3, PAIR, WIDTH), BF),
            gate_src=V((TENSOR, 8, ROWS), F32),
            gate_all=V((TENSOR, 8, ROWS), F32),
            query_all=V((TENSOR, HEAD, ROWS), BF),
            back_src=V((TENSOR, ROWS, ROWS), BF),
            back_all=V((TENSOR, ROWS, ROWS), BF),
            out_twins=V((CHIPS, HEAD, WIDTH), BF),
            out_joined=V((HEAD, WIDTH), BF),
            out_rows=V((HEAD, WIDTH), F32),
            out_in=V((DP, 8, WIDTH), F32),
            tail_in=V((DP, TAIL, ROWS), BF),
            pieces=V((TENSOR, 8, PAIR), F32),
            last=V((TENSOR, 8, PAIR), F32),
        )
        | sems(
            h_send=1,
            h_recv=24,
            c_send=1,
            c_recv=24,
            o_send=1,
            o_recv=24,
            g_send=1,
            g_recv=24,
            t1_send=1,
            t1_recv=1,
            t2_send=1,
            t2_recv=1,
            t2x_recv=1,
            rdx_recv=1,
            rd_send=1,
            rd_recv=1,
            wq_send=1,
            wq_recv=1,
            e_send=4,
            e_recv=40,
            a_send=1,
            a_recv=1,
            ntw_send=SLOTS,
            ntw_recv=SLOTS,
            nc_send=4,
            nc_recv=4,
            n_send=3,
            n_recv=3,
            mtw_send=SLOTS,
            mtw_recv=SLOTS,
            m_send=5,
            m_recv=5,
            mx_send=1,
            mx_recv=1,
            gg_send=1,
            gg_recv=1,
            b_send=1,
            b_recv=1,
            ot_send=1,
            ot_recv=1,
            oz_send=4,
            oz_recv=4,
            qb_send=1,
            qb_recv=1,
            kb_send=1,
            kb_recv=1,
            x_send=8,
            x_recv=8,
            y_send=8,
            y_recv=8,
            tx_send=4,
            tx_recv=4,
            t_send=1,
            t_recv=1,
            od_send=1,
            od_recv=1,
            l_send=1,
            l_recv=1,
            local=20,
        ),
    )
    values = {name: getattr(c, name) for name in STORED}
    done = call(
        store_kernel,
        0,
        values,
        {name + "_done": (value.shape, value.dtype) for name, value in values.items()},
        {name + "_kept": V(value.shape, value.dtype) for name, value in values.items()}
        | sems(local=2 * len(STORED)),
        reaches=False,
    )
    return (
        done.output_done[None],
        done.hidden_grad_done[None],
        done.gain_one_out_done.reshape(8),
        done.query_out_done.T,
        done.kv_out_done,
        done.out_grad_done.T,
        done.gain_two_out_done.reshape(8),
        done.router_out_done,
        done.gu_out_done,
        done.down_out_done,
    )


def solution(mesh):
    return jax.shard_map(
        body,
        mesh=mesh,
        in_specs=(
            P("dp", "tensor", None),
            P("dp", None),
            P("dp", None),
            P("dp", None, None),
            P(("dp", "tensor")),
            P("dp", "tensor"),
            P(("dp", "tensor"), None),
            P(None, ("dp", "tensor")),
            P(("dp", "tensor")),
            P(("dp", "tensor"), None),
            P("tensor", "dp", None),
            P("tensor", None, "dp"),
            P("dp", "tensor", None),
        ),
        out_specs=(
            P("dp", "tensor", None),
            P("dp", "tensor", None),
            P(("dp", "tensor")),
            P("dp", "tensor"),
            P(("dp", "tensor"), None),
            P(None, ("dp", "tensor")),
            P(("dp", "tensor")),
            P(("dp", "tensor"), None),
            P("tensor", "dp", None),
            P("tensor", None, "dp"),
        ),
        check_vma=False,
    )
```

```python
import math

import jax
import jax.numpy as jnp
import numpy as np
from jax import lax
from jax.experimental import pallas as pl
from jax.experimental.pallas import tpu as pltpu
from jax.sharding import PartitionSpec as P

HEAD = 64
LENGTH = 2048
WIDTH = 1024
UNITS = 512
ROWS = 128
PAIR = 256
CHUNK = 384
REACH = 896
SPAN = REACH + PAIR
PADDED = REACH + LENGTH
CHIPS = 8
TENSOR = 16
DP = 8
TAIL = 240
SLOTS = 2
STEP_Z = (0, 0, 1, 3, 1, 3, 2, 2)
STEP_X = (0, 1, 0, 0, 1, 1, 0, 1)
SUM_Z = (2, 2, 1, 1, 3, 3, 0, 0)
SUM_X = (1, 0, 1, 0, 1, 0, 1, 0)
LOWEST = -1e30
TP = "tensor"
SP = "dp"
BF = jnp.bfloat16
F32 = jnp.float32
MESH = pl.DeviceIdType.MESH
VMEM_BYTES = 63 * 1024 * 1024

NN = (((1,), (0,)), ((), ()))
NT = (((1,), (1,)), ((), ()))
TN = (((0,), (0,)), ((), ()))


def dot(left, right, dims=NN):
    return lax.dot_general(left, right, dims, preferred_element_type=F32)


def aligned(value, size):
    return pl.ds(pl.multiple_of(value * size, size), size)


def remote(src, dst, send, recv, axis, index):
    return pltpu.make_async_remote_copy(
        src_ref=src,
        dst_ref=dst,
        send_sem=send,
        recv_sem=recv,
        device_id={axis: index},
        device_id_type=MESH,
    )


def all_sent(ref, sem, place):
    remote(ref, ref, sem, sem, TP, place.twin).wait_send()


def all_landed(ref, sem, place):
    remote(ref, ref, sem, sem, TP, place.twin).wait_recv()


class Place:
    def __init__(self):
        self.t = lax.axis_index(TP)
        self.d = lax.axis_index(SP)
        self.core = lax.rem(self.t, 2)
        self.chip = self.t // 2
        self.twin = self.t + 1 - 2 * self.core
        self.x = lax.rem(self.d, 2)
        self.y = self.d // 2
        self.across = self.d + 1 - 2 * self.x
        self.z = self.chip // 2
        self.x_far = lax.rem(self.chip, 2)

    def chip_at(self, k):
        return lax.rem(self.chip + k, CHIPS)

    def same_core(self, k):
        return 2 * self.chip_at(k) + self.core

    def near(self, dz, dx):
        return 2 * lax.rem(self.z + dz, 4) + lax.rem(self.x_far + dx, 2)

    def near_core(self, dz, dx):
        return 2 * self.near(dz, dx) + self.core

    def listed(self, i, all_z, all_x):
        if isinstance(i, int):
            return self.near(all_z[i], all_x[i])
        dz, dx = jnp.int32(0), jnp.int32(0)
        for k in range(CHIPS):
            dz = jnp.where(i == k, all_z[k], dz)
            dx = jnp.where(i == k, all_x[k], dx)
        return self.near(dz, dx)

    def step(self, i):
        return self.listed(i, STEP_Z, STEP_X)

    def sum_step(self, i):
        return self.listed(i, SUM_Z, SUM_X)

    def step_core(self, i):
        return 2 * self.step(i) + self.core

    def tensor_at(self, k):
        return lax.rem(self.t + k, TENSOR)

    def dp_at(self, k):
        return lax.rem(self.d + k, DP)

    def y_at(self, k):
        return lax.rem(self.y + k, 4)

    def enter(self):
        barrier = pltpu.get_barrier_semaphore()
        for k in range(1, TENSOR):
            pl.semaphore_signal(
                barrier, inc=1, device_id={TP: self.tensor_at(k)}, device_id_type=MESH
            )
        for k in range(1, DP):
            pl.semaphore_signal(
                barrier, inc=1, device_id={SP: self.dp_at(k)}, device_id_type=MESH
            )
        pl.semaphore_wait(barrier, TENSOR + DP - 2)


class Ring:
    def __init__(self, place, block, half, send, recv, most, source=None, source_half=None):
        self.place, self.block, self.half = place, block, half
        self.send, self.recv, self.most = send, recv, most
        self.source, self.source_half = source, source_half

    def send_sem(self, number):
        return self.send.at[0]

    def copy(self, number, index, dest, source=None):
        src = self.block(index) if source is None else source
        return remote(
            src, self.block(index), self.send_sem(number), self.recv.at[index], TP, dest
        )

    def piece(self, number, index, part, dest, source=None):
        ref = self.half(index, part)
        place = TENSOR + index // 2 if part else index
        return remote(
            ref if source is None else source,
            ref,
            self.send_sem(number),
            self.recv.at[place],
            TP,
            dest,
        )

    def sent(self, number):
        at = self.place
        if number == 0:
            return self.copy(0, at.t, at.twin, self.source)
        if number < 4:
            return self.copy(number, at.t, at.step_core(number), self.source)
        if number < 6:
            return self.copy(number, at.step_core(1), at.step_core(number - 2))
        if number < 8:
            return self.piece(number, at.step_core(2 * number - 9), 0, at.step_core(2))
        if number < 10:
            return self.piece(number, at.step_core(2 * number - 14), 1, at.step_core(3))
        return self.copy(number, at.step_core(number - 9), at.twin)

    def start(self):
        at = self.place
        for part in range(2):
            src = None if self.source_half is None else self.source_half(part)
            self.piece(1, at.t, part, at.step_core(1), src).start()
        for number in (2, 3, 0):
            self.sent(number).start()

    def piece_arrived(self, index, part):
        self.piece(0, index, part, self.place.twin).wait_recv()

    def pass_on(self, i):
        at = self.place
        index = at.step_core(i)
        if i in (2, 3):
            self.copy(0, index, at.twin).wait_recv()
            self.sent(8 if i == 2 else 6).start()
        elif i == 1:
            for part in range(2):
                self.piece_arrived(index, part)
                self.piece(4, index, part, at.step_core(2)).start()
                self.piece(5, index, part, at.step_core(3)).start()
        elif i == 4:
            self.piece_arrived(index, 1)
            self.sent(9).start()
            self.piece_arrived(index, 0)
        elif i == 5:
            self.piece_arrived(index, 0)
            self.sent(7).start()
            self.piece_arrived(index, 1)
        else:
            self.piece_arrived(index, 0)
            self.piece_arrived(index, 1)
        self.sent(9 + i).start()

    def pass_on_at(self, i):
        for k in range(1, CHIPS):

            @pl.when(i == k - 1)
            def _(k=k):
                self.pass_on(k)

    def second(self, i):
        self.copy(0, 2 * self.place.step(i) + 1 - self.place.core, self.place.twin).wait_recv()

    def end(self):
        all_sent(self.most, self.send.at[0], self.place)


def whole_ring(place, ref, send, recv, source=None):
    return Ring(
        place,
        lambda b: ref.at[aligned(b, ROWS)],
        lambda b, part: ref.at[pl.ds(pl.multiple_of(b * ROWS + part * HEAD, HEAD), HEAD)],
        send,
        recv,
        ref.at[pl.ds(0, 15 * ROWS)],
        source,
        None if source is None else lambda part: source.at[pl.ds(part * HEAD, HEAD)],
    )


class Copies:
    def __init__(self, sems):
        self.sems, self.pending, self.free, self.used = sems, [], [], 0

    def start(self, src, dst):
        if self.free:
            number = self.free.pop()
        else:
            number, self.used = self.used, self.used + 1
        copy = pltpu.make_async_copy(src, dst, self.sems.at[number])
        copy.start()
        self.pending.append((copy, number))
        return copy

    def wait(self, count=None):
        count = len(self.pending) if count is None else count
        for copy, number in self.pending[:count]:
            copy.wait()
            self.free.append(number)
        self.pending = self.pending[count:]

    def need(self, *copies):
        for copy in copies:
            copy.wait()
            self.free += [number for other, number in self.pending if other is copy]
            self.pending = [pair for pair in self.pending if pair[0] is not copy]


def lanes(shape):
    return lax.broadcasted_iota(jnp.int32, shape, len(shape) - 1)


def sublanes(shape):
    return lax.broadcasted_iota(jnp.int32, shape, 0)


def swapped(values):
    return jnp.where(
        lanes(values.shape) < HEAD // 2,
        pltpu.roll(values, 2 * HEAD - HEAD // 2, 1),
        pltpu.roll(values, HEAD // 2, 1),
    )


def document_starts(seg):
    starts = jnp.zeros(seg.shape, F32)
    for document in range(8):
        before = jnp.sum(jnp.where(seg < document, 1.0, 0.0), axis=1, keepdims=True)
        starts = starts + jnp.where(seg == document, before, 0.0)
    return starts


def key_codes(mask, code):
    code[0:REACH, :] = jnp.full((REACH, ROWS), -1.0, F32)

    @pl.loop(0, TENSOR)
    def _(i):
        row = mask[:, aligned(i, ROWS)].astype(F32)
        live = jnp.broadcast_to(row, (ROWS, ROWS)).T == 1.0
        places = (sublanes((ROWS, ROWS)) + i * ROWS).astype(F32)
        code[pl.ds(pl.multiple_of(REACH + i * ROWS, ROWS), ROWS), :] = jnp.where(
            live, places, -1.0
        )


def allowed(code, start_row, chunk):
    ok = jnp.concatenate([code, code], axis=1) >= start_row
    if (chunk + 1) * CHUNK > REACH:
        key = sublanes((CHUNK, PAIR)) + (chunk * CHUNK - REACH)
        query = lanes((CHUNK, PAIR))
        ok = (ok & (key < query)) | (key == query)
    return ok


def turned_back(grad, r, here):
    cos, sin = r.cosine_t[:, here], r.sine_t[:, here]
    first, second = grad[0 : HEAD // 2], grad[HEAD // 2 : HEAD]
    return jnp.concatenate([first * cos + second * sin, second * cos - first * sin], axis=0)


class Halves:
    def __init__(self, place, parts, twins, sums, send, recv, credit):
        self.place, self.parts, self.twins, self.sums = place, parts, twins, sums
        self.send, self.recv, self.credit = send, recv, credit

    def half(self, k):
        at, slot = self.place, lax.rem(k, SLOTS)
        return remote(
            self.parts.at[slot, aligned(1 - at.core, ROWS), :],
            self.twins.at[slot],
            self.send.at[slot],
            self.recv.at[slot],
            TP,
            at.twin,
        )

    def put(self, k, value):
        @pl.when(k >= SLOTS)
        def _():
            self.half(k - SLOTS).wait_send()
            pl.semaphore_wait(self.credit, 1)

        self.parts[lax.rem(k, SLOTS)] = value.astype(BF)
        self.half(k).start()

    def add(self, k):
        slot = lax.rem(k, SLOTS)
        self.half(k).wait_recv()
        own = self.parts[slot, aligned(self.place.core, ROWS), :].astype(F32)
        self.sums(k)[...] = (own + self.twins[slot].astype(F32)).astype(BF)

        @pl.when(k < CHIPS - SLOTS)
        def _():
            pl.semaphore_signal(
                self.credit, inc=1, device_id={TP: self.place.twin}, device_id_type=MESH
            )

    def end(self):
        for k in range(CHIPS - SLOTS, CHIPS):
            self.half(k).wait_send()


class Joined:
    def __init__(self, place, sums, crossed, landed, sems):
        self.place, self.sums, self.crossed, self.landed = place, sums, crossed, landed
        self.c_send, self.c_recv, self.send, self.recv = sems

    def cross(self, j):
        return remote(
            self.sums.at[2 * j],
            self.crossed.at[j],
            self.c_send.at[j],
            self.c_recv.at[j],
            TP,
            self.place.near_core(0, 1),
        )

    def whole(self, j):
        return remote(
            self.sums.at[2 * j + 1],
            self.landed.at[j],
            self.send.at[j],
            self.recv.at[j],
            TP,
            self.place.near_core(SUM_Z[2 * j], 0),
        )

    def join(self, j):
        self.cross(j).wait_recv()
        total = self.sums[2 * j + 1].astype(F32) + self.crossed[j].astype(F32)
        self.sums[2 * j + 1] = total.astype(BF)
        self.whole(j).start()

    def result(self):
        self.cross(3).wait_recv()
        total = self.sums[7].astype(F32) + self.crossed[3].astype(F32)
        for j in range(3):
            self.whole(j).wait_recv()
            total = total + self.landed[j].astype(F32)
        return total

    def end(self):
        for j in range(4):
            self.cross(j).wait_send()
        for j in range(3):
            self.whole(j).wait_send()


def unpacked(both):
    return both[:, 0:8].reshape(ROWS, WIDTH), both[:, 8:16].reshape(ROWS, WIDTH)


def aligned_rows(ref, unit):
    def block(src, part=None):
        if part is None:
            return ref.at[pl.ds(pl.multiple_of(src * 2 * unit, unit), 2 * unit), :]
        return ref.at[pl.ds(pl.multiple_of((src * 2 + part) * unit, unit), unit), :]

    return block


def column_blocks(ref):
    def block(src, part=None):
        if part is None:
            return ref.at[:, aligned(src, ROWS)]
        return ref.at[pl.ds(part * PAIR, PAIR), aligned(src, ROWS)]

    return block


class Stream:
    def __init__(self, place, own, block, most, r, number):
        self.place, self.own, self.block, self.most = place, own, block, most
        self.send, self.recv = r.e_send, r.e_recv
        self.number, self.first_recv = number, 10 * number

    def at_y(self, k, other=False):
        at = self.place
        column = 1 - at.x if other else at.x
        return 2 * at.y_at(k) + column

    def copy(self, number, src, dest, part=None, source=None):
        ref = self.block(src, part)
        return remote(
            ref if source is None else source,
            ref,
            self.send.at[self.number],
            self.recv.at[self.first_recv + (8 + lax.rem(src, 2) if part else src)],
            SP,
            dest,
        )

    def sent(self, number):
        at, at_y = self.place, self.at_y
        if number == 0:
            return self.copy(0, at.d, at.across, source=self.own)
        if number < 3:
            return self.copy(number, at.d, at_y(2 * number - 1), source=self.own)
        if number < 5:
            return self.copy(number, at.across, at_y(2 * number - 5))
        other = number > 6
        if number % 2:
            return self.copy(number, at_y(3, other), at_y(1), 0)
        return self.copy(number, at_y(1, other), at_y(3), 1)

    def arrived(self, src, halves=False):
        for part in (0, 1) if halves else (None,):
            self.copy(0, src, self.place.across, part).wait_recv()

    def start_x(self):
        self.sent(0).start()

    def start_y(self):
        self.sent(1).start()
        self.sent(2).start()

    def from_across(self):
        self.arrived(self.place.across)
        self.sent(3).start()
        self.sent(4).start()

    def from_y(self):
        self.arrived(self.at_y(3))
        self.sent(5).start()
        self.arrived(self.at_y(1))
        self.sent(6).start()

    def from_y_across(self):
        self.arrived(self.at_y(3, True))
        self.sent(7).start()
        self.arrived(self.at_y(1, True))
        self.sent(8).start()

    def finish(self):
        self.arrived(self.at_y(2), True)
        self.arrived(self.at_y(2, True), True)

    def end(self):
        all_sent(self.most, self.send.at[self.number], self.place)


def expert_streams(at, r, e):
    downs = r.downs.at[pl.ds(e * UNITS, UNITS)]
    return (
        Stream(
            at,
            r.gu.at[e],
            aligned_rows(r.gus.at[e], HEAD),
            r.gus.at[e, pl.ds(0, 7 * ROWS)],
            r,
            2 * e,
        ),
        Stream(
            at,
            r.down.at[e],
            column_blocks(downs),
            downs.at[:, pl.ds(0, 7 * ROWS)],
            r,
            2 * e + 1,
        ),
    )


def layer_kernel(r):
    at = Place()
    t, d = at.t, at.d
    copies = Copies(r.local)
    r.load()
    r.hidden_all[aligned(t, ROWS), :] = r.hid[...]
    keyval, out_rows = r.w_keyval[...].astype(F32), r.w_out_t[...].astype(F32)
    r.rows[...] = jnp.concatenate([keyval, out_rows], axis=0).astype(BF)
    r.row_dp[d] = r.rows[...]
    r.shares[...] = jnp.zeros((8, ROWS), F32)
    r.shares[:, 0:32] = r.router[...].astype(F32)
    same = sublanes((8, 8)) == lanes((8, 8))
    for column, gain in ((32, r.gain_one), (33, r.gain_two)):
        wide = jnp.broadcast_to(gain[...].astype(F32), (8, 8))
        r.shares[:, column : column + 1] = jnp.sum(
            jnp.where(same, wide, 0.0), axis=1, keepdims=True
        )
    for j in range(CHIPS):
        tile = jnp.concatenate([keyval[:, j * ROWS : (j + 1) * ROWS], r.shares[...]], axis=0)
        r.tiles[2 * j] = tile.astype(BF)
        r.tiles[2 * j + 1] = tile.astype(BF)
    r.tile_all[d, t] = r.tiles[t]
    r.wq_all[HEAD : 2 * HEAD, :] = jnp.zeros((HEAD, WIDTH), BF)
    r.wq_all[0:HEAD, aligned(d, ROWS)] = r.w_query_t[...]
    at.enter()

    def tile_one(k, src):
        dest = at.tensor_at(k)
        return remote(
            r.tiles.at[dest],
            r.tile_all.at[d, src],
            r.t1_send.at[0],
            r.t1_recv.at[0],
            TP,
            dest,
        )

    def y_peer(k):
        return 2 * at.y_at(k) + at.x

    def tile_two(src, dest, recv):
        ref = r.tile_all.at[src]
        return remote(ref, ref, r.t2_send.at[0], recv.at[0], SP, dest)

    def rows_dp(src, dest, recv, source=None):
        ref = r.row_dp.at[src]
        return remote(
            ref if source is None else source, ref, r.rd_send.at[0], recv.at[0], SP, dest
        )

    def wq_dp(k, src):
        return remote(
            r.w_query_t,
            r.wq_all.at[pl.ds(0, HEAD), aligned(src, ROWS)],
            r.wq_send.at[0],
            r.wq_recv.at[0],
            SP,
            at.dp_at(k),
        )

    first_expert, second_expert = expert_streams(at, r, 0), expert_streams(at, r, 1)

    for k in range(1, TENSOR):
        tile_one(k, t).start()
    for k in range(1, DP):
        wq_dp(k, d).start()
    ring_h = whole_ring(at, r.hidden_all, r.h_send, r.h_recv)
    ring_h.start()
    for e in range(2):
        copies.start(r.gu.at[e], r.gus.at[e, aligned(d, ROWS)])
        copies.start(r.down.at[e], r.downs.at[pl.ds(e * UNITS, UNITS), aligned(d, ROWS)])
    copies.start(r.cot, r.cots.at[aligned(t, ROWS)])

    key_codes(r.mask, r.code)
    r.starts[...] = document_starts(r.seg[...])
    r.keyvals[0:REACH, :] = jnp.zeros((REACH, 2 * HEAD), BF)
    r.keyvals_t[:, 0:REACH] = jnp.zeros((2 * HEAD, REACH), BF)

    all_landed(r.tile_all.at[0, pl.ds(0, 15)], r.t1_recv.at[0], at)
    tile_two(d, at.across, r.t2x_recv).start()
    rows_dp(d, at.across, r.rdx_recv, r.rows).start()
    for k in range(1, 4):
        tile_two(d, y_peer(k), r.t2_recv).start()
        rows_dp(d, y_peer(k), r.rd_recv, r.rows).start()
    for stream in first_expert:
        stream.start_x()
    for i in range(1, 4):
        ring_h.pass_on(i)
    tile_two(at.across, at.across, r.t2x_recv).wait_recv()
    for k in range(1, 4):
        tile_two(at.across, y_peer(k), r.t2_recv).start()
    rows_dp(at.across, at.across, r.rdx_recv).wait_recv()
    for k in range(1, 4):
        rows_dp(at.across, y_peer(k), r.rd_recv).start()
    for stream in first_expert:
        stream.start_y()
    seven_wq = r.wq_all.at[pl.ds(0, HEAD), pl.ds(0, 7 * ROWS)]
    all_landed(seven_wq, r.wq_recv.at[0], at)
    all_landed(r.tile_all.at[pl.ds(0, 6)], r.t2_recv.at[0], at)
    for j in range(DP):
        both = r.tile_all[j].astype(F32)
        r.wqk[j * ROWS : (j + 1) * ROWS, ROWS:PAIR] = both[:, 0:8].reshape(ROWS, ROWS).astype(BF)
        r.small[j * ROWS : (j + 1) * ROWS, :] = both[:, 8:16].reshape(ROWS, ROWS).astype(BF)
    r.wqk[:, 0:ROWS] = r.wq_all[...].astype(F32).T.astype(BF)
    columns = r.small[...].astype(F32).T
    gain_one = columns[32:33, :]
    gain_two = columns[33:34, :]
    r.need("turns")
    ring_o = Ring(
        at,
        lambda b: r.out_all.at[b // 2, aligned(lax.rem(b, 2), HEAD)],
        lambda b, part: r.out_all.at[b // 2, aligned(2 * lax.rem(b, 2) + part, 32)],
        r.o_send,
        r.o_recv,
        r.nm_all.at[pl.ds(0, 15 * HEAD)],
    )

    ring_c = whole_ring(at, r.cots, r.c_send, r.c_recv, r.cot)
    @pl.loop(0, CHIPS)
    def _(i):
        @pl.when(i == 1)
        def _():
            ring_h.pass_on(4)
            ring_h.pass_on(5)

        @pl.when(i == 2)
        def _():
            all_landed(r.row_dp.at[pl.ds(0, 6)], r.rd_recv.at[0], at)
            both = r.row_dp[...].astype(F32)
            r.wqkv_own[0:HEAD, :] = r.wq_all[0:HEAD, :]
            r.wqkv_own[HEAD : 2 * HEAD, :] = both[:, 0:8].reshape(HEAD, WIDTH).astype(BF)
            r.out_all[at.chip, aligned(at.core, HEAD), :] = (
                both[:, 8:16].reshape(HEAD, WIDTH).astype(BF)
            )
            ring_o.start()

        @pl.when(i == 4)
        def _():
            ring_c.start()

        @pl.when(i == 5)
        def _():
            ring_h.pass_on(6)
            ring_h.pass_on(7)

        ring_h.second(i)
        block = at.step(i)
        here = aligned(block, PAIR)
        hidden = r.hidden_all[here, :].astype(F32)
        inverse = lax.rsqrt(jnp.mean(hidden * hidden, axis=1, keepdims=True) + 1e-6)
        unit = (hidden * inverse * gain_one).astype(BF)
        r.normed[here, :] = unit
        table = r.turns[here, :]
        turned = lanes(table.shape) < HEAD
        cos = jnp.where(turned, table, 1.0)
        sin = jnp.where(turned, pltpu.roll(table, HEAD, 1), 0.0)
        projected = dot(unit, r.wqk[...])
        query, keyval = projected[:, 0:ROWS], projected[:, ROWS:PAIR]
        query = (query * cos + swapped(query) * sin).astype(BF)
        r.queries[here, :] = (query.astype(F32) * (1.0 / math.sqrt(HEAD))).astype(BF)
        keyval = keyval * cos + swapped(keyval) * sin
        later = pl.ds(pl.multiple_of(REACH + block * PAIR, ROWS), PAIR)
        r.keyvals[later, :] = keyval.astype(BF)
        r.keyvals_t[:, later] = keyval.T.astype(BF)

    r.save("normed")

    def att_copy(dest, src):
        return remote(
            r.att_src.at[dest],
            r.att_t.at[aligned(src, HEAD), :],
            r.a_send.at[0],
            r.a_recv.at[0],
            TP,
            dest,
        )

    @pl.loop(0, CHIPS)
    def _(i):
        @pl.when(i == 0)
        def _():
            for stream in first_expert:
                stream.from_across()

        @pl.when(i == 1)
        def _():
            for k in range(1, 4):
                ring_o.pass_on(k)

        @pl.when(i == 3)
        def _():
            for stream in first_expert:
                stream.from_y()

        @pl.when(i == 5)
        def _():
            ring_o.pass_on(4)
            ring_o.pass_on(5)

        block = at.chip_at(i + 1)
        here = aligned(block, PAIR)
        query = r.queries[here, :]
        start_row = r.starts[:, here]
        top = jnp.full((1, PAIR), LOWEST, F32)
        for chunk in range(SPAN // CHUNK):
            keys = pl.ds(pl.multiple_of(block * PAIR + chunk * CHUNK, ROWS), CHUNK)
            score = dot(r.keyvals[keys, :], query, NT)
            score = jnp.where(allowed(r.code[keys, :], start_row, chunk), score, LOWEST)
            r.scores[chunk * CHUNK : (chunk + 1) * CHUNK, :] = score
            top = jnp.maximum(top, jnp.max(score, axis=0, keepdims=True))
        total = jnp.zeros((1, PAIR), F32)
        for chunk in range(SPAN // CHUNK):
            place = slice(chunk * CHUNK, (chunk + 1) * CHUNK)
            weight = jnp.exp(r.scores[place, :] - top)
            total = total + jnp.sum(weight, axis=0, keepdims=True)
            r.weighted[place, 0:PAIR] = weight.astype(BF)
        window = pl.ds(pl.multiple_of(block * PAIR, ROWS), SPAN)
        head = dot(r.keyvals_t[HEAD : 2 * HEAD, window], r.weighted[0:SPAN, 0:PAIR]) / total
        r.heads_t[:, here] = head
        r.stats[:, here] = top + jnp.log(total)
        r.att_src[2 * block] = head[:, 0:ROWS].astype(BF)
        r.att_src[2 * block + 1] = head[:, ROWS:PAIR].astype(BF)

        @pl.when(i < CHIPS - 1)
        def _():
            att_copy(2 * block, t).start()
            att_copy(2 * block + 1, t).start()

        @pl.when(i == CHIPS - 1)
        def _():
            att_copy(at.twin, t).start()

    ring_c.pass_on(1)
    r.att_t[aligned(t, HEAD), :] = r.att_src[t]
    ring_o.pass_on(6)
    ring_o.pass_on(7)
    for stream in first_expert:
        stream.from_y_across()
    for i in range(CHIPS):
        ring_o.second(i)

    @pl.loop(0, 4)
    def _(j):
        sides = [
            r.out_all[:, pl.ds(pl.multiple_of(core * HEAD + j * 16, 16), 16), :].astype(F32)
            for core in range(2)
        ]
        first, second = unpacked(jnp.stack(sides, axis=1).reshape(TENSOR, 16, WIDTH))
        r.out_t[aligned(2 * j, ROWS), :] = first.astype(BF)
        r.out_t[aligned(2 * j + 1, ROWS), :] = second.astype(BF)

    r.save("out_t")
    all_landed(r.att_t.at[pl.ds(0, 15 * HEAD)], r.a_recv.at[0], at)
    attended = r.att_t[...].astype(F32).T.astype(BF)
    r.att_rows[...] = attended
    middle = r.hid[...].astype(F32) + dot(attended, r.out_t[...], NT)
    r.mid[...] = middle
    inverse = lax.rsqrt(jnp.mean(middle * middle, axis=1, keepdims=True) + 1e-6)
    r.nm_all[aligned(t, ROWS), :] = (middle * inverse * gain_two).astype(BF)
    ring = whole_ring(at, r.nm_all, r.g_send, r.g_recv)
    ring.start()
    for stream in second_expert:
        stream.start_x()
        stream.start_y()
    ring_c.pass_on(2)
    ring_c.pass_on(3)
    for stream in first_expert:
        stream.finish()
    copies.wait()
    ring_h.end()
    ring_o.end()
    r.finish("normed")
    r.finish("out_t")
    r.proj_grads, r.n_first, r.gates, r.n_sums = r.hidden_all, r.normed, r.turns, r.out_all
    r.m_sums = r.out_t


    def moe_sums(k, count=1):
        return r.m_sums.at[pl.ds(pl.multiple_of(k * ROWS, ROWS), count * ROWS)]

    halves_n = Halves(at, r.n_parts, r.n_twins, lambda k: r.n_sums.at[k], r.ntw_send, r.ntw_recv, r.n_credit)
    halves_m = Halves(at, r.m_parts, r.m_twins, moe_sums, r.mtw_send, r.mtw_recv, r.m_credit)
    joined = Joined(
        at,
        r.n_sums,
        r.n_crossed,
        r.n_landed,
        (r.nc_send, r.nc_recv, r.n_send, r.n_recv),
    )
    ring_w = whole_ring(at, r.wqkv, r.h_send, r.h_recv, r.wqkv_own)
    own_weights = copies.start(r.wqkv_own, r.wqkv.at[aligned(t, ROWS)])

    def moe_first():
        return remote(
            moe_sums(0, 2),
            r.m_landed.at[0],
            r.m_send.at[0],
            r.m_recv.at[0],
            TP,
            at.near_core(SUM_Z[0], 0),
        )

    def moe_along(j, part):
        number = 2 * j - 1 + part
        return remote(
            moe_sums(2 * j + part),
            r.m_landed.at[j, pl.ds(part * ROWS, ROWS)],
            r.m_send.at[number],
            r.m_recv.at[number],
            TP,
            at.near_core(SUM_Z[2 * j], 0),
        )

    def gu_over_y(e, k):
        y = at.y_at(k)
        return remote(
            r.gus.at[e, aligned(y, PAIR), :],
            r.y_gu.at[e, k - 1],
            r.x_send.at[4 * e + k],
            r.x_recv.at[4 * e + k],
            SP,
            2 * y + at.x,
        )

    def down_over_y(e, k):
        y = at.y_at(k)
        return remote(
            r.down_grads.at[e, :, aligned(y, PAIR)],
            r.y_down.at[e, k - 1],
            r.y_send.at[4 * e + k],
            r.y_recv.at[4 * e + k],
            SP,
            2 * y + at.x,
        )

    def across_x(number, src, dst):
        return remote(src, dst, r.tx_send.at[number], r.tx_recv.at[number], SP, at.across)

    def gu_half(part):
        rows = pl.ds(part * HEAD, HEAD)
        return remote(
            r.ys_gu.at[1, 1 - at.x, rows],
            r.yx_gu.at[1, rows],
            r.tx_send.at[1 + 3 * part],
            r.tx_recv.at[1 + 3 * part],
            SP,
            at.across,
        )

    def gu_across(e):
        return across_x(e, r.ys_gu.at[e, 1 - at.x], r.yx_gu.at[e])

    def down_across(e):
        return across_x(2 + e, r.ys_down.at[e, 1 - at.x], r.yx_down.at[e])

    def gate_copy(dest, src):
        return remote(
            r.gate_src.at[dest],
            r.gate_all.at[src],
            r.gg_send.at[0],
            r.gg_recv.at[0],
            TP,
            dest,
        )

    def one_pass(e):
        @pl.loop(0, CHIPS)
        def _(i):
            if e == 0:
                for k in range(2, CHIPS):

                    @pl.when(i == k - 1)
                    def _(k=k):
                        ring.pass_on(k)

                ring.second(i)

                @pl.when(i == 1)
                def _():
                    ring_c.pass_on(4)
                    ring_c.pass_on(5)

                @pl.when(i == 2)
                def _():
                    for stream in second_expert:
                        stream.from_across()

                @pl.when(i == 4)
                def _():
                    for stream in second_expert:
                        stream.from_y()

                @pl.when(i == 5)
                def _():
                    ring_c.pass_on(6)
                    ring_c.pass_on(7)

                ring_c.second(i)

                @pl.when(i == 6)
                def _():
                    ring_w.start()

            here = aligned(at.step(i) if e == 0 else at.sum_step(i), PAIR)
            nm = r.nm_all[here, :]
            place = lanes((PAIR, ROWS))
            if e == 0:
                expert = sublanes((ROWS, PAIR))
                named = expert == r.routes_t[0:1, here]
                for j in range(1, 8):
                    named = named | (expert == r.routes_t[j : j + 1, here])
                named = jnp.where(named, 1.0, 0.0).T > 0.5
                logits = jnp.where(named, dot(nm, r.small[...]), LOWEST)
                powers = jnp.exp(logits - jnp.max(logits, axis=1, keepdims=True))
                powers = jnp.where(named, powers, 0.0)
                gates = powers / jnp.sum(powers, axis=1, keepdims=True)
            else:
                kept = r.gates[here, :]
                gates = jnp.where(place == 2 * HEAD - 1, 0.0, kept)
                earlier = kept[:, 2 * HEAD - 1 : 2 * HEAD]
            mine = place == 2 * t + e
            gate = jnp.sum(jnp.where(mine, gates, 0.0), axis=1, keepdims=True)
            act_grad = dot(r.cots[here, :], r.downs[e * UNITS : (e + 1) * UNITS, :], NT)
            projected = dot(nm, r.gus[e])
            first, up = projected[:, :UNITS], projected[:, UNITS:]
            sigmoid = 1.0 / (1.0 + jnp.exp(-first))
            silu = first * sigmoid
            activated = silu * up
            gate_grad = jnp.sum(activated * act_grad, axis=1, keepdims=True)
            weighted = (activated * gate).astype(BF)
            r.weighted_t[:, here] = weighted.T
            act_grad = act_grad * gate
            r.proj_grads[here, 0:UNITS] = (
                act_grad * up * (sigmoid * (1.0 + first * (1.0 - sigmoid)))
            ).astype(BF)
            r.proj_grads[here, UNITS:WIDTH] = (act_grad * silu).astype(BF)
            normed_part = dot(r.proj_grads[here, :], r.gus[e], NT)
            if e == 0:
                r.gates[here, :] = jnp.where(place == 2 * HEAD - 1, gate_grad, gates)
                r.weighted[here, :] = weighted
                r.n_first[here, :] = normed_part.astype(BF)

                @pl.when(i == 0)
                def _():
                    ring.pass_on(1)

                return
            row = 2 * lax.rem(t, 4)
            gate_grads = jnp.where(
                place == row, earlier, jnp.where(place == row + 1, gate_grad, 0.0)
            ).T
            chip = at.sum_step(i)
            r.gate_src[2 * chip] = gate_grads[0:8, 0:ROWS]
            r.gate_src[2 * chip + 1] = gate_grads[0:8, ROWS:PAIR]

            @pl.when(i < CHIPS - 1)
            def _():
                gate_copy(2 * chip, t).start()
                gate_copy(2 * chip + 1, t).start()

            @pl.when(i == CHIPS - 1)
            def _():
                gate_copy(at.twin, t).start()

            halves_n.put(i, normed_part + r.n_first[here, :].astype(F32))
            both = jnp.concatenate([r.weighted[here, :], weighted], axis=1)
            halves_m.put(i, dot(both, r.downs[...]))

            @pl.when(i > 0)
            def _():
                halves_n.add(i - 1)
                halves_m.add(i - 1)

            for j in range(4):

                @pl.when(i == 2 * j + 1)
                def _(j=j):
                    joined.cross(j).start()

            for j in range(2):

                @pl.when(i == 2 * j + 4)
                def _(j=j):
                    joined.join(j)

            @pl.when(i == 2)
            def _():
                moe_first().start()

            for step, chips in ((0, (2, 3)), (2, (4, 5))):

                @pl.when(i == step)
                def _(chips=chips):
                    for k in chips:
                        ring_w.pass_on(k)

    def down_gradients(e):
        @pl.loop(0, 2)
        def _(j):
            strip = aligned(j, PAIR)
            r.down_grads[e, strip, :] = dot(r.weighted_t[strip, :], r.cots[...]).astype(BF)

    def gate_up_gradients(e):
        @pl.loop(0, 4)
        def _(j):
            strip = aligned(j, PAIR)
            r.gus[e, strip, :] = dot(r.nm_all[:, strip], r.proj_grads[...], TN).astype(BF)

    one_pass(0)
    for stream in second_expert:
        stream.from_y_across()
    for stream in first_expert:
        stream.end()
    down_gradients(0)
    for k in range(1, 4):
        down_over_y(0, k).start()
    gate_up_gradients(0)
    ring_w.pass_on(1)
    for k in range(1, 4):
        gu_over_y(0, k).start()
    for stream in second_expert:
        stream.finish()
    one_pass(1)
    joined.join(2)
    halves_n.add(CHIPS - 1)
    halves_m.add(CHIPS - 1)
    def gu_loads(e):
        ref, first = (r.n_first, WIDTH) if e == 0 else (r.proj_grads, 0)
        places = [ref.at[pl.ds(first + k * PAIR, PAIR)] for k in range(3)]
        loads = []
        for k in range(3):
            gu_over_y(e, k + 1).wait_recv()
            loads.append(copies.start(r.y_gu.at[e, k], places[k]))
        return places, loads

    def gu_sums(e, places, loads):
        copies.need(*loads)
        total = r.gus[e, aligned(at.y, PAIR), :].astype(F32)
        for place in places:
            total = total + place[...].astype(F32)
        r.ys_gu[e, 0] = total[0:ROWS].astype(BF)
        r.ys_gu[e, 1] = total[ROWS:PAIR].astype(BF)
        (gu_half(0) if e else gu_across(0)).start()

    def down_loads(e):
        places = [
            r.weighted.at[pl.ds(k * UNITS, UNITS), pl.ds(e * PAIR, PAIR)] for k in range(3)
        ]
        loads = []
        for k in range(3):
            down_over_y(e, k + 1).wait_recv()
            loads.append(copies.start(r.y_down.at[e, k], places[k]))
        return places, loads

    def down_sums(e, places, loads):
        copies.need(*loads)
        total = r.down_grads[e, :, aligned(at.y, PAIR)].astype(F32)
        for place in places:
            total = total + place[...].astype(F32)
        r.ys_down[e, 0] = total[:, 0:ROWS].astype(BF)
        r.ys_down[e, 1] = total[:, ROWS:PAIR].astype(BF)
        down_across(e).start()

    out_rows = r.n_first.at[pl.ds(0, WIDTH)]
    out_load = copies.start(r.out_t_d, out_rows)
    for stream in second_expert:
        stream.end()
    down_gradients(1)
    for k in range(1, 4):
        down_over_y(1, k).start()
    gate_up_gradients(1)
    first_down, first_gu = down_loads(0), gu_loads(0)
    for k in range(1, 4):
        gu_over_y(1, k).start()
    r.gate_all[t] = r.gate_src[t]
    all_landed(r.gate_all.at[pl.ds(0, 15)], r.gg_recv.at[0], at)
    groups = r.gate_all[...].reshape(4, 4, 8, ROWS)
    gate_grads = (groups[:, 0] + groups[:, 1] + groups[:, 2] + groups[:, 3]).reshape(32, ROWS)
    gate_grads = jnp.concatenate([gate_grads, jnp.zeros((ROWS - 32, ROWS), F32)], axis=0).T
    own_rows = aligned(t, ROWS)
    gates = jnp.where(lanes((ROWS, ROWS)) < 32, r.gates[own_rows, :], 0.0)
    mean = jnp.sum(gates * gate_grads, axis=1, keepdims=True)
    logit_grad = gates * (gate_grads - mean)
    r.router_t[...] = dot(logit_grad.T.astype(BF), r.nm_all[own_rows, :])[0:32, :]
    by_router = dot(logit_grad.astype(BF), r.small[...], NT)

    gain_two = r.small[...].astype(F32).T[33:34, :]
    normed_grad = joined.result() + by_router
    middle = r.mid[...]
    inverse = lax.rsqrt(jnp.mean(middle * middle, axis=1, keepdims=True) + 1e-6)
    unit = middle * inverse
    r.gain_grad[...] = jnp.sum(normed_grad * unit, axis=0, keepdims=True)
    scaled = normed_grad * gain_two
    grad = r.cots[aligned(t, ROWS), :].astype(F32) + inverse * (
        scaled - unit * jnp.mean(scaled * unit, axis=1, keepdims=True)
    )
    r.mid_grad[...] = grad
    turned = grad.T.reshape(DP, TENSOR, 8, ROWS).transpose(1, 0, 2, 3)
    r.att_grad_t, r.mid_t = r.att_t, r.wqk.at[:, pl.ds(0, ROWS)]
    r.mid_t[...] = turned.reshape(WIDTH, ROWS).astype(BF)
    copies.need(out_load)
    r.att_grad_t[...] = dot(grad.astype(BF), out_rows[...]).T.astype(BF)

    def back_copy(k, src):
        dest = at.tensor_at(k)
        return remote(
            r.att_grad_t.at[aligned(dest, HEAD), :],
            r.grads.at[:, aligned(src, ROWS)],
            r.b_send.at[0],
            r.b_recv.at[0],
            TP,
            dest,
        )

    for k in range(1, TENSOR):
        back_copy(k, t).start()
    r.grads[:, aligned(t, ROWS)] = r.att_grad_t[aligned(t, HEAD), :]
    joined.end()
    r.n_sums[...] = (
        dot(r.mid_t[...], r.att_rows[...]).reshape(CHIPS, ROWS, WIDTH).astype(BF)
    )

    def out_half():
        return remote(
            r.n_sums.at[:, aligned(1 - at.core, HEAD), :],
            r.out_twins,
            r.ot_send.at[0],
            r.ot_recv.at[0],
            TP,
            at.twin,
        )

    out_half().start()
    r.kv_sum, r.query_src = r.gates, r.att_src
    r.tail_left = r.weighted_t.at[pl.ds(0, 3 * HEAD)]
    r.kv_sum[...] = jnp.zeros((LENGTH, 2 * HEAD), F32)
    all_sent(r.att_src.at[pl.ds(0, 15)], r.a_send.at[0], at)
    halves_n.end()
    halves_m.end()
    r.tail = r.n_parts.at[0]
    r.s_gu, r.m_joined = r.m_parts.at[0, pl.ds(0, ROWS)], r.m_parts.at[0, pl.ds(ROWS, ROWS)]

    down_sums(0, *first_down)
    gu_sums(0, *first_gu)
    normed_load = copies.start(r.normed_d, r.normed)

    def out_along(k):
        return remote(
            r.out_twins.at[pl.ds(2 * lax.rem(at.z + k, 4), 2)],
            r.out_landed.at[k - 1],
            r.oz_send.at[k],
            r.oz_recv.at[k],
            TP,
            at.near_core(k, 0),
        )

    def out_across():
        return remote(
            r.out_joined, r.out_crossed, r.oz_send.at[0], r.oz_recv.at[0], TP, at.near_core(0, 1)
        )

    out_half().wait_recv()
    r.out_twins[...] = (
        r.n_sums[:, aligned(at.core, HEAD), :].astype(F32) + r.out_twins[...].astype(F32)
    ).astype(BF)
    for k in range(1, 4):
        out_along(k).start()
    all_landed(r.grads.at[:, pl.ds(0, 15 * ROWS)], r.b_recv.at[0], at)
    r.need("cosine_t", "sine_t")

    def query_copy(dest, src):
        return remote(
            r.query_src.at[dest],
            r.query_all.at[src],
            r.qb_send.at[0],
            r.qb_recv.at[0],
            TP,
            dest,
        )

    @pl.loop(0, CHIPS)
    def _(i):
        block = at.chip_at(i + 1)
        here = aligned(block, PAIR)
        query = r.queries[here, :]
        start_row = r.starts[:, here]
        stat = r.stats[:, here]
        grad_t = jnp.concatenate([jnp.zeros((HEAD, PAIR), BF), r.grads[:, here]], axis=0)
        grad_rows = grad_t.astype(F32).T.astype(BF)
        head = r.heads_t[:, here]
        delta = jnp.sum(head * grad_t[HEAD : 2 * HEAD, :].astype(F32), axis=0, keepdims=True)
        query_grad = jnp.zeros((HEAD, PAIR), F32)
        for chunk in range(SPAN // CHUNK):
            keys = pl.ds(pl.multiple_of(block * PAIR + chunk * CHUNK, ROWS), CHUNK)
            both = r.keyvals[keys, :]
            score = dot(both, query, NT)
            ok = allowed(r.code[keys, :], start_row, chunk)
            prob = jnp.exp(jnp.where(ok, score - stat, LOWEST))
            prob_grad = dot(both, grad_t)
            score_grad = (prob * (prob_grad - delta)).astype(BF)
            update = dot(score_grad, query) + dot(prob.astype(BF), grad_rows)
            for part in range(CHUNK // ROWS):
                row = jnp.maximum(block * PAIR + (chunk * CHUNK + part * ROWS - REACH), 0)
                place = pl.ds(pl.multiple_of(row, ROWS), ROWS)
                r.kv_sum[place, :] += update[part * ROWS : (part + 1) * ROWS]

            query_grad = query_grad + dot(r.keyvals_t[0:HEAD, keys], score_grad)
        turned = turned_back(query_grad * (1.0 / math.sqrt(HEAD)), r, here).astype(BF)
        r.tail_left[0:HEAD, here] = turned
        r.query_src[2 * block] = turned[:, 0:ROWS]
        r.query_src[2 * block + 1] = turned[:, ROWS:PAIR]

        @pl.when(i < CHIPS - 1)
        def _():
            query_copy(2 * block, t).start()
            query_copy(2 * block + 1, t).start()

        @pl.when(i == CHIPS - 1)
        def _():
            query_copy(at.twin, t).start()

    @pl.loop(0, CHIPS)
    def _(i):
        here = aligned(i, PAIR)
        grad = r.kv_sum[here, :].T
        grad = jnp.concatenate(
            [turned_back(grad[0:HEAD], r, here), grad[HEAD : 2 * HEAD]], axis=0
        ).astype(BF)
        r.tail_left[HEAD : 3 * HEAD, here] = grad
        r.back_src[2 * i] = grad[:, 0:ROWS]
        r.back_src[2 * i + 1] = grad[:, ROWS:PAIR]

    def grad_copy(k, src):
        dest = at.tensor_at(k)
        return remote(
            r.back_src.at[dest],
            r.back_all.at[src],
            r.kb_send.at[0],
            r.kb_recv.at[0],
            TP,
            dest,
        )

    for k in range(1, TENSOR):
        grad_copy(k, t).start()
    r.back_all[t] = r.back_src[t]
    r.query_all[t] = r.query_src[t]
    for part in range(2):
        for j in (1, 2):
            moe_along(j, part).start()
    down_sums(1, *down_loads(1))
    landed = [
        [r.nm_all.at[pl.ds((2 * k + x) * HEAD, HEAD)] for x in range(2)] for k in range(3)
    ]
    ring.end()
    loads = []
    for k in range(3):
        out_along(k + 1).wait_recv()
        for x in range(2):
            loads.append(copies.start(r.out_landed.at[k, x], landed[k][x]))
    copies.need(*loads)

    def out_total(x):
        total = r.out_twins[2 * at.z + x].astype(F32)
        for k in range(3):
            rows = aligned(2 * k + x, HEAD)
            total = total + r.nm_all[rows, :].astype(F32)
        return total

    r.out_joined[...] = out_total(1 - at.x_far).astype(BF)
    out_across().start()
    for number in (6, 7):
        ring_w.pass_on(number)
    for i in range(CHIPS):
        ring_w.second(i)
    ring_c.end()
    copies.need(own_weights)
    weights_load = copies.start(r.wqkv, r.cots)
    copies.need(normed_load)
    r.tail[0 : 3 * HEAD, :] = dot(r.tail_left[...], r.normed[...]).astype(BF)

    copies.need(weights_load)
    whole = r.cots
    for j in range(4):
        rows = [
            whole[i * ROWS + HEAD + j * 16 : i * ROWS + HEAD + (j + 1) * 16, :].astype(F32)
            for i in range(TENSOR)
        ]
        first, second = unpacked(jnp.stack(rows, axis=0))
        r.downs[2 * j * ROWS : (2 * j + 1) * ROWS, :] = first.astype(BF)
        r.downs[(2 * j + 1) * ROWS : (2 * j + 2) * ROWS, :] = second.astype(BF)
    all_landed(r.query_all.at[pl.ds(0, 15)], r.qb_recv.at[0], at)
    all_landed(r.back_all.at[pl.ds(0, 15)], r.kb_recv.at[0], at)
    query_rows = r.query_all[...].astype(F32).reshape(WIDTH, ROWS).T.astype(BF)
    pairs = r.back_all[...].astype(F32).reshape(CHIPS, 2, ROWS, ROWS)
    kv_rows = (pairs[:, 0] + pairs[:, 1]).reshape(WIDTH, ROWS).T.astype(BF)
    wq_full = jnp.concatenate(
        [whole[i * ROWS : i * ROWS + HEAD, :] for i in range(TENSOR)], axis=0
    )
    normed_grad = dot(query_rows, wq_full) + dot(kv_rows, r.downs[...], NT)
    hidden = r.hid[...].astype(F32)
    inverse = lax.rsqrt(jnp.mean(hidden * hidden, axis=1, keepdims=True) + 1e-6)
    unit = hidden * inverse
    gain_one = r.small[...].astype(F32).T[32:33, :]
    gain_one_grad = jnp.sum(normed_grad * unit, axis=0, keepdims=True)
    scaled = normed_grad * gain_one
    r.hidden_grad[...] = (
        r.mid_grad[...]
        + inverse * (scaled - unit * jnp.mean(scaled * unit, axis=1, keepdims=True))
    ).astype(BF)
    r.save("hidden_grad")
    r.tail[3 * HEAD : 3 * HEAD + 32, :] = r.router_t[...].astype(BF)
    row = sublanes((16, WIDTH))
    r.tail[3 * HEAD + 32 : TAIL, :] = jnp.where(
        row == 0, gain_one_grad, jnp.where(row == 1, r.gain_grad[...], 0.0)
    ).astype(BF)

    def tail_along(k):
        y = at.y_at(k)
        return remote(
            r.tail.at[pl.ds(0, TAIL), aligned(y, PAIR)],
            r.tail_in.at[k - 1],
            r.t_send.at[k],
            r.t_recv.at[k],
            SP,
            2 * y + at.x,
        )

    def tail_across():
        return remote(r.tail_src, r.tail_x, r.t_send.at[0], r.t_recv.at[0], SP, at.across)

    for k in range(1, 4):
        tail_along(k).start()

    gu_sums(1, *gu_loads(1))
    out_across().wait_recv()
    crossed = r.proj_grads.at[pl.ds(6 * PAIR, HEAD)]
    copies.need(copies.start(r.out_crossed, crossed))
    r.out_rows[...] = out_total(at.x_far) + crossed[...].astype(F32)

    def out_dp_along(k):
        y = at.y_at(k)
        return remote(
            r.out_rows.at[aligned(y, 16), :],
            r.out_in.at[k - 1],
            r.od_send.at[k],
            r.od_recv.at[k],
            SP,
            2 * y + at.x,
        )

    def out_dp_across():
        return remote(
            r.out_sum.at[aligned(1 - at.x, 8), :],
            r.out_x,
            r.od_send.at[0],
            r.od_recv.at[0],
            SP,
            at.across,
        )

    for k in range(1, 4):
        out_dp_along(k).start()
    def moe_across():
        return remote(
            r.m_joined, r.m_crossed, r.mx_send.at[0], r.mx_recv.at[0], TP, at.near_core(0, 1)
        )

    moe_first().wait_recv()
    across = moe_sums(6)[...].astype(F32) + r.m_landed[0, 0:ROWS].astype(F32)
    for j in (1, 2):
        moe_along(j, 0).wait_recv()
        across = across + r.m_landed[j, 0:ROWS].astype(F32)
    r.m_joined[...] = across.astype(BF)
    moe_across().start()
    loads, crossed = [], []
    for e in range(2):
        down_across(e).wait_recv()
        crossed.append(r.weighted.at[pl.ds(3 * UNITS, UNITS), pl.ds(e * ROWS, ROWS)])
        loads.append(copies.start(r.yx_down.at[e], crossed[-1]))
    gu_across(0).wait_recv()
    crossed.append(r.nm_all.at[pl.ds(WIDTH, ROWS)])
    loads.append(copies.start(r.yx_gu.at[0], crossed[-1]))
    copies.need(*loads)
    for e in range(2):
        r.down_out[e] = r.ys_down[e, at.x].astype(F32) + crossed[e][...].astype(F32)
    r.mid_grad[...] = r.ys_gu[0, at.x].astype(F32) + crossed[2][...].astype(F32)
    copies.start(r.mid_grad, r.gu_out.at[0])
    r.save("down_out")
    total = r.tail[0:TAIL, aligned(at.y, PAIR)].astype(F32)
    for k in range(1, 4):
        tail_along(k).wait_recv()
        total = total + r.tail_in[k - 1].astype(F32)
    r.scores[0:TAIL, :] = total
    r.tail_src[...] = r.scores[0:TAIL, aligned(1 - at.x, ROWS)].astype(BF)
    tail_across().start()
    gu_half(1).start()
    total = r.out_rows[aligned(at.y, 16), :]
    for k in range(1, 4):
        out_dp_along(k).wait_recv()
        total = total + r.out_in[k - 1]
    r.out_sum[...] = total
    out_dp_across().start()
    tail_across().wait_recv()
    total = r.scores[0:TAIL, aligned(at.x, ROWS)] + r.tail_x[...].astype(F32)
    r.query_out[...] = total[0:HEAD, :]
    r.save("query_out")
    turned = jnp.concatenate(
        [total[HEAD:TAIL], jnp.zeros((256 + HEAD - TAIL, ROWS), F32)], axis=0
    ).T
    for j in range(TENSOR):
        r.pieces[j] = turned[j * 8 : (j + 1) * 8, :]

    def last_copy(k, src):
        dest = at.tensor_at(k)
        return remote(
            r.pieces.at[dest], r.last.at[src], r.l_send.at[0], r.l_recv.at[0], TP, dest
        )

    for k in range(1, TENSOR):
        last_copy(k, t).start()
    r.last[t] = r.pieces[t]

    own = r.mid[...] + moe_sums(7)[...].astype(F32) + r.m_landed[0, ROWS:PAIR].astype(F32)
    for j in (1, 2):
        moe_along(j, 1).wait_recv()
        own = own + r.m_landed[j, ROWS:PAIR].astype(F32)
    place = r.nm_all.at[pl.ds(WIDTH + PAIR, ROWS)]
    moe_across().wait_recv()
    copies.need(copies.start(r.m_crossed, place))
    r.output[...] = (own + place[...].astype(F32)).astype(BF)
    r.save("output")
    for part in range(2):
        gu_half(part).wait_recv()
    place = r.nm_all.at[pl.ds(WIDTH + ROWS, ROWS)]
    copies.need(copies.start(r.yx_gu.at[1], place))
    r.mid[...] = r.ys_gu[1, at.x].astype(F32) + place[...].astype(F32)
    copies.start(r.mid, r.gu_out.at[1])
    out_dp_across().wait_recv()
    r.out_grad[...] = r.out_sum[aligned(at.x, 8), :] + r.out_x[...]
    all_landed(r.last.at[pl.ds(0, 15)], r.l_recv.at[0], at)
    r.kv_out[...] = jnp.concatenate(
        [r.last[2 * j, :, 0:ROWS] + r.last[2 * j + 1, :, 0:ROWS] for j in range(CHIPS)], axis=1
    )
    shared = r.last[0, :, ROWS:PAIR]
    for j in range(1, TENSOR):
        shared = shared + r.last[j, :, ROWS:PAIR]
    r.router_out[...] = shared[:, 0:32]
    wide = jnp.concatenate([shared, jnp.zeros((ROWS - 8, ROWS), F32)], axis=0).T
    r.gain_one_out[...] = wide[32:33, 0:8]
    r.gain_two_out[...] = wide[33:34, 0:8]
    r.save("out_grad", "kv_out", "router_out", "gain_one_out", "gain_two_out")

    all_sent(r.tiles.at[pl.ds(0, 15)], r.t1_send.at[0], at)
    all_sent(r.tile_all.at[pl.ds(0, 7)], r.t2_send.at[0], at)
    all_sent(r.row_dp.at[pl.ds(0, 7)], r.rd_send.at[0], at)
    all_sent(seven_wq, r.wq_send.at[0], at)
    all_sent(r.gate_src.at[pl.ds(0, 15)], r.gg_send.at[0], at)
    all_sent(r.att_grad_t.at[pl.ds(0, 15 * HEAD)], r.b_send.at[0], at)
    all_sent(r.query_src.at[pl.ds(0, 15)], r.qb_send.at[0], at)
    all_sent(r.back_src.at[pl.ds(0, 15)], r.kb_send.at[0], at)
    all_sent(r.pieces.at[pl.ds(0, 15)], r.l_send.at[0], at)
    for k in range(1, 4):
        tail_along(k).wait_send()
        out_dp_along(k).wait_send()
    tail_across().wait_send()
    out_dp_across().wait_send()
    moe_first().wait_send()
    for j in (1, 2):
        for part in range(2):
            moe_along(j, part).wait_send()
    moe_across().wait_send()
    for k in range(1, 4):
        out_along(k).wait_send()
    out_across().wait_send()
    out_half().wait_send()
    for e in range(2):
        for k in range(1, 4):
            gu_over_y(e, k).wait_send()
            down_over_y(e, k).wait_send()
        gu_half(e).wait_send()
        down_across(e).wait_send()
    gu_across(0).wait_send()
    ring_w.end()
    copies.wait()
    r.end()


def store_kernel(r):
    copies = Copies(r.local)
    for name in STORED:
        copies.start(getattr(r, name), getattr(r, name + "_kept"))
    for name in STORED:
        copies.wait(1)
        copies.start(getattr(r, name + "_kept"), getattr(r, name + "_done"))
    copies.wait()


STORED = (
    "output",
    "hidden_grad",
    "gain_one_out",
    "query_out",
    "kv_out",
    "out_grad",
    "gain_two_out",
    "router_out",
    "gu_out",
    "down_out",
)


class Refs:
    def __init__(self, names, refs, loads=(), saves=()):
        for name, ref in zip(names, refs):
            setattr(self, name, ref)
        self.loads, self.saves, self.saved = list(loads), list(saves), []

    def copy_in(self, name):
        sem = self.load_sems.at[self.loads.index(name)]
        return pltpu.make_async_copy(getattr(self, name + "_d"), getattr(self, name), sem)

    def copy_out(self, name):
        sem = self.save_sems.at[self.saves.index(name)]
        return pltpu.make_async_copy(getattr(self, name), getattr(self, name + "_d"), sem)

    def load(self):
        for name in self.loads:
            self.copy_in(name).start()

    def need(self, *names):
        for name in names:
            self.copy_in(name).wait()

    def save(self, *names):
        for name in names:
            self.copy_out(name).start()
            self.saved.append(name)

    def finish(self, name):
        self.copy_out(name).wait()
        self.saved.remove(name)

    def end(self):
        for name in self.saved:
            self.copy_out(name).wait()


def call(kernel, number, inputs, outputs, scratch, reaches=True):
    def space(name):
        return pl.BlockSpec(memory_space=pltpu.VMEM if name.endswith("_v") else pl.ANY)

    outputs = {name: jax.ShapeDtypeStruct(shape, dtype) for name, (shape, dtype) in outputs.items()}
    loads = [name[:-2] for name in inputs if name.endswith("_d")]
    saves = [name[:-2] for name in outputs if name.endswith("_d")]
    scratch = dict(scratch)
    for name in loads:
        scratch[name] = pltpu.VMEM(inputs[name + "_d"].shape, inputs[name + "_d"].dtype)
    for name in saves:
        scratch[name] = pltpu.VMEM(outputs[name + "_d"].shape, outputs[name + "_d"].dtype)
    scratch |= sems(load_sems=max(1, len(loads)), save_sems=max(1, len(saves)))
    names = [name.removesuffix("_v") for name in (*inputs, *outputs)] + list(scratch)
    params = {"vmem_limit_bytes": VMEM_BYTES}
    if reaches:
        params |= {"collective_id": number, "has_side_effects": True}
    values = pl.pallas_call(
        lambda *refs: kernel(Refs(names, refs, loads, saves)),
        out_shape=list(outputs.values()),
        in_specs=[space(name) for name in inputs],
        out_specs=[space(name) for name in outputs],
        scratch_shapes=list(scratch.values()),
        compiler_params=pltpu.CompilerParams(**params),
        name=kernel.__name__,
    )(*inputs.values())
    return Refs([name.removesuffix("_v").removesuffix("_d") for name in outputs], values)


def sems(**counts):
    return {name: pltpu.SemaphoreType.DMA((count,)) for name, count in counts.items()}


def rope_tables():
    half = HEAD // 2
    freqs = np.exp(
        np.arange(half, dtype=np.float32) * np.float32(-2.0 * math.log(10000.0) / HEAD)
    ).astype(np.float32)
    angles = np.arange(LENGTH, dtype=np.float32)[:, None] * freqs[None, :]
    cos, sin = np.cos(angles).astype(np.float32), np.sin(angles).astype(np.float32)
    return (
        np.concatenate([cos, cos, -sin, sin], axis=1),
        np.ascontiguousarray(cos.T),
        np.ascontiguousarray(sin.T),
    )


def body(
    hidden,
    seg_ids,
    key_mask,
    routes,
    gain_attn,
    w_query,
    w_keyval,
    w_out,
    gain_mlp,
    w_router,
    w_gate_up,
    w_down,
    cotangent,
):
    V = pltpu.VMEM
    turns, cosine_t, sine_t = rope_tables()
    hid, cot = hidden[0], cotangent[0]
    c = call(
        layer_kernel,
        1,
        dict(
            hid_v=hid,
            cot=cot,
            w_keyval_v=w_keyval,
            w_out_t_v=w_out.T,
            w_query_t_v=w_query.T,
            router_v=w_router,
            gain_one_v=gain_attn.reshape(1, 8),
            gain_two_v=gain_mlp.reshape(1, 8),
            gu=w_gate_up,
            down=w_down,
            turns_d=turns,
            cosine_t_d=cosine_t,
            sine_t_d=sine_t,
            mask_v=key_mask,
            seg_v=seg_ids,
            routes_t_v=routes[0].T,
        ),
        dict(
            output_d=((ROWS, WIDTH), BF),
            hidden_grad_d=((ROWS, WIDTH), BF),
            gain_one_out_d=((1, 8), F32),
            query_out_d=((HEAD, ROWS), F32),
            kv_out_d=((8, WIDTH), F32),
            out_grad_d=((8, WIDTH), F32),
            gain_two_out_d=((1, 8), F32),
            router_out_d=((8, 32), F32),
            gu_out=((2, ROWS, WIDTH), F32),
            down_out_d=((2, UNITS, ROWS), F32),
            normed_d=((LENGTH, WIDTH), BF),
            out_t_d=((WIDTH, WIDTH), BF),
            wqkv=((LENGTH, WIDTH), BF),
            y_gu=((2, 3, PAIR, WIDTH), BF),
            y_down=((2, 3, UNITS, PAIR), BF),
            yx_gu=((2, ROWS, WIDTH), BF),
            yx_down=((2, UNITS, ROWS), BF),
            out_landed=((3, 2, HEAD, WIDTH), BF),
            out_crossed=((HEAD, WIDTH), BF),
            m_crossed=((ROWS, WIDTH), BF),
        ),
        dict(
            hidden_all=V((LENGTH, WIDTH), BF),
            nm_all=V((LENGTH, WIDTH), BF),
            cots=V((LENGTH, WIDTH), BF),
            gus=V((2, WIDTH, WIDTH), BF),
            downs=V((WIDTH, WIDTH), BF),
            down_grads=V((2, UNITS, WIDTH), BF),
            weighted=V((LENGTH, UNITS), BF),
            weighted_t=V((UNITS, LENGTH), BF),
            queries=V((LENGTH, 2 * HEAD), BF),
            keyvals=V((PADDED, 2 * HEAD), BF),
            keyvals_t=V((2 * HEAD, PADDED), BF),
            stats=V((1, LENGTH), F32),
            heads_t=V((HEAD, LENGTH), F32),
            small=V((WIDTH, ROWS), BF),
            mid=V((ROWS, WIDTH), F32),
            mid_grad=V((ROWS, WIDTH), F32),
            router_t=V((32, WIDTH), F32),
            gain_grad=V((1, WIDTH), F32),
            wqkv_own=V((ROWS, WIDTH), BF),
            rows=V((16, WIDTH), BF),
            row_dp=V((DP, 16, WIDTH), BF),
            shares=V((8, ROWS), F32),
            tiles=V((TENSOR, 16, ROWS), BF),
            tile_all=V((DP, TENSOR, 16, ROWS), BF),
            out_all=V((CHIPS, ROWS, WIDTH), BF),
            wq_all=V((2 * HEAD, WIDTH), BF),
            code=V((PADDED, ROWS), F32),
            scores=V((SPAN, PAIR), F32),
            starts=V((1, LENGTH), F32),
            wqk=V((WIDTH, PAIR), BF),
            att_src=V((TENSOR, HEAD, ROWS), BF),
            att_t=V((WIDTH, ROWS), BF),
            att_rows=V((ROWS, WIDTH), BF),
            ys_gu=V((2, 2, ROWS, WIDTH), BF),
            ys_down=V((2, 2, UNITS, ROWS), BF),
            n_parts=V((SLOTS, PAIR, WIDTH), BF),
            n_twins=V((SLOTS, ROWS, WIDTH), BF),
            n_credit=pltpu.SemaphoreType.REGULAR,
            n_crossed=V((4, ROWS, WIDTH), BF),
            n_landed=V((3, ROWS, WIDTH), BF),
            m_parts=V((SLOTS, PAIR, WIDTH), BF),
            m_twins=V((SLOTS, ROWS, WIDTH), BF),
            m_credit=pltpu.SemaphoreType.REGULAR,
            m_landed=V((3, PAIR, WIDTH), BF),
            gate_src=V((TENSOR, 8, ROWS), F32),
            gate_all=V((TENSOR, 8, ROWS), F32),
            grads=V((HEAD, LENGTH), BF),
            query_all=V((TENSOR, HEAD, ROWS), BF),
            back_src=V((TENSOR, ROWS, ROWS), BF),
            back_all=V((TENSOR, ROWS, ROWS), BF),
            out_twins=V((CHIPS, HEAD, WIDTH), BF),
            out_joined=V((HEAD, WIDTH), BF),
            out_rows=V((HEAD, WIDTH), F32),
            out_in=V((3, 16, WIDTH), F32),
            out_sum=V((16, WIDTH), F32),
            out_x=V((8, WIDTH), F32),
            tail_in=V((3, TAIL, PAIR), BF),
            tail_src=V((TAIL, ROWS), BF),
            tail_x=V((TAIL, ROWS), BF),
            pieces=V((TENSOR, 8, PAIR), F32),
            last=V((TENSOR, 8, PAIR), F32),
        )
        | sems(
            h_send=1,
            h_recv=24,
            c_send=1,
            c_recv=24,
            o_send=1,
            o_recv=24,
            g_send=1,
            g_recv=24,
            t1_send=1,
            t1_recv=1,
            t2_send=1,
            t2_recv=1,
            t2x_recv=1,
            rdx_recv=1,
            rd_send=1,
            rd_recv=1,
            wq_send=1,
            wq_recv=1,
            e_send=4,
            e_recv=40,
            a_send=1,
            a_recv=1,
            ntw_send=SLOTS,
            ntw_recv=SLOTS,
            nc_send=4,
            nc_recv=4,
            n_send=3,
            n_recv=3,
            mtw_send=SLOTS,
            mtw_recv=SLOTS,
            m_send=5,
            m_recv=5,
            mx_send=1,
            mx_recv=1,
            gg_send=1,
            gg_recv=1,
            b_send=1,
            b_recv=1,
            ot_send=1,
            ot_recv=1,
            oz_send=4,
            oz_recv=4,
            qb_send=1,
            qb_recv=1,
            kb_send=1,
            kb_recv=1,
            x_send=8,
            x_recv=8,
            y_send=8,
            y_recv=8,
            tx_send=5,
            tx_recv=5,
            t_send=4,
            t_recv=4,
            od_send=4,
            od_recv=4,
            l_send=1,
            l_recv=1,
            local=20,
        ),
    )
    values = {name: getattr(c, name) for name in STORED}
    done = call(
        store_kernel,
        0,
        values,
        {name + "_done": (value.shape, value.dtype) for name, value in values.items()},
        {name + "_kept": V(value.shape, value.dtype) for name, value in values.items()}
        | sems(local=2 * len(STORED)),
        reaches=False,
    )
    return (
        done.output_done[None],
        done.hidden_grad_done[None],
        done.gain_one_out_done.reshape(8),
        done.query_out_done.T,
        done.kv_out_done,
        done.out_grad_done.T,
        done.gain_two_out_done.reshape(8),
        done.router_out_done,
        done.gu_out_done,
        done.down_out_done,
    )


def solution(mesh):
    return jax.shard_map(
        body,
        mesh=mesh,
        in_specs=(
            P("dp", "tensor", None),
            P("dp", None),
            P("dp", None),
            P("dp", None, None),
            P(("dp", "tensor")),
            P("dp", "tensor"),
            P(("dp", "tensor"), None),
            P(None, ("dp", "tensor")),
            P(("dp", "tensor")),
            P(("dp", "tensor"), None),
            P("tensor", "dp", None),
            P("tensor", None, "dp"),
            P("dp", "tensor", None),
        ),
        out_specs=(
            P("dp", "tensor", None),
            P("dp", "tensor", None),
            P(("dp", "tensor")),
            P("dp", "tensor"),
            P(("dp", "tensor"), None),
            P(None, ("dp", "tensor")),
            P(("dp", "tensor")),
            P(("dp", "tensor"), None),
            P("tensor", "dp", None),
            P("tensor", None, "dp"),
        ),
        check_vma=False,
    )
```

```python
import math

import jax
import jax.numpy as jnp
import numpy as np
from jax import lax
from jax.experimental import pallas as pl
from jax.experimental.pallas import tpu as pltpu
from jax.sharding import PartitionSpec as P

HEAD = 64
LENGTH = 2048
WIDTH = 1024
UNITS = 512
ROWS = 128
PAIR = 256
CHUNK = 384
REACH = 896
SPAN = REACH + PAIR
PADDED = REACH + LENGTH
CHIPS = 8
TENSOR = 16
DP = 8
TAIL = 240
SLOTS = 2
STEP_Z = (0, 0, 1, 3, 1, 3, 2, 2)
STEP_X = (0, 1, 0, 0, 1, 1, 0, 1)
SUM_Z = (2, 2, 1, 1, 3, 3, 0, 0)
SUM_X = (1, 0, 1, 0, 1, 0, 1, 0)
LOWEST = -1e30
TP = "tensor"
SP = "dp"
BF = jnp.bfloat16
F32 = jnp.float32
MESH = pl.DeviceIdType.MESH
VMEM_BYTES = 63 * 1024 * 1024

NN = (((1,), (0,)), ((), ()))
NT = (((1,), (1,)), ((), ()))
TN = (((0,), (0,)), ((), ()))


def dot(left, right, dims=NN):
    return lax.dot_general(left, right, dims, preferred_element_type=F32)


def aligned(value, size):
    return pl.ds(pl.multiple_of(value * size, size), size)


def remote(src, dst, send, recv, axis, index):
    return pltpu.make_async_remote_copy(
        src_ref=src,
        dst_ref=dst,
        send_sem=send,
        recv_sem=recv,
        device_id={axis: index},
        device_id_type=MESH,
    )


def all_sent(ref, sem, place):
    remote(ref, ref, sem, sem, TP, place.twin).wait_send()


def all_landed(ref, sem, place):
    remote(ref, ref, sem, sem, TP, place.twin).wait_recv()


class Place:
    def __init__(self):
        self.t = lax.axis_index(TP)
        self.d = lax.axis_index(SP)
        self.core = lax.rem(self.t, 2)
        self.chip = self.t // 2
        self.twin = self.t + 1 - 2 * self.core
        self.x = lax.rem(self.d, 2)
        self.y = self.d // 2
        self.across = self.d + 1 - 2 * self.x
        self.z = self.chip // 2
        self.x_far = lax.rem(self.chip, 2)

    def chip_at(self, k):
        return lax.rem(self.chip + k, CHIPS)

    def same_core(self, k):
        return 2 * self.chip_at(k) + self.core

    def near(self, dz, dx):
        return 2 * lax.rem(self.z + dz, 4) + lax.rem(self.x_far + dx, 2)

    def near_core(self, dz, dx):
        return 2 * self.near(dz, dx) + self.core

    def listed(self, i, all_z, all_x):
        if isinstance(i, int):
            return self.near(all_z[i], all_x[i])
        dz, dx = jnp.int32(0), jnp.int32(0)
        for k in range(CHIPS):
            dz = jnp.where(i == k, all_z[k], dz)
            dx = jnp.where(i == k, all_x[k], dx)
        return self.near(dz, dx)

    def step(self, i):
        return self.listed(i, STEP_Z, STEP_X)

    def sum_step(self, i):
        return self.listed(i, SUM_Z, SUM_X)

    def step_core(self, i):
        return 2 * self.step(i) + self.core

    def tensor_at(self, k):
        return lax.rem(self.t + k, TENSOR)

    def dp_at(self, k):
        return lax.rem(self.d + k, DP)

    def y_at(self, k):
        return lax.rem(self.y + k, 4)

    def enter(self):
        barrier = pltpu.get_barrier_semaphore()
        for k in range(1, TENSOR):
            pl.semaphore_signal(
                barrier, inc=1, device_id={TP: self.tensor_at(k)}, device_id_type=MESH
            )
        for k in range(1, DP):
            pl.semaphore_signal(
                barrier, inc=1, device_id={SP: self.dp_at(k)}, device_id_type=MESH
            )
        pl.semaphore_wait(barrier, TENSOR + DP - 2)


class Ring:
    def __init__(self, place, block, half, send, recv, most, source=None, source_half=None):
        self.place, self.block, self.half = place, block, half
        self.send, self.recv, self.most = send, recv, most
        self.source, self.source_half = source, source_half

    def send_sem(self, number):
        return self.send.at[0]

    def copy(self, number, index, dest, source=None):
        src = self.block(index) if source is None else source
        return remote(
            src, self.block(index), self.send_sem(number), self.recv.at[index], TP, dest
        )

    def piece(self, number, index, part, dest, source=None):
        ref = self.half(index, part)
        place = TENSOR + index // 2 if part else index
        return remote(
            ref if source is None else source,
            ref,
            self.send_sem(number),
            self.recv.at[place],
            TP,
            dest,
        )

    def sent(self, number):
        at = self.place
        if number == 0:
            return self.copy(0, at.t, at.twin, self.source)
        if number < 4:
            return self.copy(number, at.t, at.step_core(number), self.source)
        if number < 6:
            return self.copy(number, at.step_core(1), at.step_core(number - 2))
        if number < 8:
            return self.piece(number, at.step_core(2 * number - 9), 0, at.step_core(2))
        if number < 10:
            return self.piece(number, at.step_core(2 * number - 14), 1, at.step_core(3))
        return self.copy(number, at.step_core(number - 9), at.twin)

    def start(self):
        at = self.place
        for part in range(2):
            src = None if self.source_half is None else self.source_half(part)
            self.piece(1, at.t, part, at.step_core(1), src).start()
        for number in (2, 3, 0):
            self.sent(number).start()

    def piece_arrived(self, index, part):
        self.piece(0, index, part, self.place.twin).wait_recv()

    def pass_on(self, i):
        at = self.place
        index = at.step_core(i)
        if i in (2, 3):
            self.copy(0, index, at.twin).wait_recv()
            self.sent(8 if i == 2 else 6).start()
        elif i == 1:
            for part in range(2):
                self.piece_arrived(index, part)
                self.piece(4, index, part, at.step_core(2)).start()
                self.piece(5, index, part, at.step_core(3)).start()
        elif i == 4:
            self.piece_arrived(index, 1)
            self.sent(9).start()
            self.piece_arrived(index, 0)
        elif i == 5:
            self.piece_arrived(index, 0)
            self.sent(7).start()
            self.piece_arrived(index, 1)
        else:
            self.piece_arrived(index, 0)
            self.piece_arrived(index, 1)
        self.sent(9 + i).start()

    def pass_on_at(self, i):
        for k in range(1, CHIPS):

            @pl.when(i == k - 1)
            def _(k=k):
                self.pass_on(k)

    def second(self, i):
        self.copy(0, 2 * self.place.step(i) + 1 - self.place.core, self.place.twin).wait_recv()

    def end(self):
        all_sent(self.most, self.send.at[0], self.place)


def whole_ring(place, ref, send, recv, source=None):
    return Ring(
        place,
        lambda b: ref.at[aligned(b, ROWS)],
        lambda b, part: ref.at[pl.ds(pl.multiple_of(b * ROWS + part * HEAD, HEAD), HEAD)],
        send,
        recv,
        ref.at[pl.ds(0, 15 * ROWS)],
        source,
        None if source is None else lambda part: source.at[pl.ds(part * HEAD, HEAD)],
    )


class Copies:
    def __init__(self, sems):
        self.sems, self.pending, self.free, self.used = sems, [], [], 0

    def start(self, src, dst):
        if self.free:
            number = self.free.pop()
        else:
            number, self.used = self.used, self.used + 1
        copy = pltpu.make_async_copy(src, dst, self.sems.at[number])
        copy.start()
        self.pending.append((copy, number))
        return copy

    def wait(self, count=None):
        count = len(self.pending) if count is None else count
        for copy, number in self.pending[:count]:
            copy.wait()
            self.free.append(number)
        self.pending = self.pending[count:]

    def need(self, *copies):
        for copy in copies:
            copy.wait()
            self.free += [number for other, number in self.pending if other is copy]
            self.pending = [pair for pair in self.pending if pair[0] is not copy]


def lanes(shape):
    return lax.broadcasted_iota(jnp.int32, shape, len(shape) - 1)


def sublanes(shape):
    return lax.broadcasted_iota(jnp.int32, shape, 0)


def swapped(values):
    return jnp.where(
        lanes(values.shape) < HEAD // 2,
        pltpu.roll(values, 2 * HEAD - HEAD // 2, 1),
        pltpu.roll(values, HEAD // 2, 1),
    )


def document_starts(seg):
    starts = jnp.zeros(seg.shape, F32)
    for document in range(8):
        before = jnp.sum(jnp.where(seg < document, 1.0, 0.0), axis=1, keepdims=True)
        starts = starts + jnp.where(seg == document, before, 0.0)
    return starts


def key_codes(mask, code):
    code[0:REACH, :] = jnp.full((REACH, ROWS), -1.0, F32)

    @pl.loop(0, TENSOR)
    def _(i):
        row = mask[:, aligned(i, ROWS)].astype(F32)
        live = jnp.broadcast_to(row, (ROWS, ROWS)).T == 1.0
        places = (sublanes((ROWS, ROWS)) + i * ROWS).astype(F32)
        code[pl.ds(pl.multiple_of(REACH + i * ROWS, ROWS), ROWS), :] = jnp.where(
            live, places, -1.0
        )


def allowed(code, start_row, chunk):
    ok = jnp.concatenate([code, code], axis=1) >= start_row
    if (chunk + 1) * CHUNK > REACH:
        key = sublanes((CHUNK, PAIR)) + (chunk * CHUNK - REACH)
        query = lanes((CHUNK, PAIR))
        ok = (ok & (key < query)) | (key == query)
    return ok


def turned_back(grad, r, here):
    cos, sin = r.cosine_t[:, here], r.sine_t[:, here]
    first, second = grad[0 : HEAD // 2], grad[HEAD // 2 : HEAD]
    return jnp.concatenate([first * cos + second * sin, second * cos - first * sin], axis=0)


class Halves:
    def __init__(self, place, parts, twins, sums, send, recv, credit):
        self.place, self.parts, self.twins, self.sums = place, parts, twins, sums
        self.send, self.recv, self.credit = send, recv, credit

    def half(self, k):
        at, slot = self.place, lax.rem(k, SLOTS)
        return remote(
            self.parts.at[slot, aligned(1 - at.core, ROWS), :],
            self.twins.at[slot],
            self.send.at[slot],
            self.recv.at[slot],
            TP,
            at.twin,
        )

    def put(self, k, value):
        @pl.when(k >= SLOTS)
        def _():
            self.half(k - SLOTS).wait_send()
            pl.semaphore_wait(self.credit, 1)

        self.parts[lax.rem(k, SLOTS)] = value.astype(BF)
        self.half(k).start()

    def add(self, k):
        slot = lax.rem(k, SLOTS)
        self.half(k).wait_recv()
        own = self.parts[slot, aligned(self.place.core, ROWS), :].astype(F32)
        self.sums(k)[...] = (own + self.twins[slot].astype(F32)).astype(BF)

        @pl.when(k < CHIPS - SLOTS)
        def _():
            pl.semaphore_signal(
                self.credit, inc=1, device_id={TP: self.place.twin}, device_id_type=MESH
            )

    def end(self):
        for k in range(CHIPS - SLOTS, CHIPS):
            self.half(k).wait_send()


class Joined:
    def __init__(self, place, sums, crossed, landed, sems):
        self.place, self.sums, self.crossed, self.landed = place, sums, crossed, landed
        self.c_send, self.c_recv, self.send, self.recv = sems

    def cross(self, j):
        return remote(
            self.sums.at[2 * j],
            self.crossed.at[j],
            self.c_send.at[j],
            self.c_recv.at[j],
            TP,
            self.place.near_core(0, 1),
        )

    def whole(self, j):
        return remote(
            self.sums.at[2 * j + 1],
            self.landed.at[j],
            self.send.at[j],
            self.recv.at[j],
            TP,
            self.place.near_core(SUM_Z[2 * j], 0),
        )

    def join(self, j):
        self.cross(j).wait_recv()
        total = self.sums[2 * j + 1].astype(F32) + self.crossed[j].astype(F32)
        self.sums[2 * j + 1] = total.astype(BF)
        self.whole(j).start()

    def result(self):
        self.cross(3).wait_recv()
        total = self.sums[7].astype(F32) + self.crossed[3].astype(F32)
        for j in range(3):
            self.whole(j).wait_recv()
            total = total + self.landed[j].astype(F32)
        return total

    def end(self):
        for j in range(4):
            self.cross(j).wait_send()
        for j in range(3):
            self.whole(j).wait_send()


def unpacked(both):
    return both[:, 0:8].reshape(ROWS, WIDTH), both[:, 8:16].reshape(ROWS, WIDTH)


def aligned_rows(ref, unit):
    def block(src, part=None):
        if part is None:
            return ref.at[pl.ds(pl.multiple_of(src * 2 * unit, unit), 2 * unit), :]
        return ref.at[pl.ds(pl.multiple_of((src * 2 + part) * unit, unit), unit), :]

    return block


def column_blocks(ref):
    def block(src, part=None):
        if part is None:
            return ref.at[:, aligned(src, ROWS)]
        return ref.at[pl.ds(part * PAIR, PAIR), aligned(src, ROWS)]

    return block


class Stream:
    def __init__(self, place, own, block, most, r, number):
        self.place, self.own, self.block, self.most = place, own, block, most
        self.send, self.recv = r.e_send, r.e_recv
        self.number, self.first_recv = number, 10 * number

    def at_y(self, k, other=False):
        at = self.place
        column = 1 - at.x if other else at.x
        return 2 * at.y_at(k) + column

    def copy(self, number, src, dest, part=None, source=None):
        ref = self.block(src, part)
        return remote(
            ref if source is None else source,
            ref,
            self.send.at[self.number],
            self.recv.at[self.first_recv + (8 + lax.rem(src, 2) if part else src)],
            SP,
            dest,
        )

    def sent(self, number):
        at, at_y = self.place, self.at_y
        if number == 0:
            return self.copy(0, at.d, at.across, source=self.own)
        if number < 3:
            return self.copy(number, at.d, at_y(2 * number - 1), source=self.own)
        if number < 5:
            return self.copy(number, at.across, at_y(2 * number - 5))
        other = number > 6
        if number % 2:
            return self.copy(number, at_y(3, other), at_y(1), 0)
        return self.copy(number, at_y(1, other), at_y(3), 1)

    def arrived(self, src, halves=False):
        for part in (0, 1) if halves else (None,):
            self.copy(0, src, self.place.across, part).wait_recv()

    def start_x(self):
        self.sent(0).start()

    def start_y(self):
        self.sent(1).start()
        self.sent(2).start()

    def from_across(self):
        self.arrived(self.place.across)
        self.sent(3).start()
        self.sent(4).start()

    def from_y(self):
        self.arrived(self.at_y(3))
        self.sent(5).start()
        self.arrived(self.at_y(1))
        self.sent(6).start()

    def from_y_across(self):
        self.arrived(self.at_y(3, True))
        self.sent(7).start()
        self.arrived(self.at_y(1, True))
        self.sent(8).start()

    def finish(self):
        self.arrived(self.at_y(2), True)
        self.arrived(self.at_y(2, True), True)

    def end(self):
        all_sent(self.most, self.send.at[self.number], self.place)


def expert_streams(at, r, e):
    downs = r.downs.at[pl.ds(e * UNITS, UNITS)]
    return (
        Stream(
            at,
            r.gu.at[e],
            aligned_rows(r.gus.at[e], HEAD),
            r.gus.at[e, pl.ds(0, 7 * ROWS)],
            r,
            2 * e,
        ),
        Stream(
            at,
            r.down.at[e],
            column_blocks(downs),
            downs.at[:, pl.ds(0, 7 * ROWS)],
            r,
            2 * e + 1,
        ),
    )


def layer_kernel(r):
    at = Place()
    t, d = at.t, at.d
    copies = Copies(r.local)
    r.load()
    r.hidden_all[aligned(t, ROWS), :] = r.hid[...]
    keyval, out_rows = r.w_keyval[...].astype(F32), r.w_out_t[...].astype(F32)
    r.rows[...] = jnp.concatenate([keyval, out_rows], axis=0).astype(BF)
    r.row_dp[d] = r.rows[...]
    r.shares[...] = jnp.zeros((8, ROWS), F32)
    r.shares[:, 0:32] = r.router[...].astype(F32)
    same = sublanes((8, 8)) == lanes((8, 8))
    for column, gain in ((32, r.gain_one), (33, r.gain_two)):
        wide = jnp.broadcast_to(gain[...].astype(F32), (8, 8))
        r.shares[:, column : column + 1] = jnp.sum(
            jnp.where(same, wide, 0.0), axis=1, keepdims=True
        )
    for j in range(CHIPS):
        tile = jnp.concatenate([keyval[:, j * ROWS : (j + 1) * ROWS], r.shares[...]], axis=0)
        r.tiles[2 * j] = tile.astype(BF)
        r.tiles[2 * j + 1] = tile.astype(BF)
    r.tile_all[d, t] = r.tiles[t]
    r.wq_all[HEAD : 2 * HEAD, :] = jnp.zeros((HEAD, WIDTH), BF)
    r.wq_all[0:HEAD, aligned(d, ROWS)] = r.w_query_t[...]
    at.enter()

    def tile_one(k, src):
        dest = at.tensor_at(k)
        return remote(
            r.tiles.at[dest],
            r.tile_all.at[d, src],
            r.t1_send.at[0],
            r.t1_recv.at[0],
            TP,
            dest,
        )

    def y_peer(k):
        return 2 * at.y_at(k) + at.x

    def tile_two(src, dest, recv):
        ref = r.tile_all.at[src]
        return remote(ref, ref, r.t2_send.at[0], recv.at[0], SP, dest)

    def rows_dp(src, dest, recv, source=None):
        ref = r.row_dp.at[src]
        return remote(
            ref if source is None else source, ref, r.rd_send.at[0], recv.at[0], SP, dest
        )

    def wq_dp(k, src):
        return remote(
            r.w_query_t,
            r.wq_all.at[pl.ds(0, HEAD), aligned(src, ROWS)],
            r.wq_send.at[0],
            r.wq_recv.at[0],
            SP,
            at.dp_at(k),
        )

    first_expert, second_expert = expert_streams(at, r, 0), expert_streams(at, r, 1)

    for k in range(1, TENSOR):
        tile_one(k, t).start()
    for k in range(1, DP):
        wq_dp(k, d).start()
    ring_h = whole_ring(at, r.hidden_all, r.h_send, r.h_recv)
    ring_h.start()
    for e in range(2):
        copies.start(r.gu.at[e], r.gus.at[e, aligned(d, ROWS)])
        copies.start(r.down.at[e], r.downs.at[pl.ds(e * UNITS, UNITS), aligned(d, ROWS)])
    copies.start(r.cot, r.cots.at[aligned(t, ROWS)])

    key_codes(r.mask, r.code)
    r.starts[...] = document_starts(r.seg[...])
    r.keyvals[0:REACH, :] = jnp.zeros((REACH, 2 * HEAD), BF)
    r.keyvals_t[:, 0:REACH] = jnp.zeros((2 * HEAD, REACH), BF)

    all_landed(r.tile_all.at[0, pl.ds(0, 15)], r.t1_recv.at[0], at)
    tile_two(d, at.across, r.t2x_recv).start()
    rows_dp(d, at.across, r.rdx_recv, r.rows).start()
    for k in range(1, 4):
        tile_two(d, y_peer(k), r.t2_recv).start()
        rows_dp(d, y_peer(k), r.rd_recv, r.rows).start()
    for stream in first_expert:
        stream.start_x()
    for i in range(1, 4):
        ring_h.pass_on(i)
    tile_two(at.across, at.across, r.t2x_recv).wait_recv()
    for k in range(1, 4):
        tile_two(at.across, y_peer(k), r.t2_recv).start()
    rows_dp(at.across, at.across, r.rdx_recv).wait_recv()
    for k in range(1, 4):
        rows_dp(at.across, y_peer(k), r.rd_recv).start()
    for stream in first_expert:
        stream.start_y()
    seven_wq = r.wq_all.at[pl.ds(0, HEAD), pl.ds(0, 7 * ROWS)]
    all_landed(seven_wq, r.wq_recv.at[0], at)
    all_landed(r.tile_all.at[pl.ds(0, 6)], r.t2_recv.at[0], at)
    for j in range(DP):
        both = r.tile_all[j].astype(F32)
        r.wqk[j * ROWS : (j + 1) * ROWS, ROWS:PAIR] = both[:, 0:8].reshape(ROWS, ROWS).astype(BF)
        r.small[j * ROWS : (j + 1) * ROWS, :] = both[:, 8:16].reshape(ROWS, ROWS).astype(BF)
    r.wqk[:, 0:ROWS] = r.wq_all[...].astype(F32).T.astype(BF)
    columns = r.small[...].astype(F32).T
    gain_one = columns[32:33, :]
    gain_two = columns[33:34, :]
    r.need("turns")
    ring_o = Ring(
        at,
        lambda b: r.out_all.at[b // 2, aligned(lax.rem(b, 2), HEAD)],
        lambda b, part: r.out_all.at[b // 2, aligned(2 * lax.rem(b, 2) + part, 32)],
        r.o_send,
        r.o_recv,
        r.nm_all.at[pl.ds(0, 15 * HEAD)],
    )

    ring_c = whole_ring(at, r.cots, r.c_send, r.c_recv, r.cot)
    @pl.loop(0, CHIPS)
    def _(i):
        @pl.when(i == 1)
        def _():
            ring_h.pass_on(4)
            ring_h.pass_on(5)

        @pl.when(i == 2)
        def _():
            all_landed(r.row_dp.at[pl.ds(0, 6)], r.rd_recv.at[0], at)
            both = r.row_dp[...].astype(F32)
            r.wqkv_own[0:HEAD, :] = r.wq_all[0:HEAD, :]
            r.wqkv_own[HEAD : 2 * HEAD, :] = both[:, 0:8].reshape(HEAD, WIDTH).astype(BF)
            r.out_all[at.chip, aligned(at.core, HEAD), :] = (
                both[:, 8:16].reshape(HEAD, WIDTH).astype(BF)
            )
            ring_o.start()

        @pl.when(i == 4)
        def _():
            ring_c.start()

        @pl.when(i == 5)
        def _():
            ring_h.pass_on(6)
            ring_h.pass_on(7)

        ring_h.second(i)
        block = at.step(i)
        here = aligned(block, PAIR)
        hidden = r.hidden_all[here, :].astype(F32)
        inverse = lax.rsqrt(jnp.mean(hidden * hidden, axis=1, keepdims=True) + 1e-6)
        unit = (hidden * inverse * gain_one).astype(BF)
        r.normed[here, :] = unit
        table = r.turns[here, :]
        turned = lanes(table.shape) < HEAD
        cos = jnp.where(turned, table, 1.0)
        sin = jnp.where(turned, pltpu.roll(table, HEAD, 1), 0.0)
        projected = dot(unit, r.wqk[...])
        query, keyval = projected[:, 0:ROWS], projected[:, ROWS:PAIR]
        query = (query * cos + swapped(query) * sin).astype(BF)
        r.queries[here, :] = (query.astype(F32) * (1.0 / math.sqrt(HEAD))).astype(BF)
        keyval = keyval * cos + swapped(keyval) * sin
        later = pl.ds(pl.multiple_of(REACH + block * PAIR, ROWS), PAIR)
        r.keyvals[later, :] = keyval.astype(BF)
        r.keyvals_t[:, later] = keyval.T.astype(BF)

    r.save("normed")

    def att_copy(dest, src):
        return remote(
            r.att_src.at[dest],
            r.att_t.at[aligned(src, HEAD), :],
            r.a_send.at[0],
            r.a_recv.at[0],
            TP,
            dest,
        )

    @pl.loop(0, CHIPS)
    def _(i):
        @pl.when(i == 0)
        def _():
            for stream in first_expert:
                stream.from_across()

        @pl.when(i == 1)
        def _():
            for k in range(1, 4):
                ring_o.pass_on(k)

        @pl.when(i == 3)
        def _():
            for stream in first_expert:
                stream.from_y()

        @pl.when(i == 5)
        def _():
            ring_o.pass_on(4)
            ring_o.pass_on(5)

        block = at.chip_at(i + 1)
        here = aligned(block, PAIR)
        query = r.queries[here, :]
        start_row = r.starts[:, here]
        top = jnp.full((1, PAIR), LOWEST, F32)
        for chunk in range(SPAN // CHUNK):
            keys = pl.ds(pl.multiple_of(block * PAIR + chunk * CHUNK, ROWS), CHUNK)
            score = dot(r.keyvals[keys, :], query, NT)
            score = jnp.where(allowed(r.code[keys, :], start_row, chunk), score, LOWEST)
            r.scores[chunk * CHUNK : (chunk + 1) * CHUNK, :] = score
            top = jnp.maximum(top, jnp.max(score, axis=0, keepdims=True))
        total = jnp.zeros((1, PAIR), F32)
        for chunk in range(SPAN // CHUNK):
            place = slice(chunk * CHUNK, (chunk + 1) * CHUNK)
            weight = jnp.exp(r.scores[place, :] - top)
            total = total + jnp.sum(weight, axis=0, keepdims=True)
            r.weighted[place, 0:PAIR] = weight.astype(BF)
        window = pl.ds(pl.multiple_of(block * PAIR, ROWS), SPAN)
        head = dot(r.keyvals_t[HEAD : 2 * HEAD, window], r.weighted[0:SPAN, 0:PAIR]) / total
        r.heads_t[:, here] = head
        r.stats[:, here] = top + jnp.log(total)
        r.att_src[2 * block] = head[:, 0:ROWS].astype(BF)
        r.att_src[2 * block + 1] = head[:, ROWS:PAIR].astype(BF)

        @pl.when(i < CHIPS - 1)
        def _():
            att_copy(2 * block, t).start()
            att_copy(2 * block + 1, t).start()

        @pl.when(i == CHIPS - 1)
        def _():
            att_copy(at.twin, t).start()

    ring_c.pass_on(1)
    r.att_t[aligned(t, HEAD), :] = r.att_src[t]
    ring_o.pass_on(6)
    ring_o.pass_on(7)
    for stream in first_expert:
        stream.from_y_across()
    for i in range(CHIPS):
        ring_o.second(i)

    @pl.loop(0, 4)
    def _(j):
        sides = [
            r.out_all[:, pl.ds(pl.multiple_of(core * HEAD + j * 16, 16), 16), :].astype(F32)
            for core in range(2)
        ]
        first, second = unpacked(jnp.stack(sides, axis=1).reshape(TENSOR, 16, WIDTH))
        r.out_t[aligned(2 * j, ROWS), :] = first.astype(BF)
        r.out_t[aligned(2 * j + 1, ROWS), :] = second.astype(BF)

    r.save("out_t")
    all_landed(r.att_t.at[pl.ds(0, 15 * HEAD)], r.a_recv.at[0], at)
    attended = r.att_t[...].astype(F32).T.astype(BF)
    r.att_rows[...] = attended
    middle = r.hid[...].astype(F32) + dot(attended, r.out_t[...], NT)
    r.mid[...] = middle
    inverse = lax.rsqrt(jnp.mean(middle * middle, axis=1, keepdims=True) + 1e-6)
    r.nm_all[aligned(t, ROWS), :] = (middle * inverse * gain_two).astype(BF)
    ring = whole_ring(at, r.nm_all, r.g_send, r.g_recv)
    ring.start()
    for stream in second_expert:
        stream.start_x()
        stream.start_y()
    ring_c.pass_on(2)
    ring_c.pass_on(3)
    for stream in first_expert:
        stream.finish()
    copies.wait()
    ring_h.end()
    ring_o.end()
    r.finish("normed")
    r.finish("out_t")
    r.proj_grads, r.n_first, r.gates, r.n_sums = r.hidden_all, r.normed, r.turns, r.out_all
    r.m_sums = r.out_t


    def moe_sums(k, count=1):
        return r.m_sums.at[pl.ds(pl.multiple_of(k * ROWS, ROWS), count * ROWS)]

    halves_n = Halves(at, r.n_parts, r.n_twins, lambda k: r.n_sums.at[k], r.ntw_send, r.ntw_recv, r.n_credit)
    halves_m = Halves(at, r.m_parts, r.m_twins, moe_sums, r.mtw_send, r.mtw_recv, r.m_credit)
    joined = Joined(
        at,
        r.n_sums,
        r.n_crossed,
        r.n_landed,
        (r.nc_send, r.nc_recv, r.n_send, r.n_recv),
    )
    ring_w = whole_ring(at, r.wqkv, r.h_send, r.h_recv, r.wqkv_own)
    own_weights = copies.start(r.wqkv_own, r.wqkv.at[aligned(t, ROWS)])

    def moe_first():
        return remote(
            moe_sums(0, 2),
            r.m_landed.at[0],
            r.m_send.at[0],
            r.m_recv.at[0],
            TP,
            at.near_core(SUM_Z[0], 0),
        )

    def moe_along(j, part):
        number = 2 * j - 1 + part
        return remote(
            moe_sums(2 * j + part),
            r.m_landed.at[j, pl.ds(part * ROWS, ROWS)],
            r.m_send.at[number],
            r.m_recv.at[number],
            TP,
            at.near_core(SUM_Z[2 * j], 0),
        )

    def gu_over_y(e, k):
        y = at.y_at(k)
        return remote(
            r.gus.at[e, aligned(y, PAIR), :],
            r.y_gu.at[e, k - 1],
            r.x_send.at[4 * e + k],
            r.x_recv.at[4 * e + k],
            SP,
            2 * y + at.x,
        )

    def down_over_y(e, k):
        y = at.y_at(k)
        return remote(
            r.down_grads.at[e, :, aligned(y, PAIR)],
            r.y_down.at[e, k - 1],
            r.y_send.at[4 * e + k],
            r.y_recv.at[4 * e + k],
            SP,
            2 * y + at.x,
        )

    def across_x(number, src, dst):
        return remote(src, dst, r.tx_send.at[number], r.tx_recv.at[number], SP, at.across)

    def gu_half(part):
        rows = pl.ds(part * HEAD, HEAD)
        return remote(
            r.ys_gu.at[1, 1 - at.x, rows],
            r.yx_gu.at[1, rows],
            r.tx_send.at[1 + 3 * part],
            r.tx_recv.at[1 + 3 * part],
            SP,
            at.across,
        )

    def gu_across(e):
        return across_x(e, r.ys_gu.at[e, 1 - at.x], r.yx_gu.at[e])

    def down_across(e):
        return across_x(2 + e, r.ys_down.at[e, 1 - at.x], r.yx_down.at[e])

    def gate_copy(dest, src):
        return remote(
            r.gate_src.at[dest],
            r.gate_all.at[src],
            r.gg_send.at[0],
            r.gg_recv.at[0],
            TP,
            dest,
        )

    def one_pass(e):
        @pl.loop(0, CHIPS)
        def _(i):
            if e == 0:
                for k in range(2, CHIPS):

                    @pl.when(i == k - 1)
                    def _(k=k):
                        ring.pass_on(k)

                ring.second(i)

                @pl.when(i == 1)
                def _():
                    ring_c.pass_on(4)
                    ring_c.pass_on(5)

                @pl.when(i == 2)
                def _():
                    for stream in second_expert:
                        stream.from_across()

                @pl.when(i == 4)
                def _():
                    for stream in second_expert:
                        stream.from_y()

                @pl.when(i == 5)
                def _():
                    ring_c.pass_on(6)
                    ring_c.pass_on(7)

                ring_c.second(i)

                @pl.when(i == 6)
                def _():
                    ring_w.start()

                @pl.when(i == 7)
                def _():
                    for stream in second_expert:
                        stream.from_y_across()

            here = aligned(at.step(i) if e == 0 else at.sum_step(i), PAIR)
            nm = r.nm_all[here, :]
            place = lanes((PAIR, ROWS))
            if e == 0:
                expert = sublanes((ROWS, PAIR))
                named = expert == r.routes_t[0:1, here]
                for j in range(1, 8):
                    named = named | (expert == r.routes_t[j : j + 1, here])
                named = jnp.where(named, 1.0, 0.0).T > 0.5
                logits = jnp.where(named, dot(nm, r.small[...]), LOWEST)
                powers = jnp.exp(logits - jnp.max(logits, axis=1, keepdims=True))
                powers = jnp.where(named, powers, 0.0)
                gates = powers / jnp.sum(powers, axis=1, keepdims=True)
            else:
                kept = r.gates[here, :]
                gates = jnp.where(place == 2 * HEAD - 1, 0.0, kept)
                earlier = kept[:, 2 * HEAD - 1 : 2 * HEAD]
            mine = place == 2 * t + e
            gate = jnp.sum(jnp.where(mine, gates, 0.0), axis=1, keepdims=True)
            act_grad = dot(r.cots[here, :], r.downs[e * UNITS : (e + 1) * UNITS, :], NT)
            projected = dot(nm, r.gus[e])
            first, up = projected[:, :UNITS], projected[:, UNITS:]
            sigmoid = 1.0 / (1.0 + jnp.exp(-first))
            silu = first * sigmoid
            activated = silu * up
            gate_grad = jnp.sum(activated * act_grad, axis=1, keepdims=True)
            weighted = (activated * gate).astype(BF)
            r.weighted_t[:, here] = weighted.T
            act_grad = act_grad * gate
            r.proj_grads[here, 0:UNITS] = (
                act_grad * up * (sigmoid * (1.0 + first * (1.0 - sigmoid)))
            ).astype(BF)
            r.proj_grads[here, UNITS:WIDTH] = (act_grad * silu).astype(BF)
            normed_part = dot(r.proj_grads[here, :], r.gus[e], NT)
            if e == 0:
                r.gates[here, :] = jnp.where(place == 2 * HEAD - 1, gate_grad, gates)
                r.weighted[here, :] = weighted
                r.n_first[here, :] = normed_part.astype(BF)

                @pl.when(i == 0)
                def _():
                    ring.pass_on(1)

                return
            row = 2 * lax.rem(t, 4)
            gate_grads = jnp.where(
                place == row, earlier, jnp.where(place == row + 1, gate_grad, 0.0)
            ).T
            chip = at.sum_step(i)
            r.gate_src[2 * chip] = gate_grads[0:8, 0:ROWS]
            r.gate_src[2 * chip + 1] = gate_grads[0:8, ROWS:PAIR]

            @pl.when(i < CHIPS - 1)
            def _():
                gate_copy(2 * chip, t).start()
                gate_copy(2 * chip + 1, t).start()

            @pl.when(i == CHIPS - 1)
            def _():
                gate_copy(at.twin, t).start()

            halves_n.put(i, normed_part + r.n_first[here, :].astype(F32))
            both = jnp.concatenate([r.weighted[here, :], weighted], axis=1)
            halves_m.put(i, dot(both, r.downs[...]))

            @pl.when(i > 0)
            def _():
                halves_n.add(i - 1)
                halves_m.add(i - 1)

            for j in range(4):

                @pl.when(i == 2 * j + 1)
                def _(j=j):
                    joined.cross(j).start()

            for j in range(2):

                @pl.when(i == 2 * j + 4)
                def _(j=j):
                    joined.join(j)

            @pl.when(i == 2)
            def _():
                moe_first().start()

            for step, chips in ((0, (2, 3)), (2, (4, 5))):

                @pl.when(i == step)
                def _(chips=chips):
                    for k in chips:
                        ring_w.pass_on(k)

    def down_gradients(e):
        r.down_grads[e] = dot(r.weighted_t[...], r.cots[...]).astype(BF)

    def gate_up_gradients(e):
        @pl.loop(0, 2)
        def _(j):
            strip = aligned(j, 2 * PAIR)
            r.gus[e, strip, :] = dot(r.nm_all[:, strip], r.proj_grads[...], TN).astype(BF)

    one_pass(0)
    for stream in first_expert:
        stream.end()
    down_gradients(0)
    for k in range(1, 4):
        down_over_y(0, k).start()
    gate_up_gradients(0)
    ring_w.pass_on(1)
    for k in range(1, 4):
        gu_over_y(0, k).start()
    for stream in second_expert:
        stream.finish()
    one_pass(1)
    joined.join(2)
    halves_n.add(CHIPS - 1)
    halves_m.add(CHIPS - 1)
    def gu_loads(e):
        ref, first = (r.n_first, WIDTH) if e == 0 else (r.proj_grads, 0)
        places = [ref.at[pl.ds(first + k * PAIR, PAIR)] for k in range(3)]
        loads = []
        for k in range(3):
            gu_over_y(e, k + 1).wait_recv()
            loads.append(copies.start(r.y_gu.at[e, k], places[k]))
        return places, loads

    def gu_sums(e, places, loads):
        copies.need(*loads)
        total = r.gus[e, aligned(at.y, PAIR), :].astype(F32)
        for place in places:
            total = total + place[...].astype(F32)
        r.ys_gu[e, 0] = total[0:ROWS].astype(BF)
        r.ys_gu[e, 1] = total[ROWS:PAIR].astype(BF)
        (gu_half(0) if e else gu_across(0)).start()

    def down_loads(e):
        places = [
            r.weighted.at[pl.ds(k * UNITS, UNITS), pl.ds(e * PAIR, PAIR)] for k in range(3)
        ]
        loads = []
        for k in range(3):
            down_over_y(e, k + 1).wait_recv()
            loads.append(copies.start(r.y_down.at[e, k], places[k]))
        return places, loads

    def down_sums(e, places, loads):
        copies.need(*loads)
        total = r.down_grads[e, :, aligned(at.y, PAIR)].astype(F32)
        for place in places:
            total = total + place[...].astype(F32)
        r.ys_down[e, 0] = total[:, 0:ROWS].astype(BF)
        r.ys_down[e, 1] = total[:, ROWS:PAIR].astype(BF)
        down_across(e).start()

    out_rows = r.n_first.at[pl.ds(0, WIDTH)]
    out_load = copies.start(r.out_t_d, out_rows)
    for stream in second_expert:
        stream.end()
    down_gradients(1)
    for k in range(1, 4):
        down_over_y(1, k).start()
    gate_up_gradients(1)
    first_down, first_gu = down_loads(0), gu_loads(0)
    for k in range(1, 4):
        gu_over_y(1, k).start()
    r.gate_all[t] = r.gate_src[t]
    all_landed(r.gate_all.at[pl.ds(0, 15)], r.gg_recv.at[0], at)
    groups = r.gate_all[...].reshape(4, 4, 8, ROWS)
    gate_grads = (groups[:, 0] + groups[:, 1] + groups[:, 2] + groups[:, 3]).reshape(32, ROWS)
    gate_grads = jnp.concatenate([gate_grads, jnp.zeros((ROWS - 32, ROWS), F32)], axis=0).T
    own_rows = aligned(t, ROWS)
    gates = jnp.where(lanes((ROWS, ROWS)) < 32, r.gates[own_rows, :], 0.0)
    mean = jnp.sum(gates * gate_grads, axis=1, keepdims=True)
    logit_grad = gates * (gate_grads - mean)
    r.router_t[...] = dot(logit_grad.T.astype(BF), r.nm_all[own_rows, :])[0:32, :]
    by_router = dot(logit_grad.astype(BF), r.small[...], NT)

    gain_two = r.small[...].astype(F32).T[33:34, :]
    normed_grad = joined.result() + by_router
    middle = r.mid[...]
    inverse = lax.rsqrt(jnp.mean(middle * middle, axis=1, keepdims=True) + 1e-6)
    unit = middle * inverse
    r.gain_grad[...] = jnp.sum(normed_grad * unit, axis=0, keepdims=True)
    scaled = normed_grad * gain_two
    grad = r.cots[aligned(t, ROWS), :].astype(F32) + inverse * (
        scaled - unit * jnp.mean(scaled * unit, axis=1, keepdims=True)
    )
    r.mid_grad[...] = grad
    turned = grad.T.reshape(DP, TENSOR, 8, ROWS).transpose(1, 0, 2, 3)
    r.att_grad_t, r.mid_t = r.att_t, r.wqk.at[:, pl.ds(0, ROWS)]
    r.mid_t[...] = turned.reshape(WIDTH, ROWS).astype(BF)
    copies.need(out_load)
    r.att_grad_t[...] = dot(grad.astype(BF), out_rows[...]).T.astype(BF)

    def back_copy(k, src):
        dest = at.tensor_at(k)
        return remote(
            r.att_grad_t.at[aligned(dest, HEAD), :],
            r.grads.at[:, aligned(src, ROWS)],
            r.b_send.at[0],
            r.b_recv.at[0],
            TP,
            dest,
        )

    for k in range(1, TENSOR):
        back_copy(k, t).start()
    r.grads[:, aligned(t, ROWS)] = r.att_grad_t[aligned(t, HEAD), :]
    joined.end()
    r.n_sums[...] = (
        dot(r.mid_t[...], r.att_rows[...]).reshape(CHIPS, ROWS, WIDTH).astype(BF)
    )

    def out_half():
        return remote(
            r.n_sums.at[:, aligned(1 - at.core, HEAD), :],
            r.out_twins,
            r.ot_send.at[0],
            r.ot_recv.at[0],
            TP,
            at.twin,
        )

    out_half().start()
    r.kv_sum, r.query_src = r.gates, r.att_src
    r.tail_left = r.weighted_t.at[pl.ds(0, 3 * HEAD)]
    r.kv_sum[...] = jnp.zeros((LENGTH, 2 * HEAD), F32)
    all_sent(r.att_src.at[pl.ds(0, 15)], r.a_send.at[0], at)
    halves_n.end()
    halves_m.end()
    r.tail = r.n_parts.at[0]
    r.s_gu, r.m_joined = r.m_parts.at[0, pl.ds(0, ROWS)], r.m_parts.at[0, pl.ds(ROWS, ROWS)]

    down_sums(0, *first_down)
    gu_sums(0, *first_gu)
    normed_load = copies.start(r.normed_d, r.normed)

    def out_along(k):
        return remote(
            r.out_twins.at[pl.ds(2 * lax.rem(at.z + k, 4), 2)],
            r.out_landed.at[k - 1],
            r.oz_send.at[k],
            r.oz_recv.at[k],
            TP,
            at.near_core(k, 0),
        )

    def out_across():
        return remote(
            r.out_joined, r.out_crossed, r.oz_send.at[0], r.oz_recv.at[0], TP, at.near_core(0, 1)
        )

    out_half().wait_recv()
    r.out_twins[...] = (
        r.n_sums[:, aligned(at.core, HEAD), :].astype(F32) + r.out_twins[...].astype(F32)
    ).astype(BF)
    for k in range(1, 4):
        out_along(k).start()
    all_landed(r.grads.at[:, pl.ds(0, 15 * ROWS)], r.b_recv.at[0], at)
    r.need("cosine_t", "sine_t")

    def query_copy(dest, src):
        return remote(
            r.query_src.at[dest],
            r.query_all.at[src],
            r.qb_send.at[0],
            r.qb_recv.at[0],
            TP,
            dest,
        )

    @pl.loop(0, CHIPS)
    def _(i):
        block = at.chip_at(i + 1)
        here = aligned(block, PAIR)
        query = r.queries[here, :]
        start_row = r.starts[:, here]
        stat = r.stats[:, here]
        grad_t = jnp.concatenate([jnp.zeros((HEAD, PAIR), BF), r.grads[:, here]], axis=0)
        grad_rows = grad_t.astype(F32).T.astype(BF)
        head = r.heads_t[:, here]
        delta = jnp.sum(head * grad_t[HEAD : 2 * HEAD, :].astype(F32), axis=0, keepdims=True)
        query_grad = jnp.zeros((HEAD, PAIR), F32)
        for chunk in range(SPAN // CHUNK):
            keys = pl.ds(pl.multiple_of(block * PAIR + chunk * CHUNK, ROWS), CHUNK)
            both = r.keyvals[keys, :]
            score = dot(both, query, NT)
            ok = allowed(r.code[keys, :], start_row, chunk)
            prob = jnp.exp(jnp.where(ok, score - stat, LOWEST))
            prob_grad = dot(both, grad_t)
            score_grad = (prob * (prob_grad - delta)).astype(BF)
            update = dot(score_grad, query) + dot(prob.astype(BF), grad_rows)
            for part in range(CHUNK // ROWS):
                row = jnp.maximum(block * PAIR + (chunk * CHUNK + part * ROWS - REACH), 0)
                place = pl.ds(pl.multiple_of(row, ROWS), ROWS)
                r.kv_sum[place, :] += update[part * ROWS : (part + 1) * ROWS]

            query_grad = query_grad + dot(r.keyvals_t[0:HEAD, keys], score_grad)
        turned = turned_back(query_grad * (1.0 / math.sqrt(HEAD)), r, here).astype(BF)
        r.tail_left[0:HEAD, here] = turned
        r.query_src[2 * block] = turned[:, 0:ROWS]
        r.query_src[2 * block + 1] = turned[:, ROWS:PAIR]

        @pl.when(i < CHIPS - 1)
        def _():
            query_copy(2 * block, t).start()
            query_copy(2 * block + 1, t).start()

        @pl.when(i == CHIPS - 1)
        def _():
            query_copy(at.twin, t).start()

    @pl.loop(0, CHIPS)
    def _(i):
        here = aligned(i, PAIR)
        grad = r.kv_sum[here, :].T
        grad = jnp.concatenate(
            [turned_back(grad[0:HEAD], r, here), grad[HEAD : 2 * HEAD]], axis=0
        ).astype(BF)
        r.tail_left[HEAD : 3 * HEAD, here] = grad
        r.back_src[2 * i] = grad[:, 0:ROWS]
        r.back_src[2 * i + 1] = grad[:, ROWS:PAIR]

    def grad_copy(k, src):
        dest = at.tensor_at(k)
        return remote(
            r.back_src.at[dest],
            r.back_all.at[src],
            r.kb_send.at[0],
            r.kb_recv.at[0],
            TP,
            dest,
        )

    for k in range(1, TENSOR):
        grad_copy(k, t).start()
    r.back_all[t] = r.back_src[t]
    r.query_all[t] = r.query_src[t]
    for part in range(2):
        for j in (1, 2):
            moe_along(j, part).start()
    down_sums(1, *down_loads(1))
    landed = [
        [r.nm_all.at[pl.ds((2 * k + x) * HEAD, HEAD)] for x in range(2)] for k in range(3)
    ]
    ring.end()
    loads = []
    for k in range(3):
        out_along(k + 1).wait_recv()
        for x in range(2):
            loads.append(copies.start(r.out_landed.at[k, x], landed[k][x]))
    copies.need(*loads)

    def out_total(x):
        total = r.out_twins[2 * at.z + x].astype(F32)
        for k in range(3):
            rows = aligned(2 * k + x, HEAD)
            total = total + r.nm_all[rows, :].astype(F32)
        return total

    r.out_joined[...] = out_total(1 - at.x_far).astype(BF)
    out_across().start()
    for number in (6, 7):
        ring_w.pass_on(number)
    for i in range(CHIPS):
        ring_w.second(i)
    ring_c.end()
    copies.need(own_weights)
    weights_load = copies.start(r.wqkv, r.cots)
    copies.need(normed_load)
    r.tail[0 : 3 * HEAD, :] = dot(r.tail_left[...], r.normed[...]).astype(BF)

    copies.need(weights_load)
    whole = r.cots
    for j in range(4):
        rows = [
            whole[i * ROWS + HEAD + j * 16 : i * ROWS + HEAD + (j + 1) * 16, :].astype(F32)
            for i in range(TENSOR)
        ]
        first, second = unpacked(jnp.stack(rows, axis=0))
        r.downs[2 * j * ROWS : (2 * j + 1) * ROWS, :] = first.astype(BF)
        r.downs[(2 * j + 1) * ROWS : (2 * j + 2) * ROWS, :] = second.astype(BF)
    all_landed(r.query_all.at[pl.ds(0, 15)], r.qb_recv.at[0], at)
    all_landed(r.back_all.at[pl.ds(0, 15)], r.kb_recv.at[0], at)
    query_rows = r.query_all[...].astype(F32).reshape(WIDTH, ROWS).T.astype(BF)
    pairs = r.back_all[...].astype(F32).reshape(CHIPS, 2, ROWS, ROWS)
    kv_rows = (pairs[:, 0] + pairs[:, 1]).reshape(WIDTH, ROWS).T.astype(BF)
    wq_full = jnp.concatenate(
        [whole[i * ROWS : i * ROWS + HEAD, :] for i in range(TENSOR)], axis=0
    )
    normed_grad = dot(query_rows, wq_full) + dot(kv_rows, r.downs[...], NT)
    hidden = r.hid[...].astype(F32)
    inverse = lax.rsqrt(jnp.mean(hidden * hidden, axis=1, keepdims=True) + 1e-6)
    unit = hidden * inverse
    gain_one = r.small[...].astype(F32).T[32:33, :]
    gain_one_grad = jnp.sum(normed_grad * unit, axis=0, keepdims=True)
    scaled = normed_grad * gain_one
    r.hidden_grad[...] = (
        r.mid_grad[...]
        + inverse * (scaled - unit * jnp.mean(scaled * unit, axis=1, keepdims=True))
    ).astype(BF)
    r.save("hidden_grad")
    r.tail[3 * HEAD : 3 * HEAD + 32, :] = r.router_t[...].astype(BF)
    row = sublanes((16, WIDTH))
    r.tail[3 * HEAD + 32 : TAIL, :] = jnp.where(
        row == 0, gain_one_grad, jnp.where(row == 1, r.gain_grad[...], 0.0)
    ).astype(BF)

    def tail_along(k):
        y = at.y_at(k)
        return remote(
            r.tail.at[pl.ds(0, TAIL), aligned(y, PAIR)],
            r.tail_in.at[k - 1],
            r.t_send.at[k],
            r.t_recv.at[k],
            SP,
            2 * y + at.x,
        )

    def tail_across():
        return remote(r.tail_src, r.tail_x, r.t_send.at[0], r.t_recv.at[0], SP, at.across)

    for k in range(1, 4):
        tail_along(k).start()

    gu_sums(1, *gu_loads(1))
    out_across().wait_recv()
    crossed = r.proj_grads.at[pl.ds(6 * PAIR, HEAD)]
    copies.need(copies.start(r.out_crossed, crossed))
    r.out_rows[...] = out_total(at.x_far) + crossed[...].astype(F32)

    def out_dp_along(k):
        y = at.y_at(k)
        return remote(
            r.out_rows.at[aligned(y, 16), :],
            r.out_in.at[k - 1],
            r.od_send.at[k],
            r.od_recv.at[k],
            SP,
            2 * y + at.x,
        )

    def out_dp_across():
        return remote(
            r.out_sum.at[aligned(1 - at.x, 8), :],
            r.out_x,
            r.od_send.at[0],
            r.od_recv.at[0],
            SP,
            at.across,
        )

    for k in range(1, 4):
        out_dp_along(k).start()
    def moe_across():
        return remote(
            r.m_joined, r.m_crossed, r.mx_send.at[0], r.mx_recv.at[0], TP, at.near_core(0, 1)
        )

    moe_first().wait_recv()
    across = moe_sums(6)[...].astype(F32) + r.m_landed[0, 0:ROWS].astype(F32)
    for j in (1, 2):
        moe_along(j, 0).wait_recv()
        across = across + r.m_landed[j, 0:ROWS].astype(F32)
    r.m_joined[...] = across.astype(BF)
    moe_across().start()
    loads, crossed = [], []
    for e in range(2):
        down_across(e).wait_recv()
        crossed.append(r.weighted.at[pl.ds(3 * UNITS, UNITS), pl.ds(e * ROWS, ROWS)])
        loads.append(copies.start(r.yx_down.at[e], crossed[-1]))
    gu_across(0).wait_recv()
    crossed.append(r.nm_all.at[pl.ds(WIDTH, ROWS)])
    loads.append(copies.start(r.yx_gu.at[0], crossed[-1]))
    copies.need(*loads)
    for e in range(2):
        r.down_out[e] = r.ys_down[e, at.x].astype(F32) + crossed[e][...].astype(F32)
    r.mid_grad[...] = r.ys_gu[0, at.x].astype(F32) + crossed[2][...].astype(F32)
    copies.start(r.mid_grad, r.gu_out.at[0])
    r.save("down_out")
    total = r.tail[0:TAIL, aligned(at.y, PAIR)].astype(F32)
    for k in range(1, 4):
        tail_along(k).wait_recv()
        total = total + r.tail_in[k - 1].astype(F32)
    r.scores[0:TAIL, :] = total
    r.tail_src[...] = r.scores[0:TAIL, aligned(1 - at.x, ROWS)].astype(BF)
    tail_across().start()
    gu_half(1).start()
    total = r.out_rows[aligned(at.y, 16), :]
    for k in range(1, 4):
        out_dp_along(k).wait_recv()
        total = total + r.out_in[k - 1]
    r.out_sum[...] = total
    out_dp_across().start()
    tail_across().wait_recv()
    total = r.scores[0:TAIL, aligned(at.x, ROWS)] + r.tail_x[...].astype(F32)
    r.query_out[...] = total[0:HEAD, :]
    r.save("query_out")
    turned = jnp.concatenate(
        [total[HEAD:TAIL], jnp.zeros((256 + HEAD - TAIL, ROWS), F32)], axis=0
    ).T
    for j in range(TENSOR):
        r.pieces[j] = turned[j * 8 : (j + 1) * 8, :]

    def last_copy(k, src):
        dest = at.tensor_at(k)
        return remote(
            r.pieces.at[dest], r.last.at[src], r.l_send.at[0], r.l_recv.at[0], TP, dest
        )

    for k in range(1, TENSOR):
        last_copy(k, t).start()
    r.last[t] = r.pieces[t]

    own = r.mid[...] + moe_sums(7)[...].astype(F32) + r.m_landed[0, ROWS:PAIR].astype(F32)
    for j in (1, 2):
        moe_along(j, 1).wait_recv()
        own = own + r.m_landed[j, ROWS:PAIR].astype(F32)
    place = r.nm_all.at[pl.ds(WIDTH + PAIR, ROWS)]
    moe_across().wait_recv()
    copies.need(copies.start(r.m_crossed, place))
    r.output[...] = (own + place[...].astype(F32)).astype(BF)
    r.save("output")
    for part in range(2):
        gu_half(part).wait_recv()
    place = r.nm_all.at[pl.ds(WIDTH + ROWS, ROWS)]
    copies.need(copies.start(r.yx_gu.at[1], place))
    r.mid[...] = r.ys_gu[1, at.x].astype(F32) + place[...].astype(F32)
    copies.start(r.mid, r.gu_out.at[1])
    out_dp_across().wait_recv()
    r.out_grad[...] = r.out_sum[aligned(at.x, 8), :] + r.out_x[...]
    all_landed(r.last.at[pl.ds(0, 15)], r.l_recv.at[0], at)
    r.kv_out[...] = jnp.concatenate(
        [r.last[2 * j, :, 0:ROWS] + r.last[2 * j + 1, :, 0:ROWS] for j in range(CHIPS)], axis=1
    )
    shared = r.last[0, :, ROWS:PAIR]
    for j in range(1, TENSOR):
        shared = shared + r.last[j, :, ROWS:PAIR]
    r.router_out[...] = shared[:, 0:32]
    wide = jnp.concatenate([shared, jnp.zeros((ROWS - 8, ROWS), F32)], axis=0).T
    r.gain_one_out[...] = wide[32:33, 0:8]
    r.gain_two_out[...] = wide[33:34, 0:8]
    r.save("out_grad", "kv_out", "router_out", "gain_one_out", "gain_two_out")

    all_sent(r.tiles.at[pl.ds(0, 15)], r.t1_send.at[0], at)
    all_sent(r.tile_all.at[pl.ds(0, 7)], r.t2_send.at[0], at)
    all_sent(r.row_dp.at[pl.ds(0, 7)], r.rd_send.at[0], at)
    all_sent(seven_wq, r.wq_send.at[0], at)
    all_sent(r.gate_src.at[pl.ds(0, 15)], r.gg_send.at[0], at)
    all_sent(r.att_grad_t.at[pl.ds(0, 15 * HEAD)], r.b_send.at[0], at)
    all_sent(r.query_src.at[pl.ds(0, 15)], r.qb_send.at[0], at)
    all_sent(r.back_src.at[pl.ds(0, 15)], r.kb_send.at[0], at)
    all_sent(r.pieces.at[pl.ds(0, 15)], r.l_send.at[0], at)
    for k in range(1, 4):
        tail_along(k).wait_send()
        out_dp_along(k).wait_send()
    tail_across().wait_send()
    out_dp_across().wait_send()
    moe_first().wait_send()
    for j in (1, 2):
        for part in range(2):
            moe_along(j, part).wait_send()
    moe_across().wait_send()
    for k in range(1, 4):
        out_along(k).wait_send()
    out_across().wait_send()
    out_half().wait_send()
    for e in range(2):
        for k in range(1, 4):
            gu_over_y(e, k).wait_send()
            down_over_y(e, k).wait_send()
        gu_half(e).wait_send()
        down_across(e).wait_send()
    gu_across(0).wait_send()
    ring_w.end()
    copies.wait()
    r.end()


def store_kernel(r):
    copies = Copies(r.local)
    for name in STORED:
        copies.start(getattr(r, name), getattr(r, name + "_kept"))
    for name in STORED:
        copies.wait(1)
        copies.start(getattr(r, name + "_kept"), getattr(r, name + "_done"))
    copies.wait()


STORED = (
    "output",
    "hidden_grad",
    "gain_one_out",
    "query_out",
    "kv_out",
    "out_grad",
    "gain_two_out",
    "router_out",
    "gu_out",
    "down_out",
)


class Refs:
    def __init__(self, names, refs, loads=(), saves=()):
        for name, ref in zip(names, refs):
            setattr(self, name, ref)
        self.loads, self.saves, self.saved = list(loads), list(saves), []

    def copy_in(self, name):
        sem = self.load_sems.at[self.loads.index(name)]
        return pltpu.make_async_copy(getattr(self, name + "_d"), getattr(self, name), sem)

    def copy_out(self, name):
        sem = self.save_sems.at[self.saves.index(name)]
        return pltpu.make_async_copy(getattr(self, name), getattr(self, name + "_d"), sem)

    def load(self):
        for name in self.loads:
            self.copy_in(name).start()

    def need(self, *names):
        for name in names:
            self.copy_in(name).wait()

    def save(self, *names):
        for name in names:
            self.copy_out(name).start()
            self.saved.append(name)

    def finish(self, name):
        self.copy_out(name).wait()
        self.saved.remove(name)

    def end(self):
        for name in self.saved:
            self.copy_out(name).wait()


def call(kernel, number, inputs, outputs, scratch, reaches=True):
    def space(name):
        return pl.BlockSpec(memory_space=pltpu.VMEM if name.endswith("_v") else pl.ANY)

    outputs = {name: jax.ShapeDtypeStruct(shape, dtype) for name, (shape, dtype) in outputs.items()}
    loads = [name[:-2] for name in inputs if name.endswith("_d")]
    saves = [name[:-2] for name in outputs if name.endswith("_d")]
    scratch = dict(scratch)
    for name in loads:
        scratch[name] = pltpu.VMEM(inputs[name + "_d"].shape, inputs[name + "_d"].dtype)
    for name in saves:
        scratch[name] = pltpu.VMEM(outputs[name + "_d"].shape, outputs[name + "_d"].dtype)
    scratch |= sems(load_sems=max(1, len(loads)), save_sems=max(1, len(saves)))
    names = [name.removesuffix("_v") for name in (*inputs, *outputs)] + list(scratch)
    params = {"vmem_limit_bytes": VMEM_BYTES}
    if reaches:
        params |= {"collective_id": number, "has_side_effects": True}
    values = pl.pallas_call(
        lambda *refs: kernel(Refs(names, refs, loads, saves)),
        out_shape=list(outputs.values()),
        in_specs=[space(name) for name in inputs],
        out_specs=[space(name) for name in outputs],
        scratch_shapes=list(scratch.values()),
        compiler_params=pltpu.CompilerParams(**params),
        name=kernel.__name__,
    )(*inputs.values())
    return Refs([name.removesuffix("_v").removesuffix("_d") for name in outputs], values)


def sems(**counts):
    return {name: pltpu.SemaphoreType.DMA((count,)) for name, count in counts.items()}


def rope_tables():
    half = HEAD // 2
    freqs = np.exp(
        np.arange(half, dtype=np.float32) * np.float32(-2.0 * math.log(10000.0) / HEAD)
    ).astype(np.float32)
    angles = np.arange(LENGTH, dtype=np.float32)[:, None] * freqs[None, :]
    cos, sin = np.cos(angles).astype(np.float32), np.sin(angles).astype(np.float32)
    return (
        np.concatenate([cos, cos, -sin, sin], axis=1),
        np.ascontiguousarray(cos.T),
        np.ascontiguousarray(sin.T),
    )


def body(
    hidden,
    seg_ids,
    key_mask,
    routes,
    gain_attn,
    w_query,
    w_keyval,
    w_out,
    gain_mlp,
    w_router,
    w_gate_up,
    w_down,
    cotangent,
):
    V = pltpu.VMEM
    turns, cosine_t, sine_t = rope_tables()
    hid, cot = hidden[0], cotangent[0]
    c = call(
        layer_kernel,
        1,
        dict(
            hid_v=hid,
            cot=cot,
            w_keyval_v=w_keyval,
            w_out_t_v=w_out.T,
            w_query_t_v=w_query.T,
            router_v=w_router,
            gain_one_v=gain_attn.reshape(1, 8),
            gain_two_v=gain_mlp.reshape(1, 8),
            gu=w_gate_up,
            down=w_down,
            turns_d=turns,
            cosine_t_d=cosine_t,
            sine_t_d=sine_t,
            mask_v=key_mask,
            seg_v=seg_ids,
            routes_t_v=routes[0].T,
        ),
        dict(
            output_d=((ROWS, WIDTH), BF),
            hidden_grad_d=((ROWS, WIDTH), BF),
            gain_one_out_d=((1, 8), F32),
            query_out_d=((HEAD, ROWS), F32),
            kv_out_d=((8, WIDTH), F32),
            out_grad_d=((8, WIDTH), F32),
            gain_two_out_d=((1, 8), F32),
            router_out_d=((8, 32), F32),
            gu_out=((2, ROWS, WIDTH), F32),
            down_out_d=((2, UNITS, ROWS), F32),
            normed_d=((LENGTH, WIDTH), BF),
            out_t_d=((WIDTH, WIDTH), BF),
            wqkv=((LENGTH, WIDTH), BF),
            y_gu=((2, 3, PAIR, WIDTH), BF),
            y_down=((2, 3, UNITS, PAIR), BF),
            yx_gu=((2, ROWS, WIDTH), BF),
            yx_down=((2, UNITS, ROWS), BF),
            out_landed=((3, 2, HEAD, WIDTH), BF),
            out_crossed=((HEAD, WIDTH), BF),
            m_crossed=((ROWS, WIDTH), BF),
        ),
        dict(
            hidden_all=V((LENGTH, WIDTH), BF),
            nm_all=V((LENGTH, WIDTH), BF),
            cots=V((LENGTH, WIDTH), BF),
            gus=V((2, WIDTH, WIDTH), BF),
            downs=V((WIDTH, WIDTH), BF),
            down_grads=V((2, UNITS, WIDTH), BF),
            weighted=V((LENGTH, UNITS), BF),
            weighted_t=V((UNITS, LENGTH), BF),
            queries=V((LENGTH, 2 * HEAD), BF),
            keyvals=V((PADDED, 2 * HEAD), BF),
            keyvals_t=V((2 * HEAD, PADDED), BF),
            stats=V((1, LENGTH), F32),
            heads_t=V((HEAD, LENGTH), F32),
            small=V((WIDTH, ROWS), BF),
            mid=V((ROWS, WIDTH), F32),
            mid_grad=V((ROWS, WIDTH), F32),
            router_t=V((32, WIDTH), F32),
            gain_grad=V((1, WIDTH), F32),
            wqkv_own=V((ROWS, WIDTH), BF),
            rows=V((16, WIDTH), BF),
            row_dp=V((DP, 16, WIDTH), BF),
            shares=V((8, ROWS), F32),
            tiles=V((TENSOR, 16, ROWS), BF),
            tile_all=V((DP, TENSOR, 16, ROWS), BF),
            out_all=V((CHIPS, ROWS, WIDTH), BF),
            wq_all=V((2 * HEAD, WIDTH), BF),
            code=V((PADDED, ROWS), F32),
            scores=V((SPAN, PAIR), F32),
            starts=V((1, LENGTH), F32),
            wqk=V((WIDTH, PAIR), BF),
            att_src=V((TENSOR, HEAD, ROWS), BF),
            att_t=V((WIDTH, ROWS), BF),
            att_rows=V((ROWS, WIDTH), BF),
            ys_gu=V((2, 2, ROWS, WIDTH), BF),
            ys_down=V((2, 2, UNITS, ROWS), BF),
            n_parts=V((SLOTS, PAIR, WIDTH), BF),
            n_twins=V((SLOTS, ROWS, WIDTH), BF),
            n_credit=pltpu.SemaphoreType.REGULAR,
            n_crossed=V((4, ROWS, WIDTH), BF),
            n_landed=V((3, ROWS, WIDTH), BF),
            m_parts=V((SLOTS, PAIR, WIDTH), BF),
            m_twins=V((SLOTS, ROWS, WIDTH), BF),
            m_credit=pltpu.SemaphoreType.REGULAR,
            m_landed=V((3, PAIR, WIDTH), BF),
            gate_src=V((TENSOR, 8, ROWS), F32),
            gate_all=V((TENSOR, 8, ROWS), F32),
            grads=V((HEAD, LENGTH), BF),
            query_all=V((TENSOR, HEAD, ROWS), BF),
            back_src=V((TENSOR, ROWS, ROWS), BF),
            back_all=V((TENSOR, ROWS, ROWS), BF),
            out_twins=V((CHIPS, HEAD, WIDTH), BF),
            out_joined=V((HEAD, WIDTH), BF),
            out_rows=V((HEAD, WIDTH), F32),
            out_in=V((3, 16, WIDTH), F32),
            out_sum=V((16, WIDTH), F32),
            out_x=V((8, WIDTH), F32),
            tail_in=V((3, TAIL, PAIR), BF),
            tail_src=V((TAIL, ROWS), BF),
            tail_x=V((TAIL, ROWS), BF),
            pieces=V((TENSOR, 8, PAIR), F32),
            last=V((TENSOR, 8, PAIR), F32),
        )
        | sems(
            h_send=1,
            h_recv=24,
            c_send=1,
            c_recv=24,
            o_send=1,
            o_recv=24,
            g_send=1,
            g_recv=24,
            t1_send=1,
            t1_recv=1,
            t2_send=1,
            t2_recv=1,
            t2x_recv=1,
            rdx_recv=1,
            rd_send=1,
            rd_recv=1,
            wq_send=1,
            wq_recv=1,
            e_send=4,
            e_recv=40,
            a_send=1,
            a_recv=1,
            ntw_send=SLOTS,
            ntw_recv=SLOTS,
            nc_send=4,
            nc_recv=4,
            n_send=3,
            n_recv=3,
            mtw_send=SLOTS,
            mtw_recv=SLOTS,
            m_send=5,
            m_recv=5,
            mx_send=1,
            mx_recv=1,
            gg_send=1,
            gg_recv=1,
            b_send=1,
            b_recv=1,
            ot_send=1,
            ot_recv=1,
            oz_send=4,
            oz_recv=4,
            qb_send=1,
            qb_recv=1,
            kb_send=1,
            kb_recv=1,
            x_send=8,
            x_recv=8,
            y_send=8,
            y_recv=8,
            tx_send=5,
            tx_recv=5,
            t_send=4,
            t_recv=4,
            od_send=4,
            od_recv=4,
            l_send=1,
            l_recv=1,
            local=20,
        ),
    )
    values = {name: getattr(c, name) for name in STORED}
    done = call(
        store_kernel,
        0,
        values,
        {name + "_done": (value.shape, value.dtype) for name, value in values.items()},
        {name + "_kept": V(value.shape, value.dtype) for name, value in values.items()}
        | sems(local=2 * len(STORED)),
        reaches=False,
    )
    return (
        done.output_done[None],
        done.hidden_grad_done[None],
        done.gain_one_out_done.reshape(8),
        done.query_out_done.T,
        done.kv_out_done,
        done.out_grad_done.T,
        done.gain_two_out_done.reshape(8),
        done.router_out_done,
        done.gu_out_done,
        done.down_out_done,
    )


def solution(mesh):
    return jax.shard_map(
        body,
        mesh=mesh,
        in_specs=(
            P("dp", "tensor", None),
            P("dp", None),
            P("dp", None),
            P("dp", None, None),
            P(("dp", "tensor")),
            P("dp", "tensor"),
            P(("dp", "tensor"), None),
            P(None, ("dp", "tensor")),
            P(("dp", "tensor")),
            P(("dp", "tensor"), None),
            P("tensor", "dp", None),
            P("tensor", None, "dp"),
            P("dp", "tensor", None),
        ),
        out_specs=(
            P("dp", "tensor", None),
            P("dp", "tensor", None),
            P(("dp", "tensor")),
            P("dp", "tensor"),
            P(("dp", "tensor"), None),
            P(None, ("dp", "tensor")),
            P(("dp", "tensor")),
            P(("dp", "tensor"), None),
            P("tensor", "dp", None),
            P("tensor", None, "dp"),
        ),
        check_vma=False,
    )
```

```python
import math

import jax
import jax.numpy as jnp
import numpy as np
from jax import lax
from jax.experimental import pallas as pl
from jax.experimental.pallas import tpu as pltpu
from jax.sharding import PartitionSpec as P

HEAD = 64
LENGTH = 2048
WIDTH = 1024
UNITS = 512
ROWS = 128
PAIR = 256
CHUNK = 384
REACH = 896
SPAN = REACH + PAIR
PADDED = REACH + LENGTH
CHIPS = 8
TENSOR = 16
DP = 8
TAIL = 240
SLOTS = 2
STEP_Z = (0, 0, 1, 3, 1, 3, 2, 2)
STEP_X = (0, 1, 0, 0, 1, 1, 0, 1)
SUM_Z = (2, 2, 1, 1, 3, 3, 0, 0)
SUM_X = (1, 0, 1, 0, 1, 0, 1, 0)
LOWEST = -1e30
TP = "tensor"
SP = "dp"
BF = jnp.bfloat16
F32 = jnp.float32
MESH = pl.DeviceIdType.MESH
VMEM_BYTES = 63 * 1024 * 1024

NN = (((1,), (0,)), ((), ()))
NT = (((1,), (1,)), ((), ()))
TN = (((0,), (0,)), ((), ()))


def dot(left, right, dims=NN):
    return lax.dot_general(left, right, dims, preferred_element_type=F32)


def aligned(value, size):
    return pl.ds(pl.multiple_of(value * size, size), size)


def remote(src, dst, send, recv, axis, index):
    return pltpu.make_async_remote_copy(
        src_ref=src,
        dst_ref=dst,
        send_sem=send,
        recv_sem=recv,
        device_id={axis: index},
        device_id_type=MESH,
    )


def all_sent(ref, sem, place):
    remote(ref, ref, sem, sem, TP, place.twin).wait_send()


def all_landed(ref, sem, place):
    remote(ref, ref, sem, sem, TP, place.twin).wait_recv()


class Place:
    def __init__(self):
        self.t = lax.axis_index(TP)
        self.d = lax.axis_index(SP)
        self.core = lax.rem(self.t, 2)
        self.chip = self.t // 2
        self.twin = self.t + 1 - 2 * self.core
        self.x = lax.rem(self.d, 2)
        self.y = self.d // 2
        self.across = self.d + 1 - 2 * self.x
        self.z = self.chip // 2
        self.x_far = lax.rem(self.chip, 2)

    def chip_at(self, k):
        return lax.rem(self.chip + k, CHIPS)

    def same_core(self, k):
        return 2 * self.chip_at(k) + self.core

    def near(self, dz, dx):
        return 2 * lax.rem(self.z + dz, 4) + lax.rem(self.x_far + dx, 2)

    def near_core(self, dz, dx):
        return 2 * self.near(dz, dx) + self.core

    def listed(self, i, all_z, all_x):
        if isinstance(i, int):
            return self.near(all_z[i], all_x[i])
        dz, dx = jnp.int32(0), jnp.int32(0)
        for k in range(CHIPS):
            dz = jnp.where(i == k, all_z[k], dz)
            dx = jnp.where(i == k, all_x[k], dx)
        return self.near(dz, dx)

    def step(self, i):
        return self.listed(i, STEP_Z, STEP_X)

    def sum_step(self, i):
        return self.listed(i, SUM_Z, SUM_X)

    def step_core(self, i):
        return 2 * self.step(i) + self.core

    def tensor_at(self, k):
        return lax.rem(self.t + k, TENSOR)

    def dp_at(self, k):
        return lax.rem(self.d + k, DP)

    def y_at(self, k):
        return lax.rem(self.y + k, 4)

    def enter(self):
        barrier = pltpu.get_barrier_semaphore()
        for k in range(1, TENSOR):
            pl.semaphore_signal(
                barrier, inc=1, device_id={TP: self.tensor_at(k)}, device_id_type=MESH
            )
        for k in range(1, DP):
            pl.semaphore_signal(
                barrier, inc=1, device_id={SP: self.dp_at(k)}, device_id_type=MESH
            )
        pl.semaphore_wait(barrier, TENSOR + DP - 2)


class Ring:
    def __init__(self, place, block, half, send, recv, most, source=None, source_half=None):
        self.place, self.block, self.half = place, block, half
        self.send, self.recv, self.most = send, recv, most
        self.source, self.source_half = source, source_half

    def send_sem(self, number):
        return self.send.at[0]

    def copy(self, number, index, dest, source=None):
        src = self.block(index) if source is None else source
        return remote(
            src, self.block(index), self.send_sem(number), self.recv.at[index], TP, dest
        )

    def piece(self, number, index, part, dest, source=None):
        ref = self.half(index, part)
        place = TENSOR + index // 2 if part else index
        return remote(
            ref if source is None else source,
            ref,
            self.send_sem(number),
            self.recv.at[place],
            TP,
            dest,
        )

    def sent(self, number):
        at = self.place
        if number == 0:
            return self.copy(0, at.t, at.twin, self.source)
        if number < 4:
            return self.copy(number, at.t, at.step_core(number), self.source)
        if number < 6:
            return self.copy(number, at.step_core(1), at.step_core(number - 2))
        if number < 8:
            return self.piece(number, at.step_core(2 * number - 9), 0, at.step_core(2))
        if number < 10:
            return self.piece(number, at.step_core(2 * number - 14), 1, at.step_core(3))
        return self.copy(number, at.step_core(number - 9), at.twin)

    def start(self):
        at = self.place
        for part in range(2):
            src = None if self.source_half is None else self.source_half(part)
            self.piece(1, at.t, part, at.step_core(1), src).start()
        for number in (2, 3, 0):
            self.sent(number).start()

    def piece_arrived(self, index, part):
        self.piece(0, index, part, self.place.twin).wait_recv()

    def pass_on(self, i):
        at = self.place
        index = at.step_core(i)
        if i in (2, 3):
            self.copy(0, index, at.twin).wait_recv()
            self.sent(8 if i == 2 else 6).start()
        elif i == 1:
            for part in range(2):
                self.piece_arrived(index, part)
                self.piece(4, index, part, at.step_core(2)).start()
                self.piece(5, index, part, at.step_core(3)).start()
        elif i == 4:
            self.piece_arrived(index, 1)
            self.sent(9).start()
            self.piece_arrived(index, 0)
        elif i == 5:
            self.piece_arrived(index, 0)
            self.sent(7).start()
            self.piece_arrived(index, 1)
        else:
            self.piece_arrived(index, 0)
            self.piece_arrived(index, 1)
        self.sent(9 + i).start()

    def pass_on_at(self, i):
        for k in range(1, CHIPS):

            @pl.when(i == k - 1)
            def _(k=k):
                self.pass_on(k)

    def second(self, i):
        self.copy(0, 2 * self.place.step(i) + 1 - self.place.core, self.place.twin).wait_recv()

    def end(self):
        all_sent(self.most, self.send.at[0], self.place)


def whole_ring(place, ref, send, recv, source=None):
    return Ring(
        place,
        lambda b: ref.at[aligned(b, ROWS)],
        lambda b, part: ref.at[pl.ds(pl.multiple_of(b * ROWS + part * HEAD, HEAD), HEAD)],
        send,
        recv,
        ref.at[pl.ds(0, 15 * ROWS)],
        source,
        None if source is None else lambda part: source.at[pl.ds(part * HEAD, HEAD)],
    )


class Copies:
    def __init__(self, sems):
        self.sems, self.pending, self.free, self.used = sems, [], [], 0

    def start(self, src, dst):
        if self.free:
            number = self.free.pop()
        else:
            number, self.used = self.used, self.used + 1
        copy = pltpu.make_async_copy(src, dst, self.sems.at[number])
        copy.start()
        self.pending.append((copy, number))
        return copy

    def wait(self, count=None):
        count = len(self.pending) if count is None else count
        for copy, number in self.pending[:count]:
            copy.wait()
            self.free.append(number)
        self.pending = self.pending[count:]

    def need(self, *copies):
        for copy in copies:
            copy.wait()
            self.free += [number for other, number in self.pending if other is copy]
            self.pending = [pair for pair in self.pending if pair[0] is not copy]


def lanes(shape):
    return lax.broadcasted_iota(jnp.int32, shape, len(shape) - 1)


def sublanes(shape):
    return lax.broadcasted_iota(jnp.int32, shape, 0)


def swapped(values):
    return jnp.where(
        lanes(values.shape) < HEAD // 2,
        pltpu.roll(values, 2 * HEAD - HEAD // 2, 1),
        pltpu.roll(values, HEAD // 2, 1),
    )


def document_starts(seg):
    starts = jnp.zeros(seg.shape, F32)
    for document in range(8):
        before = jnp.sum(jnp.where(seg < document, 1.0, 0.0), axis=1, keepdims=True)
        starts = starts + jnp.where(seg == document, before, 0.0)
    return starts


def key_codes(mask, code):
    code[0:REACH, :] = jnp.full((REACH, ROWS), -1.0, F32)

    @pl.loop(0, TENSOR)
    def _(i):
        row = mask[:, aligned(i, ROWS)].astype(F32)
        live = jnp.broadcast_to(row, (ROWS, ROWS)).T == 1.0
        places = (sublanes((ROWS, ROWS)) + i * ROWS).astype(F32)
        code[pl.ds(pl.multiple_of(REACH + i * ROWS, ROWS), ROWS), :] = jnp.where(
            live, places, -1.0
        )


def allowed(code, start_row, chunk):
    ok = jnp.concatenate([code, code], axis=1) >= start_row
    if (chunk + 1) * CHUNK > REACH:
        key = sublanes((CHUNK, PAIR)) + (chunk * CHUNK - REACH)
        query = lanes((CHUNK, PAIR))
        ok = (ok & (key < query)) | (key == query)
    return ok


def turned_back(grad, r, here):
    cos, sin = r.cosine_t[:, here], r.sine_t[:, here]
    first, second = grad[0 : HEAD // 2], grad[HEAD // 2 : HEAD]
    return jnp.concatenate([first * cos + second * sin, second * cos - first * sin], axis=0)


class Halves:
    def __init__(self, place, parts, twins, sums, send, recv, credit):
        self.place, self.parts, self.twins, self.sums = place, parts, twins, sums
        self.send, self.recv, self.credit = send, recv, credit

    def half(self, k):
        at, slot = self.place, lax.rem(k, SLOTS)
        return remote(
            self.parts.at[slot, aligned(1 - at.core, ROWS), :],
            self.twins.at[slot],
            self.send.at[slot],
            self.recv.at[slot],
            TP,
            at.twin,
        )

    def put(self, k, value):
        @pl.when(k >= SLOTS)
        def _():
            self.half(k - SLOTS).wait_send()
            pl.semaphore_wait(self.credit, 1)

        self.parts[lax.rem(k, SLOTS)] = value.astype(BF)
        self.half(k).start()

    def add(self, k):
        slot = lax.rem(k, SLOTS)
        self.half(k).wait_recv()
        own = self.parts[slot, aligned(self.place.core, ROWS), :].astype(F32)
        self.sums(k)[...] = (own + self.twins[slot].astype(F32)).astype(BF)

        @pl.when(k < CHIPS - SLOTS)
        def _():
            pl.semaphore_signal(
                self.credit, inc=1, device_id={TP: self.place.twin}, device_id_type=MESH
            )

    def end(self):
        for k in range(CHIPS - SLOTS, CHIPS):
            self.half(k).wait_send()


class Joined:
    def __init__(self, place, sums, crossed, landed, sems):
        self.place, self.sums, self.crossed, self.landed = place, sums, crossed, landed
        self.c_send, self.c_recv, self.send, self.recv = sems

    def cross(self, j):
        return remote(
            self.sums.at[2 * j],
            self.crossed.at[j],
            self.c_send.at[j],
            self.c_recv.at[j],
            TP,
            self.place.near_core(0, 1),
        )

    def whole(self, j):
        return remote(
            self.sums.at[2 * j + 1],
            self.landed.at[j],
            self.send.at[j],
            self.recv.at[j],
            TP,
            self.place.near_core(SUM_Z[2 * j], 0),
        )

    def join(self, j):
        self.cross(j).wait_recv()
        total = self.sums[2 * j + 1].astype(F32) + self.crossed[j].astype(F32)
        self.sums[2 * j + 1] = total.astype(BF)
        self.whole(j).start()

    def result(self):
        self.cross(3).wait_recv()
        total = self.sums[7].astype(F32) + self.crossed[3].astype(F32)
        for j in range(3):
            self.whole(j).wait_recv()
            total = total + self.landed[j].astype(F32)
        return total

    def end(self):
        for j in range(4):
            self.cross(j).wait_send()
        for j in range(3):
            self.whole(j).wait_send()


def unpacked(both):
    return both[:, 0:8].reshape(ROWS, WIDTH), both[:, 8:16].reshape(ROWS, WIDTH)


def aligned_rows(ref, unit):
    def block(src, part=None):
        if part is None:
            return ref.at[pl.ds(pl.multiple_of(src * 2 * unit, unit), 2 * unit), :]
        return ref.at[pl.ds(pl.multiple_of((src * 2 + part) * unit, unit), unit), :]

    return block


def column_blocks(ref):
    def block(src, part=None):
        if part is None:
            return ref.at[:, aligned(src, ROWS)]
        return ref.at[pl.ds(part * PAIR, PAIR), aligned(src, ROWS)]

    return block


class Stream:
    def __init__(self, place, own, block, most, r, number):
        self.place, self.own, self.block, self.most = place, own, block, most
        self.send, self.recv = r.e_send, r.e_recv
        self.number, self.first_recv = number, 10 * number

    def at_y(self, k, other=False):
        at = self.place
        column = 1 - at.x if other else at.x
        return 2 * at.y_at(k) + column

    def copy(self, number, src, dest, part=None, source=None):
        ref = self.block(src, part)
        return remote(
            ref if source is None else source,
            ref,
            self.send.at[self.number],
            self.recv.at[self.first_recv + (8 + lax.rem(src, 2) if part else src)],
            SP,
            dest,
        )

    def sent(self, number):
        at, at_y = self.place, self.at_y
        if number == 0:
            return self.copy(0, at.d, at.across, source=self.own)
        if number < 3:
            return self.copy(number, at.d, at_y(2 * number - 1), source=self.own)
        if number < 5:
            return self.copy(number, at.across, at_y(2 * number - 5))
        other = number > 6
        if number % 2:
            return self.copy(number, at_y(3, other), at_y(1), 0)
        return self.copy(number, at_y(1, other), at_y(3), 1)

    def arrived(self, src, halves=False):
        for part in (0, 1) if halves else (None,):
            self.copy(0, src, self.place.across, part).wait_recv()

    def start_x(self):
        self.sent(0).start()

    def start_y(self):
        self.sent(1).start()
        self.sent(2).start()

    def from_across(self):
        self.arrived(self.place.across)
        self.sent(3).start()
        self.sent(4).start()

    def from_y(self):
        self.arrived(self.at_y(3))
        self.sent(5).start()
        self.arrived(self.at_y(1))
        self.sent(6).start()

    def from_y_across(self):
        self.arrived(self.at_y(3, True))
        self.sent(7).start()
        self.arrived(self.at_y(1, True))
        self.sent(8).start()

    def finish(self):
        self.arrived(self.at_y(2), True)
        self.arrived(self.at_y(2, True), True)

    def end(self):
        all_sent(self.most, self.send.at[self.number], self.place)


def expert_streams(at, r, e):
    downs = r.downs.at[pl.ds(e * UNITS, UNITS)]
    return (
        Stream(
            at,
            r.gu.at[e],
            aligned_rows(r.gus.at[e], HEAD),
            r.gus.at[e, pl.ds(0, 7 * ROWS)],
            r,
            2 * e,
        ),
        Stream(
            at,
            r.down.at[e],
            column_blocks(downs),
            downs.at[:, pl.ds(0, 7 * ROWS)],
            r,
            2 * e + 1,
        ),
    )


def layer_kernel(r):
    at = Place()
    t, d = at.t, at.d
    copies = Copies(r.local)
    r.load()
    r.hidden_all[aligned(t, ROWS), :] = r.hid[...]
    keyval, out_rows = r.w_keyval[...].astype(F32), r.w_out_t[...].astype(F32)
    r.rows[...] = jnp.concatenate([keyval, out_rows], axis=0).astype(BF)
    r.row_dp[d] = r.rows[...]
    r.shares[...] = jnp.zeros((8, ROWS), F32)
    r.shares[:, 0:32] = r.router[...].astype(F32)
    same = sublanes((8, 8)) == lanes((8, 8))
    for column, gain in ((32, r.gain_one), (33, r.gain_two)):
        wide = jnp.broadcast_to(gain[...].astype(F32), (8, 8))
        r.shares[:, column : column + 1] = jnp.sum(
            jnp.where(same, wide, 0.0), axis=1, keepdims=True
        )
    for j in range(CHIPS):
        tile = jnp.concatenate([keyval[:, j * ROWS : (j + 1) * ROWS], r.shares[...]], axis=0)
        r.tiles[2 * j] = tile.astype(BF)
        r.tiles[2 * j + 1] = tile.astype(BF)
    r.tile_all[d, t] = r.tiles[t]
    r.wq_all[HEAD : 2 * HEAD, :] = jnp.zeros((HEAD, WIDTH), BF)
    r.wq_all[0:HEAD, aligned(d, ROWS)] = r.w_query_t[...]
    at.enter()

    def tile_one(k, src):
        dest = at.tensor_at(k)
        return remote(
            r.tiles.at[dest],
            r.tile_all.at[d, src],
            r.t1_send.at[0],
            r.t1_recv.at[0],
            TP,
            dest,
        )

    def y_peer(k):
        return 2 * at.y_at(k) + at.x

    def tile_two(src, dest, recv):
        ref = r.tile_all.at[src]
        return remote(ref, ref, r.t2_send.at[0], recv.at[0], SP, dest)

    def rows_dp(src, dest, recv, source=None):
        ref = r.row_dp.at[src]
        return remote(
            ref if source is None else source, ref, r.rd_send.at[0], recv.at[0], SP, dest
        )

    def wq_dp(k, src):
        return remote(
            r.w_query_t,
            r.wq_all.at[pl.ds(0, HEAD), aligned(src, ROWS)],
            r.wq_send.at[0],
            r.wq_recv.at[0],
            SP,
            at.dp_at(k),
        )

    first_expert, second_expert = expert_streams(at, r, 0), expert_streams(at, r, 1)

    for k in range(1, TENSOR):
        tile_one(k, t).start()
    for k in range(1, DP):
        wq_dp(k, d).start()
    ring_h = whole_ring(at, r.hidden_all, r.h_send, r.h_recv)
    ring_h.start()
    for e in range(2):
        copies.start(r.gu.at[e], r.gus.at[e, aligned(d, ROWS)])
        copies.start(r.down.at[e], r.downs.at[pl.ds(e * UNITS, UNITS), aligned(d, ROWS)])
    copies.start(r.cot, r.cots.at[aligned(t, ROWS)])

    key_codes(r.mask, r.code)
    r.starts[...] = document_starts(r.seg[...])
    r.keyvals[0:REACH, :] = jnp.zeros((REACH, 2 * HEAD), BF)
    r.keyvals_t[:, 0:REACH] = jnp.zeros((2 * HEAD, REACH), BF)

    all_landed(r.tile_all.at[0, pl.ds(0, 15)], r.t1_recv.at[0], at)
    tile_two(d, at.across, r.t2x_recv).start()
    rows_dp(d, at.across, r.rdx_recv, r.rows).start()
    for k in range(1, 4):
        tile_two(d, y_peer(k), r.t2_recv).start()
        rows_dp(d, y_peer(k), r.rd_recv, r.rows).start()
    for stream in first_expert:
        stream.start_x()
    for i in range(1, 4):
        ring_h.pass_on(i)
    tile_two(at.across, at.across, r.t2x_recv).wait_recv()
    for k in range(1, 4):
        tile_two(at.across, y_peer(k), r.t2_recv).start()
    rows_dp(at.across, at.across, r.rdx_recv).wait_recv()
    for k in range(1, 4):
        rows_dp(at.across, y_peer(k), r.rd_recv).start()
    for stream in first_expert:
        stream.start_y()
    seven_wq = r.wq_all.at[pl.ds(0, HEAD), pl.ds(0, 7 * ROWS)]
    all_landed(seven_wq, r.wq_recv.at[0], at)
    all_landed(r.tile_all.at[pl.ds(0, 6)], r.t2_recv.at[0], at)
    for j in range(DP):
        both = r.tile_all[j].astype(F32)
        r.wqk[j * ROWS : (j + 1) * ROWS, ROWS:PAIR] = both[:, 0:8].reshape(ROWS, ROWS).astype(BF)
        r.small[j * ROWS : (j + 1) * ROWS, :] = both[:, 8:16].reshape(ROWS, ROWS).astype(BF)
    r.wqk[:, 0:ROWS] = r.wq_all[...].astype(F32).T.astype(BF)
    columns = r.small[...].astype(F32).T
    gain_one = columns[32:33, :]
    gain_two = columns[33:34, :]
    r.need("turns")
    ring_o = Ring(
        at,
        lambda b: r.out_all.at[b // 2, aligned(lax.rem(b, 2), HEAD)],
        lambda b, part: r.out_all.at[b // 2, aligned(2 * lax.rem(b, 2) + part, 32)],
        r.o_send,
        r.o_recv,
        r.nm_all.at[pl.ds(0, 15 * HEAD)],
    )

    ring_c = whole_ring(at, r.cots, r.c_send, r.c_recv, r.cot)
    @pl.loop(0, CHIPS)
    def _(i):
        @pl.when(i == 1)
        def _():
            ring_h.pass_on(4)
            ring_h.pass_on(5)

        @pl.when(i == 2)
        def _():
            all_landed(r.row_dp.at[pl.ds(0, 6)], r.rd_recv.at[0], at)
            both = r.row_dp[...].astype(F32)
            r.wqkv_own[0:HEAD, :] = r.wq_all[0:HEAD, :]
            r.wqkv_own[HEAD : 2 * HEAD, :] = both[:, 0:8].reshape(HEAD, WIDTH).astype(BF)
            r.out_all[at.chip, aligned(at.core, HEAD), :] = (
                both[:, 8:16].reshape(HEAD, WIDTH).astype(BF)
            )
            ring_o.start()

        @pl.when(i == 4)
        def _():
            ring_c.start()

        @pl.when(i == 5)
        def _():
            ring_h.pass_on(6)
            ring_h.pass_on(7)

        @pl.when(i == 7)
        def _():
            for stream in first_expert:
                stream.from_across()

        ring_h.second(i)
        block = at.step(i)
        here = aligned(block, PAIR)
        hidden = r.hidden_all[here, :].astype(F32)
        inverse = lax.rsqrt(jnp.mean(hidden * hidden, axis=1, keepdims=True) + 1e-6)
        unit = (hidden * inverse * gain_one).astype(BF)
        r.normed[here, :] = unit
        table = r.turns[here, :]
        turned = lanes(table.shape) < HEAD
        cos = jnp.where(turned, table, 1.0)
        sin = jnp.where(turned, pltpu.roll(table, HEAD, 1), 0.0)
        projected = dot(unit, r.wqk[...])
        query, keyval = projected[:, 0:ROWS], projected[:, ROWS:PAIR]
        query = (query * cos + swapped(query) * sin).astype(BF)
        r.queries[here, :] = (query.astype(F32) * (1.0 / math.sqrt(HEAD))).astype(BF)
        keyval = keyval * cos + swapped(keyval) * sin
        later = pl.ds(pl.multiple_of(REACH + block * PAIR, ROWS), PAIR)
        r.keyvals[later, :] = keyval.astype(BF)
        r.keyvals_t[:, later] = keyval.T.astype(BF)

    r.save("normed")

    def att_copy(dest, src):
        return remote(
            r.att_src.at[dest],
            r.att_t.at[aligned(src, HEAD), :],
            r.a_send.at[0],
            r.a_recv.at[0],
            TP,
            dest,
        )

    @pl.loop(0, CHIPS)
    def _(i):
        @pl.when(i == 1)
        def _():
            for k in range(1, 4):
                ring_o.pass_on(k)

        @pl.when(i == 3)
        def _():
            for stream in first_expert:
                stream.from_y()

        @pl.when(i == 5)
        def _():
            ring_o.pass_on(4)
            ring_o.pass_on(5)

        block = at.chip_at(i + 1)
        here = aligned(block, PAIR)
        query = r.queries[here, :]
        start_row = r.starts[:, here]
        top = jnp.full((1, PAIR), LOWEST, F32)
        for chunk in range(SPAN // CHUNK):
            keys = pl.ds(pl.multiple_of(block * PAIR + chunk * CHUNK, ROWS), CHUNK)
            score = dot(r.keyvals[keys, :], query, NT)
            score = jnp.where(allowed(r.code[keys, :], start_row, chunk), score, LOWEST)
            r.scores[chunk * CHUNK : (chunk + 1) * CHUNK, :] = score
            top = jnp.maximum(top, jnp.max(score, axis=0, keepdims=True))
        total = jnp.zeros((1, PAIR), F32)
        for chunk in range(SPAN // CHUNK):
            place = slice(chunk * CHUNK, (chunk + 1) * CHUNK)
            weight = jnp.exp(r.scores[place, :] - top)
            total = total + jnp.sum(weight, axis=0, keepdims=True)
            r.weighted[place, 0:PAIR] = weight.astype(BF)
        window = pl.ds(pl.multiple_of(block * PAIR, ROWS), SPAN)
        head = dot(r.keyvals_t[HEAD : 2 * HEAD, window], r.weighted[0:SPAN, 0:PAIR]) / total
        r.heads_t[:, here] = head
        r.stats[:, here] = top + jnp.log(total)
        r.att_src[2 * block] = head[:, 0:ROWS].astype(BF)
        r.att_src[2 * block + 1] = head[:, ROWS:PAIR].astype(BF)

        @pl.when(i < CHIPS - 1)
        def _():
            att_copy(2 * block, t).start()
            att_copy(2 * block + 1, t).start()

        @pl.when(i == CHIPS - 1)
        def _():
            att_copy(at.twin, t).start()

    ring_c.pass_on(1)
    r.att_t[aligned(t, HEAD), :] = r.att_src[t]
    ring_o.pass_on(6)
    ring_o.pass_on(7)
    for stream in first_expert:
        stream.from_y_across()
    for i in range(CHIPS):
        ring_o.second(i)

    @pl.loop(0, 4)
    def _(j):
        sides = [
            r.out_all[:, pl.ds(pl.multiple_of(core * HEAD + j * 16, 16), 16), :].astype(F32)
            for core in range(2)
        ]
        first, second = unpacked(jnp.stack(sides, axis=1).reshape(TENSOR, 16, WIDTH))
        r.out_t[aligned(2 * j, ROWS), :] = first.astype(BF)
        r.out_t[aligned(2 * j + 1, ROWS), :] = second.astype(BF)

    r.save("out_t")
    all_landed(r.att_t.at[pl.ds(0, 15 * HEAD)], r.a_recv.at[0], at)
    attended = r.att_t[...].astype(F32).T.astype(BF)
    r.att_rows[...] = attended
    middle = r.hid[...].astype(F32) + dot(attended, r.out_t[...], NT)
    r.mid[...] = middle
    inverse = lax.rsqrt(jnp.mean(middle * middle, axis=1, keepdims=True) + 1e-6)
    r.nm_all[aligned(t, ROWS), :] = (middle * inverse * gain_two).astype(BF)
    ring = whole_ring(at, r.nm_all, r.g_send, r.g_recv)
    ring.start()
    for stream in second_expert:
        stream.start_x()
        stream.start_y()
    ring_c.pass_on(2)
    ring_c.pass_on(3)
    for stream in first_expert:
        stream.finish()
    copies.wait()
    ring_h.end()
    ring_o.end()
    r.finish("normed")
    r.finish("out_t")
    r.proj_grads, r.n_first, r.gates, r.n_sums = r.hidden_all, r.normed, r.turns, r.out_all
    r.m_sums = r.out_t


    def moe_sums(k, count=1):
        return r.m_sums.at[pl.ds(pl.multiple_of(k * ROWS, ROWS), count * ROWS)]

    halves_n = Halves(at, r.n_parts, r.n_twins, lambda k: r.n_sums.at[k], r.ntw_send, r.ntw_recv, r.n_credit)
    halves_m = Halves(at, r.m_parts, r.m_twins, moe_sums, r.mtw_send, r.mtw_recv, r.m_credit)
    joined = Joined(
        at,
        r.n_sums,
        r.n_crossed,
        r.n_landed,
        (r.nc_send, r.nc_recv, r.n_send, r.n_recv),
    )
    ring_w = whole_ring(at, r.wqkv, r.h_send, r.h_recv, r.wqkv_own)
    own_weights = copies.start(r.wqkv_own, r.wqkv.at[aligned(t, ROWS)])

    def moe_first():
        return remote(
            moe_sums(0, 2),
            r.m_landed.at[0],
            r.m_send.at[0],
            r.m_recv.at[0],
            TP,
            at.near_core(SUM_Z[0], 0),
        )

    def moe_along(j, part):
        number = 2 * j - 1 + part
        return remote(
            moe_sums(2 * j + part),
            r.m_landed.at[j, pl.ds(part * ROWS, ROWS)],
            r.m_send.at[number],
            r.m_recv.at[number],
            TP,
            at.near_core(SUM_Z[2 * j], 0),
        )

    def gu_over_y(e, k):
        y = at.y_at(k)
        return remote(
            r.gus.at[e, aligned(y, PAIR), :],
            r.y_gu.at[e, k - 1],
            r.x_send.at[4 * e + k],
            r.x_recv.at[4 * e + k],
            SP,
            2 * y + at.x,
        )

    def down_over_y(e, k):
        y = at.y_at(k)
        return remote(
            r.down_grads.at[e, :, aligned(y, PAIR)],
            r.y_down.at[e, k - 1],
            r.y_send.at[4 * e + k],
            r.y_recv.at[4 * e + k],
            SP,
            2 * y + at.x,
        )

    def across_x(number, src, dst):
        return remote(src, dst, r.tx_send.at[number], r.tx_recv.at[number], SP, at.across)

    def gu_half(part):
        rows = pl.ds(part * HEAD, HEAD)
        return remote(
            r.ys_gu.at[1, 1 - at.x, rows],
            r.yx_gu.at[1, rows],
            r.tx_send.at[1 + 3 * part],
            r.tx_recv.at[1 + 3 * part],
            SP,
            at.across,
        )

    def gu_across(e):
        return across_x(e, r.ys_gu.at[e, 1 - at.x], r.yx_gu.at[e])

    def down_across(e):
        return across_x(2 + e, r.ys_down.at[e, 1 - at.x], r.yx_down.at[e])

    def gate_copy(dest, src):
        return remote(
            r.gate_src.at[dest],
            r.gate_all.at[src],
            r.gg_send.at[0],
            r.gg_recv.at[0],
            TP,
            dest,
        )

    def one_pass(e):
        @pl.loop(0, CHIPS)
        def _(i):
            if e == 0:
                for k in range(2, CHIPS):

                    @pl.when(i == k - 1)
                    def _(k=k):
                        ring.pass_on(k)

                ring.second(i)

                @pl.when(i == 1)
                def _():
                    ring_c.pass_on(4)
                    ring_c.pass_on(5)

                @pl.when(i == 2)
                def _():
                    for stream in second_expert:
                        stream.from_across()

                @pl.when(i == 4)
                def _():
                    for stream in second_expert:
                        stream.from_y()

                @pl.when(i == 5)
                def _():
                    ring_c.pass_on(6)
                    ring_c.pass_on(7)

                ring_c.second(i)

                @pl.when(i == 6)
                def _():
                    ring_w.start()

                @pl.when(i == 7)
                def _():
                    for stream in second_expert:
                        stream.from_y_across()

            here = aligned(at.step(i) if e == 0 else at.sum_step(i), PAIR)
            nm = r.nm_all[here, :]
            place = lanes((PAIR, ROWS))
            if e == 0:
                expert = sublanes((ROWS, PAIR))
                named = expert == r.routes_t[0:1, here]
                for j in range(1, 8):
                    named = named | (expert == r.routes_t[j : j + 1, here])
                named = jnp.where(named, 1.0, 0.0).T > 0.5
                logits = jnp.where(named, dot(nm, r.small[...]), LOWEST)
                powers = jnp.exp(logits - jnp.max(logits, axis=1, keepdims=True))
                powers = jnp.where(named, powers, 0.0)
                gates = powers / jnp.sum(powers, axis=1, keepdims=True)
            else:
                kept = r.gates[here, :]
                gates = jnp.where(place == 2 * HEAD - 1, 0.0, kept)
                earlier = kept[:, 2 * HEAD - 1 : 2 * HEAD]
            mine = place == 2 * t + e
            gate = jnp.sum(jnp.where(mine, gates, 0.0), axis=1, keepdims=True)
            act_grad = dot(r.cots[here, :], r.downs[e * UNITS : (e + 1) * UNITS, :], NT)
            projected = dot(nm, r.gus[e])
            first, up = projected[:, :UNITS], projected[:, UNITS:]
            sigmoid = 1.0 / (1.0 + jnp.exp(-first))
            silu = first * sigmoid
            activated = silu * up
            gate_grad = jnp.sum(activated * act_grad, axis=1, keepdims=True)
            weighted = (activated * gate).astype(BF)
            r.weighted_t[:, here] = weighted.T
            act_grad = act_grad * gate
            r.proj_grads[here, 0:UNITS] = (
                act_grad * up * (sigmoid * (1.0 + first * (1.0 - sigmoid)))
            ).astype(BF)
            r.proj_grads[here, UNITS:WIDTH] = (act_grad * silu).astype(BF)
            normed_part = dot(r.proj_grads[here, :], r.gus[e], NT)
            if e == 0:
                r.gates[here, :] = jnp.where(place == 2 * HEAD - 1, gate_grad, gates)
                r.weighted[here, :] = weighted
                r.n_first[here, :] = normed_part.astype(BF)

                @pl.when(i == 0)
                def _():
                    ring.pass_on(1)

                return
            row = 2 * lax.rem(t, 4)
            gate_grads = jnp.where(
                place == row, earlier, jnp.where(place == row + 1, gate_grad, 0.0)
            ).T
            chip = at.sum_step(i)
            r.gate_src[2 * chip] = gate_grads[0:8, 0:ROWS]
            r.gate_src[2 * chip + 1] = gate_grads[0:8, ROWS:PAIR]

            @pl.when(i < CHIPS - 1)
            def _():
                gate_copy(2 * chip, t).start()
                gate_copy(2 * chip + 1, t).start()

            @pl.when(i == CHIPS - 1)
            def _():
                gate_copy(at.twin, t).start()

            halves_n.put(i, normed_part + r.n_first[here, :].astype(F32))
            both = jnp.concatenate([r.weighted[here, :], weighted], axis=1)
            halves_m.put(i, dot(both, r.downs[...]))

            @pl.when(i > 0)
            def _():
                halves_n.add(i - 1)
                halves_m.add(i - 1)

            for j in range(4):

                @pl.when(i == 2 * j + 1)
                def _(j=j):
                    joined.cross(j).start()

            for j in range(2):

                @pl.when(i == 2 * j + 4)
                def _(j=j):
                    joined.join(j)

            @pl.when(i == 2)
            def _():
                moe_first().start()

            for step, chips in ((0, (2, 3)), (2, (4, 5))):

                @pl.when(i == step)
                def _(chips=chips):
                    for k in chips:
                        ring_w.pass_on(k)

    def down_gradients(e):
        r.down_grads[e] = dot(r.weighted_t[...], r.cots[...]).astype(BF)

    def gate_up_gradients(e):
        @pl.loop(0, 2)
        def _(j):
            strip = aligned(j, 2 * PAIR)
            r.gus[e, strip, :] = dot(r.nm_all[:, strip], r.proj_grads[...], TN).astype(BF)

    one_pass(0)
    for stream in first_expert:
        stream.end()
    down_gradients(0)
    for k in range(1, 4):
        down_over_y(0, k).start()
    gate_up_gradients(0)
    ring_w.pass_on(1)
    for k in range(1, 4):
        gu_over_y(0, k).start()
    for stream in second_expert:
        stream.finish()
    one_pass(1)
    joined.join(2)
    halves_n.add(CHIPS - 1)
    halves_m.add(CHIPS - 1)
    def gu_loads(e):
        ref, first = (r.n_first, WIDTH) if e == 0 else (r.proj_grads, 0)
        places = [ref.at[pl.ds(first + k * PAIR, PAIR)] for k in range(3)]
        loads = []
        for k in range(3):
            gu_over_y(e, k + 1).wait_recv()
            loads.append(copies.start(r.y_gu.at[e, k], places[k]))
        return places, loads

    def gu_sums(e, places, loads):
        copies.need(*loads)
        total = r.gus[e, aligned(at.y, PAIR), :].astype(F32)
        for place in places:
            total = total + place[...].astype(F32)
        r.ys_gu[e, 0] = total[0:ROWS].astype(BF)
        r.ys_gu[e, 1] = total[ROWS:PAIR].astype(BF)
        (gu_half(0) if e else gu_across(0)).start()

    def down_loads(e):
        places = [
            r.weighted.at[pl.ds(k * UNITS, UNITS), pl.ds(e * PAIR, PAIR)] for k in range(3)
        ]
        loads = []
        for k in range(3):
            down_over_y(e, k + 1).wait_recv()
            loads.append(copies.start(r.y_down.at[e, k], places[k]))
        return places, loads

    def down_sums(e, places, loads):
        copies.need(*loads)
        total = r.down_grads[e, :, aligned(at.y, PAIR)].astype(F32)
        for place in places:
            total = total + place[...].astype(F32)
        r.ys_down[e, 0] = total[:, 0:ROWS].astype(BF)
        r.ys_down[e, 1] = total[:, ROWS:PAIR].astype(BF)
        down_across(e).start()

    out_rows = r.n_first.at[pl.ds(0, WIDTH)]
    out_load = copies.start(r.out_t_d, out_rows)
    for stream in second_expert:
        stream.end()
    down_gradients(1)
    for k in range(1, 4):
        down_over_y(1, k).start()
    gate_up_gradients(1)
    first_down, first_gu = down_loads(0), gu_loads(0)
    for k in range(1, 4):
        gu_over_y(1, k).start()
    r.gate_all[t] = r.gate_src[t]
    all_landed(r.gate_all.at[pl.ds(0, 15)], r.gg_recv.at[0], at)
    groups = r.gate_all[...].reshape(4, 4, 8, ROWS)
    gate_grads = (groups[:, 0] + groups[:, 1] + groups[:, 2] + groups[:, 3]).reshape(32, ROWS)
    gate_grads = jnp.concatenate([gate_grads, jnp.zeros((ROWS - 32, ROWS), F32)], axis=0).T
    own_rows = aligned(t, ROWS)
    gates = jnp.where(lanes((ROWS, ROWS)) < 32, r.gates[own_rows, :], 0.0)
    mean = jnp.sum(gates * gate_grads, axis=1, keepdims=True)
    logit_grad = gates * (gate_grads - mean)
    r.router_t[...] = dot(logit_grad.T.astype(BF), r.nm_all[own_rows, :])[0:32, :]
    by_router = dot(logit_grad.astype(BF), r.small[...], NT)

    gain_two = r.small[...].astype(F32).T[33:34, :]
    normed_grad = joined.result() + by_router
    middle = r.mid[...]
    inverse = lax.rsqrt(jnp.mean(middle * middle, axis=1, keepdims=True) + 1e-6)
    unit = middle * inverse
    r.gain_grad[...] = jnp.sum(normed_grad * unit, axis=0, keepdims=True)
    scaled = normed_grad * gain_two
    grad = r.cots[aligned(t, ROWS), :].astype(F32) + inverse * (
        scaled - unit * jnp.mean(scaled * unit, axis=1, keepdims=True)
    )
    r.mid_grad[...] = grad
    turned = grad.T.reshape(DP, TENSOR, 8, ROWS).transpose(1, 0, 2, 3)
    r.att_grad_t, r.mid_t = r.att_t, r.wqk.at[:, pl.ds(0, ROWS)]
    r.mid_t[...] = turned.reshape(WIDTH, ROWS).astype(BF)
    copies.need(out_load)
    r.att_grad_t[...] = dot(grad.astype(BF), out_rows[...]).T.astype(BF)

    def back_copy(k, src):
        dest = at.tensor_at(k)
        return remote(
            r.att_grad_t.at[aligned(dest, HEAD), :],
            r.grads.at[:, aligned(src, ROWS)],
            r.b_send.at[0],
            r.b_recv.at[0],
            TP,
            dest,
        )

    for k in range(1, TENSOR):
        back_copy(k, t).start()
    r.grads[:, aligned(t, ROWS)] = r.att_grad_t[aligned(t, HEAD), :]
    joined.end()
    r.n_sums[...] = (
        dot(r.mid_t[...], r.att_rows[...]).reshape(CHIPS, ROWS, WIDTH).astype(BF)
    )

    def out_half():
        return remote(
            r.n_sums.at[:, aligned(1 - at.core, HEAD), :],
            r.out_twins,
            r.ot_send.at[0],
            r.ot_recv.at[0],
            TP,
            at.twin,
        )

    out_half().start()
    r.kv_sum, r.query_src = r.gates, r.att_src
    r.tail_left = r.weighted_t.at[pl.ds(0, 3 * HEAD)]
    r.kv_sum[...] = jnp.zeros((LENGTH, 2 * HEAD), F32)
    all_sent(r.att_src.at[pl.ds(0, 15)], r.a_send.at[0], at)
    halves_n.end()
    halves_m.end()
    r.tail = r.n_parts.at[0]
    r.s_gu, r.m_joined = r.m_parts.at[0, pl.ds(0, ROWS)], r.m_parts.at[0, pl.ds(ROWS, ROWS)]

    down_sums(0, *first_down)
    gu_sums(0, *first_gu)
    normed_load = copies.start(r.normed_d, r.normed)

    def out_along(k):
        return remote(
            r.out_twins.at[pl.ds(2 * lax.rem(at.z + k, 4), 2)],
            r.out_landed.at[k - 1],
            r.oz_send.at[k],
            r.oz_recv.at[k],
            TP,
            at.near_core(k, 0),
        )

    def out_across():
        return remote(
            r.out_joined, r.out_crossed, r.oz_send.at[0], r.oz_recv.at[0], TP, at.near_core(0, 1)
        )

    out_half().wait_recv()
    r.out_twins[...] = (
        r.n_sums[:, aligned(at.core, HEAD), :].astype(F32) + r.out_twins[...].astype(F32)
    ).astype(BF)
    for k in range(1, 4):
        out_along(k).start()
    all_landed(r.grads.at[:, pl.ds(0, 15 * ROWS)], r.b_recv.at[0], at)
    r.need("cosine_t", "sine_t")

    def query_copy(dest, src):
        return remote(
            r.query_src.at[dest],
            r.query_all.at[src],
            r.qb_send.at[0],
            r.qb_recv.at[0],
            TP,
            dest,
        )

    @pl.loop(0, CHIPS)
    def _(i):
        block = at.chip_at(i + 1)
        here = aligned(block, PAIR)
        query = r.queries[here, :]
        start_row = r.starts[:, here]
        stat = r.stats[:, here]
        grad_t = jnp.concatenate([jnp.zeros((HEAD, PAIR), BF), r.grads[:, here]], axis=0)
        grad_rows = grad_t.astype(F32).T.astype(BF)
        head = r.heads_t[:, here]
        delta = jnp.sum(head * grad_t[HEAD : 2 * HEAD, :].astype(F32), axis=0, keepdims=True)
        query_grad = jnp.zeros((HEAD, PAIR), F32)
        for chunk in range(SPAN // CHUNK):
            keys = pl.ds(pl.multiple_of(block * PAIR + chunk * CHUNK, ROWS), CHUNK)
            both = r.keyvals[keys, :]
            score = dot(both, query, NT)
            ok = allowed(r.code[keys, :], start_row, chunk)
            prob = jnp.exp(jnp.where(ok, score - stat, LOWEST))
            prob_grad = dot(both, grad_t)
            score_grad = (prob * (prob_grad - delta)).astype(BF)
            update = dot(score_grad, query) + dot(prob.astype(BF), grad_rows)
            for part in range(CHUNK // ROWS):
                row = jnp.maximum(block * PAIR + (chunk * CHUNK + part * ROWS - REACH), 0)
                place = pl.ds(pl.multiple_of(row, ROWS), ROWS)
                r.kv_sum[place, :] += update[part * ROWS : (part + 1) * ROWS]

            query_grad = query_grad + dot(r.keyvals_t[0:HEAD, keys], score_grad)
        turned = turned_back(query_grad * (1.0 / math.sqrt(HEAD)), r, here).astype(BF)
        r.tail_left[0:HEAD, here] = turned
        r.query_src[2 * block] = turned[:, 0:ROWS]
        r.query_src[2 * block + 1] = turned[:, ROWS:PAIR]

        @pl.when(i < CHIPS - 1)
        def _():
            query_copy(2 * block, t).start()
            query_copy(2 * block + 1, t).start()

        @pl.when(i == CHIPS - 1)
        def _():
            query_copy(at.twin, t).start()

    @pl.loop(0, CHIPS)
    def _(i):
        here = aligned(i, PAIR)
        grad = r.kv_sum[here, :].T
        grad = jnp.concatenate(
            [turned_back(grad[0:HEAD], r, here), grad[HEAD : 2 * HEAD]], axis=0
        ).astype(BF)
        r.tail_left[HEAD : 3 * HEAD, here] = grad
        r.back_src[2 * i] = grad[:, 0:ROWS]
        r.back_src[2 * i + 1] = grad[:, ROWS:PAIR]

    def grad_copy(k, src):
        dest = at.tensor_at(k)
        return remote(
            r.back_src.at[dest],
            r.back_all.at[src],
            r.kb_send.at[0],
            r.kb_recv.at[0],
            TP,
            dest,
        )

    for k in range(1, TENSOR):
        grad_copy(k, t).start()
    r.back_all[t] = r.back_src[t]
    r.query_all[t] = r.query_src[t]
    for part in range(2):
        for j in (1, 2):
            moe_along(j, part).start()
    down_sums(1, *down_loads(1))
    landed = [
        [r.nm_all.at[pl.ds((2 * k + x) * HEAD, HEAD)] for x in range(2)] for k in range(3)
    ]
    ring.end()
    loads = []
    for k in range(3):
        out_along(k + 1).wait_recv()
        for x in range(2):
            loads.append(copies.start(r.out_landed.at[k, x], landed[k][x]))
    copies.need(*loads)

    def out_total(x):
        total = r.out_twins[2 * at.z + x].astype(F32)
        for k in range(3):
            rows = aligned(2 * k + x, HEAD)
            total = total + r.nm_all[rows, :].astype(F32)
        return total

    r.out_joined[...] = out_total(1 - at.x_far).astype(BF)
    out_across().start()
    for number in (6, 7):
        ring_w.pass_on(number)
    for i in range(CHIPS):
        ring_w.second(i)
    ring_c.end()
    copies.need(own_weights)
    weights_load = copies.start(r.wqkv, r.cots)
    copies.need(normed_load)
    r.tail[0 : 3 * HEAD, :] = dot(r.tail_left[...], r.normed[...]).astype(BF)

    copies.need(weights_load)
    whole = r.cots
    for j in range(4):
        rows = [
            whole[i * ROWS + HEAD + j * 16 : i * ROWS + HEAD + (j + 1) * 16, :].astype(F32)
            for i in range(TENSOR)
        ]
        first, second = unpacked(jnp.stack(rows, axis=0))
        r.downs[2 * j * ROWS : (2 * j + 1) * ROWS, :] = first.astype(BF)
        r.downs[(2 * j + 1) * ROWS : (2 * j + 2) * ROWS, :] = second.astype(BF)
    all_landed(r.query_all.at[pl.ds(0, 15)], r.qb_recv.at[0], at)
    all_landed(r.back_all.at[pl.ds(0, 15)], r.kb_recv.at[0], at)
    query_rows = r.query_all[...].astype(F32).reshape(WIDTH, ROWS).T.astype(BF)
    pairs = r.back_all[...].astype(F32).reshape(CHIPS, 2, ROWS, ROWS)
    kv_rows = (pairs[:, 0] + pairs[:, 1]).reshape(WIDTH, ROWS).T.astype(BF)
    wq_full = jnp.concatenate(
        [whole[i * ROWS : i * ROWS + HEAD, :] for i in range(TENSOR)], axis=0
    )
    normed_grad = dot(query_rows, wq_full) + dot(kv_rows, r.downs[...], NT)
    hidden = r.hid[...].astype(F32)
    inverse = lax.rsqrt(jnp.mean(hidden * hidden, axis=1, keepdims=True) + 1e-6)
    unit = hidden * inverse
    gain_one = r.small[...].astype(F32).T[32:33, :]
    gain_one_grad = jnp.sum(normed_grad * unit, axis=0, keepdims=True)
    scaled = normed_grad * gain_one
    r.hidden_grad[...] = (
        r.mid_grad[...]
        + inverse * (scaled - unit * jnp.mean(scaled * unit, axis=1, keepdims=True))
    ).astype(BF)
    r.save("hidden_grad")
    r.tail[3 * HEAD : 3 * HEAD + 32, :] = r.router_t[...].astype(BF)
    row = sublanes((16, WIDTH))
    r.tail[3 * HEAD + 32 : TAIL, :] = jnp.where(
        row == 0, gain_one_grad, jnp.where(row == 1, r.gain_grad[...], 0.0)
    ).astype(BF)

    def tail_along(k):
        y = at.y_at(k)
        return remote(
            r.tail.at[pl.ds(0, TAIL), aligned(y, PAIR)],
            r.tail_in.at[k - 1],
            r.t_send.at[k],
            r.t_recv.at[k],
            SP,
            2 * y + at.x,
        )

    def tail_across():
        return remote(r.tail_src, r.tail_x, r.t_send.at[0], r.t_recv.at[0], SP, at.across)

    for k in range(1, 4):
        tail_along(k).start()

    gu_sums(1, *gu_loads(1))
    out_across().wait_recv()
    crossed = r.proj_grads.at[pl.ds(6 * PAIR, HEAD)]
    copies.need(copies.start(r.out_crossed, crossed))
    r.out_rows[...] = out_total(at.x_far) + crossed[...].astype(F32)

    def out_dp_along(k):
        y = at.y_at(k)
        return remote(
            r.out_rows.at[aligned(y, 16), :],
            r.out_in.at[k - 1],
            r.od_send.at[k],
            r.od_recv.at[k],
            SP,
            2 * y + at.x,
        )

    def out_dp_across():
        return remote(
            r.out_sum.at[aligned(1 - at.x, 8), :],
            r.out_x,
            r.od_send.at[0],
            r.od_recv.at[0],
            SP,
            at.across,
        )

    for k in range(1, 4):
        out_dp_along(k).start()
    def moe_across():
        return remote(
            r.m_joined, r.m_crossed, r.mx_send.at[0], r.mx_recv.at[0], TP, at.near_core(0, 1)
        )

    moe_first().wait_recv()
    across = moe_sums(6)[...].astype(F32) + r.m_landed[0, 0:ROWS].astype(F32)
    for j in (1, 2):
        moe_along(j, 0).wait_recv()
        across = across + r.m_landed[j, 0:ROWS].astype(F32)
    r.m_joined[...] = across.astype(BF)
    moe_across().start()
    loads, crossed = [], []
    for e in range(2):
        down_across(e).wait_recv()
        crossed.append(r.weighted.at[pl.ds(3 * UNITS, UNITS), pl.ds(e * ROWS, ROWS)])
        loads.append(copies.start(r.yx_down.at[e], crossed[-1]))
    gu_across(0).wait_recv()
    crossed.append(r.nm_all.at[pl.ds(WIDTH, ROWS)])
    loads.append(copies.start(r.yx_gu.at[0], crossed[-1]))
    copies.need(*loads)
    for e in range(2):
        r.down_out[e] = r.ys_down[e, at.x].astype(F32) + crossed[e][...].astype(F32)
    r.mid_grad[...] = r.ys_gu[0, at.x].astype(F32) + crossed[2][...].astype(F32)
    copies.start(r.mid_grad, r.gu_out.at[0])
    r.save("down_out")
    total = r.tail[0:TAIL, aligned(at.y, PAIR)].astype(F32)
    for k in range(1, 4):
        tail_along(k).wait_recv()
        total = total + r.tail_in[k - 1].astype(F32)
    r.scores[0:TAIL, :] = total
    r.tail_src[...] = r.scores[0:TAIL, aligned(1 - at.x, ROWS)].astype(BF)
    tail_across().start()
    gu_half(1).start()
    total = r.out_rows[aligned(at.y, 16), :]
    for k in range(1, 4):
        out_dp_along(k).wait_recv()
        total = total + r.out_in[k - 1]
    r.out_sum[...] = total
    out_dp_across().start()
    tail_across().wait_recv()
    total = r.scores[0:TAIL, aligned(at.x, ROWS)] + r.tail_x[...].astype(F32)
    r.query_out[...] = total[0:HEAD, :]
    r.save("query_out")
    turned = jnp.concatenate(
        [total[HEAD:TAIL], jnp.zeros((256 + HEAD - TAIL, ROWS), F32)], axis=0
    ).T
    for j in range(TENSOR):
        r.pieces[j] = turned[j * 8 : (j + 1) * 8, :]

    def last_copy(k, src):
        dest = at.tensor_at(k)
        return remote(
            r.pieces.at[dest], r.last.at[src], r.l_send.at[0], r.l_recv.at[0], TP, dest
        )

    for k in range(1, TENSOR):
        last_copy(k, t).start()
    r.last[t] = r.pieces[t]

    own = r.mid[...] + moe_sums(7)[...].astype(F32) + r.m_landed[0, ROWS:PAIR].astype(F32)
    for j in (1, 2):
        moe_along(j, 1).wait_recv()
        own = own + r.m_landed[j, ROWS:PAIR].astype(F32)
    place = r.nm_all.at[pl.ds(WIDTH + PAIR, ROWS)]
    moe_across().wait_recv()
    copies.need(copies.start(r.m_crossed, place))
    r.output[...] = (own + place[...].astype(F32)).astype(BF)
    r.save("output")
    for part in range(2):
        gu_half(part).wait_recv()
    place = r.nm_all.at[pl.ds(WIDTH + ROWS, ROWS)]
    copies.need(copies.start(r.yx_gu.at[1], place))
    r.mid[...] = r.ys_gu[1, at.x].astype(F32) + place[...].astype(F32)
    copies.start(r.mid, r.gu_out.at[1])
    out_dp_across().wait_recv()
    r.out_grad[...] = r.out_sum[aligned(at.x, 8), :] + r.out_x[...]
    all_landed(r.last.at[pl.ds(0, 15)], r.l_recv.at[0], at)
    r.kv_out[...] = jnp.concatenate(
        [r.last[2 * j, :, 0:ROWS] + r.last[2 * j + 1, :, 0:ROWS] for j in range(CHIPS)], axis=1
    )
    shared = r.last[0, :, ROWS:PAIR]
    for j in range(1, TENSOR):
        shared = shared + r.last[j, :, ROWS:PAIR]
    r.router_out[...] = shared[:, 0:32]
    wide = jnp.concatenate([shared, jnp.zeros((ROWS - 8, ROWS), F32)], axis=0).T
    r.gain_one_out[...] = wide[32:33, 0:8]
    r.gain_two_out[...] = wide[33:34, 0:8]
    r.save("out_grad", "kv_out", "router_out", "gain_one_out", "gain_two_out")

    all_sent(r.tiles.at[pl.ds(0, 15)], r.t1_send.at[0], at)
    all_sent(r.tile_all.at[pl.ds(0, 7)], r.t2_send.at[0], at)
    all_sent(r.row_dp.at[pl.ds(0, 7)], r.rd_send.at[0], at)
    all_sent(seven_wq, r.wq_send.at[0], at)
    all_sent(r.gate_src.at[pl.ds(0, 15)], r.gg_send.at[0], at)
    all_sent(r.att_grad_t.at[pl.ds(0, 15 * HEAD)], r.b_send.at[0], at)
    all_sent(r.query_src.at[pl.ds(0, 15)], r.qb_send.at[0], at)
    all_sent(r.back_src.at[pl.ds(0, 15)], r.kb_send.at[0], at)
    all_sent(r.pieces.at[pl.ds(0, 15)], r.l_send.at[0], at)
    for k in range(1, 4):
        tail_along(k).wait_send()
        out_dp_along(k).wait_send()
    tail_across().wait_send()
    out_dp_across().wait_send()
    moe_first().wait_send()
    for j in (1, 2):
        for part in range(2):
            moe_along(j, part).wait_send()
    moe_across().wait_send()
    for k in range(1, 4):
        out_along(k).wait_send()
    out_across().wait_send()
    out_half().wait_send()
    for e in range(2):
        for k in range(1, 4):
            gu_over_y(e, k).wait_send()
            down_over_y(e, k).wait_send()
        gu_half(e).wait_send()
        down_across(e).wait_send()
    gu_across(0).wait_send()
    ring_w.end()
    copies.wait()
    r.end()


def store_kernel(r):
    copies = Copies(r.local)
    for name in STORED:
        copies.start(getattr(r, name), getattr(r, name + "_kept"))
    for name in STORED:
        copies.wait(1)
        copies.start(getattr(r, name + "_kept"), getattr(r, name + "_done"))
    copies.wait()


STORED = (
    "output",
    "hidden_grad",
    "gain_one_out",
    "query_out",
    "kv_out",
    "out_grad",
    "gain_two_out",
    "router_out",
    "gu_out",
    "down_out",
)


class Refs:
    def __init__(self, names, refs, loads=(), saves=()):
        for name, ref in zip(names, refs):
            setattr(self, name, ref)
        self.loads, self.saves, self.saved = list(loads), list(saves), []

    def copy_in(self, name):
        sem = self.load_sems.at[self.loads.index(name)]
        return pltpu.make_async_copy(getattr(self, name + "_d"), getattr(self, name), sem)

    def copy_out(self, name):
        sem = self.save_sems.at[self.saves.index(name)]
        return pltpu.make_async_copy(getattr(self, name), getattr(self, name + "_d"), sem)

    def load(self):
        for name in self.loads:
            self.copy_in(name).start()

    def need(self, *names):
        for name in names:
            self.copy_in(name).wait()

    def save(self, *names):
        for name in names:
            self.copy_out(name).start()
            self.saved.append(name)

    def finish(self, name):
        self.copy_out(name).wait()
        self.saved.remove(name)

    def end(self):
        for name in self.saved:
            self.copy_out(name).wait()


def call(kernel, number, inputs, outputs, scratch, reaches=True):
    def space(name):
        return pl.BlockSpec(memory_space=pltpu.VMEM if name.endswith("_v") else pl.ANY)

    outputs = {name: jax.ShapeDtypeStruct(shape, dtype) for name, (shape, dtype) in outputs.items()}
    loads = [name[:-2] for name in inputs if name.endswith("_d")]
    saves = [name[:-2] for name in outputs if name.endswith("_d")]
    scratch = dict(scratch)
    for name in loads:
        scratch[name] = pltpu.VMEM(inputs[name + "_d"].shape, inputs[name + "_d"].dtype)
    for name in saves:
        scratch[name] = pltpu.VMEM(outputs[name + "_d"].shape, outputs[name + "_d"].dtype)
    scratch |= sems(load_sems=max(1, len(loads)), save_sems=max(1, len(saves)))
    names = [name.removesuffix("_v") for name in (*inputs, *outputs)] + list(scratch)
    params = {"vmem_limit_bytes": VMEM_BYTES}
    if reaches:
        params |= {"collective_id": number, "has_side_effects": True}
    values = pl.pallas_call(
        lambda *refs: kernel(Refs(names, refs, loads, saves)),
        out_shape=list(outputs.values()),
        in_specs=[space(name) for name in inputs],
        out_specs=[space(name) for name in outputs],
        scratch_shapes=list(scratch.values()),
        compiler_params=pltpu.CompilerParams(**params),
        name=kernel.__name__,
    )(*inputs.values())
    return Refs([name.removesuffix("_v").removesuffix("_d") for name in outputs], values)


def sems(**counts):
    return {name: pltpu.SemaphoreType.DMA((count,)) for name, count in counts.items()}


def rope_tables():
    half = HEAD // 2
    freqs = np.exp(
        np.arange(half, dtype=np.float32) * np.float32(-2.0 * math.log(10000.0) / HEAD)
    ).astype(np.float32)
    angles = np.arange(LENGTH, dtype=np.float32)[:, None] * freqs[None, :]
    cos, sin = np.cos(angles).astype(np.float32), np.sin(angles).astype(np.float32)
    return (
        np.concatenate([cos, cos, -sin, sin], axis=1),
        np.ascontiguousarray(cos.T),
        np.ascontiguousarray(sin.T),
    )


def body(
    hidden,
    seg_ids,
    key_mask,
    routes,
    gain_attn,
    w_query,
    w_keyval,
    w_out,
    gain_mlp,
    w_router,
    w_gate_up,
    w_down,
    cotangent,
):
    V = pltpu.VMEM
    turns, cosine_t, sine_t = rope_tables()
    hid, cot = hidden[0], cotangent[0]
    c = call(
        layer_kernel,
        1,
        dict(
            hid_v=hid,
            cot=cot,
            w_keyval_v=w_keyval,
            w_out_t_v=w_out.T,
            w_query_t_v=w_query.T,
            router_v=w_router,
            gain_one_v=gain_attn.reshape(1, 8),
            gain_two_v=gain_mlp.reshape(1, 8),
            gu=w_gate_up,
            down=w_down,
            turns_d=turns,
            cosine_t_d=cosine_t,
            sine_t_d=sine_t,
            mask_v=key_mask,
            seg_v=seg_ids,
            routes_t_v=routes[0].T,
        ),
        dict(
            output_d=((ROWS, WIDTH), BF),
            hidden_grad_d=((ROWS, WIDTH), BF),
            gain_one_out_d=((1, 8), F32),
            query_out_d=((HEAD, ROWS), F32),
            kv_out_d=((8, WIDTH), F32),
            out_grad_d=((8, WIDTH), F32),
            gain_two_out_d=((1, 8), F32),
            router_out_d=((8, 32), F32),
            gu_out=((2, ROWS, WIDTH), F32),
            down_out_d=((2, UNITS, ROWS), F32),
            normed_d=((LENGTH, WIDTH), BF),
            out_t_d=((WIDTH, WIDTH), BF),
            wqkv=((LENGTH, WIDTH), BF),
            y_gu=((2, 3, PAIR, WIDTH), BF),
            y_down=((2, 3, UNITS, PAIR), BF),
            yx_gu=((2, ROWS, WIDTH), BF),
            yx_down=((2, UNITS, ROWS), BF),
            out_landed=((3, 2, HEAD, WIDTH), BF),
            out_crossed=((HEAD, WIDTH), BF),
            m_crossed=((ROWS, WIDTH), BF),
        ),
        dict(
            hidden_all=V((LENGTH, WIDTH), BF),
            nm_all=V((LENGTH, WIDTH), BF),
            cots=V((LENGTH, WIDTH), BF),
            gus=V((2, WIDTH, WIDTH), BF),
            downs=V((WIDTH, WIDTH), BF),
            down_grads=V((2, UNITS, WIDTH), BF),
            weighted=V((LENGTH, UNITS), BF),
            weighted_t=V((UNITS, LENGTH), BF),
            queries=V((LENGTH, 2 * HEAD), BF),
            keyvals=V((PADDED, 2 * HEAD), BF),
            keyvals_t=V((2 * HEAD, PADDED), BF),
            stats=V((1, LENGTH), F32),
            heads_t=V((HEAD, LENGTH), F32),
            small=V((WIDTH, ROWS), BF),
            mid=V((ROWS, WIDTH), F32),
            mid_grad=V((ROWS, WIDTH), F32),
            router_t=V((32, WIDTH), F32),
            gain_grad=V((1, WIDTH), F32),
            wqkv_own=V((ROWS, WIDTH), BF),
            rows=V((16, WIDTH), BF),
            row_dp=V((DP, 16, WIDTH), BF),
            shares=V((8, ROWS), F32),
            tiles=V((TENSOR, 16, ROWS), BF),
            tile_all=V((DP, TENSOR, 16, ROWS), BF),
            out_all=V((CHIPS, ROWS, WIDTH), BF),
            wq_all=V((2 * HEAD, WIDTH), BF),
            code=V((PADDED, ROWS), F32),
            scores=V((SPAN, PAIR), F32),
            starts=V((1, LENGTH), F32),
            wqk=V((WIDTH, PAIR), BF),
            att_src=V((TENSOR, HEAD, ROWS), BF),
            att_t=V((WIDTH, ROWS), BF),
            att_rows=V((ROWS, WIDTH), BF),
            ys_gu=V((2, 2, ROWS, WIDTH), BF),
            ys_down=V((2, 2, UNITS, ROWS), BF),
            n_parts=V((SLOTS, PAIR, WIDTH), BF),
            n_twins=V((SLOTS, ROWS, WIDTH), BF),
            n_credit=pltpu.SemaphoreType.REGULAR,
            n_crossed=V((4, ROWS, WIDTH), BF),
            n_landed=V((3, ROWS, WIDTH), BF),
            m_parts=V((SLOTS, PAIR, WIDTH), BF),
            m_twins=V((SLOTS, ROWS, WIDTH), BF),
            m_credit=pltpu.SemaphoreType.REGULAR,
            m_landed=V((3, PAIR, WIDTH), BF),
            gate_src=V((TENSOR, 8, ROWS), F32),
            gate_all=V((TENSOR, 8, ROWS), F32),
            grads=V((HEAD, LENGTH), BF),
            query_all=V((TENSOR, HEAD, ROWS), BF),
            back_src=V((TENSOR, ROWS, ROWS), BF),
            back_all=V((TENSOR, ROWS, ROWS), BF),
            out_twins=V((CHIPS, HEAD, WIDTH), BF),
            out_joined=V((HEAD, WIDTH), BF),
            out_rows=V((HEAD, WIDTH), F32),
            out_in=V((3, 16, WIDTH), F32),
            out_sum=V((16, WIDTH), F32),
            out_x=V((8, WIDTH), F32),
            tail_in=V((3, TAIL, PAIR), BF),
            tail_src=V((TAIL, ROWS), BF),
            tail_x=V((TAIL, ROWS), BF),
            pieces=V((TENSOR, 8, PAIR), F32),
            last=V((TENSOR, 8, PAIR), F32),
        )
        | sems(
            h_send=1,
            h_recv=24,
            c_send=1,
            c_recv=24,
            o_send=1,
            o_recv=24,
            g_send=1,
            g_recv=24,
            t1_send=1,
            t1_recv=1,
            t2_send=1,
            t2_recv=1,
            t2x_recv=1,
            rdx_recv=1,
            rd_send=1,
            rd_recv=1,
            wq_send=1,
            wq_recv=1,
            e_send=4,
            e_recv=40,
            a_send=1,
            a_recv=1,
            ntw_send=SLOTS,
            ntw_recv=SLOTS,
            nc_send=4,
            nc_recv=4,
            n_send=3,
            n_recv=3,
            mtw_send=SLOTS,
            mtw_recv=SLOTS,
            m_send=5,
            m_recv=5,
            mx_send=1,
            mx_recv=1,
            gg_send=1,
            gg_recv=1,
            b_send=1,
            b_recv=1,
            ot_send=1,
            ot_recv=1,
            oz_send=4,
            oz_recv=4,
            qb_send=1,
            qb_recv=1,
            kb_send=1,
            kb_recv=1,
            x_send=8,
            x_recv=8,
            y_send=8,
            y_recv=8,
            tx_send=5,
            tx_recv=5,
            t_send=4,
            t_recv=4,
            od_send=4,
            od_recv=4,
            l_send=1,
            l_recv=1,
            local=20,
        ),
    )
    values = {name: getattr(c, name) for name in STORED}
    done = call(
        store_kernel,
        0,
        values,
        {name + "_done": (value.shape, value.dtype) for name, value in values.items()},
        {name + "_kept": V(value.shape, value.dtype) for name, value in values.items()}
        | sems(local=2 * len(STORED)),
        reaches=False,
    )
    return (
        done.output_done[None],
        done.hidden_grad_done[None],
        done.gain_one_out_done.reshape(8),
        done.query_out_done.T,
        done.kv_out_done,
        done.out_grad_done.T,
        done.gain_two_out_done.reshape(8),
        done.router_out_done,
        done.gu_out_done,
        done.down_out_done,
    )


def solution(mesh):
    return jax.shard_map(
        body,
        mesh=mesh,
        in_specs=(
            P("dp", "tensor", None),
            P("dp", None),
            P("dp", None),
            P("dp", None, None),
            P(("dp", "tensor")),
            P("dp", "tensor"),
            P(("dp", "tensor"), None),
            P(None, ("dp", "tensor")),
            P(("dp", "tensor")),
            P(("dp", "tensor"), None),
            P("tensor", "dp", None),
            P("tensor", None, "dp"),
            P("dp", "tensor", None),
        ),
        out_specs=(
            P("dp", "tensor", None),
            P("dp", "tensor", None),
            P(("dp", "tensor")),
            P("dp", "tensor"),
            P(("dp", "tensor"), None),
            P(None, ("dp", "tensor")),
            P(("dp", "tensor")),
            P(("dp", "tensor"), None),
            P("tensor", "dp", None),
            P("tensor", None, "dp"),
        ),
        check_vma=False,
    )
```
